32 devices in a mesh: seq: 2 (over y), ctx: 4 (over x, core), exp: 4 (over z).
Axes of the slice: x: 2, y: 2, z: 4, core: 2. Of those that a mesh axis runs over, the one named last changes fastest.
Arguments:
- tokens: bfloat16 [8, 1024, 768], P(('seq', 'exp'), 'ctx'), may hold values from -6 to 6
- expert_ids: int32 [8, 1024, 2], P(('seq', 'exp'), 'ctx'), may hold values from 0 to 3, all different within a row; in each aligned block of 256 rows (0 to 255, 256 to 511, ..., all dimensions but the last counted through in order) at most 256 rows name the same one
- norm_one: float32 [768], replicated, may hold values from 0.5 to 1.5
- w_query: bfloat16 [768, 768], replicated, may hold values from -0.21875 to 0.21875
- w_key: bfloat16 [768, 768], replicated, may hold values from -0.21875 to 0.21875
- w_value: bfloat16 [768, 768], replicated, may hold values from -0.21875 to 0.21875
- w_out: bfloat16 [768, 768], replicated, may hold values from -1.75 to 1.75
- norm_two: float32 [768], replicated, may hold values from 0.5 to 1.5
- w_router: bfloat16 [768, 4], replicated, may hold values from -0.21875 to 0.21875
- expert_gate: bfloat16 [4, 768, 2048], P('exp'), may hold values from -0.21875 to 0.21875
- expert_up: bfloat16 [4, 768, 2048], P('exp'), may hold values from -0.21875 to 0.21875
- expert_down: bfloat16 [4, 2048, 768], P('exp'), may hold values from -0.125 to 0.125
- shared_gate: bfloat16 [768, 2048], replicated, may hold values from -0.21875 to 0.21875
- shared_up: bfloat16 [768, 2048], replicated, may hold values from -0.21875 to 0.21875
- shared_down: bfloat16 [2048, 768], replicated, may hold values from -0.125 to 0.125
- cotangent: bfloat16 [8, 1024, 768], P(('seq', 'exp'), 'ctx'), may hold values from -6 to 6
Outputs:
- output: bfloat16 [8, 1024, 768], P(('seq', 'exp'), 'ctx')
- grad_tokens: float32 [8, 1024, 768], P(('seq', 'exp'), 'ctx')
- grad_norm_one: float32 [768], replicated
- grad_query: float32 [768, 768], P(('seq', 'ctx'), 'exp')
- grad_key: float32 [768, 768], P(('seq', 'ctx'), 'exp')
- grad_value: float32 [768, 768], P(('seq', 'ctx'), 'exp')
- grad_out: float32 [768, 768], P(('seq', 'ctx'), 'exp')
- grad_norm_two: float32 [768], replicated
- grad_router: float32 [768, 4], P(('seq', 'ctx'), 'exp')
- grad_expert_gate: float32 [4, 768, 2048], P('exp')
- grad_expert_up: float32 [4, 768, 2048], P('exp')
- grad_expert_down: float32 [4, 2048, 768], P('exp')
- grad_shared_gate: float32 [768, 2048], P(('seq', 'ctx'), 'exp')
- grad_shared_up: float32 [768, 2048], P(('seq', 'ctx'), 'exp')
- grad_shared_down: float32 [2048, 768], P(('seq', 'ctx'), 'exp')
The draws below stay inside these ranges and needn't reach their ends.
Inputs may be any that keep to these rules, and one draw needn't show every extreme that they name: `expert_ids`: each token names 2 different experts; the tokens of one device name no expert more than 256 times, and on some device some expert is named exactly 256 times.
All inputs are finite; a program needn't handle non-finite values.
Results may differ from the reference program's by a relative error of at most 0.024.
Values may be sent and summed in bfloat16 or wider, within the bound.
A program may use at most 192 MiB of HBM per device.

```python
import math
import jax
import jax.numpy as jnp
import numpy as np
from jax import lax

D = 768
HEADS = 12
HEAD_DIM = 64
FF = 2048
SHARED_FF = 2048
TOP = 2
BLOCK = 256
KEY_ROWS = 512
TOKENS_DEV = 256
LENGTH = 1024
BATCH = 8
EXPERTS = 4
CAP = 256


def steps_of(stream_key, extent, split, smallest, high):
    gain, own = 1.0, jax.random.fold_in(stream_key, 6)
    for dim, blocks in split:
        draws = jnp.exp(jax.random.uniform(jax.random.fold_in(own, dim), (blocks,), jnp.float32, smallest / len(split), high / len(split)))
        gain = gain * jnp.repeat(draws, extent[dim] // blocks).reshape([-1 if axis == dim else 1 for axis in range(len(extent))])
    return gain


def deal_out(stream_key, own, number, rows, amount, top, reach, slope):
    ranking = jax.random.permutation(stream_key, amount)
    crowded, ordinary = load_shares(amount, rows * top, reach, slope, True), load_shares(amount, rows * top, reach, slope, False)
    places = jnp.arange(amount)

    def named(tallies, offset_by):
        used = int((tallies > 0).sum())
        fixed = max(1, used // 4)
        shifted = fixed + (places - fixed + offset_by * (used - fixed)) % max(1, amount - fixed)
        return jnp.zeros((amount,), jnp.int32).at[ranking[jnp.where(places < fixed, places, shifted)]].set(jnp.asarray(tallies, jnp.int32))

    tallies = jnp.where(number % 4 == 0, named(crowded, number // 4), named(ordinary, number - number // 4 - 1))
    mixed = jax.random.permutation(jax.random.fold_in(own, 3), amount)
    donor, sink = mixed[0:amount // 2 * 2:2], mixed[1:amount // 2 * 2:2]
    slack = jnp.minimum(tallies[donor] - 1, reach - tallies[sink]) // 2
    slack = jnp.where((donor == ranking[0]) | (sink == ranking[0]) | (tallies[sink] == 0), 0, jnp.maximum(slack, 0))
    shifted = jax.random.randint(jax.random.fold_in(own, 4), (amount // 2,), 0, 1 << 20) % (slack + 1)
    tallies = tallies.at[donor].add(-shifted).at[sink].add(shifted)
    items = jnp.searchsorted(jnp.cumsum(tallies), jnp.arange(rows * top), side="right").astype(jnp.int32)
    grid = items.reshape(top, rows).T
    grid = grid[jax.random.permutation(jax.random.fold_in(own, 1), rows)]
    offset_by = jax.random.randint(jax.random.fold_in(own, 2), (rows, 1), 0, top)
    return jnp.take_along_axis(grid, (jnp.arange(top)[None, :] + offset_by) % top, axis=1)


def load_shares(number_of, total, most, slope, full):
    weights = [(1 << 20) // math.isqrt(rank ** slope) + 1 for rank in range(1, number_of + 1)]
    largest = most if full else min(most, max(-(-total // number_of), total * weights[0] // sum(weights)))
    least = 1 if total - largest >= number_of - 1 else 0
    holding, spare = [largest] + [least] * (number_of - 1), total - largest - least * (number_of - 1)
    while spare > 0:
        movable = [i for i in range(1, number_of) if holding[i] < largest] or [i for i in range(1, number_of) if holding[i] < most]
        pool, remaining = sum([weights[i] for i in movable]), spare
        for i in movable:
            extra = min(most - holding[i], max(1, remaining * weights[i] // pool), spare)
            holding[i] = holding[i] + extra
            spare = spare - extra
    return np.array(holding)


def normal_values(own_key, dims, scale, reach, pieces=(), held_as=jnp.bfloat16):
    values = scale * jax.random.normal(own_key, dims, jnp.float32)
    if pieces:
        values = values * steps_of(own_key, dims, pieces, -0.22, 0.18)
    return jnp.clip(values, -reach, reach).astype(held_as)


def setup_inputs(seed: int = 0) -> dict:
    key_list = jax.random.split(jax.random.key(seed), 17)
    tokens = normal_values(key_list[0], (BATCH, LENGTH, D), 1.0, 6.0, ((0, 8), (1, 4)))
    expert_ids_keys = jax.random.split(jax.random.fold_in(key_list[1], 1), BATCH * LENGTH // TOKENS_DEV)
    expert_ids_turns = jax.random.permutation(jax.random.fold_in(key_list[1], 3), BATCH * LENGTH // TOKENS_DEV)
    expert_ids = jax.vmap(lambda own, number: deal_out(jax.random.fold_in(key_list[1], 2), own, number, TOKENS_DEV, EXPERTS, TOP, CAP, 1))(expert_ids_keys, expert_ids_turns).reshape((BATCH, LENGTH, TOP))
    norm_one = jnp.clip(1.0 + 0.1 * jax.random.normal(key_list[2], (D,), jnp.float32), 0.5, 1.5)
    w_query = normal_values(key_list[3], (D, D), D ** -0.5, 0.21875)
    w_key = normal_values(key_list[4], (D, D), D ** -0.5, 0.21875)
    w_value = normal_values(key_list[5], (D, D), D ** -0.5, 0.21875)
    w_out = normal_values(key_list[6], (D, D), (max(1, D * 16 // LENGTH)) ** -0.5, 1.75)
    norm_two = jnp.clip(1.0 + 0.1 * jax.random.normal(key_list[7], (D,), jnp.float32), 0.5, 1.5)
    w_router = normal_values(key_list[8], (D, EXPERTS), D ** -0.5, 0.21875)
    expert_gate = normal_values(key_list[9], (EXPERTS, D, FF), D ** -0.5, 0.21875, ((0, 4),))
    expert_up = normal_values(key_list[10], (EXPERTS, D, FF), D ** -0.5, 0.21875, ((0, 4),))
    expert_down = normal_values(key_list[11], (EXPERTS, FF, D), FF ** -0.5, 0.125, ((0, 4),))
    shared_gate = normal_values(key_list[12], (D, SHARED_FF), D ** -0.5, 0.21875)
    shared_up = normal_values(key_list[13], (D, SHARED_FF), D ** -0.5, 0.21875)
    shared_down = normal_values(key_list[14], (SHARED_FF, D), SHARED_FF ** -0.5, 0.125)
    cotangent = normal_values(key_list[15], (BATCH, LENGTH, D), 1.0, 6.0, ((0, 8), (1, 4)))
    return {"tokens": tokens, "expert_ids": expert_ids, "norm_one": norm_one, "w_query": w_query, "w_key": w_key, "w_value": w_value, "w_out": w_out, "norm_two": norm_two, "w_router": w_router, "expert_gate": expert_gate, "expert_up": expert_up, "expert_down": expert_down, "shared_gate": shared_gate, "shared_up": shared_up, "shared_down": shared_down, "cotangent": cotangent}


@jax.custom_vjp
def low(v):
    return lax.optimization_barrier(v.astype(jnp.bfloat16)).astype(jnp.float32)

@jax.custom_vjp
def low_back(v):
    return v

def low_keep(v):
    return (low(v), None)

def low_pass(kept, grad):
    return (grad,)

def back_keep(v):
    return (v, None)

def back_low(kept, grad):
    return (low(grad),)
low.defvjp(low_keep, low_pass)
low_back.defvjp(back_keep, back_low)

def product(first_factor, second_factor):
    return jnp.dot(first_factor, second_factor, precision=lax.Precision.HIGHEST, preferred_element_type=jnp.float32)

def normalize(values, scaling):
    return values * lax.rsqrt(lax.optimization_barrier(jnp.mean(values * values, axis=-1, keepdims=True)) + 1e-06) * scaling

def rotate(values, places):
    halfway = values.shape[-1] // 2
    frequency = 10000.0 ** (-jnp.arange(halfway, dtype=jnp.float32) / halfway)
    angles = places.astype(jnp.float32)[:, None] * frequency[None, :]
    cosine = jnp.cos(angles)[:, None, :]
    sine_part = jnp.sin(angles)[:, None, :]
    former = values[..., :halfway]
    latter = values[..., halfway:]
    return jnp.concatenate([former * cosine - latter * sine_part, latter * cosine + former * sine_part], axis=-1)

def attend_sequence(query, keys, values):
    length = query.shape[0]
    query_rows = min(KEY_ROWS, length)
    key_blocks = jnp.arange(length) // BLOCK

    def one_block(operands):
        query_part, offset = operands
        scores = low_back(jnp.einsum('qhd,khd->hqk', query_part, keys, precision=lax.Precision.HIGHEST) * HEAD_DIM ** (-0.5))
        query_blocks = (offset + jnp.arange(query_rows)) // BLOCK
        allowed = key_blocks[None, :] <= query_blocks[:, None]
        weights = jax.nn.softmax(jnp.where(allowed[None], scores, -1e+30), axis=-1)
        return jnp.einsum('hqk,khd->qhd', low(weights), values, precision=lax.Precision.HIGHEST)
    offsets = jnp.arange(length // query_rows) * query_rows
    results = lax.map(jax.checkpoint(one_block), (query.reshape(length // query_rows, query_rows, HEADS, HEAD_DIM), offsets))
    return results.reshape(length, HEADS, HEAD_DIM)

def forward(expert_ids, tokens, norm_one, w_query, w_key, w_value, w_out, norm_two, w_router, expert_gate, expert_up, expert_down, shared_gate, shared_up, shared_down):
    sequences, length, model_width = tokens.shape
    inputs = tokens.reshape(sequences * length, model_width)
    places = jnp.tile(jnp.arange(length), sequences)
    normed = low(normalize(inputs, norm_one))
    query = low(rotate(low_back(product(normed, w_query)).reshape(-1, HEADS, HEAD_DIM), places))
    keys = low(rotate(low_back(product(normed, w_key)).reshape(-1, HEADS, HEAD_DIM), places))
    values = low(low_back(product(normed, w_value))).reshape(-1, HEADS, HEAD_DIM)
    shaped = (sequences, length, HEADS, HEAD_DIM)
    attended = lax.map(lambda group: attend_sequence(group[0], group[1], group[2]), (query.reshape(shaped), keys.reshape(shaped), values.reshape(shaped)))
    attended = low(low_back(attended.reshape(sequences * length, model_width)))
    mixed = inputs + low_back(product(attended, w_out))
    second = low(normalize(mixed, norm_two))
    logits = low_back(product(second, w_router))
    chosen = expert_ids.reshape(sequences * length, TOP)
    one_hot = (chosen[:, :, None] == jnp.arange(EXPERTS)[None, None, :]).astype(jnp.float32)
    selected = lax.optimization_barrier(jnp.sum(logits[:, None, :] * one_hot, axis=-1))
    gates = jax.nn.softmax(selected, axis=-1)
    shares = lax.optimization_barrier(jnp.sum(gates[:, :, None] * one_hot, axis=1))

    def expert_step(summed, operands):
        gate_weight, up_weight, down_weight, share = operands
        routed = low_back(second)
        gate_pre = low_back(product(routed, gate_weight))
        up_pre = low_back(product(routed, up_weight))
        hidden = low(jax.nn.silu(gate_pre) * up_pre)
        result = low(low_back(product(hidden, down_weight)))
        return (summed + share[:, None] * result, None)
    mixture, unused = lax.scan(jax.checkpoint(expert_step), jnp.zeros_like(mixed), (expert_gate, expert_up, expert_down, shares.T))
    shared_hidden = low(jax.nn.silu(low_back(product(second, shared_gate))) * low_back(product(second, shared_up)))
    combined = mixed + mixture + product(shared_hidden, shared_down)
    return combined.reshape(sequences, length, model_width)

def reference(tokens, expert_ids, norm_one, w_query, w_key, w_value, w_out, norm_two, w_router, expert_gate, expert_up, expert_down, shared_gate, shared_up, shared_down, cotangent):
    floats = [operand.astype(jnp.float32) for operand in (tokens, norm_one, w_query, w_key, w_value, w_out, norm_two, w_router, expert_gate, expert_up, expert_down, shared_gate, shared_up, shared_down)]

    def wrapped(*operands):
        return forward(expert_ids, *operands)
    combined, pull_back = jax.vjp(wrapped, *floats)
    grads = pull_back(cotangent.astype(jnp.float32))
    return (combined.astype(jnp.bfloat16), grads[0], grads[1], grads[2], grads[3], grads[4], grads[5], grads[6], grads[7], grads[8], grads[9], grads[10], grads[11], grads[12], grads[13])
```

```python
import math

import jax
import jax.numpy as jnp
from jax import lax
from jax.sharding import PartitionSpec as P

HEAD_DIM = 64
TOP = 2
BLOCK = 256
KEY_ROWS = 512


def product(first_factor, second_factor):
    return jnp.dot(first_factor, second_factor, preferred_element_type=jnp.float32)


def against(first_factor, second_factor):
    return lax.dot_general(
        first_factor, second_factor, (((1,), (1,)), ((), ())), preferred_element_type=jnp.float32
    )


def outer_sum(first_factor, second_factor):
    return lax.dot_general(
        first_factor, second_factor, (((0,), (0,)), ((), ())), preferred_element_type=jnp.float32
    )


def normalize(values, scaling):
    return values * lax.rsqrt(jnp.mean(values * values, axis=-1, keepdims=True) + 1e-06) * scaling


def rotate(values, places):
    halfway = values.shape[-1] // 2
    frequency = 10000.0 ** (-jnp.arange(halfway, dtype=jnp.float32) / halfway)
    angles = places.astype(jnp.float32)[:, None] * frequency[None, :]
    cosine = jnp.cos(angles)[:, None, :]
    sine_part = jnp.sin(angles)[:, None, :]
    former = values[..., :halfway]
    latter = values[..., halfway:]
    return jnp.concatenate(
        [former * cosine - latter * sine_part, latter * cosine + former * sine_part], axis=-1
    )


def silu_parts(gate_pre):
    sigmoid_value = jax.nn.sigmoid(gate_pre)
    return (gate_pre * sigmoid_value, sigmoid_value * (1.0 + gate_pre * (1.0 - sigmoid_value)))


def tiled(matrix, row_groups, col_groups):
    row_count, col_count = matrix.shape
    blocks = matrix.reshape(
        row_groups, row_count // row_groups, col_groups, col_count // col_groups
    ).transpose(0, 2, 1, 3)
    return blocks.reshape(col_groups * row_count, col_count // col_groups)


def per_device_slots(
    tokens,
    expert_ids,
    norm_one,
    w_query,
    w_key,
    w_value,
    w_out,
    norm_two,
    w_router,
    expert_gate,
    expert_up,
    expert_down,
    shared_gate,
    shared_up,
    shared_down,
    cotangent,
):
    local_rows = tokens.shape[1]
    model_width = tokens.shape[2]
    head_count = model_width // HEAD_DIM
    score_scale = HEAD_DIM ** (-0.5)
    ctx_count = lax.axis_size("ctx")
    ctx_place = lax.axis_index("ctx")
    exp_count = lax.axis_size("exp")
    row_groups = lax.axis_size("seq") * ctx_count
    local_experts = expert_gate.shape[0]
    experts_all = local_experts * exp_count
    capacity = min(local_rows, 2 * TOP * local_rows // experts_all)
    places = ctx_place * local_rows + jnp.arange(local_rows, dtype=jnp.int32)
    query_blocks = places // BLOCK

    def spread(matrix):
        return tiled(matrix, row_groups, exp_count)

    inputs = tokens[0].astype(jnp.float32)
    normed_full, norm_one_pull = jax.vjp(normalize, inputs, norm_one)
    normed = normed_full.astype(jnp.bfloat16)
    query = rotate(
        product(normed, w_query).reshape(local_rows, head_count, HEAD_DIM), places
    ).astype(jnp.bfloat16)
    keys_local = (
        rotate(product(normed, w_key).reshape(local_rows, head_count, HEAD_DIM), places)
        .astype(jnp.bfloat16)
        .reshape(local_rows, model_width)
    )
    values_local = product(normed, w_value).astype(jnp.bfloat16)

    def block_scores(key_block, offset):
        key_heads = key_block.reshape(-1, head_count, HEAD_DIM)
        scores = (
            jnp.einsum("qhd,khd->hqk", query, key_heads, preferred_element_type=jnp.float32)
            * score_scale
        )
        key_index = (offset + jnp.arange(key_block.shape[0], dtype=jnp.int32)) // BLOCK
        allowed = key_index[None, :] <= query_blocks[:, None]
        return (scores, allowed)

    def attend_block(running, key_block, value_block, offset):
        highest, totals, accumulated = running
        scores, allowed = block_scores(key_block, offset)
        masked = jnp.where(allowed[None], scores, -1e30)
        fresh = jnp.maximum(highest, jnp.max(masked, axis=-1))
        weights = jnp.where(allowed[None], jnp.exp(masked - fresh[..., None]), 0.0)
        decay = jnp.exp(highest - fresh)
        value_heads = value_block.reshape(-1, head_count, HEAD_DIM)
        accumulated = accumulated * decay[..., None] + jnp.einsum(
            "hqk,khd->hqd",
            weights.astype(jnp.bfloat16),
            value_heads,
            preferred_element_type=jnp.float32,
        )
        return (fresh, totals * decay + jnp.sum(weights, axis=-1), accumulated)

    start_state = (
        jnp.full((head_count, local_rows), -1e30, jnp.float32),
        jnp.zeros((head_count, local_rows), jnp.float32),
        jnp.zeros((head_count, local_rows, HEAD_DIM), jnp.float32),
    )
    running = start_state
    key_part = lax.all_gather(keys_local, "ctx", axis=0, tiled=True)
    value_part = lax.all_gather(values_local, "ctx", axis=0, tiled=True)
    span_rows = key_part.shape[0]
    stride = math.gcd(span_rows, KEY_ROWS)
    step_count = span_rows // stride
    key_steps = key_part.reshape(step_count, stride, model_width)
    value_steps = value_part.reshape(step_count, stride, model_width)
    offsets = jnp.arange(step_count, dtype=jnp.int32) * stride

    def one_step(inner, operands):
        return (attend_block(inner, operands[0], operands[1], operands[2]), None)

    running, unused = lax.scan(one_step, running, (key_steps, value_steps, offsets))
    highest, totals, accumulated = running
    log_total = highest + jnp.log(totals)
    attended = (
        (accumulated / totals[..., None])
        .transpose(1, 0, 2)
        .reshape(local_rows, model_width)
        .astype(jnp.bfloat16)
    )
    mixed = inputs + product(attended, w_out)
    second_full, norm_two_pull = jax.vjp(normalize, mixed, norm_two)
    second = second_full.astype(jnp.bfloat16)
    logits = product(second, w_router)
    chosen = expert_ids[0]
    one_hot = (
        chosen[:, :, None] == jnp.arange(experts_all, dtype=jnp.int32)[None, None, :]
    ).astype(jnp.float32)
    selected = jnp.sum(logits[:, None, :] * one_hot, axis=-1)
    gates = jax.nn.softmax(selected, axis=-1)
    flat_ids = chosen.reshape(-1)
    slot_hits = (flat_ids[:, None] == jnp.arange(experts_all, dtype=jnp.int32)[None, :]).astype(
        jnp.int32
    )
    order = jnp.arange(flat_ids.shape[0], dtype=jnp.int32)
    earlier = (order[None, :] < order[:, None]).astype(jnp.bfloat16)
    counts_before = product(earlier, slot_hits.astype(jnp.bfloat16)).astype(jnp.int32)
    slot_place = jnp.sum(counts_before * slot_hits, axis=1)

    def to_slots(routed_rows):
        empty_slots = jnp.zeros((experts_all, capacity, model_width), jnp.bfloat16)
        return (
            empty_slots.at[flat_ids, slot_place]
            .set(routed_rows)
            .reshape(exp_count, local_experts, capacity, model_width)
        )

    def from_slots(arrived_back):
        picked = arrived_back.reshape(experts_all, capacity, model_width)[flat_ids, slot_place]
        return picked.astype(jnp.float32).reshape(local_rows, TOP, model_width)

    def expert_front(arrived_rows):
        gate_pre = jnp.einsum(
            "sjcd,jdf->sjcf", arrived_rows, expert_gate, preferred_element_type=jnp.float32
        )
        up_pre = jnp.einsum(
            "sjcd,jdf->sjcf", arrived_rows, expert_up, preferred_element_type=jnp.float32
        )
        hidden = (jax.nn.silu(gate_pre) * up_pre).astype(jnp.bfloat16)
        return (gate_pre, up_pre, hidden)

    send_rows = to_slots(jnp.repeat(second, TOP, axis=0))
    arrived = lax.all_to_all(send_rows, "exp", split_axis=0, concat_axis=0, tiled=True)
    gate_pre, up_pre, hidden = expert_front(arrived)
    results = jnp.einsum(
        "sjcf,jfd->sjcd", hidden, expert_down, preferred_element_type=jnp.float32
    ).astype(jnp.bfloat16)
    returned = lax.all_to_all(results, "exp", split_axis=0, concat_axis=0, tiled=True)
    expert_out = from_slots(returned)
    mixture = jnp.sum(gates[:, :, None] * expert_out, axis=1)
    shared_gate_pre = product(second, shared_gate)
    shared_up_pre = product(second, shared_up)
    shared_hidden = (jax.nn.silu(shared_gate_pre) * shared_up_pre).astype(jnp.bfloat16)
    output = (mixed + mixture + product(shared_hidden, shared_down)).astype(jnp.bfloat16)
    upstream = cotangent[0]
    upstream_full = upstream.astype(jnp.float32)
    grad_shared_down = outer_sum(shared_hidden, upstream)
    d_shared_hidden = against(upstream, shared_down)
    shared_silu, shared_slope = silu_parts(shared_gate_pre)
    d_shared_gate = (d_shared_hidden * shared_up_pre * shared_slope).astype(jnp.bfloat16)
    d_shared_up = (d_shared_hidden * shared_silu).astype(jnp.bfloat16)
    grad_shared_gate = outer_sum(second, d_shared_gate)
    grad_shared_up = outer_sum(second, d_shared_up)
    d_second = against(d_shared_gate, shared_gate) + against(d_shared_up, shared_up)
    d_gates = jnp.sum(upstream_full[:, None, :] * expert_out, axis=-1)
    d_selected = gates * (d_gates - jnp.sum(gates * d_gates, axis=-1, keepdims=True))
    d_logits = jnp.sum(d_selected[:, :, None] * one_hot, axis=1).astype(jnp.bfloat16)
    grad_router = outer_sum(second, d_logits)
    d_second = d_second + against(d_logits, w_router)
    grad_slots = to_slots(
        (gates[:, :, None] * upstream_full[:, None, :])
        .astype(jnp.bfloat16)
        .reshape(local_rows * TOP, model_width)
    )
    arrived_rows, arrived_grad = (
        lax.all_to_all(send_rows, "exp", split_axis=0, concat_axis=0, tiled=True),
        lax.all_to_all(grad_slots, "exp", split_axis=0, concat_axis=0, tiled=True),
    )
    gate_kept, up_kept, hidden_kept = expert_front(arrived_rows)
    d_hidden = jnp.einsum(
        "sjcd,jfd->sjcf", arrived_grad, expert_down, preferred_element_type=jnp.float32
    )
    expert_silu, expert_slope = silu_parts(gate_kept)
    d_gate_pre = (d_hidden * up_kept * expert_slope).astype(jnp.bfloat16)
    d_up_pre = (d_hidden * expert_silu).astype(jnp.bfloat16)
    grad_expert_down = jnp.einsum(
        "sjcf,sjcd->jfd", hidden_kept, arrived_grad, preferred_element_type=jnp.float32
    )
    grad_expert_gate = jnp.einsum(
        "sjcd,sjcf->jdf", arrived_rows, d_gate_pre, preferred_element_type=jnp.float32
    )
    grad_expert_up = jnp.einsum(
        "sjcd,sjcf->jdf", arrived_rows, d_up_pre, preferred_element_type=jnp.float32
    )
    d_routed = (
        jnp.einsum("sjcf,jdf->sjcd", d_gate_pre, expert_gate, preferred_element_type=jnp.float32)
        + jnp.einsum("sjcf,jdf->sjcd", d_up_pre, expert_up, preferred_element_type=jnp.float32)
    ).astype(jnp.bfloat16)
    returned_grad = lax.all_to_all(d_routed, "exp", split_axis=0, concat_axis=0, tiled=True)
    d_second = d_second + jnp.sum(from_slots(returned_grad), axis=1)
    grad_expert_gate, grad_expert_up, grad_expert_down = (
        lax.psum(grad_expert_gate.astype(jnp.bfloat16), ("seq", "ctx")).astype(jnp.float32),
        lax.psum(grad_expert_up.astype(jnp.bfloat16), ("seq", "ctx")).astype(jnp.float32),
        lax.psum(grad_expert_down.astype(jnp.bfloat16), ("seq", "ctx")).astype(jnp.float32),
    )
    d_mixed_part, grad_norm_two = norm_two_pull(d_second)
    d_mixed = upstream_full + d_mixed_part
    d_attention = d_mixed.astype(jnp.bfloat16)
    grad_out = outer_sum(attended, d_attention)
    grad_heads = (
        against(d_attention, w_out).astype(jnp.bfloat16).reshape(local_rows, head_count, HEAD_DIM)
    )
    keys_all, values_all = (
        lax.all_gather(keys_local, "ctx", axis=0, tiled=True),
        lax.all_gather(values_local, "ctx", axis=0, tiled=True),
    )
    block_total = ((ctx_place + 1) * local_rows + KEY_ROWS - 1) // KEY_ROWS

    def weights_at(number):
        offset = number * KEY_ROWS
        key_block = lax.dynamic_slice_in_dim(keys_all, offset, KEY_ROWS, 0)
        value_block = lax.dynamic_slice_in_dim(values_all, offset, KEY_ROWS, 0)
        scores, allowed = block_scores(key_block, offset)
        weights = jnp.where(allowed[None], jnp.exp(scores - log_total[..., None]), 0.0)
        grad_weights = jnp.einsum(
            "qhd,khd->hqk",
            grad_heads,
            value_block.reshape(KEY_ROWS, head_count, HEAD_DIM),
            preferred_element_type=jnp.float32,
        )
        return (key_block, weights, grad_weights)

    def row_dot_step(number, summed):
        unused_block, weights, grad_weights = weights_at(number)
        return summed + jnp.sum(weights * grad_weights, axis=-1)

    row_dots = lax.fori_loop(
        0, block_total, row_dot_step, jnp.zeros((head_count, local_rows), jnp.float32)
    )

    def score_grads(number):
        key_block, weights, grad_weights = weights_at(number)
        d_scores = (weights * (grad_weights - row_dots[..., None])).astype(jnp.bfloat16)
        return (key_block.reshape(KEY_ROWS, head_count, HEAD_DIM), weights, d_scores)

    query_start = jnp.zeros((local_rows, head_count, HEAD_DIM), jnp.float32)

    def grad_step(number, running):
        grad_query, key_terms = running
        key_heads, weights, d_scores = score_grads(number)
        grad_query = (
            grad_query
            + jnp.einsum("hqk,khd->qhd", d_scores, key_heads, preferred_element_type=jnp.float32)
            * score_scale
        )
        key_part = (
            jnp.einsum("hqk,qhd->khd", d_scores, query, preferred_element_type=jnp.float32)
            * score_scale
        )
        value_part = jnp.einsum(
            "hqk,qhd->khd",
            weights.astype(jnp.bfloat16),
            grad_heads,
            preferred_element_type=jnp.float32,
        )
        block_terms = jnp.concatenate(
            [key_part.reshape(KEY_ROWS, model_width), value_part.reshape(KEY_ROWS, model_width)],
            axis=1,
        )
        return (
            grad_query,
            lax.dynamic_update_slice_in_dim(key_terms, block_terms, number * KEY_ROWS, 0),
        )

    grad_query_heads, key_terms = lax.fori_loop(
        0,
        block_total,
        grad_step,
        (query_start, jnp.zeros((ctx_count * local_rows, 2 * model_width), jnp.float32)),
    )
    key_grads = lax.psum_scatter(
        key_terms.astype(jnp.bfloat16), "ctx", scatter_dimension=0, tiled=True
    ).astype(jnp.float32)
    key_grad_heads = key_grads[:, :model_width].reshape(local_rows, head_count, HEAD_DIM)
    d_value = key_grads[:, model_width:].astype(jnp.bfloat16)
    d_query_lin = (
        rotate(grad_query_heads, -places).astype(jnp.bfloat16).reshape(local_rows, model_width)
    )
    d_key_lin = (
        rotate(key_grad_heads, -places).astype(jnp.bfloat16).reshape(local_rows, model_width)
    )
    grad_query = outer_sum(normed, d_query_lin)
    grad_key = outer_sum(normed, d_key_lin)
    grad_value = outer_sum(normed, d_value)
    d_normed = against(d_query_lin, w_query) + against(d_key_lin, w_key) + against(d_value, w_value)
    d_inputs, grad_norm_one = norm_one_pull(d_normed)
    grad_tokens = (d_mixed + d_inputs)[None]
    (
        grad_query,
        grad_key,
        grad_value,
        grad_out,
        grad_router,
        grad_shared_gate,
        grad_shared_up,
        grad_shared_down,
    ) = (
        lax.psum_scatter(
            spread(grad_query), ("seq", "ctx", "exp"), scatter_dimension=0, tiled=True
        ),
        lax.psum_scatter(spread(grad_key), ("seq", "ctx", "exp"), scatter_dimension=0, tiled=True),
        lax.psum_scatter(
            spread(grad_value), ("seq", "ctx", "exp"), scatter_dimension=0, tiled=True
        ),
        lax.psum_scatter(spread(grad_out), ("seq", "ctx", "exp"), scatter_dimension=0, tiled=True),
        lax.psum_scatter(
            spread(grad_router), ("seq", "ctx", "exp"), scatter_dimension=0, tiled=True
        ),
        lax.psum_scatter(
            spread(grad_shared_gate), ("seq", "ctx", "exp"), scatter_dimension=0, tiled=True
        ),
        lax.psum_scatter(
            spread(grad_shared_up), ("seq", "ctx", "exp"), scatter_dimension=0, tiled=True
        ),
        lax.psum_scatter(
            spread(grad_shared_down), ("seq", "ctx", "exp"), scatter_dimension=0, tiled=True
        ),
    )
    grad_norm_one, grad_norm_two = lax.psum((grad_norm_one, grad_norm_two), ("seq", "ctx", "exp"))
    return (
        output[None],
        grad_tokens,
        grad_norm_one,
        grad_query,
        grad_key,
        grad_value,
        grad_out,
        grad_norm_two,
        grad_router,
        grad_expert_gate,
        grad_expert_up,
        grad_expert_down,
        grad_shared_gate,
        grad_shared_up,
        grad_shared_down,
    )


def per_device_dense(
    tokens,
    expert_ids,
    norm_one,
    w_query,
    w_key,
    w_value,
    w_out,
    norm_two,
    w_router,
    expert_gate,
    expert_up,
    expert_down,
    shared_gate,
    shared_up,
    shared_down,
    cotangent,
):
    rows = tokens.shape[1]
    width = tokens.shape[2]
    heads = width // HEAD_DIM
    scale = HEAD_DIM ** (-0.5)
    ctx_count = lax.axis_size("ctx")
    ctx_place = lax.axis_index("ctx")
    exp_count = lax.axis_size("exp")
    exp_place = lax.axis_index("exp")
    row_groups = lax.axis_size("seq") * ctx_count
    places = ctx_place * rows + jnp.arange(rows, dtype=jnp.int32)
    upstream = cotangent[0]
    ids = expert_ids[0]

    def spread(matrix):
        return tiled(matrix.astype(jnp.bfloat16), row_groups, exp_count)

    upstream_all = lax.all_gather(upstream, "exp", axis=0, tiled=True)
    ids_all = lax.all_gather(ids, "exp", axis=0, tiled=True)

    inputs = tokens[0].astype(jnp.float32)
    normed_full, norm_one_pull = jax.vjp(normalize, inputs, norm_one)
    normed = normed_full.astype(jnp.bfloat16)

    def heads_of(matrix):
        return matrix.reshape(matrix.shape[0], heads, HEAD_DIM)

    query = rotate(heads_of(product(normed, w_query)), places).astype(jnp.bfloat16)
    keys = rotate(heads_of(product(normed, w_key)), places).astype(jnp.bfloat16)
    values = product(normed, w_value).astype(jnp.bfloat16)
    both = jnp.concatenate([keys.reshape(rows, width), values], axis=1)
    both_all = lax.all_gather(both, "ctx", axis=0, tiled=True)
    keys_all, values_all = heads_of(both_all[:, :width]), heads_of(both_all[:, width:])
    span = keys_all.shape[0]
    allowed = (jnp.arange(span, dtype=jnp.int32) // BLOCK)[None, None, :] <= (
        places // BLOCK
    )[None, :, None]
    scores = jnp.einsum("qhd,khd->hqk", query, keys_all, preferred_element_type=jnp.float32)
    scores = jnp.where(allowed, scores * scale, -1e30)
    highest = jnp.max(scores, axis=-1, keepdims=True)
    unscaled = jnp.exp(scores - highest)
    totals = jnp.sum(unscaled, axis=-1, keepdims=True)
    weights = unscaled / totals
    weights_low = weights.astype(jnp.bfloat16)
    attended = (
        jnp.einsum("hqk,khd->qhd", weights_low, values_all, preferred_element_type=jnp.float32)
        .reshape(rows, width)
        .astype(jnp.bfloat16)
    )
    mixed = inputs + product(attended, w_out)
    second_full, norm_two_pull = jax.vjp(normalize, mixed, norm_two)
    second = second_full.astype(jnp.bfloat16)
    experts_all = w_router.shape[1]

    def gates_of(rows_second, rows_ids):
        logits = product(rows_second, w_router)
        named = jnp.any(
            rows_ids[:, :, None] == jnp.arange(experts_all, dtype=jnp.int32)[None, None, :], axis=1
        )
        masked = jnp.where(named, logits, -1e30)
        raised = jnp.where(named, jnp.exp(masked - jnp.max(masked, axis=-1, keepdims=True)), 0.0)
        return raised / jnp.sum(raised, axis=-1, keepdims=True), named

    shares, named = gates_of(second, ids)
    second_all = lax.all_gather(second, "exp", axis=0, tiled=True)
    shares_all, unused = gates_of(second_all, ids_all)
    mine = (jnp.arange(experts_all, dtype=jnp.int32) == exp_place)[None, :]
    share = jnp.sum(jnp.where(mine, shares_all, 0.0), axis=1, keepdims=True)
    gate_w, up_w, down_w = expert_gate[0], expert_up[0], expert_down[0]
    d_result = (share * upstream_all.astype(jnp.float32)).astype(jnp.bfloat16)
    gate_pre = product(second_all, gate_w)
    up_pre = product(second_all, up_w)
    silu, slope = silu_parts(gate_pre)
    hidden = (silu * up_pre).astype(jnp.bfloat16)
    result = product(hidden, down_w).astype(jnp.bfloat16)
    d_hidden = against(d_result, down_w)
    d_gate_pre = (d_hidden * up_pre * slope).astype(jnp.bfloat16)
    d_up_pre = (d_hidden * silu).astype(jnp.bfloat16)
    d_routed = (against(d_gate_pre, gate_w) + against(d_up_pre, up_w)).astype(jnp.bfloat16)
    expert_grads = (
        outer_sum(second_all, d_gate_pre),
        outer_sum(second_all, d_up_pre),
        outer_sum(hidden, d_result),
    )
    expert_grads = tuple(
        lax.psum(g.astype(jnp.bfloat16), ("seq", "ctx")).astype(jnp.float32)[None]
        for g in expert_grads
    )
    back = jnp.stack(
        [result.reshape(exp_count, rows, width), d_routed.reshape(exp_count, rows, width)], axis=1
    )
    back = lax.all_to_all(back, "exp", split_axis=0, concat_axis=0, tiled=True)
    expert_out = back[:, 0].astype(jnp.float32)
    shared_gate_pre = product(second, shared_gate)
    shared_up_pre = product(second, shared_up)
    shared_silu, shared_slope = silu_parts(shared_gate_pre)
    shared_hidden = (shared_silu * shared_up_pre).astype(jnp.bfloat16)
    d_shared_hidden = against(upstream, shared_down)
    d_shared_gate = (d_shared_hidden * shared_up_pre * shared_slope).astype(jnp.bfloat16)
    d_shared_up = (d_shared_hidden * shared_silu).astype(jnp.bfloat16)
    grad_shared_gate = outer_sum(second, d_shared_gate)
    grad_shared_up = outer_sum(second, d_shared_up)
    grad_shared_down = outer_sum(shared_hidden, upstream)
    mixture = jnp.sum(shares.T[:, :, None] * expert_out, axis=0)
    output = (mixed + mixture + product(shared_hidden, shared_down)).astype(jnp.bfloat16)
    upstream_full = upstream.astype(jnp.float32)
    d_gates = jnp.sum(upstream_full[None] * expert_out, axis=-1).T
    d_gates = jnp.where(named, d_gates, 0.0)
    d_logits = (shares * (d_gates - jnp.sum(shares * d_gates, axis=-1, keepdims=True))).astype(
        jnp.bfloat16
    )
    grad_router = outer_sum(second, d_logits)
    d_second = (
        against(d_shared_gate, shared_gate)
        + against(d_shared_up, shared_up)
        + against(d_logits, w_router)
        + jnp.sum(back[:, 1].astype(jnp.float32), axis=0)
    )
    d_mixed_part, grad_norm_two = norm_two_pull(d_second)
    d_mixed = upstream_full + d_mixed_part
    d_attention = d_mixed.astype(jnp.bfloat16)
    grad_out = outer_sum(attended, d_attention)
    d_attended = heads_of(against(d_attention, w_out).astype(jnp.bfloat16))
    d_weights = jnp.einsum(
        "qhd,khd->hqk", d_attended, values_all, preferred_element_type=jnp.float32
    )
    delta = jnp.sum(weights * d_weights, axis=-1, keepdims=True)
    d_scores = (weights * (d_weights - delta)).astype(jnp.bfloat16)
    d_query = (
        jnp.einsum("hqk,khd->qhd", d_scores, keys_all, preferred_element_type=jnp.float32) * scale
    )
    d_key = (
        jnp.einsum("hqk,qhd->khd", d_scores, query, preferred_element_type=jnp.float32) * scale
    )
    d_value = jnp.einsum(
        "hqk,qhd->khd", weights_low, d_attended, preferred_element_type=jnp.float32
    )
    key_terms = jnp.concatenate([d_key.reshape(span, width), d_value.reshape(span, width)], axis=1)
    key_grads = lax.psum_scatter(
        key_terms.astype(jnp.bfloat16), "ctx", scatter_dimension=0, tiled=True
    )
    d_value = key_grads[:, width:]
    d_key_lin = rotate(heads_of(key_grads[:, :width].astype(jnp.float32)), -places)
    d_key_lin = d_key_lin.astype(jnp.bfloat16).reshape(rows, width)
    d_query_lin = rotate(d_query, -places).astype(jnp.bfloat16).reshape(rows, width)
    grad_query = outer_sum(normed, d_query_lin)
    grad_key = outer_sum(normed, d_key_lin)
    grad_value = outer_sum(normed, d_value)
    d_normed = against(d_query_lin, w_query) + against(d_key_lin, w_key) + against(d_value, w_value)
    d_inputs, grad_norm_one = norm_one_pull(d_normed)
    grad_tokens = (d_mixed + d_inputs)[None]
    scattered = [
        lax.psum_scatter(
            spread(g), ("seq", "ctx", "exp"), scatter_dimension=0, tiled=True
        ).astype(jnp.float32)
        for g in (
            grad_query,
            grad_key,
            grad_value,
            grad_out,
            grad_router,
            grad_shared_gate,
            grad_shared_up,
            grad_shared_down,
        )
    ]
    grad_norm_one, grad_norm_two = lax.psum((grad_norm_one, grad_norm_two), ("seq", "ctx", "exp"))
    return (
        output[None],
        grad_tokens,
        grad_norm_one,
        *scattered[:4],
        grad_norm_two,
        scattered[4],
        *expert_grads,
        *scattered[5:],
    )


def fits(mesh):
    return dict(mesh.shape) == {"seq": 2, "ctx": 4, "exp": 4}


def solution(mesh):
    per_device = per_device_dense if fits(mesh) else per_device_slots
    in_specs = (
        P(("seq", "exp"), "ctx", None),
        P(("seq", "exp"), "ctx", None),
        P(),
        P(),
        P(),
        P(),
        P(),
        P(),
        P(),
        P("exp", None, None),
        P("exp", None, None),
        P("exp", None, None),
        P(),
        P(),
        P(),
        P(("seq", "exp"), "ctx", None),
    )
    out_specs = (
        P(("seq", "exp"), "ctx", None),
        P(("seq", "exp"), "ctx", None),
        P(),
        P(("seq", "ctx"), "exp"),
        P(("seq", "ctx"), "exp"),
        P(("seq", "ctx"), "exp"),
        P(("seq", "ctx"), "exp"),
        P(),
        P(("seq", "ctx"), "exp"),
        P("exp", None, None),
        P("exp", None, None),
        P("exp", None, None),
        P(("seq", "ctx"), "exp"),
        P(("seq", "ctx"), "exp"),
        P(("seq", "ctx"), "exp"),
    )
    return jax.shard_map(
        per_device, mesh=mesh, in_specs=in_specs, out_specs=out_specs, check_vma=False
    )
```

```python
import functools
import math

import jax
import jax.numpy as jnp
from jax import lax
from jax.experimental import pallas as pl
from jax.experimental.pallas import tpu as pltpu
from jax.sharding import PartitionSpec as P

HEAD_DIM = 64
TOP = 2
BLOCK = 256
KEY_ROWS = 512
MESH = pl.DeviceIdType.MESH


def product(first_factor, second_factor):
    return jnp.dot(first_factor, second_factor, preferred_element_type=jnp.float32)


def against(first_factor, second_factor):
    return lax.dot_general(
        first_factor, second_factor, (((1,), (1,)), ((), ())), preferred_element_type=jnp.float32
    )


def outer_sum(first_factor, second_factor):
    return lax.dot_general(
        first_factor, second_factor, (((0,), (0,)), ((), ())), preferred_element_type=jnp.float32
    )


def normalize(values, scaling):
    return values * lax.rsqrt(jnp.mean(values * values, axis=-1, keepdims=True) + 1e-06) * scaling


def rotate(values, places):
    halfway = values.shape[-1] // 2
    frequency = 10000.0 ** (-jnp.arange(halfway, dtype=jnp.float32) / halfway)
    angles = places.astype(jnp.float32)[:, None] * frequency[None, :]
    cosine = jnp.cos(angles)[:, None, :]
    sine_part = jnp.sin(angles)[:, None, :]
    former = values[..., :halfway]
    latter = values[..., halfway:]
    return jnp.concatenate(
        [former * cosine - latter * sine_part, latter * cosine + former * sine_part], axis=-1
    )


def silu_parts(gate_pre):
    sigmoid_value = jax.nn.sigmoid(gate_pre)
    return (gate_pre * sigmoid_value, sigmoid_value * (1.0 + gate_pre * (1.0 - sigmoid_value)))


def tiled(matrix, row_groups, col_groups):
    row_count, col_count = matrix.shape
    blocks = matrix.reshape(
        row_groups, row_count // row_groups, col_groups, col_count // col_groups
    ).transpose(0, 2, 1, 3)
    return blocks.reshape(col_groups * row_count, col_count // col_groups)


def per_device_slots(
    tokens,
    expert_ids,
    norm_one,
    w_query,
    w_key,
    w_value,
    w_out,
    norm_two,
    w_router,
    expert_gate,
    expert_up,
    expert_down,
    shared_gate,
    shared_up,
    shared_down,
    cotangent,
):
    local_rows = tokens.shape[1]
    model_width = tokens.shape[2]
    head_count = model_width // HEAD_DIM
    score_scale = HEAD_DIM ** (-0.5)
    ctx_count = lax.axis_size("ctx")
    ctx_place = lax.axis_index("ctx")
    exp_count = lax.axis_size("exp")
    row_groups = lax.axis_size("seq") * ctx_count
    local_experts = expert_gate.shape[0]
    experts_all = local_experts * exp_count
    capacity = min(local_rows, 2 * TOP * local_rows // experts_all)
    places = ctx_place * local_rows + jnp.arange(local_rows, dtype=jnp.int32)
    query_blocks = places // BLOCK

    def spread(matrix):
        return tiled(matrix, row_groups, exp_count)

    inputs = tokens[0].astype(jnp.float32)
    normed_full, norm_one_pull = jax.vjp(normalize, inputs, norm_one)
    normed = normed_full.astype(jnp.bfloat16)
    query = rotate(
        product(normed, w_query).reshape(local_rows, head_count, HEAD_DIM), places
    ).astype(jnp.bfloat16)
    keys_local = (
        rotate(product(normed, w_key).reshape(local_rows, head_count, HEAD_DIM), places)
        .astype(jnp.bfloat16)
        .reshape(local_rows, model_width)
    )
    values_local = product(normed, w_value).astype(jnp.bfloat16)

    def block_scores(key_block, offset):
        key_heads = key_block.reshape(-1, head_count, HEAD_DIM)
        scores = (
            jnp.einsum("qhd,khd->hqk", query, key_heads, preferred_element_type=jnp.float32)
            * score_scale
        )
        key_index = (offset + jnp.arange(key_block.shape[0], dtype=jnp.int32)) // BLOCK
        allowed = key_index[None, :] <= query_blocks[:, None]
        return (scores, allowed)

    def attend_block(running, key_block, value_block, offset):
        highest, totals, accumulated = running
        scores, allowed = block_scores(key_block, offset)
        masked = jnp.where(allowed[None], scores, -1e30)
        fresh = jnp.maximum(highest, jnp.max(masked, axis=-1))
        weights = jnp.where(allowed[None], jnp.exp(masked - fresh[..., None]), 0.0)
        decay = jnp.exp(highest - fresh)
        value_heads = value_block.reshape(-1, head_count, HEAD_DIM)
        accumulated = accumulated * decay[..., None] + jnp.einsum(
            "hqk,khd->hqd",
            weights.astype(jnp.bfloat16),
            value_heads,
            preferred_element_type=jnp.float32,
        )
        return (fresh, totals * decay + jnp.sum(weights, axis=-1), accumulated)

    start_state = (
        jnp.full((head_count, local_rows), -1e30, jnp.float32),
        jnp.zeros((head_count, local_rows), jnp.float32),
        jnp.zeros((head_count, local_rows, HEAD_DIM), jnp.float32),
    )
    running = start_state
    key_part = lax.all_gather(keys_local, "ctx", axis=0, tiled=True)
    value_part = lax.all_gather(values_local, "ctx", axis=0, tiled=True)
    span_rows = key_part.shape[0]
    stride = math.gcd(span_rows, KEY_ROWS)
    step_count = span_rows // stride
    key_steps = key_part.reshape(step_count, stride, model_width)
    value_steps = value_part.reshape(step_count, stride, model_width)
    offsets = jnp.arange(step_count, dtype=jnp.int32) * stride

    def one_step(inner, operands):
        return (attend_block(inner, operands[0], operands[1], operands[2]), None)

    running, unused = lax.scan(one_step, running, (key_steps, value_steps, offsets))
    highest, totals, accumulated = running
    log_total = highest + jnp.log(totals)
    attended = (
        (accumulated / totals[..., None])
        .transpose(1, 0, 2)
        .reshape(local_rows, model_width)
        .astype(jnp.bfloat16)
    )
    mixed = inputs + product(attended, w_out)
    second_full, norm_two_pull = jax.vjp(normalize, mixed, norm_two)
    second = second_full.astype(jnp.bfloat16)
    logits = product(second, w_router)
    chosen = expert_ids[0]
    one_hot = (
        chosen[:, :, None] == jnp.arange(experts_all, dtype=jnp.int32)[None, None, :]
    ).astype(jnp.float32)
    selected = jnp.sum(logits[:, None, :] * one_hot, axis=-1)
    gates = jax.nn.softmax(selected, axis=-1)
    flat_ids = chosen.reshape(-1)
    slot_hits = (flat_ids[:, None] == jnp.arange(experts_all, dtype=jnp.int32)[None, :]).astype(
        jnp.int32
    )
    order = jnp.arange(flat_ids.shape[0], dtype=jnp.int32)
    earlier = (order[None, :] < order[:, None]).astype(jnp.bfloat16)
    counts_before = product(earlier, slot_hits.astype(jnp.bfloat16)).astype(jnp.int32)
    slot_place = jnp.sum(counts_before * slot_hits, axis=1)

    def to_slots(routed_rows):
        empty_slots = jnp.zeros((experts_all, capacity, model_width), jnp.bfloat16)
        return (
            empty_slots.at[flat_ids, slot_place]
            .set(routed_rows)
            .reshape(exp_count, local_experts, capacity, model_width)
        )

    def from_slots(arrived_back):
        picked = arrived_back.reshape(experts_all, capacity, model_width)[flat_ids, slot_place]
        return picked.astype(jnp.float32).reshape(local_rows, TOP, model_width)

    def expert_front(arrived_rows):
        gate_pre = jnp.einsum(
            "sjcd,jdf->sjcf", arrived_rows, expert_gate, preferred_element_type=jnp.float32
        )
        up_pre = jnp.einsum(
            "sjcd,jdf->sjcf", arrived_rows, expert_up, preferred_element_type=jnp.float32
        )
        hidden = (jax.nn.silu(gate_pre) * up_pre).astype(jnp.bfloat16)
        return (gate_pre, up_pre, hidden)

    send_rows = to_slots(jnp.repeat(second, TOP, axis=0))
    arrived = lax.all_to_all(send_rows, "exp", split_axis=0, concat_axis=0, tiled=True)
    gate_pre, up_pre, hidden = expert_front(arrived)
    results = jnp.einsum(
        "sjcf,jfd->sjcd", hidden, expert_down, preferred_element_type=jnp.float32
    ).astype(jnp.bfloat16)
    returned = lax.all_to_all(results, "exp", split_axis=0, concat_axis=0, tiled=True)
    expert_out = from_slots(returned)
    mixture = jnp.sum(gates[:, :, None] * expert_out, axis=1)
    shared_gate_pre = product(second, shared_gate)
    shared_up_pre = product(second, shared_up)
    shared_hidden = (jax.nn.silu(shared_gate_pre) * shared_up_pre).astype(jnp.bfloat16)
    output = (mixed + mixture + product(shared_hidden, shared_down)).astype(jnp.bfloat16)
    upstream = cotangent[0]
    upstream_full = upstream.astype(jnp.float32)
    grad_shared_down = outer_sum(shared_hidden, upstream)
    d_shared_hidden = against(upstream, shared_down)
    shared_silu, shared_slope = silu_parts(shared_gate_pre)
    d_shared_gate = (d_shared_hidden * shared_up_pre * shared_slope).astype(jnp.bfloat16)
    d_shared_up = (d_shared_hidden * shared_silu).astype(jnp.bfloat16)
    grad_shared_gate = outer_sum(second, d_shared_gate)
    grad_shared_up = outer_sum(second, d_shared_up)
    d_second = against(d_shared_gate, shared_gate) + against(d_shared_up, shared_up)
    d_gates = jnp.sum(upstream_full[:, None, :] * expert_out, axis=-1)
    d_selected = gates * (d_gates - jnp.sum(gates * d_gates, axis=-1, keepdims=True))
    d_logits = jnp.sum(d_selected[:, :, None] * one_hot, axis=1).astype(jnp.bfloat16)
    grad_router = outer_sum(second, d_logits)
    d_second = d_second + against(d_logits, w_router)
    grad_slots = to_slots(
        (gates[:, :, None] * upstream_full[:, None, :])
        .astype(jnp.bfloat16)
        .reshape(local_rows * TOP, model_width)
    )
    arrived_rows, arrived_grad = (
        lax.all_to_all(send_rows, "exp", split_axis=0, concat_axis=0, tiled=True),
        lax.all_to_all(grad_slots, "exp", split_axis=0, concat_axis=0, tiled=True),
    )
    gate_kept, up_kept, hidden_kept = expert_front(arrived_rows)
    d_hidden = jnp.einsum(
        "sjcd,jfd->sjcf", arrived_grad, expert_down, preferred_element_type=jnp.float32
    )
    expert_silu, expert_slope = silu_parts(gate_kept)
    d_gate_pre = (d_hidden * up_kept * expert_slope).astype(jnp.bfloat16)
    d_up_pre = (d_hidden * expert_silu).astype(jnp.bfloat16)
    grad_expert_down = jnp.einsum(
        "sjcf,sjcd->jfd", hidden_kept, arrived_grad, preferred_element_type=jnp.float32
    )
    grad_expert_gate = jnp.einsum(
        "sjcd,sjcf->jdf", arrived_rows, d_gate_pre, preferred_element_type=jnp.float32
    )
    grad_expert_up = jnp.einsum(
        "sjcd,sjcf->jdf", arrived_rows, d_up_pre, preferred_element_type=jnp.float32
    )
    d_routed = (
        jnp.einsum("sjcf,jdf->sjcd", d_gate_pre, expert_gate, preferred_element_type=jnp.float32)
        + jnp.einsum("sjcf,jdf->sjcd", d_up_pre, expert_up, preferred_element_type=jnp.float32)
    ).astype(jnp.bfloat16)
    returned_grad = lax.all_to_all(d_routed, "exp", split_axis=0, concat_axis=0, tiled=True)
    d_second = d_second + jnp.sum(from_slots(returned_grad), axis=1)
    grad_expert_gate, grad_expert_up, grad_expert_down = (
        lax.psum(grad_expert_gate.astype(jnp.bfloat16), ("seq", "ctx")).astype(jnp.float32),
        lax.psum(grad_expert_up.astype(jnp.bfloat16), ("seq", "ctx")).astype(jnp.float32),
        lax.psum(grad_expert_down.astype(jnp.bfloat16), ("seq", "ctx")).astype(jnp.float32),
    )
    d_mixed_part, grad_norm_two = norm_two_pull(d_second)
    d_mixed = upstream_full + d_mixed_part
    d_attention = d_mixed.astype(jnp.bfloat16)
    grad_out = outer_sum(attended, d_attention)
    grad_heads = (
        against(d_attention, w_out).astype(jnp.bfloat16).reshape(local_rows, head_count, HEAD_DIM)
    )
    keys_all, values_all = (
        lax.all_gather(keys_local, "ctx", axis=0, tiled=True),
        lax.all_gather(values_local, "ctx", axis=0, tiled=True),
    )
    block_total = ((ctx_place + 1) * local_rows + KEY_ROWS - 1) // KEY_ROWS

    def weights_at(number):
        offset = number * KEY_ROWS
        key_block = lax.dynamic_slice_in_dim(keys_all, offset, KEY_ROWS, 0)
        value_block = lax.dynamic_slice_in_dim(values_all, offset, KEY_ROWS, 0)
        scores, allowed = block_scores(key_block, offset)
        weights = jnp.where(allowed[None], jnp.exp(scores - log_total[..., None]), 0.0)
        grad_weights = jnp.einsum(
            "qhd,khd->hqk",
            grad_heads,
            value_block.reshape(KEY_ROWS, head_count, HEAD_DIM),
            preferred_element_type=jnp.float32,
        )
        return (key_block, weights, grad_weights)

    def row_dot_step(number, summed):
        unused_block, weights, grad_weights = weights_at(number)
        return summed + jnp.sum(weights * grad_weights, axis=-1)

    row_dots = lax.fori_loop(
        0, block_total, row_dot_step, jnp.zeros((head_count, local_rows), jnp.float32)
    )

    def score_grads(number):
        key_block, weights, grad_weights = weights_at(number)
        d_scores = (weights * (grad_weights - row_dots[..., None])).astype(jnp.bfloat16)
        return (key_block.reshape(KEY_ROWS, head_count, HEAD_DIM), weights, d_scores)

    query_start = jnp.zeros((local_rows, head_count, HEAD_DIM), jnp.float32)

    def grad_step(number, running):
        grad_query, key_terms = running
        key_heads, weights, d_scores = score_grads(number)
        grad_query = (
            grad_query
            + jnp.einsum("hqk,khd->qhd", d_scores, key_heads, preferred_element_type=jnp.float32)
            * score_scale
        )
        key_part = (
            jnp.einsum("hqk,qhd->khd", d_scores, query, preferred_element_type=jnp.float32)
            * score_scale
        )
        value_part = jnp.einsum(
            "hqk,qhd->khd",
            weights.astype(jnp.bfloat16),
            grad_heads,
            preferred_element_type=jnp.float32,
        )
        block_terms = jnp.concatenate(
            [key_part.reshape(KEY_ROWS, model_width), value_part.reshape(KEY_ROWS, model_width)],
            axis=1,
        )
        return (
            grad_query,
            lax.dynamic_update_slice_in_dim(key_terms, block_terms, number * KEY_ROWS, 0),
        )

    grad_query_heads, key_terms = lax.fori_loop(
        0,
        block_total,
        grad_step,
        (query_start, jnp.zeros((ctx_count * local_rows, 2 * model_width), jnp.float32)),
    )
    key_grads = lax.psum_scatter(
        key_terms.astype(jnp.bfloat16), "ctx", scatter_dimension=0, tiled=True
    ).astype(jnp.float32)
    key_grad_heads = key_grads[:, :model_width].reshape(local_rows, head_count, HEAD_DIM)
    d_value = key_grads[:, model_width:].astype(jnp.bfloat16)
    d_query_lin = (
        rotate(grad_query_heads, -places).astype(jnp.bfloat16).reshape(local_rows, model_width)
    )
    d_key_lin = (
        rotate(key_grad_heads, -places).astype(jnp.bfloat16).reshape(local_rows, model_width)
    )
    grad_query = outer_sum(normed, d_query_lin)
    grad_key = outer_sum(normed, d_key_lin)
    grad_value = outer_sum(normed, d_value)
    d_normed = against(d_query_lin, w_query) + against(d_key_lin, w_key) + against(d_value, w_value)
    d_inputs, grad_norm_one = norm_one_pull(d_normed)
    grad_tokens = (d_mixed + d_inputs)[None]
    (
        grad_query,
        grad_key,
        grad_value,
        grad_out,
        grad_router,
        grad_shared_gate,
        grad_shared_up,
        grad_shared_down,
    ) = (
        lax.psum_scatter(
            spread(grad_query), ("seq", "ctx", "exp"), scatter_dimension=0, tiled=True
        ),
        lax.psum_scatter(spread(grad_key), ("seq", "ctx", "exp"), scatter_dimension=0, tiled=True),
        lax.psum_scatter(
            spread(grad_value), ("seq", "ctx", "exp"), scatter_dimension=0, tiled=True
        ),
        lax.psum_scatter(spread(grad_out), ("seq", "ctx", "exp"), scatter_dimension=0, tiled=True),
        lax.psum_scatter(
            spread(grad_router), ("seq", "ctx", "exp"), scatter_dimension=0, tiled=True
        ),
        lax.psum_scatter(
            spread(grad_shared_gate), ("seq", "ctx", "exp"), scatter_dimension=0, tiled=True
        ),
        lax.psum_scatter(
            spread(grad_shared_up), ("seq", "ctx", "exp"), scatter_dimension=0, tiled=True
        ),
        lax.psum_scatter(
            spread(grad_shared_down), ("seq", "ctx", "exp"), scatter_dimension=0, tiled=True
        ),
    )
    grad_norm_one, grad_norm_two = lax.psum((grad_norm_one, grad_norm_two), ("seq", "ctx", "exp"))
    return (
        output[None],
        grad_tokens,
        grad_norm_one,
        grad_query,
        grad_key,
        grad_value,
        grad_out,
        grad_norm_two,
        grad_router,
        grad_expert_gate,
        grad_expert_up,
        grad_expert_down,
        grad_shared_gate,
        grad_shared_up,
        grad_shared_down,
    )


def add_blocks(target, first, second, count, height, step):
    chunks = height // step

    def body(number, carry):
        j = number // chunks
        at = pl.ds(pl.multiple_of((number % chunks) * step, step), step)
        total = first[j, at, :].astype(jnp.float32) + second[j, at, :].astype(jnp.float32)
        target[j, at, :] = total.astype(target.dtype)
        return carry

    lax.fori_loop(0, count * chunks, body, 0)


def reduce_kernel(shapes, expert_count, *refs):
    number = len(shapes)
    plain = number - expert_count
    refs = list(refs)

    def take(n):
        out = refs[:n]
        del refs[:n]
        return out

    grads = take(number)
    (misc_in,) = take(1)
    whole = take(expert_count)
    owned = take(plain)
    (misc_out,) = take(1)
    own = take(number)
    got1 = take(number)
    got2 = take(number)
    got3 = take(number)
    zsend = take(plain)
    zgot = take(plain)
    misc_got, own_sem = take(2)
    sem1, rem1, sem2, rem2, sem3, rem3 = take(6)
    gsem, grem, lsem, zsem, zrem, msem, mrem = take(7)

    s = lax.axis_index("seq")
    c = lax.axis_index("ctx")
    e = lax.axis_index("exp")
    x, k = c // 2, c % 2
    to_core = (s, x * 2 + (1 - k), e)
    to_x = (s, (1 - x) * 2 + k, e)
    to_y = (1 - s, c, e)
    to_z = [(s, c, lax.rem(e + d, 4)) for d in (1, 2, 3)]

    barrier = pltpu.get_barrier_semaphore()
    for device in (to_core, to_x, to_y, *to_z):
        pl.semaphore_signal(barrier, inc=1, device_id=device, device_id_type=MESH)
    pl.semaphore_wait(barrier, 6)

    def send(src, dst, ssem, rsem, device):
        copy = pltpu.make_async_remote_copy(
            src_ref=src, dst_ref=dst, send_sem=ssem, recv_sem=rsem, device_id=device, device_id_type=MESH
        )
        copy.start()
        return copy

    copies = []
    first = []
    for i in range(number):
        local = pltpu.make_async_copy(grads[i].at[:, :, k], own[i], own_sem.at[i])
        local.start()
        first.append(
            (local, send(grads[i].at[:, :, 1 - k], got1[i], sem1.at[i], rem1.at[i], to_core))
        )
    mcopy = send(misc_in, misc_got.at[0], msem.at[0], mrem.at[0], to_core)
    second = []
    for i in range(number):
        rows, width = shapes[i]
        half = rows // 2
        local, copy = first[i]
        local.wait()
        copy.wait()
        for a in range(2):
            add_blocks(got1[i].at[a], got1[i].at[a], own[i].at[a], 2, rows, half)
        second.append(
            (
                send(got1[i].at[:, 1 - x, pl.ds(0, half)], got2[i].at[0], sem2.at[i, 0], rem2.at[i, 0], to_x),
                send(got1[i].at[1 - s, :, pl.ds(half, half)], got2[i].at[1], sem2.at[i, 1], rem2.at[i, 1], to_y),
            )
        )
    mcopy.wait()
    misc_out[...] = misc_in[...] + misc_got[0]
    mcopy = send(misc_out, misc_got.at[1], msem.at[1], mrem.at[1], to_x)
    third = []
    for i in range(number):
        rows, width = shapes[i]
        half = rows // 2
        second[i][0].wait()
        add_blocks(got2[i].at[0], got2[i].at[0], got1[i].at[:, x, pl.ds(0, half)], 2, half, half)
        second[i][1].wait()
        add_blocks(got2[i].at[1], got2[i].at[1], got1[i].at[s, :, pl.ds(half, half)], 2, half, half)
        third.append(
            (
                send(got2[i].at[0, 1 - s], got3[i].at[0], sem3.at[i, 0], rem3.at[i, 0], to_y),
                send(got2[i].at[1, 1 - x], got3[i].at[1], sem3.at[i, 1], rem3.at[i, 1], to_x),
            )
        )
    mcopy.wait()
    misc_got[3] = misc_out[...] + misc_got[1]
    mcopy = send(misc_got.at[3], misc_got.at[2], msem.at[2], mrem.at[2], to_y)
    gather = []
    zcopies = []
    for i in range(number):
        rows, width = shapes[i]
        half = rows // 2
        third[i][0].wait()
        third[i][1].wait()
        mine = (got2[i].at[0, s], got2[i].at[1, x])
        if i < expert_count:
            legs = []
            for h in range(2):
                got3[i][h] = (got3[i][h].astype(jnp.float32) + mine[h][...].astype(jnp.float32)).astype(jnp.bfloat16)
                here = whole[i].at[s, x, k, pl.ds(h * half, half)]
                local = pltpu.make_async_copy(got3[i].at[h], here, lsem.at[i, h])
                local.start()
                legs.append(
                    (
                        local,
                        send(got3[i].at[h], here, gsem.at[i, h, 0], grem.at[i, h, 0], (to_y, to_x)[h]),
                        send(got3[i].at[h], here, gsem.at[i, h, 1], grem.at[i, h, 1], (to_x, to_y)[h]),
                    )
                )
            gather.append(legs)
        else:
            j = i - expert_count
            columns = width // 4
            for h in range(2):
                total = (got3[i][h].astype(jnp.float32) + mine[h][...].astype(jnp.float32)).astype(jnp.bfloat16)
                for q in range(4):
                    zsend[j][q, pl.ds(h * half, half), :] = total[:, q * columns : (q + 1) * columns]
            zcopies.append(
                [
                    send(zsend[j].at[lax.rem(e + d, 4)], zgot[j].at[d - 1], zsem.at[j, d - 1], zrem.at[j, d - 1], to_z[d - 1])
                    for d in (1, 2, 3)
                ]
            )
    mcopy.wait()
    misc_got[4] = misc_got[3] + misc_got[2]
    mz = [
        send(misc_got.at[4], misc_got.at[5 + d], msem.at[3 + d], mrem.at[3 + d], to_z[d]) for d in range(3)
    ]
    onward = []
    for i in range(expert_count):
        half = shapes[i][0] // 2
        legs = []
        for h in range(2):
            gather[i][h][1].wait()
            part = pl.ds(h * half, half)
            there = whole[i].at[(1 - s, s)[h], (x, 1 - x)[h], k, part]
            legs.append(send(there, there, gsem.at[i, h, 2], grem.at[i, h, 2], (to_x, to_y)[h]))
        onward.append(legs)
    last = []
    for i in range(expert_count):
        for h in range(2):
            gather[i][h][0].wait()
            gather[i][h][2].wait()
            onward[i][h].wait()
        last.append(send(whole[i].at[:, :, k], whole[i].at[:, :, k], gsem.at[i, 0, 3], grem.at[i, 0, 3], to_core))
    for j in range(plain):
        for copy in zcopies[j]:
            copy.wait()
        owned[j][...] = (
            zsend[j][e].astype(jnp.float32)
            + zgot[j][0].astype(jnp.float32)
            + zgot[j][1].astype(jnp.float32)
            + zgot[j][2].astype(jnp.float32)
        )
    for copy in mz:
        copy.wait()
    misc_out[...] = misc_got[4] + misc_got[5] + misc_got[6] + misc_got[7]
    for copy in last:
        copy.wait()


def reduce_grads(expert_grads, plain_grads, misc):
    def blocks(matrix):
        return matrix.reshape(2, 2, 2, matrix.shape[0] // 8, matrix.shape[1])

    arrays = [blocks(m) for m in (*expert_grads, *plain_grads)]
    shapes = [(a.shape[3], a.shape[4]) for a in arrays]
    count, plain = len(expert_grads), len(plain_grads)
    low, full = jnp.bfloat16, jnp.float32
    vmem, dma = pltpu.VMEM, pltpu.SemaphoreType.DMA
    n = len(arrays)
    in_specs = [pl.BlockSpec(memory_space=pl.ANY)] * n + [pl.BlockSpec(memory_space=pltpu.VMEM)]
    out_shape = (
        [jax.ShapeDtypeStruct(a.shape, low) for a in arrays[:count]]
        + [jax.ShapeDtypeStruct((r, w // 4), full) for r, w in shapes[count:]]
        + [jax.ShapeDtypeStruct(misc.shape, full)]
    )
    out_specs = [pl.BlockSpec(memory_space=pl.ANY)] * count + [pl.BlockSpec(memory_space=pltpu.VMEM)] * (plain + 1)
    scratch = (
        [vmem((2, 2, r, w), low) for r, w in shapes]
        + [vmem((2, 2, r, w), low) for r, w in shapes]
        + [vmem((2, 2, r // 2, w), low) for r, w in shapes]
        + [vmem((2, r // 2, w), low) for r, w in shapes]
        + [vmem((4, r, w // 4), low) for r, w in shapes[count:]]
        + [vmem((3, r, w // 4), low) for r, w in shapes[count:]]
        + [vmem((8, *misc.shape), full), dma((n,))]
        + [dma((n,)), dma((n,)), dma((n, 2)), dma((n, 2)), dma((n, 2)), dma((n, 2))]
        + [dma((count, 2, 4)), dma((count, 2, 4)), dma((count, 2)), dma((plain, 3)), dma((plain, 3)), dma((6,)), dma((6,))]
    )
    results = pl.pallas_call(
        functools.partial(reduce_kernel, shapes, count),
        out_shape=out_shape,
        in_specs=in_specs,
        out_specs=out_specs,
        scratch_shapes=scratch,
        compiler_params=pltpu.CompilerParams(
            collective_id=1, has_side_effects=True, vmem_limit_bytes=58 * 2**20
        ),
        name="reduce_grads",
    )(*arrays, misc)
    whole = [r.reshape(g.shape) for r, g in zip(results[:count], expert_grads)]
    return whole, results[count : count + plain], results[-1]


def per_device_dense(
    tokens,
    expert_ids,
    norm_one,
    w_query,
    w_key,
    w_value,
    w_out,
    norm_two,
    w_router,
    expert_gate,
    expert_up,
    expert_down,
    shared_gate,
    shared_up,
    shared_down,
    cotangent,
):
    rows = tokens.shape[1]
    width = tokens.shape[2]
    heads = width // HEAD_DIM
    scale = HEAD_DIM ** (-0.5)
    ctx_count = lax.axis_size("ctx")
    ctx_place = lax.axis_index("ctx")
    exp_count = lax.axis_size("exp")
    exp_place = lax.axis_index("exp")
    row_groups = lax.axis_size("seq") * ctx_count
    places = ctx_place * rows + jnp.arange(rows, dtype=jnp.int32)
    upstream = cotangent[0]
    ids = expert_ids[0]

    upstream_all = lax.all_gather(upstream, "exp", axis=0, tiled=True)
    ids_all = lax.all_gather(ids, "exp", axis=0, tiled=True)

    inputs = tokens[0].astype(jnp.float32)
    normed_full, norm_one_pull = jax.vjp(normalize, inputs, norm_one)
    normed = normed_full.astype(jnp.bfloat16)

    def heads_of(matrix):
        return matrix.reshape(matrix.shape[0], heads, HEAD_DIM)

    query = rotate(heads_of(product(normed, w_query)), places).astype(jnp.bfloat16)
    keys = rotate(heads_of(product(normed, w_key)), places).astype(jnp.bfloat16)
    values = product(normed, w_value).astype(jnp.bfloat16)
    both = jnp.concatenate([keys.reshape(rows, width), values], axis=1)
    both_all = lax.all_gather(both, "ctx", axis=0, tiled=True)
    keys_all, values_all = heads_of(both_all[:, :width]), heads_of(both_all[:, width:])
    span = keys_all.shape[0]
    allowed = (jnp.arange(span, dtype=jnp.int32) // BLOCK)[None, None, :] <= (
        places // BLOCK
    )[None, :, None]
    scores = jnp.einsum("qhd,khd->hqk", query, keys_all, preferred_element_type=jnp.float32)
    scores = jnp.where(allowed, scores * scale, -1e30)
    highest = jnp.max(scores, axis=-1, keepdims=True)
    unscaled = jnp.exp(scores - highest)
    totals = jnp.sum(unscaled, axis=-1, keepdims=True)
    weights = unscaled / totals
    weights_low = weights.astype(jnp.bfloat16)
    attended = (
        jnp.einsum("hqk,khd->qhd", weights_low, values_all, preferred_element_type=jnp.float32)
        .reshape(rows, width)
        .astype(jnp.bfloat16)
    )
    mixed = inputs + product(attended, w_out)
    second_full, norm_two_pull = jax.vjp(normalize, mixed, norm_two)
    second = second_full.astype(jnp.bfloat16)
    experts_all = w_router.shape[1]

    def gates_of(rows_second, rows_ids):
        logits = product(rows_second, w_router)
        named = jnp.any(
            rows_ids[:, :, None] == jnp.arange(experts_all, dtype=jnp.int32)[None, None, :], axis=1
        )
        masked = jnp.where(named, logits, -1e30)
        raised = jnp.where(named, jnp.exp(masked - jnp.max(masked, axis=-1, keepdims=True)), 0.0)
        return raised / jnp.sum(raised, axis=-1, keepdims=True), named

    shares, named = gates_of(second, ids)
    second_all = lax.all_gather(second, "exp", axis=0, tiled=True)
    shares_all, unused = gates_of(second_all, ids_all)
    mine = (jnp.arange(experts_all, dtype=jnp.int32) == exp_place)[None, :]
    share = jnp.sum(jnp.where(mine, shares_all, 0.0), axis=1, keepdims=True)
    gate_w, up_w, down_w = expert_gate[0], expert_up[0], expert_down[0]
    d_result = (share * upstream_all.astype(jnp.float32)).astype(jnp.bfloat16)
    gate_pre = product(second_all, gate_w)
    up_pre = product(second_all, up_w)
    silu, slope = silu_parts(gate_pre)
    hidden = (silu * up_pre).astype(jnp.bfloat16)
    result = product(hidden, down_w).astype(jnp.bfloat16)
    d_hidden = against(d_result, down_w)
    d_gate_pre = (d_hidden * up_pre * slope).astype(jnp.bfloat16)
    d_up_pre = (d_hidden * silu).astype(jnp.bfloat16)
    d_routed = (against(d_gate_pre, gate_w) + against(d_up_pre, up_w)).astype(jnp.bfloat16)
    expert_grads = (
        outer_sum(second_all, d_gate_pre),
        outer_sum(second_all, d_up_pre),
        outer_sum(hidden, d_result),
    )
    back = jnp.stack(
        [result.reshape(exp_count, rows, width), d_routed.reshape(exp_count, rows, width)], axis=1
    )
    back = lax.all_to_all(back, "exp", split_axis=0, concat_axis=0, tiled=True)
    expert_out = back[:, 0].astype(jnp.float32)
    shared_gate_pre = product(second, shared_gate)
    shared_up_pre = product(second, shared_up)
    shared_silu, shared_slope = silu_parts(shared_gate_pre)
    shared_hidden = (shared_silu * shared_up_pre).astype(jnp.bfloat16)
    d_shared_hidden = against(upstream, shared_down)
    d_shared_gate = (d_shared_hidden * shared_up_pre * shared_slope).astype(jnp.bfloat16)
    d_shared_up = (d_shared_hidden * shared_silu).astype(jnp.bfloat16)
    grad_shared_gate = outer_sum(second, d_shared_gate)
    grad_shared_up = outer_sum(second, d_shared_up)
    grad_shared_down = outer_sum(shared_hidden, upstream)
    mixture = jnp.sum(shares.T[:, :, None] * expert_out, axis=0)
    output = (mixed + mixture + product(shared_hidden, shared_down)).astype(jnp.bfloat16)
    upstream_full = upstream.astype(jnp.float32)
    d_gates = jnp.sum(upstream_full[None] * expert_out, axis=-1).T
    d_gates = jnp.where(named, d_gates, 0.0)
    d_logits = (shares * (d_gates - jnp.sum(shares * d_gates, axis=-1, keepdims=True))).astype(
        jnp.bfloat16
    )
    grad_router = outer_sum(second, d_logits)
    d_second = (
        against(d_shared_gate, shared_gate)
        + against(d_shared_up, shared_up)
        + against(d_logits, w_router)
        + jnp.sum(back[:, 1].astype(jnp.float32), axis=0)
    )
    d_mixed_part, grad_norm_two = norm_two_pull(d_second)
    d_mixed = upstream_full + d_mixed_part
    d_attention = d_mixed.astype(jnp.bfloat16)
    grad_out = outer_sum(attended, d_attention)
    d_attended = heads_of(against(d_attention, w_out).astype(jnp.bfloat16))
    d_weights = jnp.einsum(
        "qhd,khd->hqk", d_attended, values_all, preferred_element_type=jnp.float32
    )
    delta = jnp.sum(weights * d_weights, axis=-1, keepdims=True)
    d_scores = (weights * (d_weights - delta)).astype(jnp.bfloat16)
    d_query = (
        jnp.einsum("hqk,khd->qhd", d_scores, keys_all, preferred_element_type=jnp.float32) * scale
    )
    d_key = (
        jnp.einsum("hqk,qhd->khd", d_scores, query, preferred_element_type=jnp.float32) * scale
    )
    d_value = jnp.einsum(
        "hqk,qhd->khd", weights_low, d_attended, preferred_element_type=jnp.float32
    )
    key_terms = jnp.concatenate([d_key.reshape(span, width), d_value.reshape(span, width)], axis=1)
    key_grads = lax.psum_scatter(
        key_terms.astype(jnp.bfloat16), "ctx", scatter_dimension=0, tiled=True
    )
    d_value = key_grads[:, width:]
    d_key_lin = rotate(heads_of(key_grads[:, :width].astype(jnp.float32)), -places)
    d_key_lin = d_key_lin.astype(jnp.bfloat16).reshape(rows, width)
    d_query_lin = rotate(d_query, -places).astype(jnp.bfloat16).reshape(rows, width)
    grad_query = outer_sum(normed, d_query_lin)
    grad_key = outer_sum(normed, d_key_lin)
    grad_value = outer_sum(normed, d_value)
    d_normed = against(d_query_lin, w_query) + against(d_key_lin, w_key) + against(d_value, w_value)
    d_inputs, grad_norm_one = norm_one_pull(d_normed)
    grad_tokens = (d_mixed + d_inputs)[None]
    misc = jnp.concatenate(
        [grad_norm_one[None], grad_norm_two[None], grad_router.T, jnp.zeros((2, width), jnp.float32)],
        axis=0,
    )
    low = [g.astype(jnp.bfloat16) for g in expert_grads]
    plain = [
        g.astype(jnp.bfloat16)
        for g in (
            grad_query,
            grad_key,
            grad_value,
            grad_out,
            grad_shared_gate,
            grad_shared_up,
            grad_shared_down,
        )
    ]
    whole, owned, misc = reduce_grads(low, plain, misc)
    row_place = lax.axis_index("seq") * ctx_count + ctx_place
    own_rows = width // row_groups
    router = lax.dynamic_slice(misc, (2 + exp_place, row_place * own_rows), (1, own_rows))
    return (
        output[None],
        grad_tokens,
        misc[0],
        *owned[:4],
        misc[1],
        router.T,
        *[g.astype(jnp.float32)[None] for g in whole],
        *owned[4:],
    )


def fits(mesh):
    return dict(mesh.shape) == {"seq": 2, "ctx": 4, "exp": 4}


def solution(mesh):
    per_device = per_device_dense if fits(mesh) else per_device_slots
    in_specs = (
        P(("seq", "exp"), "ctx", None),
        P(("seq", "exp"), "ctx", None),
        P(),
        P(),
        P(),
        P(),
        P(),
        P(),
        P(),
        P("exp", None, None),
        P("exp", None, None),
        P("exp", None, None),
        P(),
        P(),
        P(),
        P(("seq", "exp"), "ctx", None),
    )
    out_specs = (
        P(("seq", "exp"), "ctx", None),
        P(("seq", "exp"), "ctx", None),
        P(),
        P(("seq", "ctx"), "exp"),
        P(("seq", "ctx"), "exp"),
        P(("seq", "ctx"), "exp"),
        P(("seq", "ctx"), "exp"),
        P(),
        P(("seq", "ctx"), "exp"),
        P("exp", None, None),
        P("exp", None, None),
        P("exp", None, None),
        P(("seq", "ctx"), "exp"),
        P(("seq", "ctx"), "exp"),
        P(("seq", "ctx"), "exp"),
    )
    return jax.shard_map(
        per_device, mesh=mesh, in_specs=in_specs, out_specs=out_specs, check_vma=False
    )
```

```python
import functools
import math

import jax
import jax.numpy as jnp
import numpy as np
from jax import lax
from jax.experimental import pallas as pl
from jax.experimental.pallas import tpu as pltpu
from jax.sharding import PartitionSpec as P

HEAD_DIM = 64
TOP = 2
BLOCK = 256
KEY_ROWS = 512
MESH = pl.DeviceIdType.MESH


def product(first_factor, second_factor):
    return jnp.dot(first_factor, second_factor, preferred_element_type=jnp.float32)


def against(first_factor, second_factor):
    return lax.dot_general(
        first_factor, second_factor, (((1,), (1,)), ((), ())), preferred_element_type=jnp.float32
    )


def outer_sum(first_factor, second_factor):
    return lax.dot_general(
        first_factor, second_factor, (((0,), (0,)), ((), ())), preferred_element_type=jnp.float32
    )


def normalize(values, scaling):
    return values * lax.rsqrt(jnp.mean(values * values, axis=-1, keepdims=True) + 1e-06) * scaling


def rotate(values, places):
    halfway = values.shape[-1] // 2
    frequency = 10000.0 ** (-jnp.arange(halfway, dtype=jnp.float32) / halfway)
    angles = places.astype(jnp.float32)[:, None] * frequency[None, :]
    cosine = jnp.cos(angles)[:, None, :]
    sine_part = jnp.sin(angles)[:, None, :]
    former = values[..., :halfway]
    latter = values[..., halfway:]
    return jnp.concatenate(
        [former * cosine - latter * sine_part, latter * cosine + former * sine_part], axis=-1
    )


def silu_parts(gate_pre):
    sigmoid_value = jax.nn.sigmoid(gate_pre)
    return (gate_pre * sigmoid_value, sigmoid_value * (1.0 + gate_pre * (1.0 - sigmoid_value)))


def tiled(matrix, row_groups, col_groups):
    row_count, col_count = matrix.shape
    blocks = matrix.reshape(
        row_groups, row_count // row_groups, col_groups, col_count // col_groups
    ).transpose(0, 2, 1, 3)
    return blocks.reshape(col_groups * row_count, col_count // col_groups)


def per_device_slots(
    tokens,
    expert_ids,
    norm_one,
    w_query,
    w_key,
    w_value,
    w_out,
    norm_two,
    w_router,
    expert_gate,
    expert_up,
    expert_down,
    shared_gate,
    shared_up,
    shared_down,
    cotangent,
):
    local_rows = tokens.shape[1]
    model_width = tokens.shape[2]
    head_count = model_width // HEAD_DIM
    score_scale = HEAD_DIM ** (-0.5)
    ctx_count = lax.axis_size("ctx")
    ctx_place = lax.axis_index("ctx")
    exp_count = lax.axis_size("exp")
    row_groups = lax.axis_size("seq") * ctx_count
    local_experts = expert_gate.shape[0]
    experts_all = local_experts * exp_count
    capacity = min(local_rows, 2 * TOP * local_rows // experts_all)
    places = ctx_place * local_rows + jnp.arange(local_rows, dtype=jnp.int32)
    query_blocks = places // BLOCK

    def spread(matrix):
        return tiled(matrix, row_groups, exp_count)

    inputs = tokens[0].astype(jnp.float32)
    normed_full, norm_one_pull = jax.vjp(normalize, inputs, norm_one)
    normed = normed_full.astype(jnp.bfloat16)
    query = rotate(
        product(normed, w_query).reshape(local_rows, head_count, HEAD_DIM), places
    ).astype(jnp.bfloat16)
    keys_local = (
        rotate(product(normed, w_key).reshape(local_rows, head_count, HEAD_DIM), places)
        .astype(jnp.bfloat16)
        .reshape(local_rows, model_width)
    )
    values_local = product(normed, w_value).astype(jnp.bfloat16)

    def block_scores(key_block, offset):
        key_heads = key_block.reshape(-1, head_count, HEAD_DIM)
        scores = (
            jnp.einsum("qhd,khd->hqk", query, key_heads, preferred_element_type=jnp.float32)
            * score_scale
        )
        key_index = (offset + jnp.arange(key_block.shape[0], dtype=jnp.int32)) // BLOCK
        allowed = key_index[None, :] <= query_blocks[:, None]
        return (scores, allowed)

    def attend_block(running, key_block, value_block, offset):
        highest, totals, accumulated = running
        scores, allowed = block_scores(key_block, offset)
        masked = jnp.where(allowed[None], scores, -1e30)
        fresh = jnp.maximum(highest, jnp.max(masked, axis=-1))
        weights = jnp.where(allowed[None], jnp.exp(masked - fresh[..., None]), 0.0)
        decay = jnp.exp(highest - fresh)
        value_heads = value_block.reshape(-1, head_count, HEAD_DIM)
        accumulated = accumulated * decay[..., None] + jnp.einsum(
            "hqk,khd->hqd",
            weights.astype(jnp.bfloat16),
            value_heads,
            preferred_element_type=jnp.float32,
        )
        return (fresh, totals * decay + jnp.sum(weights, axis=-1), accumulated)

    start_state = (
        jnp.full((head_count, local_rows), -1e30, jnp.float32),
        jnp.zeros((head_count, local_rows), jnp.float32),
        jnp.zeros((head_count, local_rows, HEAD_DIM), jnp.float32),
    )
    running = start_state
    key_part = lax.all_gather(keys_local, "ctx", axis=0, tiled=True)
    value_part = lax.all_gather(values_local, "ctx", axis=0, tiled=True)
    span_rows = key_part.shape[0]
    stride = math.gcd(span_rows, KEY_ROWS)
    step_count = span_rows // stride
    key_steps = key_part.reshape(step_count, stride, model_width)
    value_steps = value_part.reshape(step_count, stride, model_width)
    offsets = jnp.arange(step_count, dtype=jnp.int32) * stride

    def one_step(inner, operands):
        return (attend_block(inner, operands[0], operands[1], operands[2]), None)

    running, unused = lax.scan(one_step, running, (key_steps, value_steps, offsets))
    highest, totals, accumulated = running
    log_total = highest + jnp.log(totals)
    attended = (
        (accumulated / totals[..., None])
        .transpose(1, 0, 2)
        .reshape(local_rows, model_width)
        .astype(jnp.bfloat16)
    )
    mixed = inputs + product(attended, w_out)
    second_full, norm_two_pull = jax.vjp(normalize, mixed, norm_two)
    second = second_full.astype(jnp.bfloat16)
    logits = product(second, w_router)
    chosen = expert_ids[0]
    one_hot = (
        chosen[:, :, None] == jnp.arange(experts_all, dtype=jnp.int32)[None, None, :]
    ).astype(jnp.float32)
    selected = jnp.sum(logits[:, None, :] * one_hot, axis=-1)
    gates = jax.nn.softmax(selected, axis=-1)
    flat_ids = chosen.reshape(-1)
    slot_hits = (flat_ids[:, None] == jnp.arange(experts_all, dtype=jnp.int32)[None, :]).astype(
        jnp.int32
    )
    order = jnp.arange(flat_ids.shape[0], dtype=jnp.int32)
    earlier = (order[None, :] < order[:, None]).astype(jnp.bfloat16)
    counts_before = product(earlier, slot_hits.astype(jnp.bfloat16)).astype(jnp.int32)
    slot_place = jnp.sum(counts_before * slot_hits, axis=1)

    def to_slots(routed_rows):
        empty_slots = jnp.zeros((experts_all, capacity, model_width), jnp.bfloat16)
        return (
            empty_slots.at[flat_ids, slot_place]
            .set(routed_rows)
            .reshape(exp_count, local_experts, capacity, model_width)
        )

    def from_slots(arrived_back):
        picked = arrived_back.reshape(experts_all, capacity, model_width)[flat_ids, slot_place]
        return picked.astype(jnp.float32).reshape(local_rows, TOP, model_width)

    def expert_front(arrived_rows):
        gate_pre = jnp.einsum(
            "sjcd,jdf->sjcf", arrived_rows, expert_gate, preferred_element_type=jnp.float32
        )
        up_pre = jnp.einsum(
            "sjcd,jdf->sjcf", arrived_rows, expert_up, preferred_element_type=jnp.float32
        )
        hidden = (jax.nn.silu(gate_pre) * up_pre).astype(jnp.bfloat16)
        return (gate_pre, up_pre, hidden)

    send_rows = to_slots(jnp.repeat(second, TOP, axis=0))
    arrived = lax.all_to_all(send_rows, "exp", split_axis=0, concat_axis=0, tiled=True)
    gate_pre, up_pre, hidden = expert_front(arrived)
    results = jnp.einsum(
        "sjcf,jfd->sjcd", hidden, expert_down, preferred_element_type=jnp.float32
    ).astype(jnp.bfloat16)
    returned = lax.all_to_all(results, "exp", split_axis=0, concat_axis=0, tiled=True)
    expert_out = from_slots(returned)
    mixture = jnp.sum(gates[:, :, None] * expert_out, axis=1)
    shared_gate_pre = product(second, shared_gate)
    shared_up_pre = product(second, shared_up)
    shared_hidden = (jax.nn.silu(shared_gate_pre) * shared_up_pre).astype(jnp.bfloat16)
    output = (mixed + mixture + product(shared_hidden, shared_down)).astype(jnp.bfloat16)
    upstream = cotangent[0]
    upstream_full = upstream.astype(jnp.float32)
    grad_shared_down = outer_sum(shared_hidden, upstream)
    d_shared_hidden = against(upstream, shared_down)
    shared_silu, shared_slope = silu_parts(shared_gate_pre)
    d_shared_gate = (d_shared_hidden * shared_up_pre * shared_slope).astype(jnp.bfloat16)
    d_shared_up = (d_shared_hidden * shared_silu).astype(jnp.bfloat16)
    grad_shared_gate = outer_sum(second, d_shared_gate)
    grad_shared_up = outer_sum(second, d_shared_up)
    d_second = against(d_shared_gate, shared_gate) + against(d_shared_up, shared_up)
    d_gates = jnp.sum(upstream_full[:, None, :] * expert_out, axis=-1)
    d_selected = gates * (d_gates - jnp.sum(gates * d_gates, axis=-1, keepdims=True))
    d_logits = jnp.sum(d_selected[:, :, None] * one_hot, axis=1).astype(jnp.bfloat16)
    grad_router = outer_sum(second, d_logits)
    d_second = d_second + against(d_logits, w_router)
    grad_slots = to_slots(
        (gates[:, :, None] * upstream_full[:, None, :])
        .astype(jnp.bfloat16)
        .reshape(local_rows * TOP, model_width)
    )
    arrived_rows, arrived_grad = (
        lax.all_to_all(send_rows, "exp", split_axis=0, concat_axis=0, tiled=True),
        lax.all_to_all(grad_slots, "exp", split_axis=0, concat_axis=0, tiled=True),
    )
    gate_kept, up_kept, hidden_kept = expert_front(arrived_rows)
    d_hidden = jnp.einsum(
        "sjcd,jfd->sjcf", arrived_grad, expert_down, preferred_element_type=jnp.float32
    )
    expert_silu, expert_slope = silu_parts(gate_kept)
    d_gate_pre = (d_hidden * up_kept * expert_slope).astype(jnp.bfloat16)
    d_up_pre = (d_hidden * expert_silu).astype(jnp.bfloat16)
    grad_expert_down = jnp.einsum(
        "sjcf,sjcd->jfd", hidden_kept, arrived_grad, preferred_element_type=jnp.float32
    )
    grad_expert_gate = jnp.einsum(
        "sjcd,sjcf->jdf", arrived_rows, d_gate_pre, preferred_element_type=jnp.float32
    )
    grad_expert_up = jnp.einsum(
        "sjcd,sjcf->jdf", arrived_rows, d_up_pre, preferred_element_type=jnp.float32
    )
    d_routed = (
        jnp.einsum("sjcf,jdf->sjcd", d_gate_pre, expert_gate, preferred_element_type=jnp.float32)
        + jnp.einsum("sjcf,jdf->sjcd", d_up_pre, expert_up, preferred_element_type=jnp.float32)
    ).astype(jnp.bfloat16)
    returned_grad = lax.all_to_all(d_routed, "exp", split_axis=0, concat_axis=0, tiled=True)
    d_second = d_second + jnp.sum(from_slots(returned_grad), axis=1)
    grad_expert_gate, grad_expert_up, grad_expert_down = (
        lax.psum(grad_expert_gate.astype(jnp.bfloat16), ("seq", "ctx")).astype(jnp.float32),
        lax.psum(grad_expert_up.astype(jnp.bfloat16), ("seq", "ctx")).astype(jnp.float32),
        lax.psum(grad_expert_down.astype(jnp.bfloat16), ("seq", "ctx")).astype(jnp.float32),
    )
    d_mixed_part, grad_norm_two = norm_two_pull(d_second)
    d_mixed = upstream_full + d_mixed_part
    d_attention = d_mixed.astype(jnp.bfloat16)
    grad_out = outer_sum(attended, d_attention)
    grad_heads = (
        against(d_attention, w_out).astype(jnp.bfloat16).reshape(local_rows, head_count, HEAD_DIM)
    )
    keys_all, values_all = (
        lax.all_gather(keys_local, "ctx", axis=0, tiled=True),
        lax.all_gather(values_local, "ctx", axis=0, tiled=True),
    )
    block_total = ((ctx_place + 1) * local_rows + KEY_ROWS - 1) // KEY_ROWS

    def weights_at(number):
        offset = number * KEY_ROWS
        key_block = lax.dynamic_slice_in_dim(keys_all, offset, KEY_ROWS, 0)
        value_block = lax.dynamic_slice_in_dim(values_all, offset, KEY_ROWS, 0)
        scores, allowed = block_scores(key_block, offset)
        weights = jnp.where(allowed[None], jnp.exp(scores - log_total[..., None]), 0.0)
        grad_weights = jnp.einsum(
            "qhd,khd->hqk",
            grad_heads,
            value_block.reshape(KEY_ROWS, head_count, HEAD_DIM),
            preferred_element_type=jnp.float32,
        )
        return (key_block, weights, grad_weights)

    def row_dot_step(number, summed):
        unused_block, weights, grad_weights = weights_at(number)
        return summed + jnp.sum(weights * grad_weights, axis=-1)

    row_dots = lax.fori_loop(
        0, block_total, row_dot_step, jnp.zeros((head_count, local_rows), jnp.float32)
    )

    def score_grads(number):
        key_block, weights, grad_weights = weights_at(number)
        d_scores = (weights * (grad_weights - row_dots[..., None])).astype(jnp.bfloat16)
        return (key_block.reshape(KEY_ROWS, head_count, HEAD_DIM), weights, d_scores)

    query_start = jnp.zeros((local_rows, head_count, HEAD_DIM), jnp.float32)

    def grad_step(number, running):
        grad_query, key_terms = running
        key_heads, weights, d_scores = score_grads(number)
        grad_query = (
            grad_query
            + jnp.einsum("hqk,khd->qhd", d_scores, key_heads, preferred_element_type=jnp.float32)
            * score_scale
        )
        key_part = (
            jnp.einsum("hqk,qhd->khd", d_scores, query, preferred_element_type=jnp.float32)
            * score_scale
        )
        value_part = jnp.einsum(
            "hqk,qhd->khd",
            weights.astype(jnp.bfloat16),
            grad_heads,
            preferred_element_type=jnp.float32,
        )
        block_terms = jnp.concatenate(
            [key_part.reshape(KEY_ROWS, model_width), value_part.reshape(KEY_ROWS, model_width)],
            axis=1,
        )
        return (
            grad_query,
            lax.dynamic_update_slice_in_dim(key_terms, block_terms, number * KEY_ROWS, 0),
        )

    grad_query_heads, key_terms = lax.fori_loop(
        0,
        block_total,
        grad_step,
        (query_start, jnp.zeros((ctx_count * local_rows, 2 * model_width), jnp.float32)),
    )
    key_grads = lax.psum_scatter(
        key_terms.astype(jnp.bfloat16), "ctx", scatter_dimension=0, tiled=True
    ).astype(jnp.float32)
    key_grad_heads = key_grads[:, :model_width].reshape(local_rows, head_count, HEAD_DIM)
    d_value = key_grads[:, model_width:].astype(jnp.bfloat16)
    d_query_lin = (
        rotate(grad_query_heads, -places).astype(jnp.bfloat16).reshape(local_rows, model_width)
    )
    d_key_lin = (
        rotate(key_grad_heads, -places).astype(jnp.bfloat16).reshape(local_rows, model_width)
    )
    grad_query = outer_sum(normed, d_query_lin)
    grad_key = outer_sum(normed, d_key_lin)
    grad_value = outer_sum(normed, d_value)
    d_normed = against(d_query_lin, w_query) + against(d_key_lin, w_key) + against(d_value, w_value)
    d_inputs, grad_norm_one = norm_one_pull(d_normed)
    grad_tokens = (d_mixed + d_inputs)[None]
    (
        grad_query,
        grad_key,
        grad_value,
        grad_out,
        grad_router,
        grad_shared_gate,
        grad_shared_up,
        grad_shared_down,
    ) = (
        lax.psum_scatter(
            spread(grad_query), ("seq", "ctx", "exp"), scatter_dimension=0, tiled=True
        ),
        lax.psum_scatter(spread(grad_key), ("seq", "ctx", "exp"), scatter_dimension=0, tiled=True),
        lax.psum_scatter(
            spread(grad_value), ("seq", "ctx", "exp"), scatter_dimension=0, tiled=True
        ),
        lax.psum_scatter(spread(grad_out), ("seq", "ctx", "exp"), scatter_dimension=0, tiled=True),
        lax.psum_scatter(
            spread(grad_router), ("seq", "ctx", "exp"), scatter_dimension=0, tiled=True
        ),
        lax.psum_scatter(
            spread(grad_shared_gate), ("seq", "ctx", "exp"), scatter_dimension=0, tiled=True
        ),
        lax.psum_scatter(
            spread(grad_shared_up), ("seq", "ctx", "exp"), scatter_dimension=0, tiled=True
        ),
        lax.psum_scatter(
            spread(grad_shared_down), ("seq", "ctx", "exp"), scatter_dimension=0, tiled=True
        ),
    )
    grad_norm_one, grad_norm_two = lax.psum((grad_norm_one, grad_norm_two), ("seq", "ctx", "exp"))
    return (
        output[None],
        grad_tokens,
        grad_norm_one,
        grad_query,
        grad_key,
        grad_value,
        grad_out,
        grad_norm_two,
        grad_router,
        grad_expert_gate,
        grad_expert_up,
        grad_expert_down,
        grad_shared_gate,
        grad_shared_up,
        grad_shared_down,
    )


def place_tables(length):
    half = HEAD_DIM // 2
    frequency = np.float32(10000.0) ** (-np.arange(half, dtype=np.float32) / np.float32(half))
    angles = np.arange(length, dtype=np.float32)[:, None] * frequency[None, :].astype(np.float32)
    cosine, sine = np.cos(angles), np.sin(angles)
    return (
        np.concatenate([cosine] * 4, axis=1).astype(np.float32),
        np.concatenate([-sine, sine, -sine, sine], axis=1).astype(np.float32),
    )


def swapped(values):
    half = HEAD_DIM // 2
    lane = lax.broadcasted_iota(jnp.int32, values.shape, 1) % HEAD_DIM
    return jnp.where(lane < half, pltpu.roll(values, 128 - half, 1), pltpu.roll(values, half, 1))


def start_copy(src, dst, ssem, rsem, device):
    copy = pltpu.make_async_remote_copy(
        src_ref=src, dst_ref=dst, send_sem=ssem, recv_sem=rsem, device_id=device, device_id_type=MESH
    )
    copy.start()
    return copy


def greet(devices):
    barrier = pltpu.get_barrier_semaphore()
    for device in devices:
        pl.semaphore_signal(barrier, inc=1, device_id=device, device_id_type=MESH)
    pl.semaphore_wait(barrier, len(devices))


def neighbours():
    s = lax.axis_index("seq")
    c = lax.axis_index("ctx")
    e = lax.axis_index("exp")
    x, k = c // 2, c % 2
    to_core = (s, x * 2 + (1 - k), e)
    to_x = (s, (1 - x) * 2 + k, e)
    to_y = (1 - s, c, e)
    near = e + 1 - 2 * (e % 2)
    far = lax.rem(e + 2, 4)
    opposite = 3 - e
    return s, x, k, e, c, to_core, to_x, to_y, (near, far, opposite)


def front_kernel(
    tokens, upstream, named, gain_one, gain_two, w_q, w_k, w_v, w_o, cosine, sine,
    q_all, k_all, v_all, upstream_all, named_all, normed_out, attended_out, mixed_out, second_out, logsum_out,
    block, tsem, trem, usem, urem, nsem, nrem,
):
    s, x, k, e, c, to_core, to_x, to_y, others = neighbours()
    rows, width = tokens.shape
    greet([to_core, to_x, *[(s, c, o) for o in others]])
    block[c] = tokens[...]
    upstream_all[0] = upstream[...]
    named_all[0] = named[...]
    core_copy = start_copy(tokens, block.at[c], tsem.at[0], trem.at[0], to_core)
    x_copy = start_copy(tokens, block.at[c], tsem.at[1], trem.at[1], to_x)
    z_copies = []
    for i in range(3):
        device = (s, c, others[i])
        z_copies.append(start_copy(named, named_all.at[i + 1], nsem.at[i], nrem.at[i], device))
        z_copies.append(start_copy(upstream, upstream_all.at[i + 1], usem.at[i], urem.at[i], device))

    def project(j):
        values = block[j].astype(jnp.float32)
        inverse = lax.rsqrt(jnp.mean(values * values, axis=-1, keepdims=True) + 1e-06)
        normed = (values * inverse * gain_one[...]).astype(jnp.bfloat16)
        for weight, out in ((w_q, q_all), (w_k, k_all)):
            lin = jnp.dot(normed, weight[...], preferred_element_type=jnp.float32)
            for g in range(width // 128):
                part = lin[:, g * 128 : (g + 1) * 128]
                turned = part * cosine[j] + swapped(part) * sine[j]
                out[j, :, g * 128 : (g + 1) * 128] = turned.astype(jnp.bfloat16)
        v_all[j] = jnp.dot(normed, w_v[...], preferred_element_type=jnp.float32).astype(jnp.bfloat16)
        return normed

    normed_out[...] = project(c)
    core_copy.wait()
    project(x * 2 + (1 - k))
    x_copy.wait()
    there = (1 - x) * 2 + k
    corner_copy = start_copy(block.at[there], block.at[there], tsem.at[2], trem.at[2], to_core)
    project(there)
    corner_copy.wait()
    project((1 - x) * 2 + (1 - k))

    span = 4 * rows
    hidden_keys = lax.broadcasted_iota(jnp.int32, (1, span), 1) // rows > c
    bias = jnp.where(hidden_keys, -1e30, 0.0)
    lane = lax.broadcasted_iota(jnp.int32, (rows, 128), 1)
    logsum_out[...] = jnp.zeros_like(logsum_out)

    def pair(g, carry):
        at = pl.ds(pl.multiple_of(g * 128, 128), 128)
        q = q_all[c, :, at]
        keys = k_all[:, :, at].reshape(span, 128)
        values = v_all[:, :, at].reshape(span, 128)
        out = jnp.zeros((rows, 128), jnp.float32)
        for h in range(2):
            inside = (lane // HEAD_DIM) == h
            scores = lax.dot_general(
                jnp.where(inside, q, jnp.zeros_like(q)), keys, (((1,), (1,)), ((), ())),
                preferred_element_type=jnp.float32,
            )
            scores = scores * (HEAD_DIM**-0.5) + bias
            highest = jnp.max(scores, axis=-1, keepdims=True)
            raised = jnp.exp(scores - highest)
            total = jnp.sum(raised, axis=-1, keepdims=True)
            mixed = jnp.dot(raised.astype(jnp.bfloat16), values, preferred_element_type=jnp.float32)
            out = jnp.where(inside, mixed / total, out)
            logsum_out[...] = jnp.where(lane == 2 * g + h, highest + jnp.log(total), logsum_out[...])
        attended_out[:, at] = out.astype(jnp.bfloat16)
        return carry

    lax.fori_loop(0, width // 128, pair, 0)
    mixed = tokens[...].astype(jnp.float32) + jnp.dot(
        attended_out[...], w_o[...], preferred_element_type=jnp.float32
    )
    mixed_out[...] = mixed
    inverse = lax.rsqrt(jnp.mean(mixed * mixed, axis=-1, keepdims=True) + 1e-06)
    second_out[...] = (mixed * inverse * gain_two[...]).astype(jnp.bfloat16)
    for copy in z_copies:
        copy.wait()


def front(tokens, upstream, named, gain_one, gain_two, w_q, w_k, w_v, w_o):
    rows, width = tokens.shape
    cosine, sine = (jnp.asarray(t).reshape(4, rows, 128) for t in place_tables(4 * rows))
    low, full = jnp.bfloat16, jnp.float32
    vmem, dma = pltpu.VMEM, pltpu.SemaphoreType.DMA
    every = jax.ShapeDtypeStruct((4, rows, width), low)
    own = jax.ShapeDtypeStruct((rows, width), low)
    spec = pl.BlockSpec(memory_space=pltpu.VMEM)
    out_shape = [
        every, every, every, every, jax.ShapeDtypeStruct((4, rows, 128), low), own, own,
        jax.ShapeDtypeStruct((rows, width), full), own, jax.ShapeDtypeStruct((rows, 128), full),
    ]
    return pl.pallas_call(
        front_kernel,
        out_shape=out_shape,
        in_specs=[spec] * 11,
        out_specs=[spec] * 10,
        scratch_shapes=[vmem((4, rows, width), low), dma((3,)), dma((3,)), dma((3,)), dma((3,)), dma((3,)), dma((3,))],
        compiler_params=pltpu.CompilerParams(
            collective_id=2, has_side_effects=True, vmem_limit_bytes=58 * 2**20
        ),
        name="front",
    )(tokens, upstream, named, gain_one.reshape(1, width), gain_two.reshape(1, width), w_q, w_k, w_v, w_o, cosine, sine)


def add_rows(target, first, second, step):
    rows = target.shape[0]

    def some(at):
        total = first[at, :].astype(jnp.float32) + second[at, :].astype(jnp.float32)
        target[at, :] = total.astype(target.dtype)

    if rows <= step:
        some(pl.ds(0, rows))
    else:

        def body(i, carry):
            some(pl.ds(pl.multiple_of(i * step, step), step))
            return carry

        lax.fori_loop(0, rows // step, body, 0)


class Piece:
    def __init__(self, place, whole, one, two, three, half, sems, step):
        self.s, self.x, self.k, self.to_core, self.to_x, self.to_y = place
        self.whole, self.one, self.two, self.three = whole, one, two, three
        self.half, self.sems, self.step = half, sems, step

    def copy(self, level, h=0):
        every, low, high = slice(None), pl.ds(0, self.half), pl.ds(self.half, self.half)
        if level == 1:
            src, dst, device = self.whole(1 - self.k), self.one(every, every, every), self.to_core
        elif level == 2:
            if h == 0:
                src, device = self.one(every, 1 - self.x, low), self.to_x
            else:
                src, device = self.one(1 - self.s, every, high), self.to_y
            dst = self.two(h, every)
        else:
            src = self.two(h, 1 - (self.s, self.x)[h])
            dst, device = self.three(h), (self.to_y, self.to_x)[h]
        ssem, rsem = self.sems(2 * (level - 1) - (1 if level > 1 else 0) + h)
        return pltpu.make_async_remote_copy(
            src_ref=src, dst_ref=dst, send_sem=ssem, recv_sem=rsem, device_id=device, device_id_type=MESH
        )

    def start(self, level):
        for h in range(1 if level == 1 else 2):
            self.copy(level, h).start()

    def finish(self, level):
        low, high = pl.ds(0, self.half), pl.ds(self.half, self.half)
        if level == 1:
            self.copy(1).wait()
            own = self.whole(self.k)
            for i in range(2):
                for j in range(2):
                    here = self.one(i, j, slice(None))
                    add_rows(here, here, own.at[i, j], self.step)
            return
        for h in range(2):
            self.copy(level, h).wait()
            if level == 2:
                for i in range(2):
                    here = self.two(h, i)
                    own = self.one(i, self.x, low) if h == 0 else self.one(self.s, i, high)
                    add_rows(here, here, own, self.step)
            else:
                here = self.three(h)
                add_rows(here, here, self.two(h, (self.s, self.x)[h]), self.step)


def gates_in(logits, named):
    masked = jnp.where(named, logits, -1e30)
    raised = jnp.where(named, jnp.exp(masked - jnp.max(masked, axis=-1, keepdims=True)), 0.0)
    return raised / jnp.sum(raised, axis=-1, keepdims=True)


def ffn_kernel(
    second, mixed, upstream_all, named_all, w_r, gain_two,
    e_gate, e_up, e_down, s_gate, s_up, s_down,
    results, shares_out, base_out, d_mixed_out, small_out, eg_out, eu_out, ed_out, sg_out, su_out, sd_out,
    rows_all, d_res, res_acc, row_acc, row_send, row_got, dg_send, dg_got, d_second,
    t_gate, t_up, t_down, wsem,
    ge_g, ge_u, ge_d, e1_g, e1_u, e1_d, e2_g, e2_u, e2_d,
    gs_g, gs_u, gs_d, s1_g, s1_u, s1_d, s2_g, s2_u, s2_d,
    es_sem, er_sem, ss_sem, sr_sem, xs_sem, xr_sem, rs_sem, rr_sem, ds_sem, dr_sem,
):
    s, x, k, e, c, to_core, to_x, to_y, others = neighbours()
    place = (s, x, k, to_core, to_x, to_y)
    rows, width = second.shape
    tile = t_gate.shape[2]
    tiles = e_gate.shape[1] // tile
    low, full = jnp.bfloat16, jnp.float32
    greet([to_core, to_x, to_y, *[(s, c, o) for o in others]])
    rows_all[0] = second[...]
    row_copies = [
        start_copy(second, rows_all.at[i + 1], xs_sem.at[i], xr_sem.at[i], (s, c, others[i])) for i in range(3)
    ]

    def columns(f):
        return pl.ds(pl.multiple_of(f * tile, tile), tile)

    def fetches(sources, f, slot):
        gate, up, down = sources
        return [
            pltpu.make_async_copy(gate.at[:, columns(f)], t_gate.at[slot], wsem.at[slot, 0]),
            pltpu.make_async_copy(up.at[:, columns(f)], t_up.at[slot], wsem.at[slot, 1]),
            pltpu.make_async_copy(down.at[columns(f), :], t_down.at[slot], wsem.at[slot, 2]),
        ]

    def next_tile(sources, following, f):
        slot = lax.rem(f, 2)

        @pl.when(f < tiles - 1)
        def _():
            for copy in fetches(sources, f + 1, 1 - slot):
                copy.start()

        if following is not None:

            @pl.when(f == tiles - 1)
            def _():
                for copy in fetches(following, 0, 1 - slot):
                    copy.start()

        for copy in fetches(sources, f, slot):
            copy.wait()
        return slot

    def piece_e(f, a):
        at = columns(f)
        sems = lambda n: (es_sem.at[f, a, n], er_sem.at[f, a, n])
        if a < 2:
            g, one, two, three = ((ge_g, e1_g, e2_g, eg_out), (ge_u, e1_u, e2_u, eu_out))[a]
            return Piece(
                place,
                lambda kk: g.at[:, :, kk, :, at],
                lambda i, j, r: one.at[i, j, r, at],
                lambda h, i: two.at[h, i, :, at],
                lambda h: three.at[h, :, at],
                g.shape[3] // 2, sems, 96,
            )
        return Piece(
            place,
            lambda kk: ge_d.at[f, :, :, kk],
            lambda i, j, r: e1_d.at[f, i, j, r],
            lambda h, i: e2_d.at[f, h, i],
            lambda h: ed_out.at[f, h],
            ge_d.shape[4] // 2, sems, 96,
        )

    def piece_s(a):
        g, one, two, three = (
            (gs_g, s1_g, s2_g, sg_out), (gs_u, s1_u, s2_u, su_out), (gs_d, s1_d, s2_d, sd_out)
        )[a]
        return Piece(
            place,
            lambda kk: g.at[:, :, kk],
            lambda i, j, r: one.at[i, j, r],
            lambda h, i: two.at[h, i],
            lambda h: three.at[h],
            g.shape[3] // 2, lambda n: (ss_sem.at[a, n], sr_sem.at[a, n]), 16 if a < 2 else 32,
        )

    shared, expert = (s_gate, s_up, s_down), (e_gate, e_up, e_down)
    for copy in fetches(shared, 0, 0):
        copy.start()

    def branch(values, d_out, slot, result_acc, d_acc):
        gate_w, up_w, down_w = t_gate[slot], t_up[slot], t_down[slot]
        gate = jnp.dot(values, gate_w, preferred_element_type=full)
        up = jnp.dot(values, up_w, preferred_element_type=full)
        d_hidden = against(d_out, down_w)
        sigmoid = 1.0 / (1.0 + jnp.exp(-gate))
        silu = gate * sigmoid
        hidden = (silu * up).astype(low)
        d_gate = (d_hidden * up * (sigmoid * (1.0 + gate * (1.0 - sigmoid)))).astype(low)
        d_up = (d_hidden * silu).astype(low)
        result_acc[...] += jnp.dot(hidden, down_w, preferred_element_type=full)
        d_acc[...] += against(d_gate, gate_w) + against(d_up, up_w)
        return hidden, d_gate, d_up

    base_out[...] = mixed[...]
    d_second[...] = jnp.zeros_like(d_second)

    def shared_tile(f, carry):
        slot = next_tile(shared, expert, f)
        values, d_out = second[...], upstream_all[0]
        hidden, d_gate, d_up = branch(values, d_out, slot, base_out, d_second)
        gs_g[:, :, :, :, columns(f)] = outer_sum(values, d_gate).astype(low).reshape(2, 2, 2, width // 8, tile)
        gs_u[:, :, :, :, columns(f)] = outer_sum(values, d_up).astype(low).reshape(2, 2, 2, width // 8, tile)
        gs_d[f // 4, (f // 2) % 2, f % 2] = outer_sum(hidden, d_out).astype(low)
        return carry

    lax.fori_loop(0, tiles, shared_tile, 0)
    for a in range(3):
        piece_s(a).start(1)
    logits = jnp.dot(second[...], w_r[...], preferred_element_type=full)
    shares_out[...] = gates_in(logits, named_all[0].astype(full) > 0.5)

    lane = lax.broadcasted_iota(jnp.int32, (2 * rows, 128), 1)
    for turn in range(2):
        if turn == 0:
            row_copies[0].wait()
        else:
            row_copies[1].wait()
            row_copies[2].wait()
        pair = pl.ds(2 * turn, 2)
        values = rows_all[pair].reshape(2 * rows, width)
        logits = jnp.dot(values, w_r[...], preferred_element_type=full)
        gates = gates_in(logits, named_all[pair].reshape(2 * rows, 128).astype(full) > 0.5)
        share = jnp.sum(jnp.where(lane == e, gates, 0.0), axis=-1, keepdims=True)
        d_res[...] = (share * upstream_all[pair].reshape(2 * rows, width).astype(full)).astype(low)
        res_acc[...] = jnp.zeros_like(res_acc)
        row_acc[...] = jnp.zeros_like(row_acc)

        def expert_tile(f, carry, turn=turn, pair=pair):
            slot = next_tile(expert, expert if turn == 0 else None, f)
            values, d_out = rows_all[pair].reshape(2 * rows, width), d_res[...]
            hidden, d_gate, d_up = branch(values, d_out, slot, res_acc, row_acc)
            for g, term in ((ge_g, outer_sum(values, d_gate)), (ge_u, outer_sum(values, d_up))):
                term = term.reshape(2, 2, 2, width // 8, tile)
                if turn == 1:
                    term = term + g[:, :, :, :, columns(f)].astype(full)
                g[:, :, :, :, columns(f)] = term.astype(low)
            term = outer_sum(hidden, d_out).reshape(2, 2, 2, tile // 8, width)
            if turn == 1:
                term = term + ge_d[f].astype(full)
            ge_d[f] = term.astype(low)
            if turn == 0:
                for a in range(3):

                    @pl.when(f == 2 * a + 2)
                    def _(a=a):
                        piece_s(a).finish(1)
                        piece_s(a).start(2)

            else:
                for a in range(3):
                    piece_e(f, a).start(1)

                @pl.when(f > 0)
                def _():
                    for a in range(3):
                        piece_e(f - 1, a).finish(1)
                        piece_e(f - 1, a).start(2)

            return carry

        lax.fori_loop(0, tiles, expert_tile, 0)
        low_result = res_acc[...].astype(low)
        results[pair] = low_result.reshape(2, rows, width)
        row_send[pair] = row_acc[...].astype(low).reshape(2, rows, width)
        terms = low_result.astype(full) * upstream_all[pair].reshape(2 * rows, width).astype(full)
        high = terms.astype(low)
        ones = jnp.ones((8, width), low)
        sums = against(ones, high) + against(ones, (terms - high.astype(full)).astype(low))
        for i in range(2):
            dg_send[2 * turn + i] = sums[:, i * rows : (i + 1) * rows]
        for i in (1,) if turn == 0 else (2, 3):
            device = (s, c, others[i - 1])
            start_copy(row_send.at[i], row_got.at[i], rs_sem.at[i], rr_sem.at[i], device)
            start_copy(dg_send.at[i], dg_got.at[i], ds_sem.at[i], dr_sem.at[i], device)

    for a in range(3):
        piece_e(tiles - 1, a).finish(1)
        piece_e(tiles - 1, a).start(2)
    for a in range(3):
        piece_s(a).finish(2)
        piece_s(a).start(3)

    def third(f, carry):
        for a in range(3):
            piece_e(f, a).finish(2)
            piece_e(f, a).start(3)
        return carry

    lax.fori_loop(0, tiles, third, 0)

    d_gates = jnp.where(lax.broadcasted_iota(jnp.int32, (8, rows), 0) == e, dg_send[0], 0.0)
    total = d_second[...] + row_send[0].astype(full)
    for i in range(1, 4):
        device = (s, c, others[i - 1])
        pltpu.make_async_remote_copy(
            src_ref=row_send.at[i], dst_ref=row_got.at[i], send_sem=rs_sem.at[i], recv_sem=rr_sem.at[i],
            device_id=device, device_id_type=MESH,
        ).wait()
        pltpu.make_async_remote_copy(
            src_ref=dg_send.at[i], dst_ref=dg_got.at[i], send_sem=ds_sem.at[i], recv_sem=dr_sem.at[i],
            device_id=device, device_id_type=MESH,
        ).wait()
        d_gates = jnp.where(
            lax.broadcasted_iota(jnp.int32, (8, rows), 0) == others[i - 1], dg_got[i], d_gates
        )
        total = total + row_got[i].astype(full)
    d_gates = jnp.concatenate([d_gates, jnp.zeros((120, rows), full)], axis=0).T
    shares = shares_out[...]
    d_logits = (shares * (d_gates - jnp.sum(shares * d_gates, axis=-1, keepdims=True))).astype(low)
    total = total + against(d_logits, w_r[...])
    router = outer_sum(d_logits, second[...])
    values = mixed[...]
    inverse = lax.rsqrt(jnp.mean(values * values, axis=-1, keepdims=True) + 1e-06)
    unit = values * inverse
    small_out[0:8, :] = router[0:8, :]
    small_out[8:16, :] = jnp.broadcast_to(jnp.sum(total * unit, axis=0, keepdims=True), (8, width))
    inner = total * gain_two[...]
    mean = jnp.mean(inner * unit, axis=-1, keepdims=True)
    d_mixed_out[...] = upstream_all[0].astype(full) + inverse * (inner - unit * mean)

    for a in range(3):
        piece_s(a).finish(3)

    def done(f, carry):
        for a in range(3):
            piece_e(f, a).finish(3)
        return carry

    lax.fori_loop(0, tiles, done, 0)


def ffn(second, mixed, upstream_all, named_all, w_router, gain_two, experts, shared):
    rows, width = second.shape
    hidden = experts[0].shape[1]
    tile = 256
    tiles = hidden // tile
    low, full = jnp.bfloat16, jnp.float32
    dma = pltpu.SemaphoreType.DMA
    ninth, small, tall = width // 8, tile // 8, hidden // 8

    def vm(*shape, dtype=low):
        return pltpu.VMEM(shape, dtype)

    def out(*shape, dtype=low):
        return jax.ShapeDtypeStruct(shape, dtype)

    w_r = jnp.pad(w_router, ((0, 0), (0, 128 - w_router.shape[1])))
    spec = pl.BlockSpec(memory_space=pltpu.VMEM)
    out_shape = [
        out(4, rows, width), out(rows, 128, dtype=full), out(rows, width, dtype=full), out(rows, width, dtype=full),
        out(16, width, dtype=full), out(2, ninth // 2, hidden), out(2, ninth // 2, hidden),
        out(tiles, 2, small // 2, width), out(2, ninth // 2, hidden), out(2, ninth // 2, hidden), out(2, tall // 2, width),
    ]
    scratch = [
        vm(4, rows, width), vm(2 * rows, width), vm(2 * rows, width, dtype=full), vm(2 * rows, width, dtype=full),
        vm(4, rows, width), vm(4, rows, width), vm(4, 8, rows, dtype=full), vm(4, 8, rows, dtype=full),
        vm(rows, width, dtype=full),
        vm(2, width, tile), vm(2, width, tile), vm(2, tile, width), dma((2, 3)),
        vm(2, 2, 2, ninth, hidden), vm(2, 2, 2, ninth, hidden), vm(tiles, 2, 2, 2, small, width),
        vm(2, 2, ninth, hidden), vm(2, 2, ninth, hidden), vm(tiles, 2, 2, small, width),
        vm(2, 2, ninth // 2, hidden), vm(2, 2, ninth // 2, hidden), vm(tiles, 2, 2, small // 2, width),
        vm(2, 2, 2, ninth, hidden), vm(2, 2, 2, ninth, hidden), vm(2, 2, 2, tall, width),
        vm(2, 2, ninth, hidden), vm(2, 2, ninth, hidden), vm(2, 2, tall, width),
        vm(2, 2, ninth // 2, hidden), vm(2, 2, ninth // 2, hidden), vm(2, 2, tall // 2, width),
        dma((tiles, 3, 5)), dma((tiles, 3, 5)), dma((3, 5)), dma((3, 5)), dma((3,)), dma((3,)),
        dma((4,)), dma((4,)), dma((4,)), dma((4,)),
    ]
    return pl.pallas_call(
        ffn_kernel,
        out_shape=out_shape,
        in_specs=[spec] * 6 + [pl.BlockSpec(memory_space=pl.ANY)] * 6,
        out_specs=[spec] * len(out_shape),
        scratch_shapes=scratch,
        compiler_params=pltpu.CompilerParams(
            collective_id=3, has_side_effects=True, vmem_limit_bytes=60 * 2**20
        ),
        name="ffn",
    )(second, mixed, upstream_all, named_all, w_r, gain_two.reshape(1, width), *experts, *shared)


def close_kernel(
    eg_own, eu_own, ed_own, sg_own, su_own, sd_own, gq, gk, gv, go, misc_in, results, base, shares,
    eg_all, eu_all, ed_all, sg_out, su_out, sd_out, q_out, k_out, v_out, o_out, misc_out, output,
    one, two, three, z_flat, z_tall, z_wide, got_flat, got_tall, got_wide, misc_got, result_got,
    lsem, gsem, grem, psem, prem, zsem, zrem, msem, mrem, rsem, rrem,
):
    s, x, k, e, c, to_core, to_x, to_y, others = neighbours()
    place = (s, x, k, to_core, to_x, to_y)
    to_z = [(s, c, o) for o in others]
    low, full = jnp.bfloat16, jnp.float32
    greet([to_core, to_x, to_y, *to_z])

    def piece(a):
        g = (gq, gk, gv, go)[a]
        return Piece(
            place,
            lambda kk: g.at[:, :, kk],
            lambda i, j, r: one.at[a, i, j, r],
            lambda h, i: two.at[a, h, i],
            lambda h: three.at[a, h],
            g.shape[3] // 2, lambda n: (psem.at[a, n], prem.at[a, n]), 48,
        )

    for a in range(4):
        piece(a).start(1)
    misc_copy = start_copy(misc_in, misc_got.at[0], msem.at[0], mrem.at[0], to_core)
    result_copies = [
        start_copy(results.at[i + 1], result_got.at[i], rsem.at[i], rrem.at[i], to_z[i]) for i in range(3)
    ]

    def block(a, h, ss, xx):
        whole = (eg_all, eu_all, ed_all)[a]
        half = whole.shape[-2] // 2
        part = pl.ds(h * half, half)
        return whole.at[ss, xx, k, part] if a < 2 else whole.at[:, ss, xx, k, part]

    legs = []
    for a, own in enumerate((eg_own, eu_own, ed_own)):
        for h in range(2):
            src = own.at[h] if a < 2 else own.at[:, h]
            here = block(a, h, s, x)
            local = pltpu.make_async_copy(src, here, lsem.at[a, h])
            local.start()
            near, wide = (to_y, to_x) if h == 0 else (to_x, to_y)
            legs.append(
                (
                    local,
                    start_copy(src, here, gsem.at[a, h, 0], grem.at[a, h, 0], near),
                    start_copy(src, here, gsem.at[a, h, 1], grem.at[a, h, 1], wide),
                )
            )

    def spread(own, buffer):
        halves, height, across = own.shape
        piece_width = across // 4
        for h in range(halves):
            for q in range(4):
                buffer[q, pl.ds(h * height, height), :] = own[h, :, q * piece_width : (q + 1) * piece_width]

    def to_owners(buffer, got, number):
        owners = (e, *others)
        return [
            start_copy(buffer.at[owners[i]], got.at[i - 1], zsem.at[number, i - 1], zrem.at[number, i - 1], to_z[i - 1])
            for i in range(1, 4)
        ]

    def settle(copies, buffer, got, target):
        for copy in copies:
            copy.wait()
        target[...] = (
            buffer[e].astype(full) + got[0].astype(full) + got[1].astype(full) + got[2].astype(full)
        )

    z_copies = []
    for number, (own, buffer, got) in enumerate(
        ((sg_own, z_wide.at[0], got_wide.at[0]), (su_own, z_wide.at[1], got_wide.at[1]), (sd_own, z_tall, got_tall))
    ):
        spread(own, buffer)
        z_copies.append(to_owners(buffer, got, number))
    for a in range(4):
        piece(a).finish(1)
        piece(a).start(2)
    misc_copy.wait()
    misc_out[...] = misc_in[...] + misc_got[0]
    misc_copy = start_copy(misc_out, misc_got.at[1], msem.at[1], mrem.at[1], to_x)
    onward = []
    for a in range(3):
        for h in range(2):
            legs[2 * a + h][1].wait()
            there = block(a, h, (1 - s, s)[h], (x, 1 - x)[h])
            onward.append(start_copy(there, there, gsem.at[a, h, 2], grem.at[a, h, 2], (to_x, to_y)[h]))
    for a in range(4):
        piece(a).finish(2)
        piece(a).start(3)
    misc_copy.wait()
    misc_got[3] = misc_out[...] + misc_got[1]
    misc_copy = start_copy(misc_got.at[3], misc_got.at[2], msem.at[2], mrem.at[2], to_y)
    for a in range(4):
        piece(a).finish(3)
        spread(three.at[a], z_flat.at[a])
        z_copies.append(to_owners(z_flat.at[a], got_flat.at[a], 3 + a))
    misc_copy.wait()
    misc_got[4] = misc_got[3] + misc_got[2]
    misc_copies = [
        start_copy(misc_got.at[4], misc_got.at[5 + i], msem.at[3 + i], mrem.at[3 + i], to_z[i]) for i in range(3)
    ]
    last = []
    for a, whole in enumerate((eg_all, eu_all, ed_all)):
        for h in range(2):
            legs[2 * a + h][0].wait()
            legs[2 * a + h][2].wait()
            onward[2 * a + h].wait()
        there = whole.at[:, :, k] if a < 2 else whole.at[:, :, :, k]
        last.append(start_copy(there, there, gsem.at[a, 0, 3], grem.at[a, 0, 3], to_core))

    lane = lax.broadcasted_iota(jnp.int32, shares.shape, 1)
    total = base[...]
    for i, owner in enumerate((e, *others)):
        share = jnp.sum(jnp.where(lane == owner, shares[...], 0.0), axis=-1, keepdims=True)
        if i == 0:
            rows_back = results[0]
        else:
            result_copies[i - 1].wait()
            rows_back = result_got[i - 1]
        total = total + share * rows_back.astype(full)
    output[...] = total.astype(low)

    settle(z_copies[0], z_wide.at[0], got_wide.at[0], sg_out)
    settle(z_copies[1], z_wide.at[1], got_wide.at[1], su_out)
    settle(z_copies[2], z_tall, got_tall, sd_out)
    for a, target in enumerate((q_out, k_out, v_out, o_out)):
        settle(z_copies[3 + a], z_flat.at[a], got_flat.at[a], target)
    for copy in misc_copies:
        copy.wait()
    misc_out[...] = misc_got[4] + misc_got[5] + misc_got[6] + misc_got[7]
    for copy in last:
        copy.wait()


def close(expert_own, shared_own, plain, misc, results, base, shares):
    low, full = jnp.bfloat16, jnp.float32
    dma = pltpu.SemaphoreType.DMA
    rows, width = base.shape
    ninth = width // 8
    hidden = expert_own[0].shape[2]
    tiles, unused, small, unused = expert_own[2].shape
    tall = 2 * shared_own[2].shape[1]

    def vm(*shape, dtype=low):
        return pltpu.VMEM(shape, dtype)

    def out(*shape, dtype=low):
        return jax.ShapeDtypeStruct(shape, dtype)

    blocks = [m.reshape(2, 2, 2, ninth, width) for m in plain]
    spec, anywhere = pl.BlockSpec(memory_space=pltpu.VMEM), pl.BlockSpec(memory_space=pl.ANY)
    out_shape = [
        out(2, 2, 2, ninth, hidden), out(2, 2, 2, ninth, hidden), out(tiles, 2, 2, 2, 2 * small, width),
        out(ninth, hidden // 4, dtype=full), out(ninth, hidden // 4, dtype=full), out(tall, width // 4, dtype=full),
        *[out(ninth, width // 4, dtype=full)] * 4, out(*misc.shape, dtype=full), out(rows, width),
    ]
    scratch = [
        vm(4, 2, 2, ninth, width), vm(4, 2, 2, ninth // 2, width), vm(4, 2, ninth // 2, width),
        vm(4, 4, ninth, width // 4), vm(4, tall, width // 4), vm(2, 4, ninth, hidden // 4),
        vm(4, 3, ninth, width // 4), vm(3, tall, width // 4), vm(2, 3, ninth, hidden // 4),
        vm(8, *misc.shape, dtype=full), vm(3, rows, width),
        dma((3, 2)), dma((3, 2, 4)), dma((3, 2, 4)), dma((4, 5)), dma((4, 5)), dma((7, 3)), dma((7, 3)),
        dma((6,)), dma((6,)), dma((3,)), dma((3,)),
    ]
    return pl.pallas_call(
        close_kernel,
        out_shape=out_shape,
        in_specs=[spec] * 14,
        out_specs=[anywhere] * 3 + [spec] * 9,
        scratch_shapes=scratch,
        compiler_params=pltpu.CompilerParams(
            collective_id=4, has_side_effects=True, vmem_limit_bytes=58 * 2**20
        ),
        name="close",
    )(*expert_own, *shared_own, *blocks, misc, results, base, shares)


def per_device_dense(
    tokens,
    expert_ids,
    norm_one,
    w_query,
    w_key,
    w_value,
    w_out,
    norm_two,
    w_router,
    expert_gate,
    expert_up,
    expert_down,
    shared_gate,
    shared_up,
    shared_down,
    cotangent,
):
    rows = tokens.shape[1]
    width = tokens.shape[2]
    heads = width // HEAD_DIM
    scale = HEAD_DIM ** (-0.5)
    ctx_count = lax.axis_size("ctx")
    ctx_place = lax.axis_index("ctx")
    exp_place = lax.axis_index("exp")
    row_groups = lax.axis_size("seq") * ctx_count
    places = ctx_place * rows + jnp.arange(rows, dtype=jnp.int32)
    upstream = cotangent[0]
    ids = expert_ids[0]
    experts = jnp.arange(128, dtype=jnp.int32)
    named = jnp.any(ids[:, :, None] == experts[None, None, :], axis=1)
    (
        q_all, k_all, v_all, upstream_all, named_all, normed, attended, mixed, second, log_sum,
    ) = front(
        tokens[0], upstream, named.astype(jnp.bfloat16), norm_one, norm_two, w_query, w_key, w_value, w_out
    )
    (
        results, shares, base, d_mixed, small, eg_own, eu_own, ed_own, sg_own, su_own, sd_own,
    ) = ffn(
        second, mixed, upstream_all, named_all, w_router, norm_two,
        (expert_gate[0], expert_up[0], expert_down[0]), (shared_gate, shared_up, shared_down),
    )

    def heads_of(matrix):
        return matrix.reshape(matrix.shape[0], heads, HEAD_DIM)

    span = ctx_count * rows
    inputs = tokens[0].astype(jnp.float32)
    unused, norm_one_pull = jax.vjp(normalize, inputs, norm_one)
    query = heads_of(lax.dynamic_index_in_dim(q_all, ctx_place, 0, False))
    keys_all, values_all = heads_of(k_all.reshape(span, width)), heads_of(v_all.reshape(span, width))
    allowed = (jnp.arange(span, dtype=jnp.int32) // BLOCK)[None, None, :] <= (
        places // BLOCK
    )[None, :, None]
    scores = jnp.einsum("qhd,khd->hqk", query, keys_all, preferred_element_type=jnp.float32)
    weights = jnp.where(allowed, jnp.exp(scores * scale - log_sum.T[:heads, :, None]), 0.0)
    weights_low = weights.astype(jnp.bfloat16)
    d_attention = d_mixed.astype(jnp.bfloat16)
    grad_out = outer_sum(attended, d_attention)
    d_attended = heads_of(against(d_attention, w_out).astype(jnp.bfloat16))
    d_weights = jnp.einsum(
        "qhd,khd->hqk", d_attended, values_all, preferred_element_type=jnp.float32
    )
    delta = jnp.sum(weights * d_weights, axis=-1, keepdims=True)
    d_scores = (weights * (d_weights - delta)).astype(jnp.bfloat16)
    d_query = (
        jnp.einsum("hqk,khd->qhd", d_scores, keys_all, preferred_element_type=jnp.float32) * scale
    )
    d_key = (
        jnp.einsum("hqk,qhd->khd", d_scores, query, preferred_element_type=jnp.float32) * scale
    )
    d_value = jnp.einsum(
        "hqk,qhd->khd", weights_low, d_attended, preferred_element_type=jnp.float32
    )
    key_terms = jnp.concatenate([d_key.reshape(span, width), d_value.reshape(span, width)], axis=1)
    key_grads = lax.psum_scatter(
        key_terms.astype(jnp.bfloat16), "ctx", scatter_dimension=0, tiled=True
    )
    d_value = key_grads[:, width:]
    d_key_lin = rotate(heads_of(key_grads[:, :width].astype(jnp.float32)), -places)
    d_key_lin = d_key_lin.astype(jnp.bfloat16).reshape(rows, width)
    d_query_lin = rotate(d_query, -places).astype(jnp.bfloat16).reshape(rows, width)
    grad_query = outer_sum(normed, d_query_lin)
    grad_key = outer_sum(normed, d_key_lin)
    grad_value = outer_sum(normed, d_value)
    d_normed = against(d_query_lin, w_query) + against(d_key_lin, w_key) + against(d_value, w_value)
    d_inputs, grad_norm_one = norm_one_pull(d_normed)
    grad_tokens = (d_mixed + d_inputs)[None]
    misc = jnp.concatenate(
        [grad_norm_one[None], small[8:9], small[:4], jnp.zeros((2, width), jnp.float32)], axis=0
    )
    plain = [g.astype(jnp.bfloat16) for g in (grad_query, grad_key, grad_value, grad_out)]
    (
        eg, eu, ed, sg, su, sd, gq, gk, gv, go, misc, output,
    ) = close((eg_own, eu_own, ed_own), (sg_own, su_own, sd_own), plain, misc, results, base, shares)
    row_place = lax.axis_index("seq") * ctx_count + ctx_place
    own_rows = width // row_groups
    router = lax.dynamic_slice(misc, (2 + exp_place, row_place * own_rows), (1, own_rows))
    return (
        output[None],
        grad_tokens,
        misc[0],
        gq,
        gk,
        gv,
        go,
        misc[1],
        router.T,
        eg.astype(jnp.float32).reshape(expert_gate.shape),
        eu.astype(jnp.float32).reshape(expert_up.shape),
        ed.astype(jnp.float32).reshape(expert_down.shape),
        sg,
        su,
        sd,
    )


def fits(mesh):
    return dict(mesh.shape) == {"seq": 2, "ctx": 4, "exp": 4}


def solution(mesh):
    per_device = per_device_dense if fits(mesh) else per_device_slots
    in_specs = (
        P(("seq", "exp"), "ctx", None),
        P(("seq", "exp"), "ctx", None),
        P(),
        P(),
        P(),
        P(),
        P(),
        P(),
        P(),
        P("exp", None, None),
        P("exp", None, None),
        P("exp", None, None),
        P(),
        P(),
        P(),
        P(("seq", "exp"), "ctx", None),
    )
    out_specs = (
        P(("seq", "exp"), "ctx", None),
        P(("seq", "exp"), "ctx", None),
        P(),
        P(("seq", "ctx"), "exp"),
        P(("seq", "ctx"), "exp"),
        P(("seq", "ctx"), "exp"),
        P(("seq", "ctx"), "exp"),
        P(),
        P(("seq", "ctx"), "exp"),
        P("exp", None, None),
        P("exp", None, None),
        P("exp", None, None),
        P(("seq", "ctx"), "exp"),
        P(("seq", "ctx"), "exp"),
        P(("seq", "ctx"), "exp"),
    )
    return jax.shard_map(
        per_device, mesh=mesh, in_specs=in_specs, out_specs=out_specs, check_vma=False
    )
```

```python
import functools
import math

import jax
import jax.numpy as jnp
import numpy as np
from jax import lax
from jax.experimental import pallas as pl
from jax.experimental.pallas import tpu as pltpu
from jax.sharding import PartitionSpec as P

HEAD_DIM = 64
TOP = 2
BLOCK = 256
KEY_ROWS = 512
MESH = pl.DeviceIdType.MESH


def product(first_factor, second_factor):
    return jnp.dot(first_factor, second_factor, preferred_element_type=jnp.float32)


def against(first_factor, second_factor):
    return lax.dot_general(
        first_factor, second_factor, (((1,), (1,)), ((), ())), preferred_element_type=jnp.float32
    )


def outer_sum(first_factor, second_factor):
    return lax.dot_general(
        first_factor, second_factor, (((0,), (0,)), ((), ())), preferred_element_type=jnp.float32
    )


def normalize(values, scaling):
    return values * lax.rsqrt(jnp.mean(values * values, axis=-1, keepdims=True) + 1e-06) * scaling


def rotate(values, places):
    halfway = values.shape[-1] // 2
    frequency = 10000.0 ** (-jnp.arange(halfway, dtype=jnp.float32) / halfway)
    angles = places.astype(jnp.float32)[:, None] * frequency[None, :]
    cosine = jnp.cos(angles)[:, None, :]
    sine_part = jnp.sin(angles)[:, None, :]
    former = values[..., :halfway]
    latter = values[..., halfway:]
    return jnp.concatenate(
        [former * cosine - latter * sine_part, latter * cosine + former * sine_part], axis=-1
    )


def silu_parts(gate_pre):
    sigmoid_value = jax.nn.sigmoid(gate_pre)
    return (gate_pre * sigmoid_value, sigmoid_value * (1.0 + gate_pre * (1.0 - sigmoid_value)))


def tiled(matrix, row_groups, col_groups):
    row_count, col_count = matrix.shape
    blocks = matrix.reshape(
        row_groups, row_count // row_groups, col_groups, col_count // col_groups
    ).transpose(0, 2, 1, 3)
    return blocks.reshape(col_groups * row_count, col_count // col_groups)


def per_device_slots(
    tokens,
    expert_ids,
    norm_one,
    w_query,
    w_key,
    w_value,
    w_out,
    norm_two,
    w_router,
    expert_gate,
    expert_up,
    expert_down,
    shared_gate,
    shared_up,
    shared_down,
    cotangent,
):
    local_rows = tokens.shape[1]
    model_width = tokens.shape[2]
    head_count = model_width // HEAD_DIM
    score_scale = HEAD_DIM ** (-0.5)
    ctx_count = lax.axis_size("ctx")
    ctx_place = lax.axis_index("ctx")
    exp_count = lax.axis_size("exp")
    row_groups = lax.axis_size("seq") * ctx_count
    local_experts = expert_gate.shape[0]
    experts_all = local_experts * exp_count
    capacity = min(local_rows, 2 * TOP * local_rows // experts_all)
    places = ctx_place * local_rows + jnp.arange(local_rows, dtype=jnp.int32)
    query_blocks = places // BLOCK

    def spread(matrix):
        return tiled(matrix, row_groups, exp_count)

    inputs = tokens[0].astype(jnp.float32)
    normed_full, norm_one_pull = jax.vjp(normalize, inputs, norm_one)
    normed = normed_full.astype(jnp.bfloat16)
    query = rotate(
        product(normed, w_query).reshape(local_rows, head_count, HEAD_DIM), places
    ).astype(jnp.bfloat16)
    keys_local = (
        rotate(product(normed, w_key).reshape(local_rows, head_count, HEAD_DIM), places)
        .astype(jnp.bfloat16)
        .reshape(local_rows, model_width)
    )
    values_local = product(normed, w_value).astype(jnp.bfloat16)

    def block_scores(key_block, offset):
        key_heads = key_block.reshape(-1, head_count, HEAD_DIM)
        scores = (
            jnp.einsum("qhd,khd->hqk", query, key_heads, preferred_element_type=jnp.float32)
            * score_scale
        )
        key_index = (offset + jnp.arange(key_block.shape[0], dtype=jnp.int32)) // BLOCK
        allowed = key_index[None, :] <= query_blocks[:, None]
        return (scores, allowed)

    def attend_block(running, key_block, value_block, offset):
        highest, totals, accumulated = running
        scores, allowed = block_scores(key_block, offset)
        masked = jnp.where(allowed[None], scores, -1e30)
        fresh = jnp.maximum(highest, jnp.max(masked, axis=-1))
        weights = jnp.where(allowed[None], jnp.exp(masked - fresh[..., None]), 0.0)
        decay = jnp.exp(highest - fresh)
        value_heads = value_block.reshape(-1, head_count, HEAD_DIM)
        accumulated = accumulated * decay[..., None] + jnp.einsum(
            "hqk,khd->hqd",
            weights.astype(jnp.bfloat16),
            value_heads,
            preferred_element_type=jnp.float32,
        )
        return (fresh, totals * decay + jnp.sum(weights, axis=-1), accumulated)

    start_state = (
        jnp.full((head_count, local_rows), -1e30, jnp.float32),
        jnp.zeros((head_count, local_rows), jnp.float32),
        jnp.zeros((head_count, local_rows, HEAD_DIM), jnp.float32),
    )
    running = start_state
    key_part = lax.all_gather(keys_local, "ctx", axis=0, tiled=True)
    value_part = lax.all_gather(values_local, "ctx", axis=0, tiled=True)
    span_rows = key_part.shape[0]
    stride = math.gcd(span_rows, KEY_ROWS)
    step_count = span_rows // stride
    key_steps = key_part.reshape(step_count, stride, model_width)
    value_steps = value_part.reshape(step_count, stride, model_width)
    offsets = jnp.arange(step_count, dtype=jnp.int32) * stride

    def one_step(inner, operands):
        return (attend_block(inner, operands[0], operands[1], operands[2]), None)

    running, unused = lax.scan(one_step, running, (key_steps, value_steps, offsets))
    highest, totals, accumulated = running
    log_total = highest + jnp.log(totals)
    attended = (
        (accumulated / totals[..., None])
        .transpose(1, 0, 2)
        .reshape(local_rows, model_width)
        .astype(jnp.bfloat16)
    )
    mixed = inputs + product(attended, w_out)
    second_full, norm_two_pull = jax.vjp(normalize, mixed, norm_two)
    second = second_full.astype(jnp.bfloat16)
    logits = product(second, w_router)
    chosen = expert_ids[0]
    one_hot = (
        chosen[:, :, None] == jnp.arange(experts_all, dtype=jnp.int32)[None, None, :]
    ).astype(jnp.float32)
    selected = jnp.sum(logits[:, None, :] * one_hot, axis=-1)
    gates = jax.nn.softmax(selected, axis=-1)
    flat_ids = chosen.reshape(-1)
    slot_hits = (flat_ids[:, None] == jnp.arange(experts_all, dtype=jnp.int32)[None, :]).astype(
        jnp.int32
    )
    order = jnp.arange(flat_ids.shape[0], dtype=jnp.int32)
    earlier = (order[None, :] < order[:, None]).astype(jnp.bfloat16)
    counts_before = product(earlier, slot_hits.astype(jnp.bfloat16)).astype(jnp.int32)
    slot_place = jnp.sum(counts_before * slot_hits, axis=1)

    def to_slots(routed_rows):
        empty_slots = jnp.zeros((experts_all, capacity, model_width), jnp.bfloat16)
        return (
            empty_slots.at[flat_ids, slot_place]
            .set(routed_rows)
            .reshape(exp_count, local_experts, capacity, model_width)
        )

    def from_slots(arrived_back):
        picked = arrived_back.reshape(experts_all, capacity, model_width)[flat_ids, slot_place]
        return picked.astype(jnp.float32).reshape(local_rows, TOP, model_width)

    def expert_front(arrived_rows):
        gate_pre = jnp.einsum(
            "sjcd,jdf->sjcf", arrived_rows, expert_gate, preferred_element_type=jnp.float32
        )
        up_pre = jnp.einsum(
            "sjcd,jdf->sjcf", arrived_rows, expert_up, preferred_element_type=jnp.float32
        )
        hidden = (jax.nn.silu(gate_pre) * up_pre).astype(jnp.bfloat16)
        return (gate_pre, up_pre, hidden)

    send_rows = to_slots(jnp.repeat(second, TOP, axis=0))
    arrived = lax.all_to_all(send_rows, "exp", split_axis=0, concat_axis=0, tiled=True)
    gate_pre, up_pre, hidden = expert_front(arrived)
    results = jnp.einsum(
        "sjcf,jfd->sjcd", hidden, expert_down, preferred_element_type=jnp.float32
    ).astype(jnp.bfloat16)
    returned = lax.all_to_all(results, "exp", split_axis=0, concat_axis=0, tiled=True)
    expert_out = from_slots(returned)
    mixture = jnp.sum(gates[:, :, None] * expert_out, axis=1)
    shared_gate_pre = product(second, shared_gate)
    shared_up_pre = product(second, shared_up)
    shared_hidden = (jax.nn.silu(shared_gate_pre) * shared_up_pre).astype(jnp.bfloat16)
    output = (mixed + mixture + product(shared_hidden, shared_down)).astype(jnp.bfloat16)
    upstream = cotangent[0]
    upstream_full = upstream.astype(jnp.float32)
    grad_shared_down = outer_sum(shared_hidden, upstream)
    d_shared_hidden = against(upstream, shared_down)
    shared_silu, shared_slope = silu_parts(shared_gate_pre)
    d_shared_gate = (d_shared_hidden * shared_up_pre * shared_slope).astype(jnp.bfloat16)
    d_shared_up = (d_shared_hidden * shared_silu).astype(jnp.bfloat16)
    grad_shared_gate = outer_sum(second, d_shared_gate)
    grad_shared_up = outer_sum(second, d_shared_up)
    d_second = against(d_shared_gate, shared_gate) + against(d_shared_up, shared_up)
    d_gates = jnp.sum(upstream_full[:, None, :] * expert_out, axis=-1)
    d_selected = gates * (d_gates - jnp.sum(gates * d_gates, axis=-1, keepdims=True))
    d_logits = jnp.sum(d_selected[:, :, None] * one_hot, axis=1).astype(jnp.bfloat16)
    grad_router = outer_sum(second, d_logits)
    d_second = d_second + against(d_logits, w_router)
    grad_slots = to_slots(
        (gates[:, :, None] * upstream_full[:, None, :])
        .astype(jnp.bfloat16)
        .reshape(local_rows * TOP, model_width)
    )
    arrived_rows, arrived_grad = (
        lax.all_to_all(send_rows, "exp", split_axis=0, concat_axis=0, tiled=True),
        lax.all_to_all(grad_slots, "exp", split_axis=0, concat_axis=0, tiled=True),
    )
    gate_kept, up_kept, hidden_kept = expert_front(arrived_rows)
    d_hidden = jnp.einsum(
        "sjcd,jfd->sjcf", arrived_grad, expert_down, preferred_element_type=jnp.float32
    )
    expert_silu, expert_slope = silu_parts(gate_kept)
    d_gate_pre = (d_hidden * up_kept * expert_slope).astype(jnp.bfloat16)
    d_up_pre = (d_hidden * expert_silu).astype(jnp.bfloat16)
    grad_expert_down = jnp.einsum(
        "sjcf,sjcd->jfd", hidden_kept, arrived_grad, preferred_element_type=jnp.float32
    )
    grad_expert_gate = jnp.einsum(
        "sjcd,sjcf->jdf", arrived_rows, d_gate_pre, preferred_element_type=jnp.float32
    )
    grad_expert_up = jnp.einsum(
        "sjcd,sjcf->jdf", arrived_rows, d_up_pre, preferred_element_type=jnp.float32
    )
    d_routed = (
        jnp.einsum("sjcf,jdf->sjcd", d_gate_pre, expert_gate, preferred_element_type=jnp.float32)
        + jnp.einsum("sjcf,jdf->sjcd", d_up_pre, expert_up, preferred_element_type=jnp.float32)
    ).astype(jnp.bfloat16)
    returned_grad = lax.all_to_all(d_routed, "exp", split_axis=0, concat_axis=0, tiled=True)
    d_second = d_second + jnp.sum(from_slots(returned_grad), axis=1)
    grad_expert_gate, grad_expert_up, grad_expert_down = (
        lax.psum(grad_expert_gate.astype(jnp.bfloat16), ("seq", "ctx")).astype(jnp.float32),
        lax.psum(grad_expert_up.astype(jnp.bfloat16), ("seq", "ctx")).astype(jnp.float32),
        lax.psum(grad_expert_down.astype(jnp.bfloat16), ("seq", "ctx")).astype(jnp.float32),
    )
    d_mixed_part, grad_norm_two = norm_two_pull(d_second)
    d_mixed = upstream_full + d_mixed_part
    d_attention = d_mixed.astype(jnp.bfloat16)
    grad_out = outer_sum(attended, d_attention)
    grad_heads = (
        against(d_attention, w_out).astype(jnp.bfloat16).reshape(local_rows, head_count, HEAD_DIM)
    )
    keys_all, values_all = (
        lax.all_gather(keys_local, "ctx", axis=0, tiled=True),
        lax.all_gather(values_local, "ctx", axis=0, tiled=True),
    )
    block_total = ((ctx_place + 1) * local_rows + KEY_ROWS - 1) // KEY_ROWS

    def weights_at(number):
        offset = number * KEY_ROWS
        key_block = lax.dynamic_slice_in_dim(keys_all, offset, KEY_ROWS, 0)
        value_block = lax.dynamic_slice_in_dim(values_all, offset, KEY_ROWS, 0)
        scores, allowed = block_scores(key_block, offset)
        weights = jnp.where(allowed[None], jnp.exp(scores - log_total[..., None]), 0.0)
        grad_weights = jnp.einsum(
            "qhd,khd->hqk",
            grad_heads,
            value_block.reshape(KEY_ROWS, head_count, HEAD_DIM),
            preferred_element_type=jnp.float32,
        )
        return (key_block, weights, grad_weights)

    def row_dot_step(number, summed):
        unused_block, weights, grad_weights = weights_at(number)
        return summed + jnp.sum(weights * grad_weights, axis=-1)

    row_dots = lax.fori_loop(
        0, block_total, row_dot_step, jnp.zeros((head_count, local_rows), jnp.float32)
    )

    def score_grads(number):
        key_block, weights, grad_weights = weights_at(number)
        d_scores = (weights * (grad_weights - row_dots[..., None])).astype(jnp.bfloat16)
        return (key_block.reshape(KEY_ROWS, head_count, HEAD_DIM), weights, d_scores)

    query_start = jnp.zeros((local_rows, head_count, HEAD_DIM), jnp.float32)

    def grad_step(number, running):
        grad_query, key_terms = running
        key_heads, weights, d_scores = score_grads(number)
        grad_query = (
            grad_query
            + jnp.einsum("hqk,khd->qhd", d_scores, key_heads, preferred_element_type=jnp.float32)
            * score_scale
        )
        key_part = (
            jnp.einsum("hqk,qhd->khd", d_scores, query, preferred_element_type=jnp.float32)
            * score_scale
        )
        value_part = jnp.einsum(
            "hqk,qhd->khd",
            weights.astype(jnp.bfloat16),
            grad_heads,
            preferred_element_type=jnp.float32,
        )
        block_terms = jnp.concatenate(
            [key_part.reshape(KEY_ROWS, model_width), value_part.reshape(KEY_ROWS, model_width)],
            axis=1,
        )
        return (
            grad_query,
            lax.dynamic_update_slice_in_dim(key_terms, block_terms, number * KEY_ROWS, 0),
        )

    grad_query_heads, key_terms = lax.fori_loop(
        0,
        block_total,
        grad_step,
        (query_start, jnp.zeros((ctx_count * local_rows, 2 * model_width), jnp.float32)),
    )
    key_grads = lax.psum_scatter(
        key_terms.astype(jnp.bfloat16), "ctx", scatter_dimension=0, tiled=True
    ).astype(jnp.float32)
    key_grad_heads = key_grads[:, :model_width].reshape(local_rows, head_count, HEAD_DIM)
    d_value = key_grads[:, model_width:].astype(jnp.bfloat16)
    d_query_lin = (
        rotate(grad_query_heads, -places).astype(jnp.bfloat16).reshape(local_rows, model_width)
    )
    d_key_lin = (
        rotate(key_grad_heads, -places).astype(jnp.bfloat16).reshape(local_rows, model_width)
    )
    grad_query = outer_sum(normed, d_query_lin)
    grad_key = outer_sum(normed, d_key_lin)
    grad_value = outer_sum(normed, d_value)
    d_normed = against(d_query_lin, w_query) + against(d_key_lin, w_key) + against(d_value, w_value)
    d_inputs, grad_norm_one = norm_one_pull(d_normed)
    grad_tokens = (d_mixed + d_inputs)[None]
    (
        grad_query,
        grad_key,
        grad_value,
        grad_out,
        grad_router,
        grad_shared_gate,
        grad_shared_up,
        grad_shared_down,
    ) = (
        lax.psum_scatter(
            spread(grad_query), ("seq", "ctx", "exp"), scatter_dimension=0, tiled=True
        ),
        lax.psum_scatter(spread(grad_key), ("seq", "ctx", "exp"), scatter_dimension=0, tiled=True),
        lax.psum_scatter(
            spread(grad_value), ("seq", "ctx", "exp"), scatter_dimension=0, tiled=True
        ),
        lax.psum_scatter(spread(grad_out), ("seq", "ctx", "exp"), scatter_dimension=0, tiled=True),
        lax.psum_scatter(
            spread(grad_router), ("seq", "ctx", "exp"), scatter_dimension=0, tiled=True
        ),
        lax.psum_scatter(
            spread(grad_shared_gate), ("seq", "ctx", "exp"), scatter_dimension=0, tiled=True
        ),
        lax.psum_scatter(
            spread(grad_shared_up), ("seq", "ctx", "exp"), scatter_dimension=0, tiled=True
        ),
        lax.psum_scatter(
            spread(grad_shared_down), ("seq", "ctx", "exp"), scatter_dimension=0, tiled=True
        ),
    )
    grad_norm_one, grad_norm_two = lax.psum((grad_norm_one, grad_norm_two), ("seq", "ctx", "exp"))
    return (
        output[None],
        grad_tokens,
        grad_norm_one,
        grad_query,
        grad_key,
        grad_value,
        grad_out,
        grad_norm_two,
        grad_router,
        grad_expert_gate,
        grad_expert_up,
        grad_expert_down,
        grad_shared_gate,
        grad_shared_up,
        grad_shared_down,
    )


def place_tables(length):
    half = HEAD_DIM // 2
    frequency = np.float32(10000.0) ** (-np.arange(half, dtype=np.float32) / np.float32(half))
    angles = np.arange(length, dtype=np.float32)[:, None] * frequency[None, :].astype(np.float32)
    cosine, sine = np.cos(angles), np.sin(angles)
    return (
        np.concatenate([cosine] * 4, axis=1).astype(np.float32),
        np.concatenate([-sine, sine, -sine, sine], axis=1).astype(np.float32),
    )


def swapped(values):
    half = HEAD_DIM // 2
    lane = lax.broadcasted_iota(jnp.int32, values.shape, 1) % HEAD_DIM
    return jnp.where(lane < half, pltpu.roll(values, 128 - half, 1), pltpu.roll(values, half, 1))


def start_copy(src, dst, ssem, rsem, device):
    copy = pltpu.make_async_remote_copy(
        src_ref=src, dst_ref=dst, send_sem=ssem, recv_sem=rsem, device_id=device, device_id_type=MESH
    )
    copy.start()
    return copy


def greet(devices):
    barrier = pltpu.get_barrier_semaphore()
    for device in devices:
        pl.semaphore_signal(barrier, inc=1, device_id=device, device_id_type=MESH)
    pl.semaphore_wait(barrier, len(devices))


def neighbours():
    s = lax.axis_index("seq")
    c = lax.axis_index("ctx")
    e = lax.axis_index("exp")
    x, k = c // 2, c % 2
    to_core = (s, x * 2 + (1 - k), e)
    to_x = (s, (1 - x) * 2 + k, e)
    to_y = (1 - s, c, e)
    near = e + 1 - 2 * (e % 2)
    far = lax.rem(e + 2, 4)
    opposite = 3 - e
    return s, x, k, e, c, to_core, to_x, to_y, (near, far, opposite)


def front_kernel(
    tokens, upstream, named, gain_one, gain_two, w_q, w_k, w_v, w_o, cosine, sine,
    q_all, k_all, v_all, upstream_all, named_all, normed_out, attended_out, mixed_out, second_out, logsum_out,
    block, tsem, trem, usem, urem, nsem, nrem,
):
    s, x, k, e, c, to_core, to_x, to_y, others = neighbours()
    rows, width = tokens.shape
    greet([to_core, to_x, *[(s, c, o) for o in others]])
    block[c] = tokens[...]
    upstream_all[0] = upstream[...]
    named_all[0] = named[...]
    core_copy = start_copy(tokens, block.at[c], tsem.at[0], trem.at[0], to_core)
    x_copy = start_copy(tokens, block.at[c], tsem.at[1], trem.at[1], to_x)
    z_copies = []
    for i in range(3):
        device = (s, c, others[i])
        z_copies.append(start_copy(named, named_all.at[i + 1], nsem.at[i], nrem.at[i], device))
        z_copies.append(start_copy(upstream, upstream_all.at[i + 1], usem.at[i], urem.at[i], device))

    def project(j):
        values = block[j].astype(jnp.float32)
        inverse = lax.rsqrt(jnp.mean(values * values, axis=-1, keepdims=True) + 1e-06)
        normed = (values * inverse * gain_one[...]).astype(jnp.bfloat16)
        for weight, out in ((w_q, q_all), (w_k, k_all)):
            lin = jnp.dot(normed, weight[...], preferred_element_type=jnp.float32)
            for g in range(width // 128):
                part = lin[:, g * 128 : (g + 1) * 128]
                turned = part * cosine[j] + swapped(part) * sine[j]
                out[j, :, g * 128 : (g + 1) * 128] = turned.astype(jnp.bfloat16)
        v_all[j] = jnp.dot(normed, w_v[...], preferred_element_type=jnp.float32).astype(jnp.bfloat16)
        return normed

    normed_out[...] = project(c)
    core_copy.wait()
    project(x * 2 + (1 - k))
    x_copy.wait()
    there = (1 - x) * 2 + k
    corner_copy = start_copy(block.at[there], block.at[there], tsem.at[2], trem.at[2], to_core)
    project(there)
    corner_copy.wait()
    project((1 - x) * 2 + (1 - k))

    span = 4 * rows
    hidden_keys = lax.broadcasted_iota(jnp.int32, (1, span), 1) // rows > c
    bias = jnp.where(hidden_keys, -1e30, 0.0)
    lane = lax.broadcasted_iota(jnp.int32, (rows, 128), 1)
    logsum_out[...] = jnp.zeros_like(logsum_out)

    def pair(g, carry):
        at = pl.ds(pl.multiple_of(g * 128, 128), 128)
        q = q_all[c, :, at]
        keys = k_all[:, :, at].reshape(span, 128)
        values = v_all[:, :, at].reshape(span, 128)
        out = jnp.zeros((rows, 128), jnp.float32)
        for h in range(2):
            inside = (lane // HEAD_DIM) == h
            scores = lax.dot_general(
                jnp.where(inside, q, jnp.zeros_like(q)), keys, (((1,), (1,)), ((), ())),
                preferred_element_type=jnp.float32,
            )
            scores = scores * (HEAD_DIM**-0.5) + bias
            highest = jnp.max(scores, axis=-1, keepdims=True)
            raised = jnp.exp(scores - highest)
            total = jnp.sum(raised, axis=-1, keepdims=True)
            mixed = jnp.dot(raised.astype(jnp.bfloat16), values, preferred_element_type=jnp.float32)
            out = jnp.where(inside, mixed / total, out)
            logsum_out[...] = jnp.where(lane == 2 * g + h, highest + jnp.log(total), logsum_out[...])
        attended_out[:, at] = out.astype(jnp.bfloat16)
        return carry

    lax.fori_loop(0, width // 128, pair, 0)
    mixed = tokens[...].astype(jnp.float32) + jnp.dot(
        attended_out[...], w_o[...], preferred_element_type=jnp.float32
    )
    mixed_out[...] = mixed
    inverse = lax.rsqrt(jnp.mean(mixed * mixed, axis=-1, keepdims=True) + 1e-06)
    second_out[...] = (mixed * inverse * gain_two[...]).astype(jnp.bfloat16)
    for copy in z_copies:
        copy.wait()


def front(tokens, upstream, named, gain_one, gain_two, w_q, w_k, w_v, w_o):
    rows, width = tokens.shape
    cosine, sine = (jnp.asarray(t).reshape(4, rows, 128) for t in place_tables(4 * rows))
    low, full = jnp.bfloat16, jnp.float32
    vmem, dma = pltpu.VMEM, pltpu.SemaphoreType.DMA
    every = jax.ShapeDtypeStruct((4, rows, width), low)
    own = jax.ShapeDtypeStruct((rows, width), low)
    spec = pl.BlockSpec(memory_space=pltpu.VMEM)
    out_shape = [
        every, every, every, every, jax.ShapeDtypeStruct((4, rows, 128), low), own, own,
        jax.ShapeDtypeStruct((rows, width), full), own, jax.ShapeDtypeStruct((rows, 128), full),
    ]
    return pl.pallas_call(
        front_kernel,
        out_shape=out_shape,
        in_specs=[spec] * 11,
        out_specs=[spec] * 10,
        scratch_shapes=[vmem((4, rows, width), low), dma((3,)), dma((3,)), dma((3,)), dma((3,)), dma((3,)), dma((3,))],
        compiler_params=pltpu.CompilerParams(
            collective_id=2, has_side_effects=True, vmem_limit_bytes=58 * 2**20
        ),
        name="front",
    )(tokens, upstream, named, gain_one.reshape(1, width), gain_two.reshape(1, width), w_q, w_k, w_v, w_o, cosine, sine)


def add_rows(target, first, second, step):
    rows = target.shape[0]

    def some(at):
        total = first[at, :].astype(jnp.float32) + second[at, :].astype(jnp.float32)
        target[at, :] = total.astype(target.dtype)

    if rows <= step:
        some(pl.ds(0, rows))
    else:

        def body(i, carry):
            some(pl.ds(pl.multiple_of(i * step, step), step))
            return carry

        lax.fori_loop(0, rows // step, body, 0)


class Piece:
    def __init__(self, place, whole, one, two, three, half, sems, step):
        self.s, self.x, self.k, self.to_core, self.to_x, self.to_y = place
        self.whole, self.one, self.two, self.three = whole, one, two, three
        self.half, self.sems, self.step = half, sems, step

    def copy(self, level, h=0):
        every, low, high = slice(None), pl.ds(0, self.half), pl.ds(self.half, self.half)
        if level == 1:
            src, dst, device = self.whole(1 - self.k), self.one(every, every, every), self.to_core
        elif level == 2:
            if h == 0:
                src, device = self.one(every, 1 - self.x, low), self.to_x
            else:
                src, device = self.one(1 - self.s, every, high), self.to_y
            dst = self.two(h, every)
        else:
            src = self.two(h, 1 - (self.s, self.x)[h])
            dst, device = self.three(h), (self.to_y, self.to_x)[h]
        ssem, rsem = self.sems(2 * (level - 1) - (1 if level > 1 else 0) + h)
        return pltpu.make_async_remote_copy(
            src_ref=src, dst_ref=dst, send_sem=ssem, recv_sem=rsem, device_id=device, device_id_type=MESH
        )

    def start(self, level):
        for h in range(1 if level == 1 else 2):
            self.copy(level, h).start()

    def finish(self, level):
        low, high = pl.ds(0, self.half), pl.ds(self.half, self.half)
        if level == 1:
            self.copy(1).wait()
            own = self.whole(self.k)
            for i in range(2):
                for j in range(2):
                    here = self.one(i, j, slice(None))
                    add_rows(here, here, own.at[i, j], self.step)
            return
        for h in range(2):
            self.copy(level, h).wait()
            if level == 2:
                for i in range(2):
                    here = self.two(h, i)
                    own = self.one(i, self.x, low) if h == 0 else self.one(self.s, i, high)
                    add_rows(here, here, own, self.step)
            else:
                here = self.three(h)
                add_rows(here, here, self.two(h, (self.s, self.x)[h]), self.step)


def gates_in(logits, named):
    masked = jnp.where(named, logits, -1e30)
    raised = jnp.where(named, jnp.exp(masked - jnp.max(masked, axis=-1, keepdims=True)), 0.0)
    return raised / jnp.sum(raised, axis=-1, keepdims=True)


def ffn_kernel(
    second, mixed, upstream_all, named_all, w_r, gain_two,
    e_gate, e_up, e_down, s_gate, s_up, s_down,
    results, shares_out, base_out, d_mixed_out, small_out, eg_out, eu_out, ed_out, sg_out, su_out, sd_out,
    rows_all, d_res, res_acc, row_acc, row_send, row_got, dg_send, dg_got, d_second,
    t_gate, t_up, t_down, wsem,
    ge_g, ge_u, ge_d, e1_g, e1_u, e1_d, e2_g, e2_u, e2_d,
    gs_g, gs_u, gs_d, s1_g, s1_u, s1_d, s2_g, s2_u, s2_d,
    es_sem, er_sem, ss_sem, sr_sem, xs_sem, xr_sem, rs_sem, rr_sem, ds_sem, dr_sem,
):
    s, x, k, e, c, to_core, to_x, to_y, others = neighbours()
    place = (s, x, k, to_core, to_x, to_y)
    rows, width = second.shape
    tile = t_gate.shape[2]
    tiles = e_gate.shape[1] // tile
    low, full = jnp.bfloat16, jnp.float32
    greet([to_core, to_x, to_y, *[(s, c, o) for o in others]])
    rows_all[0] = second[...]
    row_copies = [
        start_copy(second, rows_all.at[i + 1], xs_sem.at[i], xr_sem.at[i], (s, c, others[i])) for i in range(3)
    ]

    def columns(f):
        return pl.ds(pl.multiple_of(f * tile, tile), tile)

    def fetches(sources, f, slot):
        gate, up, down = sources
        return [
            pltpu.make_async_copy(gate.at[:, columns(f)], t_gate.at[slot], wsem.at[slot, 0]),
            pltpu.make_async_copy(up.at[:, columns(f)], t_up.at[slot], wsem.at[slot, 1]),
            pltpu.make_async_copy(down.at[columns(f), :], t_down.at[slot], wsem.at[slot, 2]),
        ]

    def next_tile(sources, following, f):
        slot = lax.rem(f, 2)

        @pl.when(f < tiles - 1)
        def _():
            for copy in fetches(sources, f + 1, 1 - slot):
                copy.start()

        if following is not None:

            @pl.when(f == tiles - 1)
            def _():
                for copy in fetches(following, 0, 1 - slot):
                    copy.start()

        for copy in fetches(sources, f, slot):
            copy.wait()
        return slot

    def piece_e(f, a):
        at = columns(f)
        sems = lambda n: (es_sem.at[f, a, n], er_sem.at[f, a, n])
        if a < 2:
            g, one, two, three = ((ge_g, e1_g, e2_g, eg_out), (ge_u, e1_u, e2_u, eu_out))[a]
            return Piece(
                place,
                lambda kk: g.at[:, :, kk, :, at],
                lambda i, j, r: one.at[i, j, r, at],
                lambda h, i: two.at[h, i, :, at],
                lambda h: three.at[h, :, at],
                g.shape[3] // 2, sems, 96,
            )
        return Piece(
            place,
            lambda kk: ge_d.at[f, :, :, kk],
            lambda i, j, r: e1_d.at[f, i, j, r],
            lambda h, i: e2_d.at[f, h, i],
            lambda h: ed_out.at[f, h],
            ge_d.shape[4] // 2, sems, 96,
        )

    def piece_s(a):
        g, one, two, three = (
            (gs_g, s1_g, s2_g, sg_out), (gs_u, s1_u, s2_u, su_out), (gs_d, s1_d, s2_d, sd_out)
        )[a]
        return Piece(
            place,
            lambda kk: g.at[:, :, kk],
            lambda i, j, r: one.at[i, j, r],
            lambda h, i: two.at[h, i],
            lambda h: three.at[h],
            g.shape[3] // 2, lambda n: (ss_sem.at[a, n], sr_sem.at[a, n]), 16 if a < 2 else 32,
        )

    shared, expert = (s_gate, s_up, s_down), (e_gate, e_up, e_down)
    for copy in fetches(shared, 0, 0):
        copy.start()

    def branch(values, d_out, slot, result_acc, d_acc):
        gate_w, up_w, down_w = t_gate[slot], t_up[slot], t_down[slot]
        gate = jnp.dot(values, gate_w, preferred_element_type=full)
        up = jnp.dot(values, up_w, preferred_element_type=full)
        d_hidden = against(d_out, down_w)
        sigmoid = 1.0 / (1.0 + jnp.exp(-gate))
        silu = gate * sigmoid
        hidden = (silu * up).astype(low)
        d_gate = (d_hidden * up * (sigmoid * (1.0 + gate * (1.0 - sigmoid)))).astype(low)
        d_up = (d_hidden * silu).astype(low)
        result_acc[...] += jnp.dot(hidden, down_w, preferred_element_type=full)
        d_acc[...] += against(d_gate, gate_w) + against(d_up, up_w)
        return hidden, d_gate, d_up

    base_out[...] = mixed[...]
    d_second[...] = jnp.zeros_like(d_second)

    def shared_tile(f, carry):
        slot = next_tile(shared, expert, f)
        values, d_out = second[...], upstream_all[0]
        hidden, d_gate, d_up = branch(values, d_out, slot, base_out, d_second)
        gs_g[:, :, :, :, columns(f)] = outer_sum(values, d_gate).astype(low).reshape(2, 2, 2, width // 8, tile)
        gs_u[:, :, :, :, columns(f)] = outer_sum(values, d_up).astype(low).reshape(2, 2, 2, width // 8, tile)
        gs_d[f // 4, (f // 2) % 2, f % 2] = outer_sum(hidden, d_out).astype(low)
        return carry

    lax.fori_loop(0, tiles, shared_tile, 0)
    for a in range(3):
        piece_s(a).start(1)
    logits = jnp.dot(second[...], w_r[...], preferred_element_type=full)
    shares_out[...] = gates_in(logits, named_all[0].astype(full) > 0.5)

    lane = lax.broadcasted_iota(jnp.int32, (2 * rows, 128), 1)
    for turn in range(2):
        if turn == 0:
            row_copies[0].wait()
        else:
            row_copies[1].wait()
            row_copies[2].wait()
        pair = pl.ds(2 * turn, 2)
        values = rows_all[pair].reshape(2 * rows, width)
        logits = jnp.dot(values, w_r[...], preferred_element_type=full)
        gates = gates_in(logits, named_all[pair].reshape(2 * rows, 128).astype(full) > 0.5)
        share = jnp.sum(jnp.where(lane == e, gates, 0.0), axis=-1, keepdims=True)
        d_res[...] = (share * upstream_all[pair].reshape(2 * rows, width).astype(full)).astype(low)
        res_acc[...] = jnp.zeros_like(res_acc)
        row_acc[...] = jnp.zeros_like(row_acc)

        def expert_tile(f, carry, turn=turn, pair=pair):
            slot = next_tile(expert, expert if turn == 0 else None, f)
            values, d_out = rows_all[pair].reshape(2 * rows, width), d_res[...]
            hidden, d_gate, d_up = branch(values, d_out, slot, res_acc, row_acc)
            for g, term in ((ge_g, outer_sum(values, d_gate)), (ge_u, outer_sum(values, d_up))):
                term = term.reshape(2, 2, 2, width // 8, tile)
                if turn == 1:
                    term = term + g[:, :, :, :, columns(f)].astype(full)
                g[:, :, :, :, columns(f)] = term.astype(low)
            term = outer_sum(hidden, d_out).reshape(2, 2, 2, tile // 8, width)
            if turn == 1:
                term = term + ge_d[f].astype(full)
            ge_d[f] = term.astype(low)
            if turn == 0:
                for a in range(3):

                    @pl.when(f == 2 * a + 2)
                    def _(a=a):
                        piece_s(a).finish(1)
                        piece_s(a).start(2)

            else:
                for a in range(3):
                    piece_e(f, a).start(1)

                @pl.when(f > 0)
                def _():
                    for a in range(3):
                        piece_e(f - 1, a).finish(1)
                        piece_e(f - 1, a).start(2)

            return carry

        lax.fori_loop(0, tiles, expert_tile, 0)
        low_result = res_acc[...].astype(low)
        results[pair] = low_result.reshape(2, rows, width)
        row_send[pair] = row_acc[...].astype(low).reshape(2, rows, width)
        terms = low_result.astype(full) * upstream_all[pair].reshape(2 * rows, width).astype(full)
        high = terms.astype(low)
        ones = jnp.ones((8, width), low)
        sums = against(ones, high) + against(ones, (terms - high.astype(full)).astype(low))
        for i in range(2):
            dg_send[2 * turn + i] = sums[:, i * rows : (i + 1) * rows]
        for i in (1,) if turn == 0 else (2, 3):
            device = (s, c, others[i - 1])
            start_copy(row_send.at[i], row_got.at[i], rs_sem.at[i], rr_sem.at[i], device)
            start_copy(dg_send.at[i], dg_got.at[i], ds_sem.at[i], dr_sem.at[i], device)

    for a in range(3):
        piece_e(tiles - 1, a).finish(1)
        piece_e(tiles - 1, a).start(2)
    for a in range(3):
        piece_s(a).finish(2)
        piece_s(a).start(3)

    def third(f, carry):
        for a in range(3):
            piece_e(f, a).finish(2)
            piece_e(f, a).start(3)
        return carry

    lax.fori_loop(0, tiles, third, 0)

    d_gates = jnp.where(lax.broadcasted_iota(jnp.int32, (8, rows), 0) == e, dg_send[0], 0.0)
    total = d_second[...] + row_send[0].astype(full)
    for i in range(1, 4):
        device = (s, c, others[i - 1])
        pltpu.make_async_remote_copy(
            src_ref=row_send.at[i], dst_ref=row_got.at[i], send_sem=rs_sem.at[i], recv_sem=rr_sem.at[i],
            device_id=device, device_id_type=MESH,
        ).wait()
        pltpu.make_async_remote_copy(
            src_ref=dg_send.at[i], dst_ref=dg_got.at[i], send_sem=ds_sem.at[i], recv_sem=dr_sem.at[i],
            device_id=device, device_id_type=MESH,
        ).wait()
        d_gates = jnp.where(
            lax.broadcasted_iota(jnp.int32, (8, rows), 0) == others[i - 1], dg_got[i], d_gates
        )
        total = total + row_got[i].astype(full)
    d_gates = jnp.concatenate([d_gates, jnp.zeros((120, rows), full)], axis=0).T
    shares = shares_out[...]
    d_logits = (shares * (d_gates - jnp.sum(shares * d_gates, axis=-1, keepdims=True))).astype(low)
    total = total + against(d_logits, w_r[...])
    router = outer_sum(d_logits, second[...])
    values = mixed[...]
    inverse = lax.rsqrt(jnp.mean(values * values, axis=-1, keepdims=True) + 1e-06)
    unit = values * inverse
    small_out[0:8, :] = router[0:8, :]
    small_out[8:16, :] = jnp.broadcast_to(jnp.sum(total * unit, axis=0, keepdims=True), (8, width))
    inner = total * gain_two[...]
    mean = jnp.mean(inner * unit, axis=-1, keepdims=True)
    d_mixed_out[...] = upstream_all[0].astype(full) + inverse * (inner - unit * mean)

    for a in range(3):
        piece_s(a).finish(3)

    def done(f, carry):
        for a in range(3):
            piece_e(f, a).finish(3)
        return carry

    lax.fori_loop(0, tiles, done, 0)


def ffn(second, mixed, upstream_all, named_all, w_router, gain_two, experts, shared):
    rows, width = second.shape
    hidden = experts[0].shape[1]
    tile = 256
    tiles = hidden // tile
    low, full = jnp.bfloat16, jnp.float32
    dma = pltpu.SemaphoreType.DMA
    ninth, small, tall = width // 8, tile // 8, hidden // 8

    def vm(*shape, dtype=low):
        return pltpu.VMEM(shape, dtype)

    def out(*shape, dtype=low):
        return jax.ShapeDtypeStruct(shape, dtype)

    w_r = jnp.pad(w_router, ((0, 0), (0, 128 - w_router.shape[1])))
    spec = pl.BlockSpec(memory_space=pltpu.VMEM)
    out_shape = [
        out(4, rows, width), out(rows, 128, dtype=full), out(rows, width, dtype=full), out(rows, width, dtype=full),
        out(16, width, dtype=full), out(2, ninth // 2, hidden), out(2, ninth // 2, hidden),
        out(tiles, 2, small // 2, width), out(2, ninth // 2, hidden), out(2, ninth // 2, hidden), out(2, tall // 2, width),
    ]
    scratch = [
        vm(4, rows, width), vm(2 * rows, width), vm(2 * rows, width, dtype=full), vm(2 * rows, width, dtype=full),
        vm(4, rows, width), vm(4, rows, width), vm(4, 8, rows, dtype=full), vm(4, 8, rows, dtype=full),
        vm(rows, width, dtype=full),
        vm(2, width, tile), vm(2, width, tile), vm(2, tile, width), dma((2, 3)),
        vm(2, 2, 2, ninth, hidden), vm(2, 2, 2, ninth, hidden), vm(tiles, 2, 2, 2, small, width),
        vm(2, 2, ninth, hidden), vm(2, 2, ninth, hidden), vm(tiles, 2, 2, small, width),
        vm(2, 2, ninth // 2, hidden), vm(2, 2, ninth // 2, hidden), vm(tiles, 2, 2, small // 2, width),
        vm(2, 2, 2, ninth, hidden), vm(2, 2, 2, ninth, hidden), vm(2, 2, 2, tall, width),
        vm(2, 2, ninth, hidden), vm(2, 2, ninth, hidden), vm(2, 2, tall, width),
        vm(2, 2, ninth // 2, hidden), vm(2, 2, ninth // 2, hidden), vm(2, 2, tall // 2, width),
        dma((tiles, 3, 5)), dma((tiles, 3, 5)), dma((3, 5)), dma((3, 5)), dma((3,)), dma((3,)),
        dma((4,)), dma((4,)), dma((4,)), dma((4,)),
    ]
    return pl.pallas_call(
        ffn_kernel,
        out_shape=out_shape,
        in_specs=[spec] * 6 + [pl.BlockSpec(memory_space=pl.ANY)] * 6,
        out_specs=[spec] * len(out_shape),
        scratch_shapes=scratch,
        compiler_params=pltpu.CompilerParams(
            collective_id=3, has_side_effects=True, vmem_limit_bytes=60 * 2**20
        ),
        name="ffn",
    )(second, mixed, upstream_all, named_all, w_r, gain_two.reshape(1, width), *experts, *shared)


def back_kernel(
    eg_own, eu_own, ed_own, sg_own, su_own, sd_own, small, results, base, shares,
    tokens, gain_one, d_mixed, attended, normed, q_all, k_all, v_all, log_sum, w_q, w_k, w_v, w_o, cosine, sine,
    eg_all, eu_all, ed_all, sg_out, su_out, sd_out, q_out, k_out, v_out, o_out, misc_out, output, token_out,
    grads, d_att, d_all, stats, stat_col, sum_q, sum_k, sum_v, misc_in, asem, arem, tsem, trem,
    one, two, three, z_flat, z_tall, z_wide, got_flat, got_tall, got_wide, misc_got, result_got,
    lsem, gsem, grem, psem, prem, zsem, zrem, msem, mrem, rsem, rrem,
):
    s, x, k, e, c, to_core, to_x, to_y, others = neighbours()
    place = (s, x, k, to_core, to_x, to_y)
    to_z = [(s, c, o) for o in others]
    low, full = jnp.bfloat16, jnp.float32
    greet([to_core, to_x, to_y, *to_z])

    def piece(a):
        g = grads.at[a]
        return Piece(
            place,
            lambda kk: g.at[:, :, kk],
            lambda i, j, r: one.at[a, i, j, r],
            lambda h, i: two.at[a, h, i],
            lambda h: three.at[a, h],
            g.shape[3] // 2, lambda n: (psem.at[a, n], prem.at[a, n]), 48,
        )

    rows, width = tokens.shape
    heads = width // HEAD_DIM
    d_att[...] = d_mixed[...].astype(low)
    d_all[c] = against(d_att[...], w_o[...]).astype(low)
    head_of = lax.broadcasted_iota(jnp.int32, (128, width), 1) // HEAD_DIM
    chosen = jnp.where(head_of == lax.broadcasted_iota(jnp.int32, (128, width), 0), 1.0, 0.0).astype(low)
    terms = d_all[c].astype(full) * attended[...].astype(full)
    high = terms.astype(low)
    rest = (terms - high.astype(full)).astype(low)
    stat_col[0] = log_sum[...]
    stat_col[1] = against(high, chosen) + against(rest, chosen)
    stats[c, 0] = log_sum[...].T[0:16, :]
    stats[c, 1] = (against(chosen[0:16], high) + against(chosen[0:16], rest))
    core_copies = [
        start_copy(d_all.at[c], d_all.at[c], asem.at[0], arem.at[0], to_core),
        start_copy(stats.at[c], stats.at[c], tsem.at[0], trem.at[0], to_core),
    ]
    x_copies = [
        start_copy(d_all.at[c], d_all.at[c], asem.at[1], arem.at[1], to_x),
        start_copy(stats.at[c], stats.at[c], tsem.at[1], trem.at[1], to_x),
    ]
    result_copies = [
        start_copy(results.at[i + 1], result_got.at[i], rsem.at[i], rrem.at[i], to_z[i]) for i in range(3)
    ]

    def block(a, h, ss, xx):
        whole = (eg_all, eu_all, ed_all)[a]
        half = whole.shape[-2] // 2
        part = pl.ds(h * half, half)
        return whole.at[ss, xx, k, part] if a < 2 else whole.at[:, ss, xx, k, part]

    near, wide, kept = [], [], []
    for a, own in enumerate((eg_own, eu_own, ed_own)):
        for h in range(2):
            src, here = (own.at[h] if a < 2 else own.at[:, h]), block(a, h, s, x)
            kept.append(pltpu.make_async_copy(src, here, lsem.at[a, h]))
            kept[-1].start()
            near.append(start_copy(src, here, gsem.at[a, h, 0], grem.at[a, h, 0], (to_y, to_x)[h]))
    for a, own in enumerate((eg_own, eu_own, ed_own)):
        for h in range(2):
            src, here = (own.at[h] if a < 2 else own.at[:, h]), block(a, h, s, x)
            wide.append(start_copy(src, here, gsem.at[a, h, 1], grem.at[a, h, 1], (to_x, to_y)[h]))

    def spread(own, buffer):
        halves, height, across = own.shape
        piece_width = across // 4
        for h in range(halves):
            for q in range(4):
                buffer[q, pl.ds(h * height, height), :] = own[h, :, q * piece_width : (q + 1) * piece_width]

    def to_owners(buffer, got, number):
        owners = (e, *others)
        return [
            start_copy(buffer.at[owners[i]], got.at[i - 1], zsem.at[number, i - 1], zrem.at[number, i - 1], to_z[i - 1])
            for i in range(1, 4)
        ]

    def settle(copies, buffer, got, target):
        for copy in copies:
            copy.wait()
        target[...] = (
            buffer[e].astype(full) + got[0].astype(full) + got[1].astype(full) + got[2].astype(full)
        )

    z_copies = []
    for number, (own, buffer, got) in enumerate(
        ((sg_own, z_wide.at[0], got_wide.at[0]), (su_own, z_wide.at[1], got_wide.at[1]), (sd_own, z_tall, got_tall))
    ):
        spread(own, buffer)
        z_copies.append(to_owners(buffer, got, number))
    def put(a, first_factor, second_factor):
        grads[a] = outer_sum(first_factor, second_factor).astype(low).reshape(2, 2, 2, width // 8, width)
        piece(a).start(1)

    put(3, attended[...], d_att[...])
    lane = lax.broadcasted_iota(jnp.int32, (rows, 128), 1)
    scale = HEAD_DIM**-0.5
    for total in (sum_q, sum_k, sum_v):
        total[...] = jnp.zeros_like(total)

    def inside(h, values):
        return jnp.where((lane // HEAD_DIM) == h, values, jnp.zeros_like(values))

    def columns(g):
        return pl.ds(pl.multiple_of(g * 128, 128), 128)

    def query_pair(g, carry):
        at = columns(g)
        q, d_out = q_all[c, :, at], d_all[c, :, at]
        sides = []
        for h in range(2):
            pick = lane == 2 * g + h
            sides.append(
                (
                    inside(h, q),
                    inside(h, d_out),
                    jnp.sum(jnp.where(pick, stat_col[0], 0.0), axis=-1, keepdims=True),
                    jnp.sum(jnp.where(pick, stat_col[1], 0.0), axis=-1, keepdims=True),
                )
            )
        for j in range(4):

            @pl.when(j <= c)
            def _(j=j):
                keys, values = k_all[j, :, at], v_all[j, :, at]
                terms = []
                for q_side, d_side, log_total, delta in sides:
                    weights = jnp.exp(against(q_side, keys) * scale - log_total)
                    d_scores = (weights * (against(d_side, values) - delta)).astype(low)
                    terms.append(jnp.dot(d_scores, keys, preferred_element_type=full))
                sum_q[:, at] += jnp.where(lane < HEAD_DIM, terms[0], terms[1])

        return carry

    lax.fori_loop(0, width // 128, query_pair, 0)

    def key_side(j):
        @pl.when(j >= c)
        def _():
            def key_pair(g, carry):
                at = columns(g)
                keys, values = k_all[c, :, at], v_all[c, :, at]
                q, d_out = q_all[j, :, at], d_all[j, :, at]
                terms = []
                for h in range(2):
                    log_total = stats[j, 0, pl.ds(2 * g + h, 1), :]
                    delta = stats[j, 1, pl.ds(2 * g + h, 1), :]
                    weights = jnp.exp(against(inside(h, keys), q) * scale - log_total)
                    d_scores = (weights * (against(inside(h, values), d_out) - delta)).astype(low)
                    terms.append(
                        (
                            jnp.dot(d_scores, q, preferred_element_type=full),
                            jnp.dot(weights.astype(low), d_out, preferred_element_type=full),
                        )
                    )
                sum_k[:, at] += jnp.where(lane < HEAD_DIM, terms[0][0], terms[1][0])
                sum_v[:, at] += jnp.where(lane < HEAD_DIM, terms[0][1], terms[1][1])
                return carry

            lax.fori_loop(0, width // 128, key_pair, 0)

    def turned_back(total):
        parts = []
        for g in range(width // 128):
            part = total[:, g * 128 : (g + 1) * 128] * scale
            parts.append((part * cosine[c] - swapped(part) * sine[c]).astype(low))
        return jnp.concatenate(parts, axis=1)

    key_side(c)
    d_query = turned_back(sum_q)
    put(0, normed[...], d_query)
    d_normed = against(d_query, w_q[...])
    piece(3).finish(1)
    piece(3).start(2)
    for copy in core_copies:
        copy.wait()
    key_side(x * 2 + (1 - k))
    for copy in x_copies:
        copy.wait()
    there = (1 - x) * 2 + k
    corner_copies = [
        start_copy(d_all.at[there], d_all.at[there], asem.at[2], arem.at[2], to_core),
        start_copy(stats.at[there], stats.at[there], tsem.at[2], trem.at[2], to_core),
    ]
    key_side(there)
    onward = []
    for a in range(3):
        for h in range(2):
            near[2 * a + h].wait()
            spot = block(a, h, (1 - s, s)[h], (x, 1 - x)[h])
            onward.append(start_copy(spot, spot, gsem.at[a, h, 2], grem.at[a, h, 2], (to_x, to_y)[h]))
    for copy in corner_copies:
        copy.wait()
    key_side((1 - x) * 2 + (1 - k))
    d_key = turned_back(sum_k)
    put(1, normed[...], d_key)
    d_value = sum_v[...].astype(low)
    put(2, normed[...], d_value)
    piece(0).finish(1)
    piece(0).start(2)
    d_normed = d_normed + against(d_key, w_k[...]) + against(d_value, w_v[...])
    values = tokens[...].astype(full)
    inverse = lax.rsqrt(jnp.mean(values * values, axis=-1, keepdims=True) + 1e-06)
    unit = values * inverse
    misc_in[0:8, :] = small[0:8, :]
    misc_in[8:9, :] = jnp.sum(d_normed * unit, axis=0, keepdims=True)
    misc_in[9:10, :] = small[8:9, :]
    misc_in[10:16, :] = jnp.zeros((6, width), full)
    misc_copy = start_copy(misc_in, misc_got.at[0], msem.at[0], mrem.at[0], to_core)
    for a in (1, 2):
        piece(a).finish(1)
        piece(a).start(2)
    inner = d_normed * gain_one[...]
    mean = jnp.mean(inner * unit, axis=-1, keepdims=True)
    token_out[...] = d_mixed[...] + inverse * (inner - unit * mean)
    misc_copy.wait()
    misc_out[...] = misc_in[...] + misc_got[0]
    misc_copy = start_copy(misc_out, misc_got.at[1], msem.at[1], mrem.at[1], to_x)
    for a in (3, 0, 1, 2):
        piece(a).finish(2)
        piece(a).start(3)
    misc_copy.wait()
    misc_got[3] = misc_out[...] + misc_got[1]
    misc_copy = start_copy(misc_got.at[3], misc_got.at[2], msem.at[2], mrem.at[2], to_y)
    flat_copies = {}
    for a in (3, 0, 1, 2):
        piece(a).finish(3)
        spread(three.at[a], z_flat.at[a])
        flat_copies[a] = to_owners(z_flat.at[a], got_flat.at[a], 3 + a)
    misc_copy.wait()
    misc_got[4] = misc_got[3] + misc_got[2]
    misc_copies = [
        start_copy(misc_got.at[4], misc_got.at[5 + i], msem.at[3 + i], mrem.at[3 + i], to_z[i]) for i in range(3)
    ]
    last = []
    for a, whole in enumerate((eg_all, eu_all, ed_all)):
        for h in range(2):
            kept[2 * a + h].wait()
            wide[2 * a + h].wait()
            onward[2 * a + h].wait()
        spot = whole.at[:, :, k] if a < 2 else whole.at[:, :, :, k]
        last.append(start_copy(spot, spot, gsem.at[a, 0, 3], grem.at[a, 0, 3], to_core))

    total = base[...]
    for i, owner in enumerate((e, *others)):
        share = jnp.sum(jnp.where(lane == owner, shares[...], 0.0), axis=-1, keepdims=True)
        if i == 0:
            rows_back = results[0]
        else:
            result_copies[i - 1].wait()
            rows_back = result_got[i - 1]
        total = total + share * rows_back.astype(full)
    output[...] = total.astype(low)

    settle(z_copies[0], z_wide.at[0], got_wide.at[0], sg_out)
    settle(z_copies[1], z_wide.at[1], got_wide.at[1], su_out)
    settle(z_copies[2], z_tall, got_tall, sd_out)
    for a, target in enumerate((q_out, k_out, v_out, o_out)):
        settle(flat_copies[a], z_flat.at[a], got_flat.at[a], target)
    for copy in misc_copies:
        copy.wait()
    misc_out[...] = misc_got[4] + misc_got[5] + misc_got[6] + misc_got[7]
    for copy in last:
        copy.wait()


def back(expert_own, shared_own, small, results, base, shares, tokens, gain_one, d_mixed, kept, weights):
    low, full = jnp.bfloat16, jnp.float32
    dma = pltpu.SemaphoreType.DMA
    rows, width = base.shape
    ninth = width // 8
    hidden = expert_own[0].shape[2]
    tiles, unused, short, unused = expert_own[2].shape
    tall = 2 * shared_own[2].shape[1]
    cosine, sine = (jnp.asarray(t).reshape(4, rows, 128) for t in place_tables(4 * rows))

    def vm(*shape, dtype=low):
        return pltpu.VMEM(shape, dtype)

    def out(*shape, dtype=low):
        return jax.ShapeDtypeStruct(shape, dtype)

    spec, anywhere = pl.BlockSpec(memory_space=pltpu.VMEM), pl.BlockSpec(memory_space=pl.ANY)
    out_shape = [
        out(2, 2, 2, ninth, hidden), out(2, 2, 2, ninth, hidden), out(tiles, 2, 2, 2, 2 * short, width),
        out(ninth, hidden // 4, dtype=full), out(ninth, hidden // 4, dtype=full), out(tall, width // 4, dtype=full),
        *[out(ninth, width // 4, dtype=full)] * 4, out(16, width, dtype=full), out(rows, width),
        out(rows, width, dtype=full),
    ]
    scratch = [
        vm(4, 2, 2, 2, ninth, width), vm(rows, width), vm(4, rows, width), vm(4, 2, 16, rows, dtype=full),
        vm(2, rows, 128, dtype=full), *[vm(rows, width, dtype=full)] * 3, vm(16, width, dtype=full),
        dma((3,)), dma((3,)), dma((3,)), dma((3,)),
        vm(4, 2, 2, ninth, width), vm(4, 2, 2, ninth // 2, width), vm(4, 2, ninth // 2, width),
        vm(4, 4, ninth, width // 4), vm(4, tall, width // 4), vm(2, 4, ninth, hidden // 4),
        vm(4, 3, ninth, width // 4), vm(3, tall, width // 4), vm(2, 3, ninth, hidden // 4),
        vm(8, 16, width, dtype=full), vm(3, rows, width),
        dma((3, 2)), dma((3, 2, 4)), dma((3, 2, 4)), dma((4, 5)), dma((4, 5)), dma((7, 3)), dma((7, 3)),
        dma((6,)), dma((6,)), dma((3,)), dma((3,)),
    ]
    operands = (
        *expert_own, *shared_own, small, results, base, shares, tokens, gain_one.reshape(1, width), d_mixed, *kept,
        *weights, cosine, sine,
    )
    return pl.pallas_call(
        back_kernel,
        out_shape=out_shape,
        in_specs=[spec] * len(operands),
        out_specs=[anywhere] * 3 + [spec] * 10,
        scratch_shapes=scratch,
        compiler_params=pltpu.CompilerParams(
            collective_id=4, has_side_effects=True, vmem_limit_bytes=60 * 2**20
        ),
        name="back",
    )(*operands)


def per_device_dense(
    tokens,
    expert_ids,
    norm_one,
    w_query,
    w_key,
    w_value,
    w_out,
    norm_two,
    w_router,
    expert_gate,
    expert_up,
    expert_down,
    shared_gate,
    shared_up,
    shared_down,
    cotangent,
):
    width = tokens.shape[2]
    ctx_count = lax.axis_size("ctx")
    ctx_place = lax.axis_index("ctx")
    exp_place = lax.axis_index("exp")
    row_groups = lax.axis_size("seq") * ctx_count
    upstream = cotangent[0]
    ids = expert_ids[0]
    experts = jnp.arange(128, dtype=jnp.int32)
    named = jnp.any(ids[:, :, None] == experts[None, None, :], axis=1)
    (
        q_all, k_all, v_all, upstream_all, named_all, normed, attended, mixed, second, log_sum,
    ) = front(
        tokens[0], upstream, named.astype(jnp.bfloat16), norm_one, norm_two, w_query, w_key, w_value, w_out
    )
    (
        results, shares, base, d_mixed, small, eg_own, eu_own, ed_own, sg_own, su_own, sd_own,
    ) = ffn(
        second, mixed, upstream_all, named_all, w_router, norm_two,
        (expert_gate[0], expert_up[0], expert_down[0]), (shared_gate, shared_up, shared_down),
    )

    (
        eg, eu, ed, sg, su, sd, gq, gk, gv, go, misc, output, grad_tokens,
    ) = back(
        (eg_own, eu_own, ed_own), (sg_own, su_own, sd_own), small, results, base, shares, tokens[0], norm_one, d_mixed,
        (attended, normed, q_all, k_all, v_all, log_sum), (w_query, w_key, w_value, w_out),
    )
    row_place = lax.axis_index("seq") * ctx_count + ctx_place
    own_rows = width // row_groups
    router = lax.dynamic_slice(misc, (exp_place, row_place * own_rows), (1, own_rows))
    return (
        output[None],
        grad_tokens[None],
        misc[8],
        gq,
        gk,
        gv,
        go,
        misc[9],
        router.T,
        eg.astype(jnp.float32).reshape(expert_gate.shape),
        eu.astype(jnp.float32).reshape(expert_up.shape),
        ed.astype(jnp.float32).reshape(expert_down.shape),
        sg,
        su,
        sd,
    )


def fits(mesh):
    return dict(mesh.shape) == {"seq": 2, "ctx": 4, "exp": 4}


def solution(mesh):
    per_device = per_device_dense if fits(mesh) else per_device_slots
    in_specs = (
        P(("seq", "exp"), "ctx", None),
        P(("seq", "exp"), "ctx", None),
        P(),
        P(),
        P(),
        P(),
        P(),
        P(),
        P(),
        P("exp", None, None),
        P("exp", None, None),
        P("exp", None, None),
        P(),
        P(),
        P(),
        P(("seq", "exp"), "ctx", None),
    )
    out_specs = (
        P(("seq", "exp"), "ctx", None),
        P(("seq", "exp"), "ctx", None),
        P(),
        P(("seq", "ctx"), "exp"),
        P(("seq", "ctx"), "exp"),
        P(("seq", "ctx"), "exp"),
        P(("seq", "ctx"), "exp"),
        P(),
        P(("seq", "ctx"), "exp"),
        P("exp", None, None),
        P("exp", None, None),
        P("exp", None, None),
        P(("seq", "ctx"), "exp"),
        P(("seq", "ctx"), "exp"),
        P(("seq", "ctx"), "exp"),
    )
    return jax.shard_map(
        per_device, mesh=mesh, in_specs=in_specs, out_specs=out_specs, check_vma=False
    )
```

```python
import functools
import math

import jax
import jax.numpy as jnp
import numpy as np
from jax import lax
from jax.experimental import pallas as pl
from jax.experimental.pallas import tpu as pltpu
from jax.sharding import PartitionSpec as P

HEAD_DIM = 64
TOP = 2
BLOCK = 256
KEY_ROWS = 512
MESH = pl.DeviceIdType.MESH


def product(first_factor, second_factor):
    return jnp.dot(first_factor, second_factor, preferred_element_type=jnp.float32)


def against(first_factor, second_factor):
    return lax.dot_general(
        first_factor, second_factor, (((1,), (1,)), ((), ())), preferred_element_type=jnp.float32
    )


def outer_sum(first_factor, second_factor):
    return lax.dot_general(
        first_factor, second_factor, (((0,), (0,)), ((), ())), preferred_element_type=jnp.float32
    )


def normalize(values, scaling):
    return values * lax.rsqrt(jnp.mean(values * values, axis=-1, keepdims=True) + 1e-06) * scaling


def rotate(values, places):
    halfway = values.shape[-1] // 2
    frequency = 10000.0 ** (-jnp.arange(halfway, dtype=jnp.float32) / halfway)
    angles = places.astype(jnp.float32)[:, None] * frequency[None, :]
    cosine = jnp.cos(angles)[:, None, :]
    sine_part = jnp.sin(angles)[:, None, :]
    former = values[..., :halfway]
    latter = values[..., halfway:]
    return jnp.concatenate(
        [former * cosine - latter * sine_part, latter * cosine + former * sine_part], axis=-1
    )


def silu_parts(gate_pre):
    sigmoid_value = jax.nn.sigmoid(gate_pre)
    return (gate_pre * sigmoid_value, sigmoid_value * (1.0 + gate_pre * (1.0 - sigmoid_value)))


def tiled(matrix, row_groups, col_groups):
    row_count, col_count = matrix.shape
    blocks = matrix.reshape(
        row_groups, row_count // row_groups, col_groups, col_count // col_groups
    ).transpose(0, 2, 1, 3)
    return blocks.reshape(col_groups * row_count, col_count // col_groups)


def per_device_slots(
    tokens,
    expert_ids,
    norm_one,
    w_query,
    w_key,
    w_value,
    w_out,
    norm_two,
    w_router,
    expert_gate,
    expert_up,
    expert_down,
    shared_gate,
    shared_up,
    shared_down,
    cotangent,
):
    local_rows = tokens.shape[1]
    model_width = tokens.shape[2]
    head_count = model_width // HEAD_DIM
    score_scale = HEAD_DIM ** (-0.5)
    ctx_count = lax.axis_size("ctx")
    ctx_place = lax.axis_index("ctx")
    exp_count = lax.axis_size("exp")
    row_groups = lax.axis_size("seq") * ctx_count
    local_experts = expert_gate.shape[0]
    experts_all = local_experts * exp_count
    capacity = min(local_rows, 2 * TOP * local_rows // experts_all)
    places = ctx_place * local_rows + jnp.arange(local_rows, dtype=jnp.int32)
    query_blocks = places // BLOCK

    def spread(matrix):
        return tiled(matrix, row_groups, exp_count)

    inputs = tokens[0].astype(jnp.float32)
    normed_full, norm_one_pull = jax.vjp(normalize, inputs, norm_one)
    normed = normed_full.astype(jnp.bfloat16)
    query = rotate(
        product(normed, w_query).reshape(local_rows, head_count, HEAD_DIM), places
    ).astype(jnp.bfloat16)
    keys_local = (
        rotate(product(normed, w_key).reshape(local_rows, head_count, HEAD_DIM), places)
        .astype(jnp.bfloat16)
        .reshape(local_rows, model_width)
    )
    values_local = product(normed, w_value).astype(jnp.bfloat16)

    def block_scores(key_block, offset):
        key_heads = key_block.reshape(-1, head_count, HEAD_DIM)
        scores = (
            jnp.einsum("qhd,khd->hqk", query, key_heads, preferred_element_type=jnp.float32)
            * score_scale
        )
        key_index = (offset + jnp.arange(key_block.shape[0], dtype=jnp.int32)) // BLOCK
        allowed = key_index[None, :] <= query_blocks[:, None]
        return (scores, allowed)

    def attend_block(running, key_block, value_block, offset):
        highest, totals, accumulated = running
        scores, allowed = block_scores(key_block, offset)
        masked = jnp.where(allowed[None], scores, -1e30)
        fresh = jnp.maximum(highest, jnp.max(masked, axis=-1))
        weights = jnp.where(allowed[None], jnp.exp(masked - fresh[..., None]), 0.0)
        decay = jnp.exp(highest - fresh)
        value_heads = value_block.reshape(-1, head_count, HEAD_DIM)
        accumulated = accumulated * decay[..., None] + jnp.einsum(
            "hqk,khd->hqd",
            weights.astype(jnp.bfloat16),
            value_heads,
            preferred_element_type=jnp.float32,
        )
        return (fresh, totals * decay + jnp.sum(weights, axis=-1), accumulated)

    start_state = (
        jnp.full((head_count, local_rows), -1e30, jnp.float32),
        jnp.zeros((head_count, local_rows), jnp.float32),
        jnp.zeros((head_count, local_rows, HEAD_DIM), jnp.float32),
    )
    running = start_state
    key_part = lax.all_gather(keys_local, "ctx", axis=0, tiled=True)
    value_part = lax.all_gather(values_local, "ctx", axis=0, tiled=True)
    span_rows = key_part.shape[0]
    stride = math.gcd(span_rows, KEY_ROWS)
    step_count = span_rows // stride
    key_steps = key_part.reshape(step_count, stride, model_width)
    value_steps = value_part.reshape(step_count, stride, model_width)
    offsets = jnp.arange(step_count, dtype=jnp.int32) * stride

    def one_step(inner, operands):
        return (attend_block(inner, operands[0], operands[1], operands[2]), None)

    running, unused = lax.scan(one_step, running, (key_steps, value_steps, offsets))
    highest, totals, accumulated = running
    log_total = highest + jnp.log(totals)
    attended = (
        (accumulated / totals[..., None])
        .transpose(1, 0, 2)
        .reshape(local_rows, model_width)
        .astype(jnp.bfloat16)
    )
    mixed = inputs + product(attended, w_out)
    second_full, norm_two_pull = jax.vjp(normalize, mixed, norm_two)
    second = second_full.astype(jnp.bfloat16)
    logits = product(second, w_router)
    chosen = expert_ids[0]
    one_hot = (
        chosen[:, :, None] == jnp.arange(experts_all, dtype=jnp.int32)[None, None, :]
    ).astype(jnp.float32)
    selected = jnp.sum(logits[:, None, :] * one_hot, axis=-1)
    gates = jax.nn.softmax(selected, axis=-1)
    flat_ids = chosen.reshape(-1)
    slot_hits = (flat_ids[:, None] == jnp.arange(experts_all, dtype=jnp.int32)[None, :]).astype(
        jnp.int32
    )
    order = jnp.arange(flat_ids.shape[0], dtype=jnp.int32)
    earlier = (order[None, :] < order[:, None]).astype(jnp.bfloat16)
    counts_before = product(earlier, slot_hits.astype(jnp.bfloat16)).astype(jnp.int32)
    slot_place = jnp.sum(counts_before * slot_hits, axis=1)

    def to_slots(routed_rows):
        empty_slots = jnp.zeros((experts_all, capacity, model_width), jnp.bfloat16)
        return (
            empty_slots.at[flat_ids, slot_place]
            .set(routed_rows)
            .reshape(exp_count, local_experts, capacity, model_width)
        )

    def from_slots(arrived_back):
        picked = arrived_back.reshape(experts_all, capacity, model_width)[flat_ids, slot_place]
        return picked.astype(jnp.float32).reshape(local_rows, TOP, model_width)

    def expert_front(arrived_rows):
        gate_pre = jnp.einsum(
            "sjcd,jdf->sjcf", arrived_rows, expert_gate, preferred_element_type=jnp.float32
        )
        up_pre = jnp.einsum(
            "sjcd,jdf->sjcf", arrived_rows, expert_up, preferred_element_type=jnp.float32
        )
        hidden = (jax.nn.silu(gate_pre) * up_pre).astype(jnp.bfloat16)
        return (gate_pre, up_pre, hidden)

    send_rows = to_slots(jnp.repeat(second, TOP, axis=0))
    arrived = lax.all_to_all(send_rows, "exp", split_axis=0, concat_axis=0, tiled=True)
    gate_pre, up_pre, hidden = expert_front(arrived)
    results = jnp.einsum(
        "sjcf,jfd->sjcd", hidden, expert_down, preferred_element_type=jnp.float32
    ).astype(jnp.bfloat16)
    returned = lax.all_to_all(results, "exp", split_axis=0, concat_axis=0, tiled=True)
    expert_out = from_slots(returned)
    mixture = jnp.sum(gates[:, :, None] * expert_out, axis=1)
    shared_gate_pre = product(second, shared_gate)
    shared_up_pre = product(second, shared_up)
    shared_hidden = (jax.nn.silu(shared_gate_pre) * shared_up_pre).astype(jnp.bfloat16)
    output = (mixed + mixture + product(shared_hidden, shared_down)).astype(jnp.bfloat16)
    upstream = cotangent[0]
    upstream_full = upstream.astype(jnp.float32)
    grad_shared_down = outer_sum(shared_hidden, upstream)
    d_shared_hidden = against(upstream, shared_down)
    shared_silu, shared_slope = silu_parts(shared_gate_pre)
    d_shared_gate = (d_shared_hidden * shared_up_pre * shared_slope).astype(jnp.bfloat16)
    d_shared_up = (d_shared_hidden * shared_silu).astype(jnp.bfloat16)
    grad_shared_gate = outer_sum(second, d_shared_gate)
    grad_shared_up = outer_sum(second, d_shared_up)
    d_second = against(d_shared_gate, shared_gate) + against(d_shared_up, shared_up)
    d_gates = jnp.sum(upstream_full[:, None, :] * expert_out, axis=-1)
    d_selected = gates * (d_gates - jnp.sum(gates * d_gates, axis=-1, keepdims=True))
    d_logits = jnp.sum(d_selected[:, :, None] * one_hot, axis=1).astype(jnp.bfloat16)
    grad_router = outer_sum(second, d_logits)
    d_second = d_second + against(d_logits, w_router)
    grad_slots = to_slots(
        (gates[:, :, None] * upstream_full[:, None, :])
        .astype(jnp.bfloat16)
        .reshape(local_rows * TOP, model_width)
    )
    arrived_rows, arrived_grad = (
        lax.all_to_all(send_rows, "exp", split_axis=0, concat_axis=0, tiled=True),
        lax.all_to_all(grad_slots, "exp", split_axis=0, concat_axis=0, tiled=True),
    )
    gate_kept, up_kept, hidden_kept = expert_front(arrived_rows)
    d_hidden = jnp.einsum(
        "sjcd,jfd->sjcf", arrived_grad, expert_down, preferred_element_type=jnp.float32
    )
    expert_silu, expert_slope = silu_parts(gate_kept)
    d_gate_pre = (d_hidden * up_kept * expert_slope).astype(jnp.bfloat16)
    d_up_pre = (d_hidden * expert_silu).astype(jnp.bfloat16)
    grad_expert_down = jnp.einsum(
        "sjcf,sjcd->jfd", hidden_kept, arrived_grad, preferred_element_type=jnp.float32
    )
    grad_expert_gate = jnp.einsum(
        "sjcd,sjcf->jdf", arrived_rows, d_gate_pre, preferred_element_type=jnp.float32
    )
    grad_expert_up = jnp.einsum(
        "sjcd,sjcf->jdf", arrived_rows, d_up_pre, preferred_element_type=jnp.float32
    )
    d_routed = (
        jnp.einsum("sjcf,jdf->sjcd", d_gate_pre, expert_gate, preferred_element_type=jnp.float32)
        + jnp.einsum("sjcf,jdf->sjcd", d_up_pre, expert_up, preferred_element_type=jnp.float32)
    ).astype(jnp.bfloat16)
    returned_grad = lax.all_to_all(d_routed, "exp", split_axis=0, concat_axis=0, tiled=True)
    d_second = d_second + jnp.sum(from_slots(returned_grad), axis=1)
    grad_expert_gate, grad_expert_up, grad_expert_down = (
        lax.psum(grad_expert_gate.astype(jnp.bfloat16), ("seq", "ctx")).astype(jnp.float32),
        lax.psum(grad_expert_up.astype(jnp.bfloat16), ("seq", "ctx")).astype(jnp.float32),
        lax.psum(grad_expert_down.astype(jnp.bfloat16), ("seq", "ctx")).astype(jnp.float32),
    )
    d_mixed_part, grad_norm_two = norm_two_pull(d_second)
    d_mixed = upstream_full + d_mixed_part
    d_attention = d_mixed.astype(jnp.bfloat16)
    grad_out = outer_sum(attended, d_attention)
    grad_heads = (
        against(d_attention, w_out).astype(jnp.bfloat16).reshape(local_rows, head_count, HEAD_DIM)
    )
    keys_all, values_all = (
        lax.all_gather(keys_local, "ctx", axis=0, tiled=True),
        lax.all_gather(values_local, "ctx", axis=0, tiled=True),
    )
    block_total = ((ctx_place + 1) * local_rows + KEY_ROWS - 1) // KEY_ROWS

    def weights_at(number):
        offset = number * KEY_ROWS
        key_block = lax.dynamic_slice_in_dim(keys_all, offset, KEY_ROWS, 0)
        value_block = lax.dynamic_slice_in_dim(values_all, offset, KEY_ROWS, 0)
        scores, allowed = block_scores(key_block, offset)
        weights = jnp.where(allowed[None], jnp.exp(scores - log_total[..., None]), 0.0)
        grad_weights = jnp.einsum(
            "qhd,khd->hqk",
            grad_heads,
            value_block.reshape(KEY_ROWS, head_count, HEAD_DIM),
            preferred_element_type=jnp.float32,
        )
        return (key_block, weights, grad_weights)

    def row_dot_step(number, summed):
        unused_block, weights, grad_weights = weights_at(number)
        return summed + jnp.sum(weights * grad_weights, axis=-1)

    row_dots = lax.fori_loop(
        0, block_total, row_dot_step, jnp.zeros((head_count, local_rows), jnp.float32)
    )

    def score_grads(number):
        key_block, weights, grad_weights = weights_at(number)
        d_scores = (weights * (grad_weights - row_dots[..., None])).astype(jnp.bfloat16)
        return (key_block.reshape(KEY_ROWS, head_count, HEAD_DIM), weights, d_scores)

    query_start = jnp.zeros((local_rows, head_count, HEAD_DIM), jnp.float32)

    def grad_step(number, running):
        grad_query, key_terms = running
        key_heads, weights, d_scores = score_grads(number)
        grad_query = (
            grad_query
            + jnp.einsum("hqk,khd->qhd", d_scores, key_heads, preferred_element_type=jnp.float32)
            * score_scale
        )
        key_part = (
            jnp.einsum("hqk,qhd->khd", d_scores, query, preferred_element_type=jnp.float32)
            * score_scale
        )
        value_part = jnp.einsum(
            "hqk,qhd->khd",
            weights.astype(jnp.bfloat16),
            grad_heads,
            preferred_element_type=jnp.float32,
        )
        block_terms = jnp.concatenate(
            [key_part.reshape(KEY_ROWS, model_width), value_part.reshape(KEY_ROWS, model_width)],
            axis=1,
        )
        return (
            grad_query,
            lax.dynamic_update_slice_in_dim(key_terms, block_terms, number * KEY_ROWS, 0),
        )

    grad_query_heads, key_terms = lax.fori_loop(
        0,
        block_total,
        grad_step,
        (query_start, jnp.zeros((ctx_count * local_rows, 2 * model_width), jnp.float32)),
    )
    key_grads = lax.psum_scatter(
        key_terms.astype(jnp.bfloat16), "ctx", scatter_dimension=0, tiled=True
    ).astype(jnp.float32)
    key_grad_heads = key_grads[:, :model_width].reshape(local_rows, head_count, HEAD_DIM)
    d_value = key_grads[:, model_width:].astype(jnp.bfloat16)
    d_query_lin = (
        rotate(grad_query_heads, -places).astype(jnp.bfloat16).reshape(local_rows, model_width)
    )
    d_key_lin = (
        rotate(key_grad_heads, -places).astype(jnp.bfloat16).reshape(local_rows, model_width)
    )
    grad_query = outer_sum(normed, d_query_lin)
    grad_key = outer_sum(normed, d_key_lin)
    grad_value = outer_sum(normed, d_value)
    d_normed = against(d_query_lin, w_query) + against(d_key_lin, w_key) + against(d_value, w_value)
    d_inputs, grad_norm_one = norm_one_pull(d_normed)
    grad_tokens = (d_mixed + d_inputs)[None]
    (
        grad_query,
        grad_key,
        grad_value,
        grad_out,
        grad_router,
        grad_shared_gate,
        grad_shared_up,
        grad_shared_down,
    ) = (
        lax.psum_scatter(
            spread(grad_query), ("seq", "ctx", "exp"), scatter_dimension=0, tiled=True
        ),
        lax.psum_scatter(spread(grad_key), ("seq", "ctx", "exp"), scatter_dimension=0, tiled=True),
        lax.psum_scatter(
            spread(grad_value), ("seq", "ctx", "exp"), scatter_dimension=0, tiled=True
        ),
        lax.psum_scatter(spread(grad_out), ("seq", "ctx", "exp"), scatter_dimension=0, tiled=True),
        lax.psum_scatter(
            spread(grad_router), ("seq", "ctx", "exp"), scatter_dimension=0, tiled=True
        ),
        lax.psum_scatter(
            spread(grad_shared_gate), ("seq", "ctx", "exp"), scatter_dimension=0, tiled=True
        ),
        lax.psum_scatter(
            spread(grad_shared_up), ("seq", "ctx", "exp"), scatter_dimension=0, tiled=True
        ),
        lax.psum_scatter(
            spread(grad_shared_down), ("seq", "ctx", "exp"), scatter_dimension=0, tiled=True
        ),
    )
    grad_norm_one, grad_norm_two = lax.psum((grad_norm_one, grad_norm_two), ("seq", "ctx", "exp"))
    return (
        output[None],
        grad_tokens,
        grad_norm_one,
        grad_query,
        grad_key,
        grad_value,
        grad_out,
        grad_norm_two,
        grad_router,
        grad_expert_gate,
        grad_expert_up,
        grad_expert_down,
        grad_shared_gate,
        grad_shared_up,
        grad_shared_down,
    )


def place_tables(length):
    half = HEAD_DIM // 2
    frequency = np.float32(10000.0) ** (-np.arange(half, dtype=np.float32) / np.float32(half))
    angles = np.arange(length, dtype=np.float32)[:, None] * frequency[None, :].astype(np.float32)
    cosine, sine = np.cos(angles), np.sin(angles)
    return (
        np.concatenate([cosine] * 4, axis=1).astype(np.float32),
        np.concatenate([-sine, sine, -sine, sine], axis=1).astype(np.float32),
    )


def swapped(values):
    half = HEAD_DIM // 2
    lane = lax.broadcasted_iota(jnp.int32, values.shape, 1) % HEAD_DIM
    return jnp.where(lane < half, pltpu.roll(values, 128 - half, 1), pltpu.roll(values, half, 1))


def start_copy(src, dst, ssem, rsem, device):
    copy = pltpu.make_async_remote_copy(
        src_ref=src, dst_ref=dst, send_sem=ssem, recv_sem=rsem, device_id=device, device_id_type=MESH
    )
    copy.start()
    return copy


def greet(devices):
    barrier = pltpu.get_barrier_semaphore()
    for device in devices:
        pl.semaphore_signal(barrier, inc=1, device_id=device, device_id_type=MESH)
    pl.semaphore_wait(barrier, len(devices))


def neighbours():
    s = lax.axis_index("seq")
    c = lax.axis_index("ctx")
    e = lax.axis_index("exp")
    x, k = c // 2, c % 2
    to_core = (s, x * 2 + (1 - k), e)
    to_x = (s, (1 - x) * 2 + k, e)
    to_y = (1 - s, c, e)
    near = e + 1 - 2 * (e % 2)
    far = lax.rem(e + 2, 4)
    opposite = 3 - e
    return s, x, k, e, c, to_core, to_x, to_y, (near, far, opposite)


def named_lanes(rows_named):
    marks = rows_named.astype(jnp.float32)
    return jnp.concatenate([marks, jnp.zeros((112, marks.shape[1]), jnp.float32)], axis=0).T > 0.5


def front_kernel(
    tokens, upstream, ids, gain_one, gain_two, w_q, w_k, w_v, w_o, cosine, sine,
    q_all, k_all, v_all, upstream_all, named_all, normed_out, attended_out, mixed_out, second_out, logsum_out,
    block, tsem, trem, usem, urem, nsem, nrem,
):
    s, x, k, e, c, to_core, to_x, to_y, others = neighbours()
    rows, width = tokens.shape
    greet([to_core, to_x, (s, c, others[0]), (s, c, others[1])])
    block[c] = tokens[...]
    upstream_all[0] = upstream[...]
    lane = lax.broadcasted_iota(jnp.int32, (rows, 128), 1)
    marks = jnp.where((lane == ids[:, 0:1]) | (lane == ids[:, 1:2]), 1.0, 0.0)
    named_all[0] = marks.T[0:16, :].astype(jnp.bfloat16)
    core_copy = start_copy(tokens, block.at[c], tsem.at[0], trem.at[0], to_core)
    x_copy = start_copy(tokens, block.at[c], tsem.at[1], trem.at[1], to_x)
    to_near, to_far = (s, c, others[0]), (s, c, others[1])

    def over_z(i, source, device):
        return [
            start_copy(upstream_all.at[source], upstream_all.at[i + 1], usem.at[i], urem.at[i], device),
            start_copy(named_all.at[source], named_all.at[i + 1], nsem.at[i], nrem.at[i], device),
        ]

    near_copies = over_z(0, 0, to_near)
    far_copies = over_z(1, 0, to_far)

    one = gain_one[...].reshape(1, width)

    def project(j):
        values = block[j].astype(jnp.float32)
        inverse = lax.rsqrt(jnp.mean(values * values, axis=-1, keepdims=True) + 1e-06)
        normed = (values * inverse * one).astype(jnp.bfloat16)
        for weight, out in ((w_q, q_all), (w_k, k_all)):
            lin = jnp.dot(normed, weight[...], preferred_element_type=jnp.float32)
            for g in range(width // 128):
                part = lin[:, g * 128 : (g + 1) * 128]
                turned = part * cosine[j] + swapped(part) * sine[j]
                out[j, :, g * 128 : (g + 1) * 128] = turned.astype(jnp.bfloat16)
        v_all[j] = jnp.dot(normed, w_v[...], preferred_element_type=jnp.float32).astype(jnp.bfloat16)
        return normed

    normed_out[...] = project(c)
    core_copy.wait()
    project(x * 2 + (1 - k))
    x_copy.wait()
    there = (1 - x) * 2 + k
    corner_copy = start_copy(block.at[there], block.at[there], tsem.at[2], trem.at[2], to_core)
    project(there)
    corner_copy.wait()
    project((1 - x) * 2 + (1 - k))

    span = 4 * rows
    hidden_keys = lax.broadcasted_iota(jnp.int32, (1, span), 1) // rows > c
    bias = jnp.where(hidden_keys, -1e30, 0.0)
    logsum_out[...] = jnp.zeros_like(logsum_out)

    def pair(g, carry):
        at = pl.ds(pl.multiple_of(g * 128, 128), 128)
        q = q_all[c, :, at]
        keys = k_all[:, :, at].reshape(span, 128)
        values = v_all[:, :, at].reshape(span, 128)
        out = jnp.zeros((rows, 128), jnp.float32)
        for h in range(2):
            inside = (lane // HEAD_DIM) == h
            scores = lax.dot_general(
                jnp.where(inside, q, jnp.zeros_like(q)), keys, (((1,), (1,)), ((), ())),
                preferred_element_type=jnp.float32,
            )
            scores = scores * (HEAD_DIM**-0.5) + bias
            highest = jnp.max(scores, axis=-1, keepdims=True)
            raised = jnp.exp(scores - highest)
            total = jnp.sum(raised, axis=-1, keepdims=True)
            mixed = jnp.dot(raised.astype(jnp.bfloat16), values, preferred_element_type=jnp.float32)
            out = jnp.where(inside, mixed / total, out)
            logsum_out[...] = jnp.where(lane == 2 * g + h, highest + jnp.log(total), logsum_out[...])
        attended_out[:, at] = out.astype(jnp.bfloat16)
        return carry

    lax.fori_loop(0, width // 128, pair, 0)
    mixed = tokens[...].astype(jnp.float32) + jnp.dot(
        attended_out[...], w_o[...], preferred_element_type=jnp.float32
    )
    mixed_out[...] = mixed
    inverse = lax.rsqrt(jnp.mean(mixed * mixed, axis=-1, keepdims=True) + 1e-06)
    second_out[...] = (mixed * inverse * gain_two[...].reshape(1, width)).astype(jnp.bfloat16)
    for copy in (*near_copies, *far_copies):
        copy.wait()


def front(tokens, upstream, ids, gain_one, gain_two, w_q, w_k, w_v, w_o):
    rows, width = tokens.shape
    cosine, sine = (jnp.asarray(t).reshape(4, rows, 128) for t in place_tables(4 * rows))
    low, full = jnp.bfloat16, jnp.float32
    vmem, dma = pltpu.VMEM, pltpu.SemaphoreType.DMA
    every, three = (jax.ShapeDtypeStruct((n, rows, width), low) for n in (4, 3))
    own = jax.ShapeDtypeStruct((rows, width), low)
    spec = pl.BlockSpec(memory_space=pltpu.VMEM)
    out_shape = [
        every, every, every, three, jax.ShapeDtypeStruct((3, 16, rows), low), own, own,
        jax.ShapeDtypeStruct((rows, width), full), own, jax.ShapeDtypeStruct((rows, 128), full),
    ]
    return pl.pallas_call(
        front_kernel,
        out_shape=out_shape,
        in_specs=[spec] * 11,
        out_specs=[spec] * 10,
        scratch_shapes=[vmem((4, rows, width), low), *[dma((3,))] * 2, *[dma((2,))] * 4],
        compiler_params=pltpu.CompilerParams(
            collective_id=2, has_side_effects=True, vmem_limit_bytes=58 * 2**20
        ),
        name="front",
    )(tokens, upstream, ids, gain_one, gain_two, w_q, w_k, w_v, w_o, cosine, sine)


def add_rows(target, first, second, step):
    rows = target.shape[0]

    def some(at):
        total = first[at, :].astype(jnp.float32) + second[at, :].astype(jnp.float32)
        target[at, :] = total.astype(target.dtype)

    if rows <= step:
        some(pl.ds(0, rows))
    else:

        def body(i, carry):
            some(pl.ds(pl.multiple_of(i * step, step), step))
            return carry

        lax.fori_loop(0, rows // step, body, 0)


class Piece:
    def __init__(self, place, whole, one, two, three, half, sems, step):
        self.s, self.x, self.k, self.to_core, self.to_x, self.to_y = place
        self.whole, self.one, self.two, self.three = whole, one, two, three
        self.half, self.sems, self.step = half, sems, step

    def copy(self, level, h=0):
        every, low, high = slice(None), pl.ds(0, self.half), pl.ds(self.half, self.half)
        if level == 1:
            src, dst, device = self.whole(1 - self.k), self.one(every, every, every), self.to_core
        elif level == 2:
            if h == 0:
                src, device = self.one(every, 1 - self.x, low), self.to_x
            else:
                src, device = self.one(1 - self.s, every, high), self.to_y
            dst = self.two(h, every)
        else:
            src = self.two(h, 1 - (self.s, self.x)[h])
            dst, device = self.three(h), (self.to_y, self.to_x)[h]
        ssem, rsem = self.sems(2 * (level - 1) - (1 if level > 1 else 0) + h)
        return pltpu.make_async_remote_copy(
            src_ref=src, dst_ref=dst, send_sem=ssem, recv_sem=rsem, device_id=device, device_id_type=MESH
        )

    def start(self, level):
        for h in range(1 if level == 1 else 2):
            self.copy(level, h).start()

    def finish(self, level):
        low, high = pl.ds(0, self.half), pl.ds(self.half, self.half)
        if level == 1:
            self.copy(1).wait()
            own = self.whole(self.k)
            for i in range(2):
                for j in range(2):
                    here = self.one(i, j, slice(None))
                    add_rows(here, here, own.at[i, j], self.step)
            return
        for h in range(2):
            self.copy(level, h).wait()
            if level == 2:
                for i in range(2):
                    here = self.two(h, i)
                    own = self.one(i, self.x, low) if h == 0 else self.one(self.s, i, high)
                    add_rows(here, here, own, self.step)
            else:
                here = self.three(h)
                add_rows(here, here, self.two(h, (self.s, self.x)[h]), self.step)


def gates_in(logits, named):
    masked = jnp.where(named, logits, -1e30)
    raised = jnp.where(named, jnp.exp(masked - jnp.max(masked, axis=-1, keepdims=True)), 0.0)
    return raised / jnp.sum(raised, axis=-1, keepdims=True)


def ffn_kernel(
    second, mixed, upstream_all, named_all, w_r, gain_two,
    e_gate, e_up, e_down, s_gate, s_up, s_down,
    results, d_mixed_out, small_out, eg_out, eu_out, ed_out, sg_out, su_out, sd_out,
    rows_all, last_up, last_named, d_res, res_acc, mix_acc, row_acc, row_send, row_got, dg_send, dg_got,
    router_w, own_shares, across, we_g, we_u, we_d, ws_g, ws_u, ws_d, wsem,
    ge_g, ge_u, ge_d, e1_g, e1_u, e1_d, e2_g, e2_u, e2_d,
    gs_g, gs_u, gs_d, s1_g, s1_u, s1_d, s2_g, s2_u, s2_d, s3_g, s3_u, s3_d, sd_got,
    es_sem, er_sem, ss_sem, sr_sem, xs_sem, xr_sem, us_sem, ur_sem, rs_sem, rr_sem, ds_sem, dr_sem, hs_sem, hr_sem,
):
    s, x, k, e, c, to_core, to_x, to_y, others = neighbours()
    place = (s, x, k, to_core, to_x, to_y)
    rows, width = second.shape
    tile = 8 * ge_d.shape[4]
    tiles, shared_tiles = e_gate.shape[1] // tile, gs_g.shape[4] // tile
    low, full = jnp.bfloat16, jnp.float32
    to_z = [(s, c, o) for o in others]
    owner_row, giver_row = 2 * e + s, 4 * s + c
    to_owner, giver = (owner_row // 4, owner_row % 4, c), (giver_row % 2, e, giver_row // 2)
    elsewhere = jnp.where((owner_row == giver_row) & (c == e), 0, 1)

    def columns(f):
        return pl.ds(pl.multiple_of(f * tile, tile), tile)

    def fetches(f, shared):
        at = columns(f)
        if shared:
            sources, here, targets, n = (s_gate, s_up, s_down), columns(e * shared_tiles + f), (ws_g, ws_u, ws_d), f
        else:
            sources, here, targets, n = (e_gate, e_up, e_down), at, (we_g, we_u, we_d), shared_tiles + f
        return [
            pltpu.make_async_copy(sources[0].at[:, here], targets[0].at[:, at], wsem.at[n, 0]),
            pltpu.make_async_copy(sources[1].at[:, here], targets[1].at[:, at], wsem.at[n, 1]),
            pltpu.make_async_copy(sources[2].at[here, :], targets[2].at[at, :], wsem.at[n, 2]),
        ]

    for n in range(shared_tiles):
        for copy in fetches(n, True):
            copy.start()
    for n in range(tiles):
        for copy in fetches(n, False):
            copy.start()
    barrier = pltpu.get_barrier_semaphore()
    for device in (to_core, to_x, to_y, *to_z):
        pl.semaphore_signal(barrier, inc=1, device_id=device, device_id_type=MESH)

    @pl.when(elsewhere == 1)
    def _():
        for device in (to_owner, giver):
            pl.semaphore_signal(barrier, inc=1, device_id=device, device_id_type=MESH)

    pl.semaphore_wait(barrier, 6 + 2 * elsewhere)
    near_copy = start_copy(second, rows_all.at[1], xs_sem.at[0], xr_sem.at[0], to_z[0])
    far_copy = start_copy(second, rows_all.at[2], xs_sem.at[1], xr_sem.at[1], to_z[1])
    rows_all[0] = second[...]
    router_w[...] = jnp.zeros_like(router_w)
    router_w[:, 0 : w_r.shape[1]] = w_r[...]

    def piece_e(f, a):
        at = columns(f)
        sems = lambda n: (es_sem.at[f, a, n], er_sem.at[f, a, n])
        if a < 2:
            g, one, two, three = ((ge_g, e1_g, e2_g, eg_out), (ge_u, e1_u, e2_u, eu_out))[a]
            return Piece(
                place,
                lambda kk: g.at[:, :, kk, :, at],
                lambda i, j, r: one.at[i, j, r, at],
                lambda h, i: two.at[h, i, :, at],
                lambda h: three.at[h, :, at],
                g.shape[3] // 2, sems, 96,
            )
        return Piece(
            place,
            lambda kk: ge_d.at[f, :, :, kk],
            lambda i, j, r: e1_d.at[f, i, j, r],
            lambda h, i: e2_d.at[f, h, i],
            lambda h: ed_out.at[f, h],
            ge_d.shape[4] // 2, sems, 96,
        )

    def piece_s(a):
        g, one, two, three = (
            (gs_g, s1_g, s2_g, s3_g), (gs_u, s1_u, s2_u, s3_u), (gs_d, s1_d, s2_d, s3_d)
        )[a]
        return Piece(
            place,
            lambda kk: g.at[:, :, kk],
            lambda i, j, r: one.at[i, j, r],
            lambda h, i: two.at[h, i],
            lambda h: three.at[h],
            g.shape[3] // 2, lambda n: (ss_sem.at[a, n], sr_sem.at[a, n]), 48 if a < 2 else 64,
        )

    def branch(values, d_out, weights, f, result_acc, d_acc):
        at = columns(f)
        gate_w, up_w, down_w = weights[0][:, at], weights[1][:, at], weights[2][at, :]
        gate = jnp.dot(values, gate_w, preferred_element_type=full)
        up = jnp.dot(values, up_w, preferred_element_type=full)
        d_hidden = against(d_out, down_w)
        sigmoid = 1.0 / (1.0 + jnp.exp(-gate))
        silu = gate * sigmoid
        hidden = (silu * up).astype(low)
        d_gate = (d_hidden * up * (sigmoid * (1.0 + gate * (1.0 - sigmoid)))).astype(low)
        d_up = (d_hidden * silu).astype(low)
        result_acc[...] += jnp.dot(hidden, down_w, preferred_element_type=full)
        d_acc[...] += against(d_gate, gate_w) + against(d_up, up_w)
        return hidden, d_gate, d_up

    def onward():
        return [
            pltpu.make_async_remote_copy(
                src_ref=src, dst_ref=dst, send_sem=ssem, recv_sem=rsem, device_id=to_z[0], device_id_type=MESH
            )
            for src, dst, ssem, rsem in (
                (rows_all.at[2], rows_all.at[3], xs_sem.at[2], xr_sem.at[2]),
                (upstream_all.at[2], last_up, us_sem.at[0], ur_sem.at[0]),
                (named_all.at[2], last_named, us_sem.at[1], ur_sem.at[1]),
            )
        ]

    def turn(first, count, again, last):
        many = count * rows
        some = pl.ds(first, count)
        values = rows_all[some].reshape(many, width)
        if first == 3:
            d_rows, marks = last_up[...], [last_named[...]]
        else:
            d_rows = upstream_all[some].reshape(many, width)
            marks = [named_all[first + i] for i in range(count)]
        logits = jnp.dot(values, router_w[...], preferred_element_type=full)
        named = jnp.concatenate([named_lanes(m) for m in marks], axis=0)
        lane = lax.broadcasted_iota(jnp.int32, (many, 128), 1)
        gates = gates_in(logits, named)
        if first == 0:
            own_shares[...] = gates[0:rows]
        share = jnp.sum(jnp.where(lane == e, gates, 0.0), axis=-1, keepdims=True)
        d_res[0:many] = d_rows
        for total in (res_acc, mix_acc, row_acc):
            total[0:many] = jnp.zeros((many, width), full)
        across[:, 0:many] = values.T
        inside = pl.ds(0, many)

        def store(ref, index, term):
            if again:
                term = term + ref[index].astype(full)
            ref[index] = term.astype(low)

        def shared_tile(f, carry):
            if first == 0:
                for copy in fetches(f, True):
                    copy.wait()
            values, d_out = rows_all[some].reshape(many, width), d_res[0:many]
            hidden, d_gate, d_up = branch(
                values, d_out, (ws_g, ws_u, ws_d), f, mix_acc.at[inside], row_acc.at[inside]
            )
            turned = across[:, 0:many]
            index = (slice(None), slice(None), slice(None), slice(None), columns(f))
            store(gs_g, index, product(turned, d_gate).reshape(2, 2, 2, width // 8, tile))
            store(gs_u, index, product(turned, d_up).reshape(2, 2, 2, width // 8, tile))
            term, quarter, half = outer_sum(hidden, d_out), width // 4, gs_d.shape[3]
            for i in range(tile // (2 * half)):
                for q in range(4):
                    for h in range(2):
                        top = (2 * i + h) * half
                        store(
                            gs_d,
                            (f * (tile // (2 * half)) + i, q // 2, q % 2, slice(None), slice(h * quarter, (h + 1) * quarter)),
                            term[top : top + half, q * quarter : (q + 1) * quarter],
                        )
            return carry

        def expert_tile(f, carry):
            if first == 0:
                for copy in fetches(f, False):
                    copy.wait()
            values, d_out = rows_all[some].reshape(many, width), d_res[0:many]
            hidden, d_gate, d_up = branch(
                values, d_out, (we_g, we_u, we_d), f, res_acc.at[inside], row_acc.at[inside]
            )
            turned = across[:, 0:many]
            index = (slice(None), slice(None), slice(None), slice(None), columns(f))
            store(ge_g, index, product(turned, d_gate).reshape(2, 2, 2, width // 8, tile))
            store(ge_u, index, product(turned, d_up).reshape(2, 2, 2, width // 8, tile))
            store(ge_d, (f,), outer_sum(hidden, d_out).reshape(2, 2, 2, tile // 8, width))
            if first == 1:

                @pl.when(f == tiles // 8)
                def _():
                    far_copy.wait()
                    for copy in onward():
                        copy.start()

            if last:
                for a in range(3):
                    piece_e(f, a).start(1)

                @pl.when(f == 0)
                def _():
                    for a in range(3):
                        piece_s(a).finish(1)
                        piece_s(a).start(2)

                @pl.when(f > 0)
                def _():
                    for a in range(3):
                        piece_e(f - 1, a).finish(1)
                        piece_e(f - 1, a).start(2)

                @pl.when(f == tiles - 1)
                def _():
                    for a in range(3):
                        piece_s(a).finish(2)
                        piece_s(a).start(3)

            return carry

        lax.fori_loop(0, shared_tiles, shared_tile, 0)
        if last:
            for a in range(3):
                piece_s(a).start(1)
        d_res[0:many] = (share * d_rows.astype(full)).astype(low)
        lax.fori_loop(0, tiles, expert_tile, 0)
        low_result = res_acc[0:many].astype(low)
        results[some] = (mix_acc[0:many] + share * low_result.astype(full)).astype(low).reshape(count, rows, width)
        row_send[some] = row_acc[0:many].astype(low).reshape(count, rows, width)
        terms = low_result.astype(full) * d_rows.astype(full)
        high = terms.astype(low)
        ones = jnp.ones((8, width), low)
        sums = against(ones, high) + against(ones, (terms - high.astype(full)).astype(low))
        for i in range(count):
            dg_send[first + i] = sums[:, i * rows : (i + 1) * rows]

    back_copies = []
    turn(0, 1, False, False)
    near_copy.wait()
    turn(1, 1, True, False)
    back_copies.append(start_copy(row_send.at[1], row_got.at[0], rs_sem.at[0], rr_sem.at[0], to_z[0]))
    turn(2, 1, True, False)
    back_copies.append(start_copy(row_send.at[2], row_got.at[1], rs_sem.at[1], rr_sem.at[1], to_z[1]))
    for copy in onward():
        copy.wait()
    turn(3, 1, True, True)
    back_copies.append(start_copy(row_send.at[3], row_got.at[2], rs_sem.at[2], rr_sem.at[2], to_z[2]))
    for i in range(3):
        back_copies.append(start_copy(dg_send.at[i + 1], dg_got.at[i], ds_sem.at[i], dr_sem.at[i], to_z[i]))
    for a in range(3):
        piece_e(tiles - 1, a).finish(1)
        piece_e(tiles - 1, a).start(2)

    def third(f, carry):
        for a in range(3):
            piece_e(f, a).finish(2)
            piece_e(f, a).start(3)
        return carry

    lax.fori_loop(0, tiles, third, 0)
    for a in range(3):
        piece_s(a).finish(3)

    @pl.when(elsewhere == 1)
    def _():
        start_copy(s3_d, sd_got, hs_sem, hr_sem, to_owner)

    @pl.when(elsewhere == 0)
    def _():
        sd_got[...] = s3_d[...]

    for h in range(2):
        part = pl.ds(h * s3_g.shape[1], s3_g.shape[1])
        sg_out[part] = s3_g[h].astype(full)
        su_out[part] = s3_u[h].astype(full)

    for copy in back_copies:
        copy.wait()
    total = row_send[0].astype(full)
    for i in range(3):
        total = total + row_got[i].astype(full)
    expert_row = lax.broadcasted_iota(jnp.int32, (8, rows), 0)
    d_gates = jnp.where(expert_row == e, dg_send[0], 0.0)
    for i in range(3):
        d_gates = jnp.where(expert_row == others[i], dg_got[i], d_gates)
    d_gates = jnp.concatenate([d_gates, jnp.zeros((120, rows), full)], axis=0).T
    shares = own_shares[...]
    d_logits = (shares * (d_gates - jnp.sum(shares * d_gates, axis=-1, keepdims=True))).astype(low)
    total = total + against(d_logits, router_w[...])
    router = outer_sum(d_logits, second[...])
    values = mixed[...]
    inverse = lax.rsqrt(jnp.mean(values * values, axis=-1, keepdims=True) + 1e-06)
    unit = values * inverse
    small_out[0:8, :] = router[0:8, :]
    small_out[8:16, :] = jnp.broadcast_to(jnp.sum(total * unit, axis=0, keepdims=True), (8, width))
    inner = total * gain_two[...].reshape(1, width)
    mean = jnp.mean(inner * unit, axis=-1, keepdims=True)
    d_mixed_out[...] = upstream_all[0].astype(full) + inverse * (inner - unit * mean)

    def done(f, carry):
        for a in range(3):
            piece_e(f, a).finish(3)
        return carry

    lax.fori_loop(0, tiles, done, 0)

    @pl.when(elsewhere == 1)
    def _():
        pltpu.make_async_remote_copy(
            src_ref=s3_d, dst_ref=sd_got, send_sem=hs_sem, recv_sem=hr_sem, device_id=to_owner, device_id_type=MESH
        ).wait()

    quarter, half = width // 4, s3_d.shape[1]
    for h in range(2):
        for i in range(2):
            top = h * 2 * half + i * half
            sd_out[top : top + half] = sd_got[i, :, h * quarter : (h + 1) * quarter].astype(full)


def ffn(second, mixed, upstream_all, named_all, w_router, gain_two, experts, shared):
    rows, width = second.shape
    hidden = experts[0].shape[1]
    slice_width = shared[0].shape[1] // 4
    tile = 512
    tiles = hidden // tile
    low, full = jnp.bfloat16, jnp.float32
    dma = pltpu.SemaphoreType.DMA
    ninth, small, half = width // 8, tile // 8, slice_width // 4

    def vm(*shape, dtype=low):
        return pltpu.VMEM(shape, dtype)

    def out(*shape, dtype=low):
        return jax.ShapeDtypeStruct(shape, dtype)

    spec = pl.BlockSpec(memory_space=pltpu.VMEM)
    out_shape = [
        out(4, rows, width), out(rows, width, dtype=full), out(16, width, dtype=full),
        out(2, ninth // 2, hidden), out(2, ninth // 2, hidden), out(tiles, 2, small // 2, width),
        out(ninth, slice_width, dtype=full), out(ninth, slice_width, dtype=full), out(2 * half, width // 4, dtype=full),
    ]
    scratch = [
        vm(4, rows, width), vm(rows, width), vm(16, rows), vm(rows, width), *[vm(rows, width, dtype=full)] * 3,
        vm(4, rows, width), vm(3, rows, width), vm(4, 8, rows, dtype=full), vm(3, 8, rows, dtype=full),
        vm(width, 128), vm(rows, 128, dtype=full), vm(width, rows),
        *[vm(width, hidden)] * 2, vm(hidden, width), *[vm(width, slice_width)] * 2, vm(slice_width, width),
        dma(((hidden + slice_width) // tile, 3)),
        *[vm(2, 2, 2, ninth, hidden)] * 2, vm(tiles, 2, 2, 2, small, width),
        *[vm(2, 2, ninth, hidden)] * 2, vm(tiles, 2, 2, small, width),
        *[vm(2, 2, ninth // 2, hidden)] * 2, vm(tiles, 2, 2, small // 2, width),
        *[vm(2, 2, 2, ninth, slice_width)] * 2, vm(2, 2, 2, half, width // 2),
        *[vm(2, 2, ninth, slice_width)] * 2, vm(2, 2, half, width // 2),
        *[vm(2, 2, ninth // 2, slice_width)] * 2, vm(2, 2, half // 2, width // 2),
        *[vm(2, ninth // 2, slice_width)] * 2, vm(2, half // 2, width // 2), vm(2, half // 2, width // 2),
        *[dma((tiles, 3, 5))] * 2, *[dma((3, 5))] * 2, *[dma((3,))] * 2, *[dma((2,))] * 2, *[dma((3,))] * 4, dma, dma,
    ]
    return pl.pallas_call(
        ffn_kernel,
        out_shape=out_shape,
        in_specs=[spec] * 6 + [pl.BlockSpec(memory_space=pl.ANY)] * 6,
        out_specs=[spec] * len(out_shape),
        scratch_shapes=scratch,
        compiler_params=pltpu.CompilerParams(
            collective_id=3, has_side_effects=True, vmem_limit_bytes=60 * 2**20
        ),
        name="ffn",
    )(second, mixed, upstream_all, named_all, w_router, gain_two, *experts, *shared)


def back_kernel(
    eg_own, eu_own, ed_own, small, results, mixed,
    tokens, gain_one, d_mixed, attended, normed, q_all, k_all, v_all, log_sum, w_q, w_k, w_v, w_o, cosine, sine,
    eg_all, eu_all, ed_all, q_out, k_out, v_out, o_out, one_out, two_out, router_out, output, token_out,
    grads, d_att, d_all, stats, stat_col, sum_q, sum_k, sum_v, misc_in, misc_out, far_sum, turned, asem, arem, tsem, trem,
    one, two, three, z_flat, got_flat, misc_got, result_got,
    lsem, gsem, grem, csem, crem, psem, prem, zsem, zrem, msem, mrem, rsem, rrem,
):
    s, x, k, e, c, to_core, to_x, to_y, others = neighbours()
    place = (s, x, k, to_core, to_x, to_y)
    to_z = [(s, c, o) for o in others]
    low, full = jnp.bfloat16, jnp.float32
    greet([to_core, to_x, to_y, *to_z])

    def piece(a):
        g = grads.at[a]
        return Piece(
            place,
            lambda kk: g.at[:, :, kk],
            lambda i, j, r: one.at[a, i, j, r],
            lambda h, i: two.at[a, h, i],
            lambda h: three.at[a, h],
            g.shape[3] // 2, lambda n: (psem.at[a, n], prem.at[a, n]), 48,
        )

    rows, width = tokens.shape
    heads = width // HEAD_DIM
    d_att[...] = d_mixed[...].astype(low)
    d_all[c] = against(d_att[...], w_o[...]).astype(low)
    head_of = lax.broadcasted_iota(jnp.int32, (128, width), 1) // HEAD_DIM
    chosen = jnp.where(head_of == lax.broadcasted_iota(jnp.int32, (128, width), 0), 1.0, 0.0).astype(low)
    terms = d_all[c].astype(full) * attended[...].astype(full)
    high = terms.astype(low)
    rest = (terms - high.astype(full)).astype(low)
    stat_col[0] = log_sum[...]
    stat_col[1] = against(high, chosen) + against(rest, chosen)
    stats[c, 0] = log_sum[...].T[0:16, :]
    stats[c, 1] = (against(chosen[0:16], high) + against(chosen[0:16], rest))
    core_copies = [
        start_copy(d_all.at[c], d_all.at[c], asem.at[0], arem.at[0], to_core),
        start_copy(stats.at[c], stats.at[c], tsem.at[0], trem.at[0], to_core),
    ]
    x_copies = [
        start_copy(d_all.at[c], d_all.at[c], asem.at[1], arem.at[1], to_x),
        start_copy(stats.at[c], stats.at[c], tsem.at[1], trem.at[1], to_x),
    ]
    near_place, far_place, opposite_place = others
    result_copies = [
        start_copy(results.at[1], result_got.at[0], rsem.at[0], rrem.at[0], to_z[0]),
        start_copy(results.at[3], result_got.at[1], rsem.at[1], rrem.at[1], to_z[0]),
    ]

    def block(a, h, ss, xx):
        whole = (eg_all, eu_all, ed_all)[a]
        half = whole.shape[-2] // 2
        part = pl.ds(h * half, half)
        return whole.at[ss, xx, k, part] if a < 2 else whole.at[:, ss, xx, k, part]

    def own_block(a, h):
        own = (eg_own, eu_own, ed_own)[a]
        return own.at[h] if a < 2 else own.at[:, h]

    def to_both_cores(a, h, n, src, spot):
        core_parts.append(start_copy(src, spot, csem.at[a, h, n], crem.at[a, h, n], to_core))

    core_parts, near, wide, kept = [], [], [], []
    parts = [(a, h) for a in range(3) for h in range(2)]

    def spread(own, buffer, first):
        halves, height, across = own.shape
        piece_width = across // 4
        for h in range(halves):
            for q in range(4):
                part = own[h, :, q * piece_width : (q + 1) * piece_width]
                buffer[q, pl.ds(h * height, height), first : first + piece_width] = part

    def to_nearest(buffer, got, number):
        return [
            start_copy(buffer.at[near_place], got.at[0], zsem.at[number, 0], zrem.at[number, 0], to_z[0]),
            start_copy(buffer.at[opposite_place], got.at[1], zsem.at[number, 1], zrem.at[number, 1], to_z[0]),
        ]

    def to_far(copies, buffer, got, number):
        for copy in copies:
            copy.wait()
        buffer[far_place] = (buffer[far_place].astype(full) + got[1].astype(full)).astype(low)
        return start_copy(buffer.at[far_place], got.at[2], zsem.at[number, 2], zrem.at[number, 2], to_z[1])

    def settled(copy, buffer, got):
        copy.wait()
        return buffer[e].astype(full) + got[0].astype(full) + got[2].astype(full)

    for a, h in parts:
        src, here = own_block(a, h), block(a, h, s, x)
        kept.append(pltpu.make_async_copy(src, here, lsem.at[a, h]))
        kept[-1].start()
        to_both_cores(a, h, 0, src, here)

    def put(a, first_factor, second_factor):
        grads[a] = outer_sum(first_factor, second_factor).astype(low).reshape(2, 2, 2, width // 8, width)
        piece(a).start(1)

    put(3, attended[...], d_att[...])
    lane = lax.broadcasted_iota(jnp.int32, (rows, 128), 1)
    scale = HEAD_DIM**-0.5
    for total in (sum_q, sum_k, sum_v):
        total[...] = jnp.zeros_like(total)

    def inside(h, values):
        return jnp.where((lane // HEAD_DIM) == h, values, jnp.zeros_like(values))

    def columns(g):
        return pl.ds(pl.multiple_of(g * 128, 128), 128)

    def query_pair(g, carry):
        at = columns(g)
        q, d_out = q_all[c, :, at], d_all[c, :, at]
        sides = []
        for h in range(2):
            pick = lane == 2 * g + h
            sides.append(
                (
                    inside(h, q),
                    inside(h, d_out),
                    jnp.sum(jnp.where(pick, stat_col[0], 0.0), axis=-1, keepdims=True),
                    jnp.sum(jnp.where(pick, stat_col[1], 0.0), axis=-1, keepdims=True),
                )
            )
        for j in range(4):

            @pl.when(j <= c)
            def _(j=j):
                keys, values = k_all[j, :, at], v_all[j, :, at]
                terms = []
                for q_side, d_side, log_total, delta in sides:
                    weights = jnp.exp(against(q_side, keys) * scale - log_total)
                    d_scores = (weights * (against(d_side, values) - delta)).astype(low)
                    terms.append(jnp.dot(d_scores, keys, preferred_element_type=full))
                sum_q[:, at] += jnp.where(lane < HEAD_DIM, terms[0], terms[1])

        return carry

    lax.fori_loop(0, width // 128, query_pair, 0)
    for a, h in parts:
        src, here = own_block(a, h), block(a, h, s, x)
        near.append(start_copy(src, here, gsem.at[a, h, 0], grem.at[a, h, 0], (to_y, to_x)[h]))
    for copy in result_copies:
        copy.wait()
    far_sum[...] = (results[2].astype(full) + result_got[1].astype(full)).astype(low)
    result_copy = start_copy(far_sum, result_got.at[2], rsem.at[2], rrem.at[2], to_z[1])

    def key_side(j):
        @pl.when(j >= c)
        def _():
            def key_pair(g, carry):
                at = columns(g)
                keys, values = k_all[c, :, at], v_all[c, :, at]
                q, d_out = q_all[j, :, at], d_all[j, :, at]
                terms = []
                for h in range(2):
                    log_total = stats[j, 0, pl.ds(2 * g + h, 1), :]
                    delta = stats[j, 1, pl.ds(2 * g + h, 1), :]
                    weights = jnp.exp(against(inside(h, keys), q) * scale - log_total)
                    d_scores = (weights * (against(inside(h, values), d_out) - delta)).astype(low)
                    terms.append(
                        (
                            jnp.dot(d_scores, q, preferred_element_type=full),
                            jnp.dot(weights.astype(low), d_out, preferred_element_type=full),
                        )
                    )
                sum_k[:, at] += jnp.where(lane < HEAD_DIM, terms[0][0], terms[1][0])
                sum_v[:, at] += jnp.where(lane < HEAD_DIM, terms[0][1], terms[1][1])
                return carry

            lax.fori_loop(0, width // 128, key_pair, 0)

    def turned_back(total):
        parts = []
        for g in range(width // 128):
            part = total[:, g * 128 : (g + 1) * 128] * scale
            parts.append((part * cosine[c] - swapped(part) * sine[c]).astype(low))
        return jnp.concatenate(parts, axis=1)

    key_side(c)
    d_query = turned_back(sum_q)
    put(0, normed[...], d_query)
    d_normed = against(d_query, w_q[...])
    piece(3).finish(1)
    piece(3).start(2)
    for copy in core_copies:
        copy.wait()
    key_side(x * 2 + (1 - k))
    for copy in x_copies:
        copy.wait()
    there = (1 - x) * 2 + k
    corner_copies = [
        start_copy(d_all.at[there], d_all.at[there], asem.at[2], arem.at[2], to_core),
        start_copy(stats.at[there], stats.at[there], tsem.at[2], trem.at[2], to_core),
    ]
    key_side(there)
    for i, (a, h) in enumerate(parts):
        near[i].wait()
        spot = block(a, h, (1 - s, s)[h], (x, 1 - x)[h])
        to_both_cores(a, h, 1, spot, spot)
        src, here = own_block(a, h), block(a, h, s, x)
        wide.append(start_copy(src, here, gsem.at[a, h, 1], grem.at[a, h, 1], (to_x, to_y)[h]))
    for copy in corner_copies:
        copy.wait()
    key_side((1 - x) * 2 + (1 - k))
    d_key = turned_back(sum_k)
    put(1, normed[...], d_key)
    d_value = sum_v[...].astype(low)
    put(2, normed[...], d_value)
    piece(0).finish(1)
    piece(0).start(2)
    d_normed = d_normed + against(d_key, w_k[...]) + against(d_value, w_v[...])
    values = tokens[...].astype(full)
    inverse = lax.rsqrt(jnp.mean(values * values, axis=-1, keepdims=True) + 1e-06)
    unit = values * inverse
    misc_in[0:8, :] = small[0:8, :]
    misc_in[8:9, :] = jnp.sum(d_normed * unit, axis=0, keepdims=True)
    misc_in[9:10, :] = small[8:9, :]
    misc_in[10:16, :] = jnp.zeros((6, width), full)
    misc_copy = start_copy(misc_in, misc_got.at[0], msem.at[0], mrem.at[0], to_core)
    for a in (1, 2):
        piece(a).finish(1)
        piece(a).start(2)
    inner = d_normed * gain_one[...].reshape(1, width)
    mean = jnp.mean(inner * unit, axis=-1, keepdims=True)
    token_out[...] = d_mixed[...] + inverse * (inner - unit * mean)
    misc_copy.wait()
    misc_out[...] = misc_in[...] + misc_got[0]
    misc_copy = start_copy(misc_out, misc_got.at[1], msem.at[1], mrem.at[1], to_x)
    for a in (3, 0, 1, 2):
        piece(a).finish(2)
        piece(a).start(3)
    misc_copy.wait()
    misc_got[3] = misc_out[...] + misc_got[1]
    misc_copy = start_copy(misc_got.at[3], misc_got.at[2], msem.at[2], mrem.at[2], to_y)
    onward = []
    for a, h in parts:
        spot = block(a, h, (1 - s, s)[h], (x, 1 - x)[h])
        onward.append(start_copy(spot, spot, gsem.at[a, h, 2], grem.at[a, h, 2], (to_x, to_y)[h]))
    z_copies = []
    for number, pair in enumerate(((3, 0), (1, 2))):
        for i, a in enumerate(pair):
            piece(a).finish(3)
            spread(three.at[a], z_flat.at[number], i * (width // 4))
        z_copies.append(to_nearest(z_flat.at[number], got_flat.at[number], number))
    misc_copy.wait()
    misc_got[4] = misc_got[3] + misc_got[2]
    misc_copies = [
        start_copy(misc_got.at[4], misc_got.at[5 + i], msem.at[3 + i], mrem.at[3 + i], to_z[i]) for i in range(3)
    ]
    for i, (a, h) in enumerate(parts):
        wide[i].wait()
        spot = block(a, h, (s, 1 - s)[h], (1 - x, x)[h])
        to_both_cores(a, h, 2, spot, spot)
    for number in range(2):
        z_copies[number] = to_far(z_copies[number], z_flat.at[number], got_flat.at[number], number)

    result_copy.wait()
    total = mixed[...] + results[0].astype(full) + result_got[0].astype(full) + result_got[2].astype(full)
    output[...] = total.astype(low)
    for i, (a, h) in enumerate(parts):
        onward[i].wait()
        spot = block(a, h, 1 - s, 1 - x)
        to_both_cores(a, h, 3, spot, spot)
    for copy in misc_copies:
        copy.wait()
    sums = misc_got[4] + misc_got[5] + misc_got[6] + misc_got[7]
    one_out[...] = sums[8:9, :].reshape(width)
    two_out[...] = sums[9:10, :].reshape(width)
    turned[...] = jnp.concatenate([sums, jnp.zeros((112, width), full)], axis=0).T
    high = router_out.shape[0]
    rows_of = turned[pl.ds(pl.multiple_of((s * 4 + c) * high, high), high), :]
    router_out[...] = jnp.sum(jnp.where(lane[0:high] == e, rows_of, 0.0), axis=-1, keepdims=True)
    quarter = width // 4
    for number, targets in enumerate(((o_out, q_out), (k_out, v_out))):
        total = settled(z_copies[number], z_flat.at[number], got_flat.at[number])
        targets[0][...] = total[:, 0:quarter]
        targets[1][...] = total[:, quarter:]
    for copy in (*kept, *core_parts):
        copy.wait()


def back(expert_own, small, results, mixed, tokens, gain_one, d_mixed, kept, weights):
    low, full = jnp.bfloat16, jnp.float32
    dma = pltpu.SemaphoreType.DMA
    rows, width = mixed.shape
    ninth = width // 8
    hidden = expert_own[0].shape[2]
    tiles, unused, short, unused = expert_own[2].shape
    cosine, sine = (jnp.asarray(t).reshape(4, rows, 128) for t in place_tables(4 * rows))

    def vm(*shape, dtype=low):
        return pltpu.VMEM(shape, dtype)

    def out(*shape, dtype=low):
        return jax.ShapeDtypeStruct(shape, dtype)

    spec, anywhere = pl.BlockSpec(memory_space=pltpu.VMEM), pl.BlockSpec(memory_space=pl.ANY)
    out_shape = [
        out(2, 2, 2, ninth, hidden), out(2, 2, 2, ninth, hidden), out(tiles, 2, 2, 2, 2 * short, width),
        *[out(ninth, width // 4, dtype=full)] * 4, out(width, dtype=full), out(width, dtype=full),
        out(ninth, 1, dtype=full), out(rows, width),
        out(rows, width, dtype=full),
    ]
    scratch = [
        vm(4, 2, 2, 2, ninth, width), vm(rows, width), vm(4, rows, width), vm(4, 2, 16, rows, dtype=full),
        vm(2, rows, 128, dtype=full), *[vm(rows, width, dtype=full)] * 3, vm(16, width, dtype=full),
        vm(16, width, dtype=full), vm(rows, width), vm(width, 128, dtype=full),
        dma((3,)), dma((3,)), dma((3,)), dma((3,)),
        vm(4, 2, 2, ninth, width), vm(4, 2, 2, ninth // 2, width), vm(4, 2, ninth // 2, width),
        vm(2, 4, ninth, width // 2),
        vm(2, 3, ninth, width // 2),
        vm(8, 16, width, dtype=full), vm(3, rows, width),
        dma((3, 2)), *[dma((3, 2, 3))] * 2, *[dma((3, 2, 4))] * 2, *[dma((4, 5))] * 2, *[dma((2, 3))] * 2,
        dma((6,)), dma((6,)), dma((3,)), dma((3,)),
    ]
    operands = (
        *expert_own, small, results, mixed, tokens, gain_one, d_mixed, *kept,
        *weights, cosine, sine,
    )
    return pl.pallas_call(
        back_kernel,
        out_shape=out_shape,
        in_specs=[spec] * len(operands),
        out_specs=[anywhere] * 3 + [spec] * 9,
        scratch_shapes=scratch,
        compiler_params=pltpu.CompilerParams(
            collective_id=4, has_side_effects=True, vmem_limit_bytes=60 * 2**20
        ),
        name="back",
    )(*operands)


def per_device_dense(
    tokens,
    expert_ids,
    norm_one,
    w_query,
    w_key,
    w_value,
    w_out,
    norm_two,
    w_router,
    expert_gate,
    expert_up,
    expert_down,
    shared_gate,
    shared_up,
    shared_down,
    cotangent,
):
    upstream = cotangent[0]
    ids = expert_ids[0]
    (
        q_all, k_all, v_all, upstream_all, named_all, normed, attended, mixed, second, log_sum,
    ) = front(
        tokens[0], upstream, ids, norm_one, norm_two, w_query, w_key, w_value, w_out
    )
    (
        results, d_mixed, small, eg_own, eu_own, ed_own, sg, su, sd,
    ) = ffn(
        second, mixed, upstream_all, named_all, w_router, norm_two,
        (expert_gate[0], expert_up[0], expert_down[0]), (shared_gate, shared_up, shared_down),
    )

    (
        eg, eu, ed, gq, gk, gv, go, grad_one, grad_two, router, output, grad_tokens,
    ) = back(
        (eg_own, eu_own, ed_own), small, results, mixed, tokens[0], norm_one, d_mixed,
        (attended, normed, q_all, k_all, v_all, log_sum), (w_query, w_key, w_value, w_out),
    )
    return (
        output[None],
        grad_tokens[None],
        grad_one,
        gq,
        gk,
        gv,
        go,
        grad_two,
        router,
        eg.astype(jnp.float32).reshape(expert_gate.shape),
        eu.astype(jnp.float32).reshape(expert_up.shape),
        ed.astype(jnp.float32).reshape(expert_down.shape),
        sg,
        su,
        sd,
    )


def fits(mesh):
    return dict(mesh.shape) == {"seq": 2, "ctx": 4, "exp": 4}


def solution(mesh):
    per_device = per_device_dense if fits(mesh) else per_device_slots
    in_specs = (
        P(("seq", "exp"), "ctx", None),
        P(("seq", "exp"), "ctx", None),
        P(),
        P(),
        P(),
        P(),
        P(),
        P(),
        P(),
        P("exp", None, None),
        P("exp", None, None),
        P("exp", None, None),
        P(),
        P(),
        P(),
        P(("seq", "exp"), "ctx", None),
    )
    out_specs = (
        P(("seq", "exp"), "ctx", None),
        P(("seq", "exp"), "ctx", None),
        P(),
        P(("seq", "ctx"), "exp"),
        P(("seq", "ctx"), "exp"),
        P(("seq", "ctx"), "exp"),
        P(("seq", "ctx"), "exp"),
        P(),
        P(("seq", "ctx"), "exp"),
        P("exp", None, None),
        P("exp", None, None),
        P("exp", None, None),
        P(("seq", "ctx"), "exp"),
        P(("seq", "ctx"), "exp"),
        P(("seq", "ctx"), "exp"),
    )
    return jax.shard_map(
        per_device, mesh=mesh, in_specs=in_specs, out_specs=out_specs, check_vma=False
    )
```

```python
import functools
import math

import jax
import jax.numpy as jnp
import numpy as np
from jax import lax
from jax.experimental import pallas as pl
from jax.experimental.pallas import tpu as pltpu
from jax.sharding import PartitionSpec as P

HEAD_DIM = 64
TOP = 2
BLOCK = 256
KEY_ROWS = 512
MESH = pl.DeviceIdType.MESH


def product(first_factor, second_factor):
    return jnp.dot(first_factor, second_factor, preferred_element_type=jnp.float32)


def against(first_factor, second_factor):
    return lax.dot_general(
        first_factor, second_factor, (((1,), (1,)), ((), ())), preferred_element_type=jnp.float32
    )


def outer_sum(first_factor, second_factor):
    return lax.dot_general(
        first_factor, second_factor, (((0,), (0,)), ((), ())), preferred_element_type=jnp.float32
    )


def normalize(values, scaling):
    return values * lax.rsqrt(jnp.mean(values * values, axis=-1, keepdims=True) + 1e-06) * scaling


def rotate(values, places):
    halfway = values.shape[-1] // 2
    frequency = 10000.0 ** (-jnp.arange(halfway, dtype=jnp.float32) / halfway)
    angles = places.astype(jnp.float32)[:, None] * frequency[None, :]
    cosine = jnp.cos(angles)[:, None, :]
    sine_part = jnp.sin(angles)[:, None, :]
    former = values[..., :halfway]
    latter = values[..., halfway:]
    return jnp.concatenate(
        [former * cosine - latter * sine_part, latter * cosine + former * sine_part], axis=-1
    )


def silu_parts(gate_pre):
    sigmoid_value = jax.nn.sigmoid(gate_pre)
    return (gate_pre * sigmoid_value, sigmoid_value * (1.0 + gate_pre * (1.0 - sigmoid_value)))


def tiled(matrix, row_groups, col_groups):
    row_count, col_count = matrix.shape
    blocks = matrix.reshape(
        row_groups, row_count // row_groups, col_groups, col_count // col_groups
    ).transpose(0, 2, 1, 3)
    return blocks.reshape(col_groups * row_count, col_count // col_groups)


def per_device_slots(
    tokens,
    expert_ids,
    norm_one,
    w_query,
    w_key,
    w_value,
    w_out,
    norm_two,
    w_router,
    expert_gate,
    expert_up,
    expert_down,
    shared_gate,
    shared_up,
    shared_down,
    cotangent,
):
    local_rows = tokens.shape[1]
    model_width = tokens.shape[2]
    head_count = model_width // HEAD_DIM
    score_scale = HEAD_DIM ** (-0.5)
    ctx_count = lax.axis_size("ctx")
    ctx_place = lax.axis_index("ctx")
    exp_count = lax.axis_size("exp")
    row_groups = lax.axis_size("seq") * ctx_count
    local_experts = expert_gate.shape[0]
    experts_all = local_experts * exp_count
    capacity = min(local_rows, 2 * TOP * local_rows // experts_all)
    places = ctx_place * local_rows + jnp.arange(local_rows, dtype=jnp.int32)
    query_blocks = places // BLOCK

    def spread(matrix):
        return tiled(matrix, row_groups, exp_count)

    inputs = tokens[0].astype(jnp.float32)
    normed_full, norm_one_pull = jax.vjp(normalize, inputs, norm_one)
    normed = normed_full.astype(jnp.bfloat16)
    query = rotate(
        product(normed, w_query).reshape(local_rows, head_count, HEAD_DIM), places
    ).astype(jnp.bfloat16)
    keys_local = (
        rotate(product(normed, w_key).reshape(local_rows, head_count, HEAD_DIM), places)
        .astype(jnp.bfloat16)
        .reshape(local_rows, model_width)
    )
    values_local = product(normed, w_value).astype(jnp.bfloat16)

    def block_scores(key_block, offset):
        key_heads = key_block.reshape(-1, head_count, HEAD_DIM)
        scores = (
            jnp.einsum("qhd,khd->hqk", query, key_heads, preferred_element_type=jnp.float32)
            * score_scale
        )
        key_index = (offset + jnp.arange(key_block.shape[0], dtype=jnp.int32)) // BLOCK
        allowed = key_index[None, :] <= query_blocks[:, None]
        return (scores, allowed)

    def attend_block(running, key_block, value_block, offset):
        highest, totals, accumulated = running
        scores, allowed = block_scores(key_block, offset)
        masked = jnp.where(allowed[None], scores, -1e30)
        fresh = jnp.maximum(highest, jnp.max(masked, axis=-1))
        weights = jnp.where(allowed[None], jnp.exp(masked - fresh[..., None]), 0.0)
        decay = jnp.exp(highest - fresh)
        value_heads = value_block.reshape(-1, head_count, HEAD_DIM)
        accumulated = accumulated * decay[..., None] + jnp.einsum(
            "hqk,khd->hqd",
            weights.astype(jnp.bfloat16),
            value_heads,
            preferred_element_type=jnp.float32,
        )
        return (fresh, totals * decay + jnp.sum(weights, axis=-1), accumulated)

    start_state = (
        jnp.full((head_count, local_rows), -1e30, jnp.float32),
        jnp.zeros((head_count, local_rows), jnp.float32),
        jnp.zeros((head_count, local_rows, HEAD_DIM), jnp.float32),
    )
    running = start_state
    key_part = lax.all_gather(keys_local, "ctx", axis=0, tiled=True)
    value_part = lax.all_gather(values_local, "ctx", axis=0, tiled=True)
    span_rows = key_part.shape[0]
    stride = math.gcd(span_rows, KEY_ROWS)
    step_count = span_rows // stride
    key_steps = key_part.reshape(step_count, stride, model_width)
    value_steps = value_part.reshape(step_count, stride, model_width)
    offsets = jnp.arange(step_count, dtype=jnp.int32) * stride

    def one_step(inner, operands):
        return (attend_block(inner, operands[0], operands[1], operands[2]), None)

    running, unused = lax.scan(one_step, running, (key_steps, value_steps, offsets))
    highest, totals, accumulated = running
    log_total = highest + jnp.log(totals)
    attended = (
        (accumulated / totals[..., None])
        .transpose(1, 0, 2)
        .reshape(local_rows, model_width)
        .astype(jnp.bfloat16)
    )
    mixed = inputs + product(attended, w_out)
    second_full, norm_two_pull = jax.vjp(normalize, mixed, norm_two)
    second = second_full.astype(jnp.bfloat16)
    logits = product(second, w_router)
    chosen = expert_ids[0]
    one_hot = (
        chosen[:, :, None] == jnp.arange(experts_all, dtype=jnp.int32)[None, None, :]
    ).astype(jnp.float32)
    selected = jnp.sum(logits[:, None, :] * one_hot, axis=-1)
    gates = jax.nn.softmax(selected, axis=-1)
    flat_ids = chosen.reshape(-1)
    slot_hits = (flat_ids[:, None] == jnp.arange(experts_all, dtype=jnp.int32)[None, :]).astype(
        jnp.int32
    )
    order = jnp.arange(flat_ids.shape[0], dtype=jnp.int32)
    earlier = (order[None, :] < order[:, None]).astype(jnp.bfloat16)
    counts_before = product(earlier, slot_hits.astype(jnp.bfloat16)).astype(jnp.int32)
    slot_place = jnp.sum(counts_before * slot_hits, axis=1)

    def to_slots(routed_rows):
        empty_slots = jnp.zeros((experts_all, capacity, model_width), jnp.bfloat16)
        return (
            empty_slots.at[flat_ids, slot_place]
            .set(routed_rows)
            .reshape(exp_count, local_experts, capacity, model_width)
        )

    def from_slots(arrived_back):
        picked = arrived_back.reshape(experts_all, capacity, model_width)[flat_ids, slot_place]
        return picked.astype(jnp.float32).reshape(local_rows, TOP, model_width)

    def expert_front(arrived_rows):
        gate_pre = jnp.einsum(
            "sjcd,jdf->sjcf", arrived_rows, expert_gate, preferred_element_type=jnp.float32
        )
        up_pre = jnp.einsum(
            "sjcd,jdf->sjcf", arrived_rows, expert_up, preferred_element_type=jnp.float32
        )
        hidden = (jax.nn.silu(gate_pre) * up_pre).astype(jnp.bfloat16)
        return (gate_pre, up_pre, hidden)

    send_rows = to_slots(jnp.repeat(second, TOP, axis=0))
    arrived = lax.all_to_all(send_rows, "exp", split_axis=0, concat_axis=0, tiled=True)
    gate_pre, up_pre, hidden = expert_front(arrived)
    results = jnp.einsum(
        "sjcf,jfd->sjcd", hidden, expert_down, preferred_element_type=jnp.float32
    ).astype(jnp.bfloat16)
    returned = lax.all_to_all(results, "exp", split_axis=0, concat_axis=0, tiled=True)
    expert_out = from_slots(returned)
    mixture = jnp.sum(gates[:, :, None] * expert_out, axis=1)
    shared_gate_pre = product(second, shared_gate)
    shared_up_pre = product(second, shared_up)
    shared_hidden = (jax.nn.silu(shared_gate_pre) * shared_up_pre).astype(jnp.bfloat16)
    output = (mixed + mixture + product(shared_hidden, shared_down)).astype(jnp.bfloat16)
    upstream = cotangent[0]
    upstream_full = upstream.astype(jnp.float32)
    grad_shared_down = outer_sum(shared_hidden, upstream)
    d_shared_hidden = against(upstream, shared_down)
    shared_silu, shared_slope = silu_parts(shared_gate_pre)
    d_shared_gate = (d_shared_hidden * shared_up_pre * shared_slope).astype(jnp.bfloat16)
    d_shared_up = (d_shared_hidden * shared_silu).astype(jnp.bfloat16)
    grad_shared_gate = outer_sum(second, d_shared_gate)
    grad_shared_up = outer_sum(second, d_shared_up)
    d_second = against(d_shared_gate, shared_gate) + against(d_shared_up, shared_up)
    d_gates = jnp.sum(upstream_full[:, None, :] * expert_out, axis=-1)
    d_selected = gates * (d_gates - jnp.sum(gates * d_gates, axis=-1, keepdims=True))
    d_logits = jnp.sum(d_selected[:, :, None] * one_hot, axis=1).astype(jnp.bfloat16)
    grad_router = outer_sum(second, d_logits)
    d_second = d_second + against(d_logits, w_router)
    grad_slots = to_slots(
        (gates[:, :, None] * upstream_full[:, None, :])
        .astype(jnp.bfloat16)
        .reshape(local_rows * TOP, model_width)
    )
    arrived_rows, arrived_grad = (
        lax.all_to_all(send_rows, "exp", split_axis=0, concat_axis=0, tiled=True),
        lax.all_to_all(grad_slots, "exp", split_axis=0, concat_axis=0, tiled=True),
    )
    gate_kept, up_kept, hidden_kept = expert_front(arrived_rows)
    d_hidden = jnp.einsum(
        "sjcd,jfd->sjcf", arrived_grad, expert_down, preferred_element_type=jnp.float32
    )
    expert_silu, expert_slope = silu_parts(gate_kept)
    d_gate_pre = (d_hidden * up_kept * expert_slope).astype(jnp.bfloat16)
    d_up_pre = (d_hidden * expert_silu).astype(jnp.bfloat16)
    grad_expert_down = jnp.einsum(
        "sjcf,sjcd->jfd", hidden_kept, arrived_grad, preferred_element_type=jnp.float32
    )
    grad_expert_gate = jnp.einsum(
        "sjcd,sjcf->jdf", arrived_rows, d_gate_pre, preferred_element_type=jnp.float32
    )
    grad_expert_up = jnp.einsum(
        "sjcd,sjcf->jdf", arrived_rows, d_up_pre, preferred_element_type=jnp.float32
    )
    d_routed = (
        jnp.einsum("sjcf,jdf->sjcd", d_gate_pre, expert_gate, preferred_element_type=jnp.float32)
        + jnp.einsum("sjcf,jdf->sjcd", d_up_pre, expert_up, preferred_element_type=jnp.float32)
    ).astype(jnp.bfloat16)
    returned_grad = lax.all_to_all(d_routed, "exp", split_axis=0, concat_axis=0, tiled=True)
    d_second = d_second + jnp.sum(from_slots(returned_grad), axis=1)
    grad_expert_gate, grad_expert_up, grad_expert_down = (
        lax.psum(grad_expert_gate.astype(jnp.bfloat16), ("seq", "ctx")).astype(jnp.float32),
        lax.psum(grad_expert_up.astype(jnp.bfloat16), ("seq", "ctx")).astype(jnp.float32),
        lax.psum(grad_expert_down.astype(jnp.bfloat16), ("seq", "ctx")).astype(jnp.float32),
    )
    d_mixed_part, grad_norm_two = norm_two_pull(d_second)
    d_mixed = upstream_full + d_mixed_part
    d_attention = d_mixed.astype(jnp.bfloat16)
    grad_out = outer_sum(attended, d_attention)
    grad_heads = (
        against(d_attention, w_out).astype(jnp.bfloat16).reshape(local_rows, head_count, HEAD_DIM)
    )
    keys_all, values_all = (
        lax.all_gather(keys_local, "ctx", axis=0, tiled=True),
        lax.all_gather(values_local, "ctx", axis=0, tiled=True),
    )
    block_total = ((ctx_place + 1) * local_rows + KEY_ROWS - 1) // KEY_ROWS

    def weights_at(number):
        offset = number * KEY_ROWS
        key_block = lax.dynamic_slice_in_dim(keys_all, offset, KEY_ROWS, 0)
        value_block = lax.dynamic_slice_in_dim(values_all, offset, KEY_ROWS, 0)
        scores, allowed = block_scores(key_block, offset)
        weights = jnp.where(allowed[None], jnp.exp(scores - log_total[..., None]), 0.0)
        grad_weights = jnp.einsum(
            "qhd,khd->hqk",
            grad_heads,
            value_block.reshape(KEY_ROWS, head_count, HEAD_DIM),
            preferred_element_type=jnp.float32,
        )
        return (key_block, weights, grad_weights)

    def row_dot_step(number, summed):
        unused_block, weights, grad_weights = weights_at(number)
        return summed + jnp.sum(weights * grad_weights, axis=-1)

    row_dots = lax.fori_loop(
        0, block_total, row_dot_step, jnp.zeros((head_count, local_rows), jnp.float32)
    )

    def score_grads(number):
        key_block, weights, grad_weights = weights_at(number)
        d_scores = (weights * (grad_weights - row_dots[..., None])).astype(jnp.bfloat16)
        return (key_block.reshape(KEY_ROWS, head_count, HEAD_DIM), weights, d_scores)

    query_start = jnp.zeros((local_rows, head_count, HEAD_DIM), jnp.float32)

    def grad_step(number, running):
        grad_query, key_terms = running
        key_heads, weights, d_scores = score_grads(number)
        grad_query = (
            grad_query
            + jnp.einsum("hqk,khd->qhd", d_scores, key_heads, preferred_element_type=jnp.float32)
            * score_scale
        )
        key_part = (
            jnp.einsum("hqk,qhd->khd", d_scores, query, preferred_element_type=jnp.float32)
            * score_scale
        )
        value_part = jnp.einsum(
            "hqk,qhd->khd",
            weights.astype(jnp.bfloat16),
            grad_heads,
            preferred_element_type=jnp.float32,
        )
        block_terms = jnp.concatenate(
            [key_part.reshape(KEY_ROWS, model_width), value_part.reshape(KEY_ROWS, model_width)],
            axis=1,
        )
        return (
            grad_query,
            lax.dynamic_update_slice_in_dim(key_terms, block_terms, number * KEY_ROWS, 0),
        )

    grad_query_heads, key_terms = lax.fori_loop(
        0,
        block_total,
        grad_step,
        (query_start, jnp.zeros((ctx_count * local_rows, 2 * model_width), jnp.float32)),
    )
    key_grads = lax.psum_scatter(
        key_terms.astype(jnp.bfloat16), "ctx", scatter_dimension=0, tiled=True
    ).astype(jnp.float32)
    key_grad_heads = key_grads[:, :model_width].reshape(local_rows, head_count, HEAD_DIM)
    d_value = key_grads[:, model_width:].astype(jnp.bfloat16)
    d_query_lin = (
        rotate(grad_query_heads, -places).astype(jnp.bfloat16).reshape(local_rows, model_width)
    )
    d_key_lin = (
        rotate(key_grad_heads, -places).astype(jnp.bfloat16).reshape(local_rows, model_width)
    )
    grad_query = outer_sum(normed, d_query_lin)
    grad_key = outer_sum(normed, d_key_lin)
    grad_value = outer_sum(normed, d_value)
    d_normed = against(d_query_lin, w_query) + against(d_key_lin, w_key) + against(d_value, w_value)
    d_inputs, grad_norm_one = norm_one_pull(d_normed)
    grad_tokens = (d_mixed + d_inputs)[None]
    (
        grad_query,
        grad_key,
        grad_value,
        grad_out,
        grad_router,
        grad_shared_gate,
        grad_shared_up,
        grad_shared_down,
    ) = (
        lax.psum_scatter(
            spread(grad_query), ("seq", "ctx", "exp"), scatter_dimension=0, tiled=True
        ),
        lax.psum_scatter(spread(grad_key), ("seq", "ctx", "exp"), scatter_dimension=0, tiled=True),
        lax.psum_scatter(
            spread(grad_value), ("seq", "ctx", "exp"), scatter_dimension=0, tiled=True
        ),
        lax.psum_scatter(spread(grad_out), ("seq", "ctx", "exp"), scatter_dimension=0, tiled=True),
        lax.psum_scatter(
            spread(grad_router), ("seq", "ctx", "exp"), scatter_dimension=0, tiled=True
        ),
        lax.psum_scatter(
            spread(grad_shared_gate), ("seq", "ctx", "exp"), scatter_dimension=0, tiled=True
        ),
        lax.psum_scatter(
            spread(grad_shared_up), ("seq", "ctx", "exp"), scatter_dimension=0, tiled=True
        ),
        lax.psum_scatter(
            spread(grad_shared_down), ("seq", "ctx", "exp"), scatter_dimension=0, tiled=True
        ),
    )
    grad_norm_one, grad_norm_two = lax.psum((grad_norm_one, grad_norm_two), ("seq", "ctx", "exp"))
    return (
        output[None],
        grad_tokens,
        grad_norm_one,
        grad_query,
        grad_key,
        grad_value,
        grad_out,
        grad_norm_two,
        grad_router,
        grad_expert_gate,
        grad_expert_up,
        grad_expert_down,
        grad_shared_gate,
        grad_shared_up,
        grad_shared_down,
    )


def place_tables(length):
    half = HEAD_DIM // 2
    frequency = np.float32(10000.0) ** (-np.arange(half, dtype=np.float32) / np.float32(half))
    angles = np.arange(length, dtype=np.float32)[:, None] * frequency[None, :].astype(np.float32)
    cosine, sine = np.cos(angles), np.sin(angles)
    return (
        np.concatenate([cosine] * 4, axis=1).astype(np.float32),
        np.concatenate([-sine, sine, -sine, sine], axis=1).astype(np.float32),
    )


def swapped(values):
    half = HEAD_DIM // 2
    lane = lax.broadcasted_iota(jnp.int32, values.shape, 1) % HEAD_DIM
    return jnp.where(lane < half, pltpu.roll(values, 128 - half, 1), pltpu.roll(values, half, 1))


def start_copy(src, dst, ssem, rsem, device):
    copy = pltpu.make_async_remote_copy(
        src_ref=src, dst_ref=dst, send_sem=ssem, recv_sem=rsem, device_id=device, device_id_type=MESH
    )
    copy.start()
    return copy


def greet(devices):
    barrier = pltpu.get_barrier_semaphore()
    for device in devices:
        pl.semaphore_signal(barrier, inc=1, device_id=device, device_id_type=MESH)
    pl.semaphore_wait(barrier, len(devices))


def neighbours():
    s = lax.axis_index("seq")
    c = lax.axis_index("ctx")
    e = lax.axis_index("exp")
    x, k = c // 2, c % 2
    to_core = (s, x * 2 + (1 - k), e)
    to_x = (s, (1 - x) * 2 + k, e)
    to_y = (1 - s, c, e)
    near = e + 1 - 2 * (e % 2)
    far = lax.rem(e + 2, 4)
    opposite = 3 - e
    return s, x, k, e, c, to_core, to_x, to_y, (near, far, opposite)


def named_lanes(rows_named):
    marks = rows_named.astype(jnp.float32)
    return jnp.concatenate([marks, jnp.zeros((112, marks.shape[1]), jnp.float32)], axis=0).T > 0.5


def front_kernel(
    tokens, upstream, ids, gain_one, gain_two, w_q, w_k, w_v, w_o, cosine, sine,
    q_all, k_all, v_all, upstream_all, named_all, normed_out, attended_out, mixed_out, second_out, logsum_out,
    block, q_keep, k_keep, v_keep, weight, tsem, trem, usem, urem, nsem, nrem, wsem, osem,
):
    s, x, k, e, c, to_core, to_x, to_y, others = neighbours()
    rows, width = tokens.shape
    loads = [pltpu.make_async_copy(w, weight.at[i], wsem.at[i]) for i, w in enumerate((w_q, w_k, w_v, w_o))]
    for load in loads:
        load.start()
    greet([to_core, to_x, (s, c, others[0]), (s, c, others[1])])
    block[c] = tokens[...]
    upstream_all[0] = upstream[...]
    expert_row = lax.broadcasted_iota(jnp.int32, (16, rows), 0)
    marks = jnp.where((expert_row == ids[0:1, :]) | (expert_row == ids[1:2, :]), 1.0, 0.0)
    named_all[0] = marks.astype(jnp.bfloat16)
    core_copy = start_copy(tokens, block.at[c], tsem.at[0], trem.at[0], to_core)
    x_copy = start_copy(tokens, block.at[c], tsem.at[1], trem.at[1], to_x)
    to_near, to_far = (s, c, others[0]), (s, c, others[1])

    def over_z(i, source, device):
        return [
            start_copy(upstream_all.at[source], upstream_all.at[i + 1], usem.at[i], urem.at[i], device),
            start_copy(named_all.at[source], named_all.at[i + 1], nsem.at[i], nrem.at[i], device),
        ]

    near_copies = over_z(0, 0, to_near)
    far_copies = over_z(1, 0, to_far)

    one = gain_one[...].reshape(1, width)

    def project(j):
        values = block[j].astype(jnp.float32)
        inverse = lax.rsqrt(jnp.mean(values * values, axis=-1, keepdims=True) + 1e-06)
        normed = (values * inverse * one).astype(jnp.bfloat16)
        for i, out in enumerate((q_keep, k_keep)):
            lin = jnp.dot(normed, weight[i], preferred_element_type=jnp.float32)
            for g in range(width // 128):
                part = lin[:, g * 128 : (g + 1) * 128]
                turned = part * cosine[j] + swapped(part) * sine[j]
                out[j, :, g * 128 : (g + 1) * 128] = turned.astype(jnp.bfloat16)
        v_keep[j] = jnp.dot(normed, weight[2], preferred_element_type=jnp.float32).astype(jnp.bfloat16)
        return normed

    for load in loads:
        load.wait()
    normed_out[...] = project(c)
    core_copy.wait()
    project(x * 2 + (1 - k))
    x_copy.wait()
    there = (1 - x) * 2 + k
    corner_copy = start_copy(block.at[there], block.at[there], tsem.at[2], trem.at[2], to_core)
    project(there)
    corner_copy.wait()
    project((1 - x) * 2 + (1 - k))

    leaves = [
        pltpu.make_async_copy(src, dst, osem.at[i])
        for i, (src, dst) in enumerate(((q_keep, q_all), (k_keep, k_all), (v_keep, v_all)))
    ]
    for leave in leaves:
        leave.start()
    span = 4 * rows
    hidden_keys = lax.broadcasted_iota(jnp.int32, (1, span), 1) // rows > c
    bias = jnp.where(hidden_keys, -1e30, 0.0)
    lane = lax.broadcasted_iota(jnp.int32, (rows, 128), 1)
    logsum_out[...] = jnp.zeros_like(logsum_out)

    def pair(g, carry):
        at = pl.ds(pl.multiple_of(g * 128, 128), 128)
        q = q_keep[c, :, at]
        keys = k_keep[:, :, at].reshape(span, 128)
        values = v_keep[:, :, at].reshape(span, 128)
        out = jnp.zeros((rows, 128), jnp.float32)
        for h in range(2):
            inside = (lane // HEAD_DIM) == h
            scores = lax.dot_general(
                jnp.where(inside, q, jnp.zeros_like(q)), keys, (((1,), (1,)), ((), ())),
                preferred_element_type=jnp.float32,
            )
            scores = scores * (HEAD_DIM**-0.5) + bias
            highest = jnp.max(scores, axis=-1, keepdims=True)
            raised = jnp.exp(scores - highest)
            total = jnp.sum(raised, axis=-1, keepdims=True)
            mixed = jnp.dot(raised.astype(jnp.bfloat16), values, preferred_element_type=jnp.float32)
            out = jnp.where(inside, mixed / total, out)
            logsum_out[...] = jnp.where(lane == 2 * g + h, highest + jnp.log(total), logsum_out[...])
        attended_out[:, at] = out.astype(jnp.bfloat16)
        return carry

    lax.fori_loop(0, width // 128, pair, 0)
    mixed = tokens[...].astype(jnp.float32) + jnp.dot(
        attended_out[...], weight[3], preferred_element_type=jnp.float32
    )
    mixed_out[...] = mixed
    inverse = lax.rsqrt(jnp.mean(mixed * mixed, axis=-1, keepdims=True) + 1e-06)
    second_out[...] = (mixed * inverse * gain_two[...].reshape(1, width)).astype(jnp.bfloat16)
    for copy in (*near_copies, *far_copies, *leaves):
        copy.wait()


def front(tokens, upstream, ids, gain_one, gain_two, w_q, w_k, w_v, w_o):
    rows, width = tokens.shape
    cosine, sine = (jnp.asarray(t).reshape(4, rows, 128) for t in place_tables(4 * rows))
    low, full = jnp.bfloat16, jnp.float32
    vmem, dma = pltpu.VMEM, pltpu.SemaphoreType.DMA
    every, three = (jax.ShapeDtypeStruct((n, rows, width), low) for n in (4, 3))
    own = jax.ShapeDtypeStruct((rows, width), low)
    spec, anywhere = pl.BlockSpec(memory_space=pltpu.VMEM), pl.BlockSpec(memory_space=pl.ANY)
    out_shape = [
        every, every, every, three, jax.ShapeDtypeStruct((3, 16, rows), low), own, own,
        jax.ShapeDtypeStruct((rows, width), full), own, jax.ShapeDtypeStruct((rows, 128), full),
    ]
    return pl.pallas_call(
        front_kernel,
        out_shape=out_shape,
        in_specs=[spec] * 5 + [anywhere] * 4 + [spec] * 2,
        out_specs=[anywhere] * 3 + [spec] * 7,
        scratch_shapes=[
            *[vmem((4, rows, width), low)] * 4, vmem((4, width, width), low), *[dma((3,))] * 2, *[dma((2,))] * 4,
            dma((4,)), dma((3,)),
        ],
        compiler_params=pltpu.CompilerParams(
            collective_id=2, has_side_effects=True, vmem_limit_bytes=58 * 2**20
        ),
        name="front",
    )(tokens, upstream, ids, gain_one, gain_two, w_q, w_k, w_v, w_o, cosine, sine)


def add_rows(target, first, second, step):
    rows = target.shape[0]

    def some(at):
        total = first[at, :].astype(jnp.float32) + second[at, :].astype(jnp.float32)
        target[at, :] = total.astype(target.dtype)

    if rows <= step:
        some(pl.ds(0, rows))
    else:

        def body(i, carry):
            some(pl.ds(pl.multiple_of(i * step, step), step))
            return carry

        lax.fori_loop(0, rows // step, body, 0)


class Piece:
    def __init__(self, place, whole, one, two, three, half, sems, step):
        self.s, self.x, self.k, self.to_core, self.to_x, self.to_y = place
        self.whole, self.one, self.two, self.three = whole, one, two, three
        self.half, self.sems, self.step = half, sems, step

    def copy(self, level, h=0):
        every, low, high = slice(None), pl.ds(0, self.half), pl.ds(self.half, self.half)
        if level == 1:
            src, dst, device = self.whole(1 - self.k), self.one(every, every, every), self.to_core
        elif level == 2:
            if h == 0:
                src, device = self.one(every, 1 - self.x, low), self.to_x
            else:
                src, device = self.one(1 - self.s, every, high), self.to_y
            dst = self.two(h, every)
        else:
            src = self.two(h, 1 - (self.s, self.x)[h])
            dst, device = self.three(h), (self.to_y, self.to_x)[h]
        ssem, rsem = self.sems(2 * (level - 1) - (1 if level > 1 else 0) + h)
        return pltpu.make_async_remote_copy(
            src_ref=src, dst_ref=dst, send_sem=ssem, recv_sem=rsem, device_id=device, device_id_type=MESH
        )

    def start(self, level):
        for h in range(1 if level == 1 else 2):
            self.copy(level, h).start()

    def finish(self, level):
        low, high = pl.ds(0, self.half), pl.ds(self.half, self.half)
        if level == 1:
            self.copy(1).wait()
            own = self.whole(self.k)
            for i in range(2):
                for j in range(2):
                    here = self.one(i, j, slice(None))
                    add_rows(here, here, own.at[i, j], self.step)
            return
        for h in range(2):
            self.copy(level, h).wait()
            if level == 2:
                for i in range(2):
                    here = self.two(h, i)
                    own = self.one(i, self.x, low) if h == 0 else self.one(self.s, i, high)
                    add_rows(here, here, own, self.step)
            else:
                here = self.three(h)
                add_rows(here, here, self.two(h, (self.s, self.x)[h]), self.step)


def gates_in(logits, named):
    masked = jnp.where(named, logits, -1e30)
    raised = jnp.where(named, jnp.exp(masked - jnp.max(masked, axis=-1, keepdims=True)), 0.0)
    return raised / jnp.sum(raised, axis=-1, keepdims=True)


def ffn_kernel(
    second, mixed, upstream_all, named_all, w_r, gain_two,
    e_gate, e_up, e_down, s_gate, s_up, s_down,
    results, d_mixed_out, small_out, eg_out, eu_out, ed_out, sg_out, su_out, sd_out,
    rows_all, last_up, last_named, d_res, res_acc, mix_acc, row_acc, row_send, row_got, dg_send, dg_got,
    router_w, own_shares, across, we_g, we_u, we_d, ws_g, ws_u, ws_d, wsem,
    ge_g, ge_u, ge_d, e1_g, e1_u, e1_d, e2_g, e2_u, e2_d,
    gs_g, gs_u, gs_d, s1_g, s1_u, s1_d, s2_g, s2_u, s2_d, s3_g, s3_u, s3_d, sd_got, square,
    es_sem, er_sem, ss_sem, sr_sem, xs_sem, xr_sem, us_sem, ur_sem, rs_sem, rr_sem, ds_sem, dr_sem, hs_sem, hr_sem,
):
    s, x, k, e, c, to_core, to_x, to_y, others = neighbours()
    place = (s, x, k, to_core, to_x, to_y)
    rows, width = second.shape
    tile = 8 * ge_d.shape[4]
    tiles, shared_tiles = e_gate.shape[1] // tile, gs_g.shape[4] // tile
    low, full = jnp.bfloat16, jnp.float32
    to_z = [(s, c, o) for o in others]
    owner_row, giver_row = 2 * e + s, 4 * s + c
    to_owner, giver = (owner_row // 4, owner_row % 4, c), (giver_row % 2, e, giver_row // 2)
    square[...] = jnp.zeros_like(square)
    elsewhere = jnp.where((owner_row == giver_row) & (c == e), 0, 1)

    def columns(f):
        return pl.ds(pl.multiple_of(f * tile, tile), tile)

    def fetches(f, shared):
        at = columns(f)
        if shared:
            sources, here, targets, n = (s_gate, s_up, s_down), columns(e * shared_tiles + f), (ws_g, ws_u, ws_d), f
        else:
            sources, here, targets, n = (e_gate, e_up, e_down), at, (we_g, we_u, we_d), shared_tiles + f
        return [
            pltpu.make_async_copy(sources[0].at[:, here], targets[0].at[:, at], wsem.at[n, 0]),
            pltpu.make_async_copy(sources[1].at[:, here], targets[1].at[:, at], wsem.at[n, 1]),
            pltpu.make_async_copy(sources[2].at[here, :], targets[2].at[at, :], wsem.at[n, 2]),
        ]

    for n in range(shared_tiles):
        for copy in fetches(n, True):
            copy.start()
    for n in range(tiles):
        for copy in fetches(n, False):
            copy.start()
    barrier = pltpu.get_barrier_semaphore()
    for device in (to_core, to_x, to_y, *to_z):
        pl.semaphore_signal(barrier, inc=1, device_id=device, device_id_type=MESH)

    @pl.when(elsewhere == 1)
    def _():
        for device in (to_owner, giver):
            pl.semaphore_signal(barrier, inc=1, device_id=device, device_id_type=MESH)

    pl.semaphore_wait(barrier, 6 + 2 * elsewhere)
    near_copy = start_copy(second, rows_all.at[1], xs_sem.at[0], xr_sem.at[0], to_z[0])
    far_copy = start_copy(second, rows_all.at[2], xs_sem.at[1], xr_sem.at[1], to_z[1])
    rows_all[0] = second[...]
    router_rows = w_r[...].astype(full)
    router_w[...] = jnp.concatenate([router_rows, jnp.zeros((128 - w_r.shape[0], width), full)], axis=0).T.astype(low)

    def piece_e(f, a):
        at = columns(f)
        sems = lambda n: (es_sem.at[f, a, n], er_sem.at[f, a, n])
        if a < 2:
            g, one, two, three = ((ge_g, e1_g, e2_g, eg_out), (ge_u, e1_u, e2_u, eu_out))[a]
            return Piece(
                place,
                lambda kk: g.at[:, :, kk, :, at],
                lambda i, j, r: one.at[i, j, r, at],
                lambda h, i: two.at[h, i, :, at],
                lambda h: three.at[h, :, at],
                g.shape[3] // 2, sems, 96,
            )
        return Piece(
            place,
            lambda kk: ge_d.at[f, :, :, kk],
            lambda i, j, r: e1_d.at[f, i, j, r],
            lambda h, i: e2_d.at[f, h, i],
            lambda h: ed_out.at[f, h],
            ge_d.shape[4] // 2, sems, 96,
        )

    def piece_s(a):
        g, one, two, three = (
            (gs_g, s1_g, s2_g, s3_g), (gs_u, s1_u, s2_u, s3_u), (gs_d, s1_d, s2_d, s3_d)
        )[a]
        return Piece(
            place,
            lambda kk: g.at[:, :, kk],
            lambda i, j, r: one.at[i, j, r],
            lambda h, i: two.at[h, i],
            lambda h: three.at[h],
            g.shape[3] // 2, lambda n: (ss_sem.at[a, n], sr_sem.at[a, n]), 48 if a < 2 else 64,
        )

    def branch(values, d_out, weights, f, result_acc, d_acc):
        at = columns(f)
        gate_w, up_w, down_w = weights[0][:, at], weights[1][:, at], weights[2][at, :]
        gate = jnp.dot(values, gate_w, preferred_element_type=full)
        up = jnp.dot(values, up_w, preferred_element_type=full)
        d_hidden = against(d_out, down_w)
        sigmoid = 1.0 / (1.0 + jnp.exp(-gate))
        silu = gate * sigmoid
        hidden = (silu * up).astype(low)
        d_gate = (d_hidden * up * (sigmoid * (1.0 + gate * (1.0 - sigmoid)))).astype(low)
        d_up = (d_hidden * silu).astype(low)
        result_acc[...] += jnp.dot(hidden, down_w, preferred_element_type=full)
        d_acc[...] += against(d_gate, gate_w) + against(d_up, up_w)
        return hidden, d_gate, d_up

    def onward():
        return [
            pltpu.make_async_remote_copy(
                src_ref=src, dst_ref=dst, send_sem=ssem, recv_sem=rsem, device_id=to_z[0], device_id_type=MESH
            )
            for src, dst, ssem, rsem in (
                (rows_all.at[2], rows_all.at[3], xs_sem.at[2], xr_sem.at[2]),
                (upstream_all.at[2], last_up, us_sem.at[0], ur_sem.at[0]),
                (named_all.at[2], last_named, us_sem.at[1], ur_sem.at[1]),
            )
        ]

    def turn(first, count, again, last):
        many = count * rows
        some = pl.ds(first, count)
        values = rows_all[some].reshape(many, width)
        if first == 3:
            d_rows, marks = last_up[...], [last_named[...]]
        else:
            d_rows = upstream_all[some].reshape(many, width)
            marks = [named_all[first + i] for i in range(count)]
        logits = jnp.dot(values, router_w[...], preferred_element_type=full)
        named = jnp.concatenate([named_lanes(m) for m in marks], axis=0)
        lane = lax.broadcasted_iota(jnp.int32, (many, 128), 1)
        gates = gates_in(logits, named)
        if first == 0:
            own_shares[...] = gates[0:rows]
        share = jnp.sum(jnp.where(lane == e, gates, 0.0), axis=-1, keepdims=True)
        d_res[0:many] = d_rows
        for total in (res_acc, mix_acc, row_acc):
            total[0:many] = jnp.zeros((many, width), full)
        across[:, 0:many] = values.T
        inside = pl.ds(0, many)

        def store(ref, index, term):
            if again:
                term = term + ref[index].astype(full)
            ref[index] = term.astype(low)

        def shared_tile(f, carry):
            if first == 0:
                for copy in fetches(f, True):
                    copy.wait()
            values, d_out = rows_all[some].reshape(many, width), d_res[0:many]
            hidden, d_gate, d_up = branch(
                values, d_out, (ws_g, ws_u, ws_d), f, mix_acc.at[inside], row_acc.at[inside]
            )
            turned = across[:, 0:many]
            index = (slice(None), slice(None), slice(None), slice(None), columns(f))
            store(gs_g, index, product(turned, d_gate).reshape(2, 2, 2, width // 8, tile))
            store(gs_u, index, product(turned, d_up).reshape(2, 2, 2, width // 8, tile))
            term, quarter, half = outer_sum(hidden, d_out), width // 4, gs_d.shape[3]
            for i in range(tile // (2 * half)):
                for q in range(4):
                    for h in range(2):
                        top = (2 * i + h) * half
                        store(
                            gs_d,
                            (f * (tile // (2 * half)) + i, q // 2, q % 2, slice(None), slice(h * quarter, (h + 1) * quarter)),
                            term[top : top + half, q * quarter : (q + 1) * quarter],
                        )
            return carry

        def expert_tile(f, carry):
            if first == 0:
                for copy in fetches(f, False):
                    copy.wait()
            values, d_out = rows_all[some].reshape(many, width), d_res[0:many]
            hidden, d_gate, d_up = branch(
                values, d_out, (we_g, we_u, we_d), f, res_acc.at[inside], row_acc.at[inside]
            )
            turned = across[:, 0:many]
            index = (slice(None), slice(None), slice(None), slice(None), columns(f))
            store(ge_g, index, product(turned, d_gate).reshape(2, 2, 2, width // 8, tile))
            store(ge_u, index, product(turned, d_up).reshape(2, 2, 2, width // 8, tile))
            store(ge_d, (f,), outer_sum(hidden, d_out).reshape(2, 2, 2, tile // 8, width))
            if first == 1:

                @pl.when(f == tiles // 8)
                def _():
                    far_copy.wait()
                    for copy in onward():
                        copy.start()

            if last:
                for a in range(3):
                    piece_e(f, a).start(1)

                @pl.when(f == 0)
                def _():
                    for a in range(3):
                        piece_s(a).finish(1)
                        piece_s(a).start(2)

                @pl.when(f > 0)
                def _():
                    for a in range(3):
                        piece_e(f - 1, a).finish(1)
                        piece_e(f - 1, a).start(2)

                @pl.when(f == tiles - 1)
                def _():
                    for a in range(3):
                        piece_s(a).finish(2)
                        piece_s(a).start(3)

            return carry

        lax.fori_loop(0, shared_tiles, shared_tile, 0)
        if last:
            for a in range(3):
                piece_s(a).start(1)
        d_res[0:many] = (share * d_rows.astype(full)).astype(low)
        lax.fori_loop(0, tiles, expert_tile, 0)
        low_result = res_acc[0:many].astype(low)
        results[some] = (mix_acc[0:many] + share * low_result.astype(full)).astype(low).reshape(count, rows, width)
        row_send[some] = row_acc[0:many].astype(low).reshape(count, rows, width)
        terms = low_result.astype(full) * d_rows.astype(full)
        high = terms.astype(low)
        ones = jnp.ones((8, width), low)
        sums = against(ones, high) + against(ones, (terms - high.astype(full)).astype(low))
        for i in range(count):
            dg_send[first + i] = sums[:, i * rows : (i + 1) * rows]

    back_copies = []
    turn(0, 1, False, False)
    near_copy.wait()
    turn(1, 1, True, False)
    back_copies.append(start_copy(row_send.at[1], row_got.at[0], rs_sem.at[0], rr_sem.at[0], to_z[0]))
    turn(2, 1, True, False)
    back_copies.append(start_copy(row_send.at[2], row_got.at[1], rs_sem.at[1], rr_sem.at[1], to_z[1]))
    for copy in onward():
        copy.wait()
    turn(3, 1, True, True)
    back_copies.append(start_copy(row_send.at[3], row_got.at[2], rs_sem.at[2], rr_sem.at[2], to_z[2]))
    for i in range(3):
        back_copies.append(start_copy(dg_send.at[i + 1], dg_got.at[i], ds_sem.at[i], dr_sem.at[i], to_z[i]))
    for a in range(3):
        piece_e(tiles - 1, a).finish(1)
        piece_e(tiles - 1, a).start(2)

    def third(f, carry):
        for a in range(3):
            piece_e(f, a).finish(2)
            piece_e(f, a).start(3)
        return carry

    lax.fori_loop(0, tiles, third, 0)
    for a in range(3):
        piece_s(a).finish(3)

    @pl.when(elsewhere == 1)
    def _():
        start_copy(s3_d, sd_got, hs_sem, hr_sem, to_owner)

    @pl.when(elsewhere == 0)
    def _():
        sd_got[...] = s3_d[...]

    for h in range(2):
        part = pl.ds(h * s3_g.shape[1], s3_g.shape[1])
        sg_out[part] = s3_g[h].astype(full)
        su_out[part] = s3_u[h].astype(full)

    for copy in back_copies:
        copy.wait()
    total = row_send[0].astype(full)
    for i in range(3):
        total = total + row_got[i].astype(full)
    expert_row = lax.broadcasted_iota(jnp.int32, (8, rows), 0)
    d_gates = jnp.where(expert_row == e, dg_send[0], 0.0)
    for i in range(3):
        d_gates = jnp.where(expert_row == others[i], dg_got[i], d_gates)
    d_gates = jnp.concatenate([d_gates, jnp.zeros((120, rows), full)], axis=0).T
    shares = own_shares[...]
    d_logits = (shares * (d_gates - jnp.sum(shares * d_gates, axis=-1, keepdims=True))).astype(low)
    total = total + against(d_logits, router_w[...])
    router = outer_sum(d_logits, second[...])
    values = mixed[...]
    inverse = lax.rsqrt(jnp.mean(values * values, axis=-1, keepdims=True) + 1e-06)
    unit = values * inverse
    small_out[0:8, :] = router[0:8, :]
    small_out[8:16, :] = jnp.broadcast_to(jnp.sum(total * unit, axis=0, keepdims=True), (8, width))
    inner = total * gain_two[...].reshape(1, width)
    mean = jnp.mean(inner * unit, axis=-1, keepdims=True)
    d_mixed_out[...] = upstream_all[0].astype(full) + inverse * (inner - unit * mean)

    def done(f, carry):
        for a in range(3):
            piece_e(f, a).finish(3)
        return carry

    lax.fori_loop(0, tiles, done, 0)

    @pl.when(elsewhere == 1)
    def _():
        pltpu.make_async_remote_copy(
            src_ref=s3_d, dst_ref=sd_got, send_sem=hs_sem, recv_sem=hr_sem, device_id=to_owner, device_id_type=MESH
        ).wait()

    quarter, half = width // 4, s3_d.shape[1]
    for h in range(2):
        for i in range(2):
            top = h * 2 * half + i * half
            square[top : top + half, 0:quarter] = sd_got[i, :, h * quarter : (h + 1) * quarter].astype(full)
    sd_out[...] = square[...].T[0:quarter, :]


def ffn(second, mixed, upstream_all, named_all, w_router, gain_two, experts, shared):
    rows, width = second.shape
    hidden = experts[0].shape[1]
    slice_width = shared[0].shape[1] // 4
    tile = 512
    tiles = hidden // tile
    low, full = jnp.bfloat16, jnp.float32
    dma = pltpu.SemaphoreType.DMA
    ninth, small, half = width // 8, tile // 8, slice_width // 4

    def vm(*shape, dtype=low):
        return pltpu.VMEM(shape, dtype)

    def out(*shape, dtype=low):
        return jax.ShapeDtypeStruct(shape, dtype)

    spec = pl.BlockSpec(memory_space=pltpu.VMEM)
    out_shape = [
        out(4, rows, width), out(rows, width, dtype=full), out(16, width, dtype=full),
        out(2, ninth // 2, hidden), out(2, ninth // 2, hidden), out(tiles, 2, small // 2, width),
        out(ninth, slice_width, dtype=full), out(ninth, slice_width, dtype=full), out(width // 4, 2 * half, dtype=full),
    ]
    scratch = [
        vm(4, rows, width), vm(rows, width), vm(16, rows), vm(rows, width), *[vm(rows, width, dtype=full)] * 3,
        vm(4, rows, width), vm(3, rows, width), vm(4, 8, rows, dtype=full), vm(3, 8, rows, dtype=full),
        vm(width, 128), vm(rows, 128, dtype=full), vm(width, rows),
        *[vm(width, hidden)] * 2, vm(hidden, width), *[vm(width, slice_width)] * 2, vm(slice_width, width),
        dma(((hidden + slice_width) // tile, 3)),
        *[vm(2, 2, 2, ninth, hidden)] * 2, vm(tiles, 2, 2, 2, small, width),
        *[vm(2, 2, ninth, hidden)] * 2, vm(tiles, 2, 2, small, width),
        *[vm(2, 2, ninth // 2, hidden)] * 2, vm(tiles, 2, 2, small // 2, width),
        *[vm(2, 2, 2, ninth, slice_width)] * 2, vm(2, 2, 2, half, width // 2),
        *[vm(2, 2, ninth, slice_width)] * 2, vm(2, 2, half, width // 2),
        *[vm(2, 2, ninth // 2, slice_width)] * 2, vm(2, 2, half // 2, width // 2),
        *[vm(2, ninth // 2, slice_width)] * 2, vm(2, half // 2, width // 2), vm(2, half // 2, width // 2),
        vm(2 * half, 2 * half, dtype=full),
        *[dma((tiles, 3, 5))] * 2, *[dma((3, 5))] * 2, *[dma((3,))] * 2, *[dma((2,))] * 2, *[dma((3,))] * 4, dma, dma,
    ]
    return pl.pallas_call(
        ffn_kernel,
        out_shape=out_shape,
        in_specs=[spec] * 6 + [pl.BlockSpec(memory_space=pl.ANY)] * 6,
        out_specs=[spec] * len(out_shape),
        scratch_shapes=scratch,
        compiler_params=pltpu.CompilerParams(
            collective_id=3, has_side_effects=True, vmem_limit_bytes=60 * 2**20
        ),
        name="ffn",
    )(second, mixed, upstream_all, named_all, w_router.T, gain_two, *experts, *shared)


def back_kernel(
    eg_own, eu_own, ed_own, small, results, mixed,
    tokens, gain_one, d_mixed, attended, normed, log_sum, cosine, sine, w_o_hbm, q_hbm, k_hbm, v_hbm, w_q_hbm, w_k_hbm, w_v_hbm,
    eg_all, eu_all, ed_all, q_out, k_out, v_out, o_out, one_out, two_out, router_out, output, token_out,
    grads, d_att, d_all, stats, stat_col, sum_q, sum_k, sum_v, misc_in, misc_out, far_sum, turned, asem, arem, tsem, trem,
    one, two, three, z_flat, got_flat, misc_got, result_got,
    w_o, q_all, k_all, v_all, w_q, w_k, w_v, hsem,
    lsem, gsem, grem, csem, crem, psem, prem, zsem, zrem, msem, mrem, rsem, rrem,
):
    s, x, k, e, c, to_core, to_x, to_y, others = neighbours()
    place = (s, x, k, to_core, to_x, to_y)
    to_z = [(s, c, o) for o in others]
    low, full = jnp.bfloat16, jnp.float32
    loads = [
        pltpu.make_async_copy(src, dst, hsem.at[i])
        for i, (src, dst) in enumerate(
            (
                (w_o_hbm, w_o), (q_hbm, q_all), (k_hbm, k_all), (v_hbm, v_all),
                (w_q_hbm, w_q), (w_k_hbm, w_k), (w_v_hbm, w_v),
            )
        )
    ]
    for load in loads:
        load.start()
    greet([to_core, to_x, to_y, *to_z])

    def piece(a):
        g = grads.at[a]
        return Piece(
            place,
            lambda kk: g.at[:, :, kk],
            lambda i, j, r: one.at[a, i, j, r],
            lambda h, i: two.at[a, h, i],
            lambda h: three.at[a, h],
            g.shape[3] // 2, lambda n: (psem.at[a, n], prem.at[a, n]), 48,
        )

    rows, width = tokens.shape
    heads = width // HEAD_DIM
    d_att[...] = d_mixed[...].astype(low)
    loads[0].wait()
    d_all[c] = against(d_att[...], w_o[...]).astype(low)
    head_of = lax.broadcasted_iota(jnp.int32, (128, width), 1) // HEAD_DIM
    chosen = jnp.where(head_of == lax.broadcasted_iota(jnp.int32, (128, width), 0), 1.0, 0.0).astype(low)
    terms = d_all[c].astype(full) * attended[...].astype(full)
    high = terms.astype(low)
    rest = (terms - high.astype(full)).astype(low)
    stat_col[0] = log_sum[...]
    stat_col[1] = against(high, chosen) + against(rest, chosen)
    stats[c, 0] = log_sum[...].T[0:16, :]
    stats[c, 1] = (against(chosen[0:16], high) + against(chosen[0:16], rest))
    core_copies = [
        start_copy(d_all.at[c], d_all.at[c], asem.at[0], arem.at[0], to_core),
        start_copy(stats.at[c], stats.at[c], tsem.at[0], trem.at[0], to_core),
    ]
    x_copies = [
        start_copy(d_all.at[c], d_all.at[c], asem.at[1], arem.at[1], to_x),
        start_copy(stats.at[c], stats.at[c], tsem.at[1], trem.at[1], to_x),
    ]
    near_place, far_place, opposite_place = others
    result_copies = [
        start_copy(results.at[1], result_got.at[0], rsem.at[0], rrem.at[0], to_z[0]),
        start_copy(results.at[3], result_got.at[1], rsem.at[1], rrem.at[1], to_z[0]),
    ]

    def block(a, h, ss, xx):
        whole = (eg_all, eu_all, ed_all)[a]
        half = whole.shape[-2] // 2
        part = pl.ds(h * half, half)
        return whole.at[ss, xx, k, part] if a < 2 else whole.at[:, ss, xx, k, part]

    def own_block(a, h):
        own = (eg_own, eu_own, ed_own)[a]
        return own.at[h] if a < 2 else own.at[:, h]

    def to_both_cores(a, h, n, src, spot):
        core_parts.append(start_copy(src, spot, csem.at[a, h, n], crem.at[a, h, n], to_core))

    core_parts, near, wide, kept = [], [], [], []
    parts = [(a, h) for a in range(3) for h in range(2)]

    def spread(own, buffer, first):
        halves, height, across = own.shape
        piece_width = across // 4
        for h in range(halves):
            for q in range(4):
                part = own[h, :, q * piece_width : (q + 1) * piece_width]
                buffer[q, pl.ds(h * height, height), first : first + piece_width] = part

    def to_nearest(buffer, got, number):
        return [
            start_copy(buffer.at[near_place], got.at[0], zsem.at[number, 0], zrem.at[number, 0], to_z[0]),
            start_copy(buffer.at[opposite_place], got.at[1], zsem.at[number, 1], zrem.at[number, 1], to_z[0]),
        ]

    def to_far(copies, buffer, got, number):
        for copy in copies:
            copy.wait()
        buffer[far_place] = (buffer[far_place].astype(full) + got[1].astype(full)).astype(low)
        return start_copy(buffer.at[far_place], got.at[2], zsem.at[number, 2], zrem.at[number, 2], to_z[1])

    def settled(copy, buffer, got):
        copy.wait()
        return buffer[e].astype(full) + got[0].astype(full) + got[2].astype(full)

    for a, h in parts:
        src, here = own_block(a, h), block(a, h, s, x)
        kept.append(pltpu.make_async_copy(src, here, lsem.at[a, h]))
        kept[-1].start()
        to_both_cores(a, h, 0, src, here)

    def put(a, first_factor, second_factor):
        grads[a] = outer_sum(first_factor, second_factor).astype(low).reshape(2, 2, 2, width // 8, width)
        piece(a).start(1)

    put(3, attended[...], d_att[...])
    for load in loads[1:]:
        load.wait()
    lane = lax.broadcasted_iota(jnp.int32, (rows, 128), 1)
    scale = HEAD_DIM**-0.5
    for total in (sum_q, sum_k, sum_v):
        total[...] = jnp.zeros_like(total)

    def inside(h, values):
        return jnp.where((lane // HEAD_DIM) == h, values, jnp.zeros_like(values))

    def columns(g):
        return pl.ds(pl.multiple_of(g * 128, 128), 128)

    def query_pair(g, carry):
        at = columns(g)
        q, d_out = q_all[c, :, at], d_all[c, :, at]
        sides = []
        for h in range(2):
            pick = lane == 2 * g + h
            sides.append(
                (
                    inside(h, q),
                    inside(h, d_out),
                    jnp.sum(jnp.where(pick, stat_col[0], 0.0), axis=-1, keepdims=True),
                    jnp.sum(jnp.where(pick, stat_col[1], 0.0), axis=-1, keepdims=True),
                )
            )
        for j in range(4):

            @pl.when(j <= c)
            def _(j=j):
                keys, values = k_all[j, :, at], v_all[j, :, at]
                terms = []
                for q_side, d_side, log_total, delta in sides:
                    weights = jnp.exp(against(q_side, keys) * scale - log_total)
                    d_scores = (weights * (against(d_side, values) - delta)).astype(low)
                    terms.append(jnp.dot(d_scores, keys, preferred_element_type=full))
                sum_q[:, at] += jnp.where(lane < HEAD_DIM, terms[0], terms[1])

        return carry

    for a, h in parts:
        src, here = own_block(a, h), block(a, h, s, x)
        near.append(start_copy(src, here, gsem.at[a, h, 0], grem.at[a, h, 0], (to_y, to_x)[h]))
    lax.fori_loop(0, width // 128, query_pair, 0)
    for a, h in parts:
        src, here = own_block(a, h), block(a, h, s, x)
        wide.append(start_copy(src, here, gsem.at[a, h, 1], grem.at[a, h, 1], (to_x, to_y)[h]))
    for copy in result_copies:
        copy.wait()
    far_sum[...] = (results[2].astype(full) + result_got[1].astype(full)).astype(low)
    result_copy = start_copy(far_sum, result_got.at[2], rsem.at[2], rrem.at[2], to_z[1])

    def key_side(j):
        @pl.when(j >= c)
        def _():
            def key_pair(g, carry):
                at = columns(g)
                keys, values = k_all[c, :, at], v_all[c, :, at]
                q, d_out = q_all[j, :, at], d_all[j, :, at]
                terms = []
                for h in range(2):
                    log_total = stats[j, 0, pl.ds(2 * g + h, 1), :]
                    delta = stats[j, 1, pl.ds(2 * g + h, 1), :]
                    weights = jnp.exp(against(inside(h, keys), q) * scale - log_total)
                    d_scores = (weights * (against(inside(h, values), d_out) - delta)).astype(low)
                    terms.append(
                        (
                            jnp.dot(d_scores, q, preferred_element_type=full),
                            jnp.dot(weights.astype(low), d_out, preferred_element_type=full),
                        )
                    )
                sum_k[:, at] += jnp.where(lane < HEAD_DIM, terms[0][0], terms[1][0])
                sum_v[:, at] += jnp.where(lane < HEAD_DIM, terms[0][1], terms[1][1])
                return carry

            lax.fori_loop(0, width // 128, key_pair, 0)

    def turned_back(total):
        parts = []
        for g in range(width // 128):
            part = total[:, g * 128 : (g + 1) * 128] * scale
            parts.append((part * cosine[c] - swapped(part) * sine[c]).astype(low))
        return jnp.concatenate(parts, axis=1)

    key_side(c)
    d_query = turned_back(sum_q)
    put(0, normed[...], d_query)
    d_normed = against(d_query, w_q[...])
    piece(3).finish(1)
    piece(3).start(2)
    for copy in core_copies:
        copy.wait()
    key_side(x * 2 + (1 - k))
    for copy in x_copies:
        copy.wait()
    there = (1 - x) * 2 + k
    corner_copies = [
        start_copy(d_all.at[there], d_all.at[there], asem.at[2], arem.at[2], to_core),
        start_copy(stats.at[there], stats.at[there], tsem.at[2], trem.at[2], to_core),
    ]
    key_side(there)
    for i, (a, h) in enumerate(parts):
        near[i].wait()
        spot = block(a, h, (1 - s, s)[h], (x, 1 - x)[h])
        to_both_cores(a, h, 1, spot, spot)
    for copy in corner_copies:
        copy.wait()
    key_side((1 - x) * 2 + (1 - k))
    d_key = turned_back(sum_k)
    put(1, normed[...], d_key)
    d_value = sum_v[...].astype(low)
    put(2, normed[...], d_value)
    piece(0).finish(1)
    piece(0).start(2)
    d_normed = d_normed + against(d_key, w_k[...]) + against(d_value, w_v[...])
    values = tokens[...].astype(full)
    inverse = lax.rsqrt(jnp.mean(values * values, axis=-1, keepdims=True) + 1e-06)
    unit = values * inverse
    misc_in[0:8, :] = small[0:8, :]
    misc_in[8:9, :] = jnp.sum(d_normed * unit, axis=0, keepdims=True)
    misc_in[9:10, :] = small[8:9, :]
    misc_in[10:16, :] = jnp.zeros((6, width), full)
    misc_copy = start_copy(misc_in, misc_got.at[0], msem.at[0], mrem.at[0], to_core)
    for a in (1, 2):
        piece(a).finish(1)
        piece(a).start(2)
    inner = d_normed * gain_one[...].reshape(1, width)
    mean = jnp.mean(inner * unit, axis=-1, keepdims=True)
    token_out[...] = d_mixed[...] + inverse * (inner - unit * mean)
    misc_copy.wait()
    misc_out[...] = misc_in[...] + misc_got[0]
    misc_copy = start_copy(misc_out, misc_got.at[1], msem.at[1], mrem.at[1], to_x)
    for a in (3, 0, 1, 2):
        piece(a).finish(2)
        piece(a).start(3)
    misc_copy.wait()
    misc_got[3] = misc_out[...] + misc_got[1]
    misc_copy = start_copy(misc_got.at[3], misc_got.at[2], msem.at[2], mrem.at[2], to_y)
    onward = []
    for a, h in parts:
        spot = block(a, h, (1 - s, s)[h], (x, 1 - x)[h])
        onward.append(start_copy(spot, spot, gsem.at[a, h, 2], grem.at[a, h, 2], (to_x, to_y)[h]))
    z_copies = []
    for number, pair in enumerate(((3, 0), (1, 2))):
        for i, a in enumerate(pair):
            piece(a).finish(3)
            spread(three.at[a], z_flat.at[number], i * (width // 4))
        z_copies.append(to_nearest(z_flat.at[number], got_flat.at[number], number))
    misc_copy.wait()
    misc_got[4] = misc_got[3] + misc_got[2]
    misc_copies = [
        start_copy(misc_got.at[4], misc_got.at[5 + i], msem.at[3 + i], mrem.at[3 + i], to_z[i]) for i in range(3)
    ]
    for i, (a, h) in enumerate(parts):
        wide[i].wait()
        spot = block(a, h, (s, 1 - s)[h], (1 - x, x)[h])
        to_both_cores(a, h, 2, spot, spot)
    for number in range(2):
        z_copies[number] = to_far(z_copies[number], z_flat.at[number], got_flat.at[number], number)

    result_copy.wait()
    total = mixed[...] + results[0].astype(full) + result_got[0].astype(full) + result_got[2].astype(full)
    output[...] = total.astype(low)
    for i, (a, h) in enumerate(parts):
        onward[i].wait()
        spot = block(a, h, 1 - s, 1 - x)
        to_both_cores(a, h, 3, spot, spot)
    for copy in misc_copies:
        copy.wait()
    sums = misc_got[4] + misc_got[5] + misc_got[6] + misc_got[7]
    one_out[...] = sums[8:9, :].reshape(width)
    two_out[...] = sums[9:10, :].reshape(width)
    mine = jnp.where(lax.broadcasted_iota(jnp.int32, (16, width), 0) == e, sums, 0.0)
    turned[...] = jnp.concatenate([mine, jnp.zeros((112, width), full)], axis=0).T
    high = router_out.shape[1]
    router_rows = turned[pl.ds(pl.multiple_of((s * 4 + c) * high, high), high), :]
    column = jnp.broadcast_to(jnp.sum(router_rows, axis=-1, keepdims=True), (high, 128))
    column = jnp.concatenate([column, jnp.zeros((128 - high, 128), full)], axis=0).T
    router_out[...] = column[0:1, 0:high]
    quarter = width // 4
    for number, targets in enumerate(((o_out, q_out), (k_out, v_out))):
        total = settled(z_copies[number], z_flat.at[number], got_flat.at[number])
        targets[0][...] = total[:, 0:quarter]
        targets[1][...] = total[:, quarter:]
    for copy in (*kept, *core_parts):
        copy.wait()


def back(expert_own, small, results, mixed, tokens, gain_one, d_mixed, kept, weights):
    low, full = jnp.bfloat16, jnp.float32
    dma = pltpu.SemaphoreType.DMA
    rows, width = mixed.shape
    ninth = width // 8
    hidden = expert_own[0].shape[2]
    tiles, unused, short, unused = expert_own[2].shape
    cosine, sine = (jnp.asarray(t).reshape(4, rows, 128) for t in place_tables(4 * rows))

    def vm(*shape, dtype=low):
        return pltpu.VMEM(shape, dtype)

    def out(*shape, dtype=low):
        return jax.ShapeDtypeStruct(shape, dtype)

    spec, anywhere = pl.BlockSpec(memory_space=pltpu.VMEM), pl.BlockSpec(memory_space=pl.ANY)
    out_shape = [
        out(2, 2, 2, ninth, hidden), out(2, 2, 2, ninth, hidden), out(tiles, 2, 2, 2, 2 * short, width),
        *[out(ninth, width // 4, dtype=full)] * 4, out(width, dtype=full), out(width, dtype=full),
        out(1, ninth, dtype=full), out(rows, width),
        out(rows, width, dtype=full),
    ]
    scratch = [
        vm(4, 2, 2, 2, ninth, width), vm(rows, width), vm(4, rows, width), vm(4, 2, 16, rows, dtype=full),
        vm(2, rows, 128, dtype=full), *[vm(rows, width, dtype=full)] * 3, vm(16, width, dtype=full),
        vm(16, width, dtype=full), vm(rows, width), vm(width, 128, dtype=full),
        dma((3,)), dma((3,)), dma((3,)), dma((3,)),
        vm(4, 2, 2, ninth, width), vm(4, 2, 2, ninth // 2, width), vm(4, 2, ninth // 2, width),
        vm(2, 4, ninth, width // 2),
        vm(2, 3, ninth, width // 2),
        vm(8, 16, width, dtype=full), vm(3, rows, width),
        vm(width, width), *[vm(4, rows, width)] * 3, *[vm(width, width)] * 3, dma((7,)),
        dma((3, 2)), *[dma((3, 2, 3))] * 2, *[dma((3, 2, 4))] * 2, *[dma((4, 5))] * 2, *[dma((2, 3))] * 2,
        dma((6,)), dma((6,)), dma((3,)), dma((3,)),
    ]
    attended, normed, q_all, k_all, v_all, log_sum = kept
    w_q, w_k, w_v, w_o = weights
    operands = (
        *expert_own, small, results, mixed, tokens, gain_one, d_mixed, attended, normed, log_sum, cosine, sine,
        w_o, q_all, k_all, v_all, w_q, w_k, w_v,
    )
    return pl.pallas_call(
        back_kernel,
        out_shape=out_shape,
        in_specs=[spec] * (len(operands) - 7) + [anywhere] * 7,
        out_specs=[anywhere] * 3 + [spec] * 9,
        scratch_shapes=scratch,
        compiler_params=pltpu.CompilerParams(
            collective_id=4, has_side_effects=True, vmem_limit_bytes=60 * 2**20
        ),
        name="back",
    )(*operands)


def finish_kernel(*refs):
    count = len(refs) // 2
    for i in range(3):
        refs[count + i][...] = refs[i][...].astype(jnp.float32)

    @pl.when(pl.program_id(0) == 0)
    def _():
        for i in range(3, count):
            refs[count + i][...] = refs[i][...]


def finish(expert_grads, others):
    steps = 8
    arrays = (*expert_grads, *others)

    def tile_of(a):
        return pl.BlockSpec((a.shape[0] // steps, a.shape[1]), lambda i: (i, 0))

    def all_of(a):
        return pl.BlockSpec(a.shape, lambda i: (0,) * a.ndim)

    specs = [tile_of(a) for a in expert_grads] + [all_of(a) for a in others]
    return pl.pallas_call(
        finish_kernel,
        out_shape=[jax.ShapeDtypeStruct(a.shape, jnp.float32) for a in expert_grads]
        + [jax.ShapeDtypeStruct(a.shape, a.dtype) for a in others],
        grid=(steps,),
        in_specs=specs,
        out_specs=specs,
        compiler_params=pltpu.CompilerParams(vmem_limit_bytes=60 * 2**20),
        name="finish",
    )(*arrays)


def per_device_dense(
    tokens,
    expert_ids,
    norm_one,
    w_query,
    w_key,
    w_value,
    w_out,
    norm_two,
    w_router,
    expert_gate,
    expert_up,
    expert_down,
    shared_gate,
    shared_up,
    shared_down,
    cotangent,
):
    upstream = cotangent[0]
    ids = expert_ids[0].T
    (
        q_all, k_all, v_all, upstream_all, named_all, normed, attended, mixed, second, log_sum,
    ) = front(
        tokens[0], upstream, ids, norm_one, norm_two, w_query, w_key, w_value, w_out
    )
    (
        results, d_mixed, small, eg_own, eu_own, ed_own, sg, su, sd,
    ) = ffn(
        second, mixed, upstream_all, named_all, w_router, norm_two,
        (expert_gate[0], expert_up[0], expert_down[0]), (shared_gate, shared_up, shared_down),
    )

    (
        eg, eu, ed, gq, gk, gv, go, grad_one, grad_two, router, output, grad_tokens,
    ) = back(
        (eg_own, eu_own, ed_own), small, results, mixed, tokens[0], norm_one, d_mixed,
        (attended, normed, q_all, k_all, v_all, log_sum), (w_query, w_key, w_value, w_out),
    )
    width = tokens.shape[2]
    (
        eg, eu, ed, output, grad_tokens, gq, gk, gv, go, grad_one, grad_two, router, sg, su, sd,
    ) = finish(
        (eg.reshape(width, -1), eu.reshape(width, -1), ed.reshape(-1, width)),
        (output, grad_tokens, gq, gk, gv, go, grad_one, grad_two, router, sg, su, sd),
    )
    return (
        output[None], grad_tokens[None], grad_one, gq, gk, gv, go, grad_two, router.T,
        eg[None], eu[None], ed[None], sg, su, sd.T,
    )


def fits(mesh):
    return dict(mesh.shape) == {"seq": 2, "ctx": 4, "exp": 4}


def solution(mesh):
    per_device = per_device_dense if fits(mesh) else per_device_slots
    in_specs = (
        P(("seq", "exp"), "ctx", None),
        P(("seq", "exp"), "ctx", None),
        P(),
        P(),
        P(),
        P(),
        P(),
        P(),
        P(),
        P("exp", None, None),
        P("exp", None, None),
        P("exp", None, None),
        P(),
        P(),
        P(),
        P(("seq", "exp"), "ctx", None),
    )
    out_specs = (
        P(("seq", "exp"), "ctx", None),
        P(("seq", "exp"), "ctx", None),
        P(),
        P(("seq", "ctx"), "exp"),
        P(("seq", "ctx"), "exp"),
        P(("seq", "ctx"), "exp"),
        P(("seq", "ctx"), "exp"),
        P(),
        P(("seq", "ctx"), "exp"),
        P("exp", None, None),
        P("exp", None, None),
        P("exp", None, None),
        P(("seq", "ctx"), "exp"),
        P(("seq", "ctx"), "exp"),
        P(("seq", "ctx"), "exp"),
    )
    return jax.shard_map(
        per_device, mesh=mesh, in_specs=in_specs, out_specs=out_specs, check_vma=False
    )
```

```python
import functools
import math

import jax
import jax.numpy as jnp
import numpy as np
from jax import lax
from jax.experimental import pallas as pl
from jax.experimental.pallas import tpu as pltpu
from jax.sharding import PartitionSpec as P

HEAD_DIM = 64
TOP = 2
BLOCK = 256
KEY_ROWS = 512
MESH = pl.DeviceIdType.MESH


def product(first_factor, second_factor):
    return jnp.dot(first_factor, second_factor, preferred_element_type=jnp.float32)


def against(first_factor, second_factor):
    return lax.dot_general(
        first_factor, second_factor, (((1,), (1,)), ((), ())), preferred_element_type=jnp.float32
    )


def outer_sum(first_factor, second_factor):
    return lax.dot_general(
        first_factor, second_factor, (((0,), (0,)), ((), ())), preferred_element_type=jnp.float32
    )


def normalize(values, scaling):
    return values * lax.rsqrt(jnp.mean(values * values, axis=-1, keepdims=True) + 1e-06) * scaling


def rotate(values, places):
    halfway = values.shape[-1] // 2
    frequency = 10000.0 ** (-jnp.arange(halfway, dtype=jnp.float32) / halfway)
    angles = places.astype(jnp.float32)[:, None] * frequency[None, :]
    cosine = jnp.cos(angles)[:, None, :]
    sine_part = jnp.sin(angles)[:, None, :]
    former = values[..., :halfway]
    latter = values[..., halfway:]
    return jnp.concatenate(
        [former * cosine - latter * sine_part, latter * cosine + former * sine_part], axis=-1
    )


def silu_parts(gate_pre):
    sigmoid_value = jax.nn.sigmoid(gate_pre)
    return (gate_pre * sigmoid_value, sigmoid_value * (1.0 + gate_pre * (1.0 - sigmoid_value)))


def tiled(matrix, row_groups, col_groups):
    row_count, col_count = matrix.shape
    blocks = matrix.reshape(
        row_groups, row_count // row_groups, col_groups, col_count // col_groups
    ).transpose(0, 2, 1, 3)
    return blocks.reshape(col_groups * row_count, col_count // col_groups)


def per_device_slots(
    tokens,
    expert_ids,
    norm_one,
    w_query,
    w_key,
    w_value,
    w_out,
    norm_two,
    w_router,
    expert_gate,
    expert_up,
    expert_down,
    shared_gate,
    shared_up,
    shared_down,
    cotangent,
):
    local_rows = tokens.shape[1]
    model_width = tokens.shape[2]
    head_count = model_width // HEAD_DIM
    score_scale = HEAD_DIM ** (-0.5)
    ctx_count = lax.axis_size("ctx")
    ctx_place = lax.axis_index("ctx")
    exp_count = lax.axis_size("exp")
    row_groups = lax.axis_size("seq") * ctx_count
    local_experts = expert_gate.shape[0]
    experts_all = local_experts * exp_count
    capacity = min(local_rows, 2 * TOP * local_rows // experts_all)
    places = ctx_place * local_rows + jnp.arange(local_rows, dtype=jnp.int32)
    query_blocks = places // BLOCK

    def spread(matrix):
        return tiled(matrix, row_groups, exp_count)

    inputs = tokens[0].astype(jnp.float32)
    normed_full, norm_one_pull = jax.vjp(normalize, inputs, norm_one)
    normed = normed_full.astype(jnp.bfloat16)
    query = rotate(
        product(normed, w_query).reshape(local_rows, head_count, HEAD_DIM), places
    ).astype(jnp.bfloat16)
    keys_local = (
        rotate(product(normed, w_key).reshape(local_rows, head_count, HEAD_DIM), places)
        .astype(jnp.bfloat16)
        .reshape(local_rows, model_width)
    )
    values_local = product(normed, w_value).astype(jnp.bfloat16)

    def block_scores(key_block, offset):
        key_heads = key_block.reshape(-1, head_count, HEAD_DIM)
        scores = (
            jnp.einsum("qhd,khd->hqk", query, key_heads, preferred_element_type=jnp.float32)
            * score_scale
        )
        key_index = (offset + jnp.arange(key_block.shape[0], dtype=jnp.int32)) // BLOCK
        allowed = key_index[None, :] <= query_blocks[:, None]
        return (scores, allowed)

    def attend_block(running, key_block, value_block, offset):
        highest, totals, accumulated = running
        scores, allowed = block_scores(key_block, offset)
        masked = jnp.where(allowed[None], scores, -1e30)
        fresh = jnp.maximum(highest, jnp.max(masked, axis=-1))
        weights = jnp.where(allowed[None], jnp.exp(masked - fresh[..., None]), 0.0)
        decay = jnp.exp(highest - fresh)
        value_heads = value_block.reshape(-1, head_count, HEAD_DIM)
        accumulated = accumulated * decay[..., None] + jnp.einsum(
            "hqk,khd->hqd",
            weights.astype(jnp.bfloat16),
            value_heads,
            preferred_element_type=jnp.float32,
        )
        return (fresh, totals * decay + jnp.sum(weights, axis=-1), accumulated)

    start_state = (
        jnp.full((head_count, local_rows), -1e30, jnp.float32),
        jnp.zeros((head_count, local_rows), jnp.float32),
        jnp.zeros((head_count, local_rows, HEAD_DIM), jnp.float32),
    )
    running = start_state
    key_part = lax.all_gather(keys_local, "ctx", axis=0, tiled=True)
    value_part = lax.all_gather(values_local, "ctx", axis=0, tiled=True)
    span_rows = key_part.shape[0]
    stride = math.gcd(span_rows, KEY_ROWS)
    step_count = span_rows // stride
    key_steps = key_part.reshape(step_count, stride, model_width)
    value_steps = value_part.reshape(step_count, stride, model_width)
    offsets = jnp.arange(step_count, dtype=jnp.int32) * stride

    def one_step(inner, operands):
        return (attend_block(inner, operands[0], operands[1], operands[2]), None)

    running, unused = lax.scan(one_step, running, (key_steps, value_steps, offsets))
    highest, totals, accumulated = running
    log_total = highest + jnp.log(totals)
    attended = (
        (accumulated / totals[..., None])
        .transpose(1, 0, 2)
        .reshape(local_rows, model_width)
        .astype(jnp.bfloat16)
    )
    mixed = inputs + product(attended, w_out)
    second_full, norm_two_pull = jax.vjp(normalize, mixed, norm_two)
    second = second_full.astype(jnp.bfloat16)
    logits = product(second, w_router)
    chosen = expert_ids[0]
    one_hot = (
        chosen[:, :, None] == jnp.arange(experts_all, dtype=jnp.int32)[None, None, :]
    ).astype(jnp.float32)
    selected = jnp.sum(logits[:, None, :] * one_hot, axis=-1)
    gates = jax.nn.softmax(selected, axis=-1)
    flat_ids = chosen.reshape(-1)
    slot_hits = (flat_ids[:, None] == jnp.arange(experts_all, dtype=jnp.int32)[None, :]).astype(
        jnp.int32
    )
    order = jnp.arange(flat_ids.shape[0], dtype=jnp.int32)
    earlier = (order[None, :] < order[:, None]).astype(jnp.bfloat16)
    counts_before = product(earlier, slot_hits.astype(jnp.bfloat16)).astype(jnp.int32)
    slot_place = jnp.sum(counts_before * slot_hits, axis=1)

    def to_slots(routed_rows):
        empty_slots = jnp.zeros((experts_all, capacity, model_width), jnp.bfloat16)
        return (
            empty_slots.at[flat_ids, slot_place]
            .set(routed_rows)
            .reshape(exp_count, local_experts, capacity, model_width)
        )

    def from_slots(arrived_back):
        picked = arrived_back.reshape(experts_all, capacity, model_width)[flat_ids, slot_place]
        return picked.astype(jnp.float32).reshape(local_rows, TOP, model_width)

    def expert_front(arrived_rows):
        gate_pre = jnp.einsum(
            "sjcd,jdf->sjcf", arrived_rows, expert_gate, preferred_element_type=jnp.float32
        )
        up_pre = jnp.einsum(
            "sjcd,jdf->sjcf", arrived_rows, expert_up, preferred_element_type=jnp.float32
        )
        hidden = (jax.nn.silu(gate_pre) * up_pre).astype(jnp.bfloat16)
        return (gate_pre, up_pre, hidden)

    send_rows = to_slots(jnp.repeat(second, TOP, axis=0))
    arrived = lax.all_to_all(send_rows, "exp", split_axis=0, concat_axis=0, tiled=True)
    gate_pre, up_pre, hidden = expert_front(arrived)
    results = jnp.einsum(
        "sjcf,jfd->sjcd", hidden, expert_down, preferred_element_type=jnp.float32
    ).astype(jnp.bfloat16)
    returned = lax.all_to_all(results, "exp", split_axis=0, concat_axis=0, tiled=True)
    expert_out = from_slots(returned)
    mixture = jnp.sum(gates[:, :, None] * expert_out, axis=1)
    shared_gate_pre = product(second, shared_gate)
    shared_up_pre = product(second, shared_up)
    shared_hidden = (jax.nn.silu(shared_gate_pre) * shared_up_pre).astype(jnp.bfloat16)
    output = (mixed + mixture + product(shared_hidden, shared_down)).astype(jnp.bfloat16)
    upstream = cotangent[0]
    upstream_full = upstream.astype(jnp.float32)
    grad_shared_down = outer_sum(shared_hidden, upstream)
    d_shared_hidden = against(upstream, shared_down)
    shared_silu, shared_slope = silu_parts(shared_gate_pre)
    d_shared_gate = (d_shared_hidden * shared_up_pre * shared_slope).astype(jnp.bfloat16)
    d_shared_up = (d_shared_hidden * shared_silu).astype(jnp.bfloat16)
    grad_shared_gate = outer_sum(second, d_shared_gate)
    grad_shared_up = outer_sum(second, d_shared_up)
    d_second = against(d_shared_gate, shared_gate) + against(d_shared_up, shared_up)
    d_gates = jnp.sum(upstream_full[:, None, :] * expert_out, axis=-1)
    d_selected = gates * (d_gates - jnp.sum(gates * d_gates, axis=-1, keepdims=True))
    d_logits = jnp.sum(d_selected[:, :, None] * one_hot, axis=1).astype(jnp.bfloat16)
    grad_router = outer_sum(second, d_logits)
    d_second = d_second + against(d_logits, w_router)
    grad_slots = to_slots(
        (gates[:, :, None] * upstream_full[:, None, :])
        .astype(jnp.bfloat16)
        .reshape(local_rows * TOP, model_width)
    )
    arrived_rows, arrived_grad = (
        lax.all_to_all(send_rows, "exp", split_axis=0, concat_axis=0, tiled=True),
        lax.all_to_all(grad_slots, "exp", split_axis=0, concat_axis=0, tiled=True),
    )
    gate_kept, up_kept, hidden_kept = expert_front(arrived_rows)
    d_hidden = jnp.einsum(
        "sjcd,jfd->sjcf", arrived_grad, expert_down, preferred_element_type=jnp.float32
    )
    expert_silu, expert_slope = silu_parts(gate_kept)
    d_gate_pre = (d_hidden * up_kept * expert_slope).astype(jnp.bfloat16)
    d_up_pre = (d_hidden * expert_silu).astype(jnp.bfloat16)
    grad_expert_down = jnp.einsum(
        "sjcf,sjcd->jfd", hidden_kept, arrived_grad, preferred_element_type=jnp.float32
    )
    grad_expert_gate = jnp.einsum(
        "sjcd,sjcf->jdf", arrived_rows, d_gate_pre, preferred_element_type=jnp.float32
    )
    grad_expert_up = jnp.einsum(
        "sjcd,sjcf->jdf", arrived_rows, d_up_pre, preferred_element_type=jnp.float32
    )
    d_routed = (
        jnp.einsum("sjcf,jdf->sjcd", d_gate_pre, expert_gate, preferred_element_type=jnp.float32)
        + jnp.einsum("sjcf,jdf->sjcd", d_up_pre, expert_up, preferred_element_type=jnp.float32)
    ).astype(jnp.bfloat16)
    returned_grad = lax.all_to_all(d_routed, "exp", split_axis=0, concat_axis=0, tiled=True)
    d_second = d_second + jnp.sum(from_slots(returned_grad), axis=1)
    grad_expert_gate, grad_expert_up, grad_expert_down = (
        lax.psum(grad_expert_gate.astype(jnp.bfloat16), ("seq", "ctx")).astype(jnp.float32),
        lax.psum(grad_expert_up.astype(jnp.bfloat16), ("seq", "ctx")).astype(jnp.float32),
        lax.psum(grad_expert_down.astype(jnp.bfloat16), ("seq", "ctx")).astype(jnp.float32),
    )
    d_mixed_part, grad_norm_two = norm_two_pull(d_second)
    d_mixed = upstream_full + d_mixed_part
    d_attention = d_mixed.astype(jnp.bfloat16)
    grad_out = outer_sum(attended, d_attention)
    grad_heads = (
        against(d_attention, w_out).astype(jnp.bfloat16).reshape(local_rows, head_count, HEAD_DIM)
    )
    keys_all, values_all = (
        lax.all_gather(keys_local, "ctx", axis=0, tiled=True),
        lax.all_gather(values_local, "ctx", axis=0, tiled=True),
    )
    block_total = ((ctx_place + 1) * local_rows + KEY_ROWS - 1) // KEY_ROWS

    def weights_at(number):
        offset = number * KEY_ROWS
        key_block = lax.dynamic_slice_in_dim(keys_all, offset, KEY_ROWS, 0)
        value_block = lax.dynamic_slice_in_dim(values_all, offset, KEY_ROWS, 0)
        scores, allowed = block_scores(key_block, offset)
        weights = jnp.where(allowed[None], jnp.exp(scores - log_total[..., None]), 0.0)
        grad_weights = jnp.einsum(
            "qhd,khd->hqk",
            grad_heads,
            value_block.reshape(KEY_ROWS, head_count, HEAD_DIM),
            preferred_element_type=jnp.float32,
        )
        return (key_block, weights, grad_weights)

    def row_dot_step(number, summed):
        unused_block, weights, grad_weights = weights_at(number)
        return summed + jnp.sum(weights * grad_weights, axis=-1)

    row_dots = lax.fori_loop(
        0, block_total, row_dot_step, jnp.zeros((head_count, local_rows), jnp.float32)
    )

    def score_grads(number):
        key_block, weights, grad_weights = weights_at(number)
        d_scores = (weights * (grad_weights - row_dots[..., None])).astype(jnp.bfloat16)
        return (key_block.reshape(KEY_ROWS, head_count, HEAD_DIM), weights, d_scores)

    query_start = jnp.zeros((local_rows, head_count, HEAD_DIM), jnp.float32)

    def grad_step(number, running):
        grad_query, key_terms = running
        key_heads, weights, d_scores = score_grads(number)
        grad_query = (
            grad_query
            + jnp.einsum("hqk,khd->qhd", d_scores, key_heads, preferred_element_type=jnp.float32)
            * score_scale
        )
        key_part = (
            jnp.einsum("hqk,qhd->khd", d_scores, query, preferred_element_type=jnp.float32)
            * score_scale
        )
        value_part = jnp.einsum(
            "hqk,qhd->khd",
            weights.astype(jnp.bfloat16),
            grad_heads,
            preferred_element_type=jnp.float32,
        )
        block_terms = jnp.concatenate(
            [key_part.reshape(KEY_ROWS, model_width), value_part.reshape(KEY_ROWS, model_width)],
            axis=1,
        )
        return (
            grad_query,
            lax.dynamic_update_slice_in_dim(key_terms, block_terms, number * KEY_ROWS, 0),
        )

    grad_query_heads, key_terms = lax.fori_loop(
        0,
        block_total,
        grad_step,
        (query_start, jnp.zeros((ctx_count * local_rows, 2 * model_width), jnp.float32)),
    )
    key_grads = lax.psum_scatter(
        key_terms.astype(jnp.bfloat16), "ctx", scatter_dimension=0, tiled=True
    ).astype(jnp.float32)
    key_grad_heads = key_grads[:, :model_width].reshape(local_rows, head_count, HEAD_DIM)
    d_value = key_grads[:, model_width:].astype(jnp.bfloat16)
    d_query_lin = (
        rotate(grad_query_heads, -places).astype(jnp.bfloat16).reshape(local_rows, model_width)
    )
    d_key_lin = (
        rotate(key_grad_heads, -places).astype(jnp.bfloat16).reshape(local_rows, model_width)
    )
    grad_query = outer_sum(normed, d_query_lin)
    grad_key = outer_sum(normed, d_key_lin)
    grad_value = outer_sum(normed, d_value)
    d_normed = against(d_query_lin, w_query) + against(d_key_lin, w_key) + against(d_value, w_value)
    d_inputs, grad_norm_one = norm_one_pull(d_normed)
    grad_tokens = (d_mixed + d_inputs)[None]
    (
        grad_query,
        grad_key,
        grad_value,
        grad_out,
        grad_router,
        grad_shared_gate,
        grad_shared_up,
        grad_shared_down,
    ) = (
        lax.psum_scatter(
            spread(grad_query), ("seq", "ctx", "exp"), scatter_dimension=0, tiled=True
        ),
        lax.psum_scatter(spread(grad_key), ("seq", "ctx", "exp"), scatter_dimension=0, tiled=True),
        lax.psum_scatter(
            spread(grad_value), ("seq", "ctx", "exp"), scatter_dimension=0, tiled=True
        ),
        lax.psum_scatter(spread(grad_out), ("seq", "ctx", "exp"), scatter_dimension=0, tiled=True),
        lax.psum_scatter(
            spread(grad_router), ("seq", "ctx", "exp"), scatter_dimension=0, tiled=True
        ),
        lax.psum_scatter(
            spread(grad_shared_gate), ("seq", "ctx", "exp"), scatter_dimension=0, tiled=True
        ),
        lax.psum_scatter(
            spread(grad_shared_up), ("seq", "ctx", "exp"), scatter_dimension=0, tiled=True
        ),
        lax.psum_scatter(
            spread(grad_shared_down), ("seq", "ctx", "exp"), scatter_dimension=0, tiled=True
        ),
    )
    grad_norm_one, grad_norm_two = lax.psum((grad_norm_one, grad_norm_two), ("seq", "ctx", "exp"))
    return (
        output[None],
        grad_tokens,
        grad_norm_one,
        grad_query,
        grad_key,
        grad_value,
        grad_out,
        grad_norm_two,
        grad_router,
        grad_expert_gate,
        grad_expert_up,
        grad_expert_down,
        grad_shared_gate,
        grad_shared_up,
        grad_shared_down,
    )


def place_tables(length):
    half = HEAD_DIM // 2
    frequency = np.float32(10000.0) ** (-np.arange(half, dtype=np.float32) / np.float32(half))
    angles = np.arange(length, dtype=np.float32)[:, None] * frequency[None, :].astype(np.float32)
    cosine, sine = np.cos(angles), np.sin(angles)
    return (
        np.concatenate([cosine] * 4, axis=1).astype(np.float32),
        np.concatenate([-sine, sine, -sine, sine], axis=1).astype(np.float32),
    )


def swapped(values):
    half = HEAD_DIM // 2
    lane = lax.broadcasted_iota(jnp.int32, values.shape, 1) % HEAD_DIM
    return jnp.where(lane < half, pltpu.roll(values, 128 - half, 1), pltpu.roll(values, half, 1))


def start_copy(src, dst, ssem, rsem, device):
    copy = pltpu.make_async_remote_copy(
        src_ref=src, dst_ref=dst, send_sem=ssem, recv_sem=rsem, device_id=device, device_id_type=MESH
    )
    copy.start()
    return copy


def greet(devices):
    barrier = pltpu.get_barrier_semaphore()
    for device in devices:
        pl.semaphore_signal(barrier, inc=1, device_id=device, device_id_type=MESH)
    pl.semaphore_wait(barrier, len(devices))


def neighbours():
    s = lax.axis_index("seq")
    c = lax.axis_index("ctx")
    e = lax.axis_index("exp")
    x, k = c // 2, c % 2
    to_core = (s, x * 2 + (1 - k), e)
    to_x = (s, (1 - x) * 2 + k, e)
    to_y = (1 - s, c, e)
    near = e + 1 - 2 * (e % 2)
    far = lax.rem(e + 2, 4)
    opposite = 3 - e
    return s, x, k, e, c, to_core, to_x, to_y, (near, far, opposite)


def named_lanes(rows_named):
    marks = rows_named.astype(jnp.float32)
    return jnp.concatenate([marks, jnp.zeros((112, marks.shape[1]), jnp.float32)], axis=0).T > 0.5


def front_kernel(
    tokens, upstream, ids, gain_one, gain_two, w_q, w_k, w_v, w_o, cosine, sine,
    q_all, k_all, v_all, upstream_all, named_all, normed_out, attended_out, mixed_out, second_out, logsum_out,
    block, q_keep, k_keep, v_keep, weight, tsem, trem, usem, urem, nsem, nrem, wsem, osem,
):
    s, x, k, e, c, to_core, to_x, to_y, others = neighbours()
    rows, width = tokens.shape
    loads = [pltpu.make_async_copy(w, weight.at[i], wsem.at[i]) for i, w in enumerate((w_q, w_k, w_v, w_o))]
    for load in loads:
        load.start()
    greet([to_core, to_x, (s, c, others[0]), (s, c, others[1])])
    block[c] = tokens[...]
    upstream_all[0] = upstream[...]
    expert_row = lax.broadcasted_iota(jnp.int32, (16, rows), 0)
    marks = jnp.where((expert_row == ids[0:1, :]) | (expert_row == ids[1:2, :]), 1.0, 0.0)
    named_all[0] = marks.astype(jnp.bfloat16)
    core_copy = start_copy(tokens, block.at[c], tsem.at[0], trem.at[0], to_core)
    x_copy = start_copy(tokens, block.at[c], tsem.at[1], trem.at[1], to_x)
    to_near, to_far = (s, c, others[0]), (s, c, others[1])

    def over_z(i, source, device):
        return [
            start_copy(upstream_all.at[source], upstream_all.at[i + 1], usem.at[i], urem.at[i], device),
            start_copy(named_all.at[source], named_all.at[i + 1], nsem.at[i], nrem.at[i], device),
        ]

    near_copies = over_z(0, 0, to_near)
    far_copies = over_z(1, 0, to_far)

    one = gain_one[...].reshape(1, width)

    def project(j):
        values = block[j].astype(jnp.float32)
        inverse = lax.rsqrt(jnp.mean(values * values, axis=-1, keepdims=True) + 1e-06)
        normed = (values * inverse * one).astype(jnp.bfloat16)
        for i, out in enumerate((q_keep, k_keep)):
            lin = jnp.dot(normed, weight[i], preferred_element_type=jnp.float32)
            for g in range(width // 128):
                part = lin[:, g * 128 : (g + 1) * 128]
                turned = part * cosine[j] + swapped(part) * sine[j]
                out[j, :, g * 128 : (g + 1) * 128] = turned.astype(jnp.bfloat16)
        v_keep[j] = jnp.dot(normed, weight[2], preferred_element_type=jnp.float32).astype(jnp.bfloat16)
        return normed

    for load in loads:
        load.wait()
    normed_out[...] = project(c)
    core_copy.wait()
    project(x * 2 + (1 - k))
    x_copy.wait()
    there = (1 - x) * 2 + k
    corner_copy = start_copy(block.at[there], block.at[there], tsem.at[2], trem.at[2], to_core)
    project(there)
    corner_copy.wait()
    project((1 - x) * 2 + (1 - k))

    leaves = [
        pltpu.make_async_copy(src, dst, osem.at[i])
        for i, (src, dst) in enumerate(((q_keep, q_all), (k_keep, k_all), (v_keep, v_all)))
    ]
    for leave in leaves:
        leave.start()
    span = 4 * rows
    hidden_keys = lax.broadcasted_iota(jnp.int32, (1, span), 1) // rows > c
    bias = jnp.where(hidden_keys, -1e30, 0.0)
    lane = lax.broadcasted_iota(jnp.int32, (rows, 128), 1)
    logsum_out[...] = jnp.zeros_like(logsum_out)

    def pair(g, carry):
        at = pl.ds(pl.multiple_of(g * 128, 128), 128)
        q = q_keep[c, :, at]
        keys = k_keep[:, :, at].reshape(span, 128)
        values = v_keep[:, :, at].reshape(span, 128)
        out = jnp.zeros((rows, 128), jnp.float32)
        for h in range(2):
            inside = (lane // HEAD_DIM) == h
            scores = lax.dot_general(
                jnp.where(inside, q, jnp.zeros_like(q)), keys, (((1,), (1,)), ((), ())),
                preferred_element_type=jnp.float32,
            )
            scores = scores * (HEAD_DIM**-0.5) + bias
            highest = jnp.max(scores, axis=-1, keepdims=True)
            raised = jnp.exp(scores - highest)
            total = jnp.sum(raised, axis=-1, keepdims=True)
            mixed = jnp.dot(raised.astype(jnp.bfloat16), values, preferred_element_type=jnp.float32)
            out = jnp.where(inside, mixed / total, out)
            logsum_out[...] = jnp.where(lane == 2 * g + h, highest + jnp.log(total), logsum_out[...])
        attended_out[:, at] = out.astype(jnp.bfloat16)
        return carry

    lax.fori_loop(0, width // 128, pair, 0)
    mixed = tokens[...].astype(jnp.float32) + jnp.dot(
        attended_out[...], weight[3], preferred_element_type=jnp.float32
    )
    mixed_out[...] = mixed
    inverse = lax.rsqrt(jnp.mean(mixed * mixed, axis=-1, keepdims=True) + 1e-06)
    second_out[...] = (mixed * inverse * gain_two[...].reshape(1, width)).astype(jnp.bfloat16)
    for copy in (*near_copies, *far_copies, *leaves):
        copy.wait()


def front(tokens, upstream, ids, gain_one, gain_two, w_q, w_k, w_v, w_o):
    rows, width = tokens.shape
    cosine, sine = (jnp.asarray(t).reshape(4, rows, 128) for t in place_tables(4 * rows))
    low, full = jnp.bfloat16, jnp.float32
    vmem, dma = pltpu.VMEM, pltpu.SemaphoreType.DMA
    every, three = (jax.ShapeDtypeStruct((n, rows, width), low) for n in (4, 3))
    own = jax.ShapeDtypeStruct((rows, width), low)
    spec, anywhere = pl.BlockSpec(memory_space=pltpu.VMEM), pl.BlockSpec(memory_space=pl.ANY)
    out_shape = [
        every, every, every, three, jax.ShapeDtypeStruct((3, 16, rows), low), own, own,
        jax.ShapeDtypeStruct((rows, width), full), own, jax.ShapeDtypeStruct((rows, 128), full),
    ]
    return pl.pallas_call(
        front_kernel,
        out_shape=out_shape,
        in_specs=[spec] * 5 + [anywhere] * 4 + [spec] * 2,
        out_specs=[anywhere] * 3 + [spec] * 7,
        scratch_shapes=[
            *[vmem((4, rows, width), low)] * 4, vmem((4, width, width), low), *[dma((3,))] * 2, *[dma((2,))] * 4,
            dma((4,)), dma((3,)),
        ],
        compiler_params=pltpu.CompilerParams(
            collective_id=2, has_side_effects=True, vmem_limit_bytes=58 * 2**20
        ),
        name="front",
    )(tokens, upstream, ids, gain_one, gain_two, w_q, w_k, w_v, w_o, cosine, sine)


def add_rows(target, first, second, step):
    rows = target.shape[0]

    def some(at):
        total = first[at, :].astype(jnp.float32) + second[at, :].astype(jnp.float32)
        target[at, :] = total.astype(target.dtype)

    if rows <= step:
        some(pl.ds(0, rows))
    else:

        def body(i, carry):
            some(pl.ds(pl.multiple_of(i * step, step), step))
            return carry

        lax.fori_loop(0, rows // step, body, 0)


class Piece:
    def __init__(self, place, whole, one, two, three, half, sems, step):
        self.s, self.x, self.k, self.to_core, self.to_x, self.to_y = place
        self.whole, self.one, self.two, self.three = whole, one, two, three
        self.half, self.sems, self.step = half, sems, step

    def copy(self, level, h=0):
        every, low, high = slice(None), pl.ds(0, self.half), pl.ds(self.half, self.half)
        if level == 1:
            src, dst, device = self.whole(1 - self.k), self.one(every, every, every), self.to_core
        elif level == 2:
            if h == 0:
                src, device = self.one(every, 1 - self.x, low), self.to_x
            else:
                src, device = self.one(1 - self.s, every, high), self.to_y
            dst = self.two(h, every)
        else:
            src = self.two(h, 1 - (self.s, self.x)[h])
            dst, device = self.three(h), (self.to_y, self.to_x)[h]
        ssem, rsem = self.sems(2 * (level - 1) - (1 if level > 1 else 0) + h)
        return pltpu.make_async_remote_copy(
            src_ref=src, dst_ref=dst, send_sem=ssem, recv_sem=rsem, device_id=device, device_id_type=MESH
        )

    def start(self, level):
        for h in range(1 if level == 1 else 2):
            self.copy(level, h).start()

    def finish(self, level):
        low, high = pl.ds(0, self.half), pl.ds(self.half, self.half)
        if level == 1:
            self.copy(1).wait()
            own = self.whole(self.k)
            for i in range(2):
                for j in range(2):
                    here = self.one(i, j, slice(None))
                    add_rows(here, here, own.at[i, j], self.step)
            return
        for h in range(2):
            self.copy(level, h).wait()
            if level == 2:
                for i in range(2):
                    here = self.two(h, i)
                    own = self.one(i, self.x, low) if h == 0 else self.one(self.s, i, high)
                    add_rows(here, here, own, self.step)
            else:
                here = self.three(h)
                add_rows(here, here, self.two(h, (self.s, self.x)[h]), self.step)


def gates_in(logits, named):
    masked = jnp.where(named, logits, -1e30)
    raised = jnp.where(named, jnp.exp(masked - jnp.max(masked, axis=-1, keepdims=True)), 0.0)
    return raised / jnp.sum(raised, axis=-1, keepdims=True)


def ffn_kernel(
    second, mixed, upstream_all, named_all, w_r, gain_two,
    e_gate, e_up, e_down, s_gate, s_up, s_down,
    results, d_mixed_out, small_out, eg_out, eu_out, ed_out, sg_out, su_out, sd_out,
    rows_all, last_up, last_named, d_res, res_acc, mix_acc, row_acc, row_send, row_got, dg_send, dg_got,
    router_w, own_shares, across, we_g, we_u, we_d, ws_g, ws_u, ws_d, wsem,
    ge_g, ge_u, ge_d, e1_g, e1_u, e1_d, e2_g, e2_u, e2_d,
    gs_g, gs_u, gs_d, s1_g, s1_u, s1_d, s2_g, s2_u, s2_d, s3_g, s3_u, s3_d, sd_got, square,
    es_sem, er_sem, ss_sem, sr_sem, xs_sem, xr_sem, us_sem, ur_sem, rs_sem, rr_sem, ds_sem, dr_sem, hs_sem, hr_sem,
):
    s, x, k, e, c, to_core, to_x, to_y, others = neighbours()
    place = (s, x, k, to_core, to_x, to_y)
    rows, width = second.shape
    tile = 8 * ge_d.shape[4]
    tiles, shared_tiles = e_gate.shape[1] // tile, gs_g.shape[4] // tile
    low, full = jnp.bfloat16, jnp.float32
    to_z = [(s, c, o) for o in others]
    owner_row, giver_row = 2 * e + s, 4 * s + c
    to_owner, giver = (owner_row // 4, owner_row % 4, c), (giver_row % 2, e, giver_row // 2)
    square[...] = jnp.zeros_like(square)
    elsewhere = jnp.where((owner_row == giver_row) & (c == e), 0, 1)

    def columns(f):
        return pl.ds(pl.multiple_of(f * tile, tile), tile)

    def fetches(f, shared):
        at = columns(f)
        if shared:
            sources, here, targets, n = (s_gate, s_up, s_down), columns(e * shared_tiles + f), (ws_g, ws_u, ws_d), f
        else:
            sources, here, targets, n = (e_gate, e_up, e_down), at, (we_g, we_u, we_d), shared_tiles + f
        return [
            pltpu.make_async_copy(sources[0].at[:, here], targets[0].at[:, at], wsem.at[n, 0]),
            pltpu.make_async_copy(sources[1].at[:, here], targets[1].at[:, at], wsem.at[n, 1]),
            pltpu.make_async_copy(sources[2].at[here, :], targets[2].at[at, :], wsem.at[n, 2]),
        ]

    for n in range(shared_tiles):
        for copy in fetches(n, True):
            copy.start()
    for n in range(tiles):
        for copy in fetches(n, False):
            copy.start()
    barrier = pltpu.get_barrier_semaphore()
    for device in (to_core, to_x, to_y, *to_z):
        pl.semaphore_signal(barrier, inc=1, device_id=device, device_id_type=MESH)

    @pl.when(elsewhere == 1)
    def _():
        for device in (to_owner, giver):
            pl.semaphore_signal(barrier, inc=1, device_id=device, device_id_type=MESH)

    pl.semaphore_wait(barrier, 6 + 2 * elsewhere)
    near_copy = start_copy(second, rows_all.at[1], xs_sem.at[0], xr_sem.at[0], to_z[0])
    far_copy = start_copy(second, rows_all.at[2], xs_sem.at[1], xr_sem.at[1], to_z[1])
    rows_all[0] = second[...]
    router_rows = w_r[...].astype(full)
    router_w[...] = jnp.concatenate([router_rows, jnp.zeros((128 - w_r.shape[0], width), full)], axis=0).T.astype(low)

    def piece_e(f, a):
        at = columns(f)
        sems = lambda n: (es_sem.at[f, a, n], er_sem.at[f, a, n])
        if a < 2:
            g, one, two, three = ((ge_g, e1_g, e2_g, eg_out), (ge_u, e1_u, e2_u, eu_out))[a]
            return Piece(
                place,
                lambda kk: g.at[:, :, kk, :, at],
                lambda i, j, r: one.at[i, j, r, at],
                lambda h, i: two.at[h, i, :, at],
                lambda h: three.at[h, :, at],
                g.shape[3] // 2, sems, 96,
            )
        return Piece(
            place,
            lambda kk: ge_d.at[f, :, :, kk],
            lambda i, j, r: e1_d.at[f, i, j, r],
            lambda h, i: e2_d.at[f, h, i],
            lambda h: ed_out.at[f, h],
            ge_d.shape[4] // 2, sems, 96,
        )

    def piece_s(a):
        g, one, two, three = (
            (gs_g, s1_g, s2_g, s3_g), (gs_u, s1_u, s2_u, s3_u), (gs_d, s1_d, s2_d, s3_d)
        )[a]
        return Piece(
            place,
            lambda kk: g.at[:, :, kk],
            lambda i, j, r: one.at[i, j, r],
            lambda h, i: two.at[h, i],
            lambda h: three.at[h],
            g.shape[3] // 2, lambda n: (ss_sem.at[a, n], sr_sem.at[a, n]), 48 if a < 2 else 64,
        )

    def branch(values, d_out, weights, f, result_acc, d_acc):
        at = columns(f)
        gate_w, up_w, down_w = weights[0][:, at], weights[1][:, at], weights[2][at, :]
        gate = jnp.dot(values, gate_w, preferred_element_type=full)
        up = jnp.dot(values, up_w, preferred_element_type=full)
        d_hidden = against(d_out, down_w)
        sigmoid = 1.0 / (1.0 + jnp.exp(-gate))
        silu = gate * sigmoid
        hidden = (silu * up).astype(low)
        d_gate = (d_hidden * up * (sigmoid * (1.0 + gate * (1.0 - sigmoid)))).astype(low)
        d_up = (d_hidden * silu).astype(low)
        result_acc[...] += jnp.dot(hidden, down_w, preferred_element_type=full)
        d_acc[...] += against(d_gate, gate_w) + against(d_up, up_w)
        return hidden, d_gate, d_up

    def onward():
        return [
            pltpu.make_async_remote_copy(
                src_ref=src, dst_ref=dst, send_sem=ssem, recv_sem=rsem, device_id=to_z[0], device_id_type=MESH
            )
            for src, dst, ssem, rsem in (
                (rows_all.at[2], rows_all.at[3], xs_sem.at[2], xr_sem.at[2]),
                (upstream_all.at[2], last_up, us_sem.at[0], ur_sem.at[0]),
                (named_all.at[2], last_named, us_sem.at[1], ur_sem.at[1]),
            )
        ]

    def turn(first, count, again, last):
        many = count * rows
        some = pl.ds(first, count)
        values = rows_all[some].reshape(many, width)
        if first == 3:
            d_rows, marks = last_up[...], [last_named[...]]
        else:
            d_rows = upstream_all[some].reshape(many, width)
            marks = [named_all[first + i] for i in range(count)]
        logits = jnp.dot(values, router_w[...], preferred_element_type=full)
        named = jnp.concatenate([named_lanes(m) for m in marks], axis=0)
        lane = lax.broadcasted_iota(jnp.int32, (many, 128), 1)
        gates = gates_in(logits, named)
        if first == 0:
            own_shares[...] = gates[0:rows]
        share = jnp.sum(jnp.where(lane == e, gates, 0.0), axis=-1, keepdims=True)
        d_res[0:many] = d_rows
        for total in (res_acc, mix_acc, row_acc):
            total[0:many] = jnp.zeros((many, width), full)
        across[:, 0:many] = values.T
        inside = pl.ds(0, many)

        def store(ref, index, term):
            if again:
                term = term + ref[index].astype(full)
            ref[index] = term.astype(low)

        def shared_tile(f, carry):
            if first == 0:
                for copy in fetches(f, True):
                    copy.wait()
            values, d_out = rows_all[some].reshape(many, width), d_res[0:many]
            hidden, d_gate, d_up = branch(
                values, d_out, (ws_g, ws_u, ws_d), f, mix_acc.at[inside], row_acc.at[inside]
            )
            turned = across[:, 0:many]
            index = (slice(None), slice(None), slice(None), slice(None), columns(f))
            store(gs_g, index, product(turned, d_gate).reshape(2, 2, 2, width // 8, tile))
            store(gs_u, index, product(turned, d_up).reshape(2, 2, 2, width // 8, tile))
            term, quarter, half = outer_sum(hidden, d_out), width // 4, gs_d.shape[3]
            for i in range(tile // (2 * half)):
                for q in range(4):
                    for h in range(2):
                        top = (2 * i + h) * half
                        store(
                            gs_d,
                            (f * (tile // (2 * half)) + i, q // 2, q % 2, slice(None), slice(h * quarter, (h + 1) * quarter)),
                            term[top : top + half, q * quarter : (q + 1) * quarter],
                        )
            return carry

        def expert_tile(f, carry):
            if first == 0:
                for copy in fetches(f, False):
                    copy.wait()
            values, d_out = rows_all[some].reshape(many, width), d_res[0:many]
            hidden, d_gate, d_up = branch(
                values, d_out, (we_g, we_u, we_d), f, res_acc.at[inside], row_acc.at[inside]
            )
            if last:

                @pl.when(f == 0)
                def _():
                    for a in range(3):
                        piece_s(a).finish(1)
                        piece_s(a).start(2)

                @pl.when(f > 0)
                def _():
                    for a in range(3):
                        piece_e(f - 1, a).finish(1)
                        piece_e(f - 1, a).start(2)

            turned = across[:, 0:many]
            index = (slice(None), slice(None), slice(None), slice(None), columns(f))
            store(ge_g, index, product(turned, d_gate).reshape(2, 2, 2, width // 8, tile))
            store(ge_u, index, product(turned, d_up).reshape(2, 2, 2, width // 8, tile))
            store(ge_d, (f,), outer_sum(hidden, d_out).reshape(2, 2, 2, tile // 8, width))
            if first == 1:

                @pl.when(f == tiles // 8)
                def _():
                    far_copy.wait()
                    for copy in onward():
                        copy.start()

            if last:
                for a in range(3):
                    piece_e(f, a).start(1)

            return carry

        lax.fori_loop(0, shared_tiles, shared_tile, 0)
        if last:
            for a in range(3):
                piece_s(a).start(1)
        d_res[0:many] = (share * d_rows.astype(full)).astype(low)
        lax.fori_loop(0, tiles, expert_tile, 0)
        low_result = res_acc[0:many].astype(low)
        results[some] = (mix_acc[0:many] + share * low_result.astype(full)).astype(low).reshape(count, rows, width)
        row_send[some] = row_acc[0:many].astype(low).reshape(count, rows, width)
        terms = low_result.astype(full) * d_rows.astype(full)
        high = terms.astype(low)
        ones = jnp.ones((8, width), low)
        sums = against(ones, high) + against(ones, (terms - high.astype(full)).astype(low))
        for i in range(count):
            dg_send[first + i] = sums[:, i * rows : (i + 1) * rows]

    back_copies = []
    turn(0, 1, False, False)
    near_copy.wait()
    turn(1, 1, True, False)
    back_copies.append(start_copy(row_send.at[1], row_got.at[0], rs_sem.at[0], rr_sem.at[0], to_z[0]))
    turn(2, 1, True, False)
    back_copies.append(start_copy(row_send.at[2], row_got.at[1], rs_sem.at[1], rr_sem.at[1], to_z[1]))
    for copy in onward():
        copy.wait()
    turn(3, 1, True, True)
    back_copies.append(start_copy(row_send.at[3], row_got.at[2], rs_sem.at[2], rr_sem.at[2], to_z[2]))
    for i in range(3):
        back_copies.append(start_copy(dg_send.at[i + 1], dg_got.at[i], ds_sem.at[i], dr_sem.at[i], to_z[i]))
    for a in range(3):
        piece_e(tiles - 1, a).finish(1)
        piece_e(tiles - 1, a).start(2)

    def third(f, carry):
        for a in range(3):
            piece_e(f, a).finish(2)
            piece_e(f, a).start(3)
        return carry

    for a in range(3):
        piece_s(a).finish(2)
        piece_s(a).start(3)
    lax.fori_loop(0, tiles, third, 0)
    for a in range(3):
        piece_s(a).finish(3)

    @pl.when(elsewhere == 1)
    def _():
        start_copy(s3_d, sd_got, hs_sem, hr_sem, to_owner)

    @pl.when(elsewhere == 0)
    def _():
        sd_got[...] = s3_d[...]

    for h in range(2):
        part = pl.ds(h * s3_g.shape[1], s3_g.shape[1])
        sg_out[part] = s3_g[h].astype(full)
        su_out[part] = s3_u[h].astype(full)

    for copy in back_copies:
        copy.wait()
    total = row_send[0].astype(full)
    for i in range(3):
        total = total + row_got[i].astype(full)
    expert_row = lax.broadcasted_iota(jnp.int32, (8, rows), 0)
    d_gates = jnp.where(expert_row == e, dg_send[0], 0.0)
    for i in range(3):
        d_gates = jnp.where(expert_row == others[i], dg_got[i], d_gates)
    d_gates = jnp.concatenate([d_gates, jnp.zeros((120, rows), full)], axis=0).T
    shares = own_shares[...]
    d_logits = (shares * (d_gates - jnp.sum(shares * d_gates, axis=-1, keepdims=True))).astype(low)
    total = total + against(d_logits, router_w[...])
    router = outer_sum(d_logits, second[...])
    values = mixed[...]
    inverse = lax.rsqrt(jnp.mean(values * values, axis=-1, keepdims=True) + 1e-06)
    unit = values * inverse
    small_out[0:8, :] = router[0:8, :]
    small_out[8:16, :] = jnp.broadcast_to(jnp.sum(total * unit, axis=0, keepdims=True), (8, width))
    inner = total * gain_two[...].reshape(1, width)
    mean = jnp.mean(inner * unit, axis=-1, keepdims=True)
    d_mixed_out[...] = upstream_all[0].astype(full) + inverse * (inner - unit * mean)

    def done(f, carry):
        for a in range(3):
            piece_e(f, a).finish(3)
        return carry

    lax.fori_loop(0, tiles, done, 0)

    @pl.when(elsewhere == 1)
    def _():
        pltpu.make_async_remote_copy(
            src_ref=s3_d, dst_ref=sd_got, send_sem=hs_sem, recv_sem=hr_sem, device_id=to_owner, device_id_type=MESH
        ).wait()

    quarter, half = width // 4, s3_d.shape[1]
    for h in range(2):
        for i in range(2):
            top = h * 2 * half + i * half
            square[top : top + half, 0:quarter] = sd_got[i, :, h * quarter : (h + 1) * quarter].astype(full)
    sd_out[...] = square[...].T[0:quarter, :]


def ffn(second, mixed, upstream_all, named_all, w_router, gain_two, experts, shared):
    rows, width = second.shape
    hidden = experts[0].shape[1]
    slice_width = shared[0].shape[1] // 4
    tile = 512
    tiles = hidden // tile
    low, full = jnp.bfloat16, jnp.float32
    dma = pltpu.SemaphoreType.DMA
    ninth, small, half = width // 8, tile // 8, slice_width // 4

    def vm(*shape, dtype=low):
        return pltpu.VMEM(shape, dtype)

    def out(*shape, dtype=low):
        return jax.ShapeDtypeStruct(shape, dtype)

    spec = pl.BlockSpec(memory_space=pltpu.VMEM)
    out_shape = [
        out(4, rows, width), out(rows, width, dtype=full), out(16, width, dtype=full),
        out(2, ninth // 2, hidden), out(2, ninth // 2, hidden), out(tiles, 2, small // 2, width),
        out(ninth, slice_width, dtype=full), out(ninth, slice_width, dtype=full), out(width // 4, 2 * half, dtype=full),
    ]
    scratch = [
        vm(4, rows, width), vm(rows, width), vm(16, rows), vm(rows, width), *[vm(rows, width, dtype=full)] * 3,
        vm(4, rows, width), vm(3, rows, width), vm(4, 8, rows, dtype=full), vm(3, 8, rows, dtype=full),
        vm(width, 128), vm(rows, 128, dtype=full), vm(width, rows),
        *[vm(width, hidden)] * 2, vm(hidden, width), *[vm(width, slice_width)] * 2, vm(slice_width, width),
        dma(((hidden + slice_width) // tile, 3)),
        *[vm(2, 2, 2, ninth, hidden)] * 2, vm(tiles, 2, 2, 2, small, width),
        *[vm(2, 2, ninth, hidden)] * 2, vm(tiles, 2, 2, small, width),
        *[vm(2, 2, ninth // 2, hidden)] * 2, vm(tiles, 2, 2, small // 2, width),
        *[vm(2, 2, 2, ninth, slice_width)] * 2, vm(2, 2, 2, half, width // 2),
        *[vm(2, 2, ninth, slice_width)] * 2, vm(2, 2, half, width // 2),
        *[vm(2, 2, ninth // 2, slice_width)] * 2, vm(2, 2, half // 2, width // 2),
        *[vm(2, ninth // 2, slice_width)] * 2, vm(2, half // 2, width // 2), vm(2, half // 2, width // 2),
        vm(2 * half, 2 * half, dtype=full),
        *[dma((tiles, 3, 5))] * 2, *[dma((3, 5))] * 2, *[dma((3,))] * 2, *[dma((2,))] * 2, *[dma((3,))] * 4, dma, dma,
    ]
    return pl.pallas_call(
        ffn_kernel,
        out_shape=out_shape,
        in_specs=[spec] * 6 + [pl.BlockSpec(memory_space=pl.ANY)] * 6,
        out_specs=[spec] * len(out_shape),
        scratch_shapes=scratch,
        compiler_params=pltpu.CompilerParams(
            collective_id=3, has_side_effects=True, vmem_limit_bytes=60 * 2**20
        ),
        name="ffn",
    )(second, mixed, upstream_all, named_all, w_router.T, gain_two, *experts, *shared)


def back_kernel(
    eg_own, eu_own, ed_own, small, results, mixed,
    tokens, gain_one, d_mixed, attended, normed, log_sum, cosine, sine, w_o_hbm, q_hbm, k_hbm, v_hbm, w_q_hbm, w_k_hbm, w_v_hbm,
    eg_all, eu_all, ed_all, q_out, k_out, v_out, o_out, one_out, two_out, router_out, output, token_out,
    grads, d_att, d_all, stats, stat_col, sum_q, sum_k, sum_v, misc_in, misc_out, far_sum, turned, asem, arem, tsem, trem,
    one, two, three, z_flat, got_flat, misc_got, result_got,
    w_o, q_all, k_all, v_all, w_q, w_k, w_v, hsem,
    lsem, gsem, grem, csem, crem, psem, prem, zsem, zrem, msem, mrem, rsem, rrem,
):
    s, x, k, e, c, to_core, to_x, to_y, others = neighbours()
    place = (s, x, k, to_core, to_x, to_y)
    to_z = [(s, c, o) for o in others]
    low, full = jnp.bfloat16, jnp.float32
    loads = [
        pltpu.make_async_copy(src, dst, hsem.at[i])
        for i, (src, dst) in enumerate(
            (
                (w_o_hbm, w_o), (q_hbm, q_all), (k_hbm, k_all), (v_hbm, v_all),
                (w_q_hbm, w_q), (w_k_hbm, w_k), (w_v_hbm, w_v),
            )
        )
    ]
    for load in loads:
        load.start()
    greet([to_core, to_x, to_y, *to_z])

    def piece(a):
        g = grads.at[a]
        return Piece(
            place,
            lambda kk: g.at[:, :, kk],
            lambda i, j, r: one.at[a, i, j, r],
            lambda h, i: two.at[a, h, i],
            lambda h: three.at[a, h],
            g.shape[3] // 2, lambda n: (psem.at[a, n], prem.at[a, n]), 48,
        )

    rows, width = tokens.shape
    heads = width // HEAD_DIM
    d_att[...] = d_mixed[...].astype(low)
    loads[0].wait()
    d_all[c] = against(d_att[...], w_o[...]).astype(low)
    head_of = lax.broadcasted_iota(jnp.int32, (128, width), 1) // HEAD_DIM
    chosen = jnp.where(head_of == lax.broadcasted_iota(jnp.int32, (128, width), 0), 1.0, 0.0).astype(low)
    terms = d_all[c].astype(full) * attended[...].astype(full)
    high = terms.astype(low)
    rest = (terms - high.astype(full)).astype(low)
    stat_col[0] = log_sum[...]
    stat_col[1] = against(high, chosen) + against(rest, chosen)
    stats[c, 0] = log_sum[...].T[0:16, :]
    stats[c, 1] = (against(chosen[0:16], high) + against(chosen[0:16], rest))
    core_copies = [
        start_copy(d_all.at[c], d_all.at[c], asem.at[0], arem.at[0], to_core),
        start_copy(stats.at[c], stats.at[c], tsem.at[0], trem.at[0], to_core),
    ]
    x_copies = [
        start_copy(d_all.at[c], d_all.at[c], asem.at[1], arem.at[1], to_x),
        start_copy(stats.at[c], stats.at[c], tsem.at[1], trem.at[1], to_x),
    ]
    near_place, far_place, opposite_place = others
    result_copies = [
        start_copy(results.at[1], result_got.at[0], rsem.at[0], rrem.at[0], to_z[0]),
        start_copy(results.at[3], result_got.at[1], rsem.at[1], rrem.at[1], to_z[0]),
    ]

    def block(a, h, ss, xx):
        whole = (eg_all, eu_all, ed_all)[a]
        half = whole.shape[-2] // 2
        part = pl.ds(h * half, half)
        return whole.at[ss, xx, k, part] if a < 2 else whole.at[:, ss, xx, k, part]

    def own_block(a, h):
        own = (eg_own, eu_own, ed_own)[a]
        return own.at[h] if a < 2 else own.at[:, h]

    def to_both_cores(a, h, n, src, spot):
        core_parts.append(start_copy(src, spot, csem.at[a, h, n], crem.at[a, h, n], to_core))

    core_parts, near, wide, kept = [], [], [], []
    parts = [(a, h) for a in range(3) for h in range(2)]

    def spread(own, buffer, first):
        halves, height, across = own.shape
        piece_width = across // 4
        for h in range(halves):
            for q in range(4):
                part = own[h, :, q * piece_width : (q + 1) * piece_width]
                buffer[q, pl.ds(h * height, height), first : first + piece_width] = part

    def to_nearest(buffer, got, number):
        return [
            start_copy(buffer.at[near_place], got.at[0], zsem.at[number, 0], zrem.at[number, 0], to_z[0]),
            start_copy(buffer.at[opposite_place], got.at[1], zsem.at[number, 1], zrem.at[number, 1], to_z[0]),
        ]

    def to_far(copies, buffer, got, number):
        for copy in copies:
            copy.wait()
        buffer[far_place] = (buffer[far_place].astype(full) + got[1].astype(full)).astype(low)
        return start_copy(buffer.at[far_place], got.at[2], zsem.at[number, 2], zrem.at[number, 2], to_z[1])

    def settled(copy, buffer, got):
        copy.wait()
        return buffer[e].astype(full) + got[0].astype(full) + got[2].astype(full)

    for a, h in parts:
        src, here = own_block(a, h), block(a, h, s, x)
        kept.append(pltpu.make_async_copy(src, here, lsem.at[a, h]))
        kept[-1].start()
        to_both_cores(a, h, 0, src, here)

    def put(a, first_factor, second_factor):
        grads[a] = outer_sum(first_factor, second_factor).astype(low).reshape(2, 2, 2, width // 8, width)
        piece(a).start(1)

    put(3, attended[...], d_att[...])
    for load in loads[1:]:
        load.wait()
    lane = lax.broadcasted_iota(jnp.int32, (rows, 128), 1)
    scale = HEAD_DIM**-0.5
    for total in (sum_q, sum_k, sum_v):
        total[...] = jnp.zeros_like(total)

    def inside(h, values):
        return jnp.where((lane // HEAD_DIM) == h, values, jnp.zeros_like(values))

    def columns(g):
        return pl.ds(pl.multiple_of(g * 128, 128), 128)

    def query_pair(g, carry):
        at = columns(g)
        q, d_out = q_all[c, :, at], d_all[c, :, at]
        sides = []
        for h in range(2):
            pick = lane == 2 * g + h
            sides.append(
                (
                    inside(h, q),
                    inside(h, d_out),
                    jnp.sum(jnp.where(pick, stat_col[0], 0.0), axis=-1, keepdims=True),
                    jnp.sum(jnp.where(pick, stat_col[1], 0.0), axis=-1, keepdims=True),
                )
            )
        for j in range(4):

            @pl.when(j <= c)
            def _(j=j):
                keys, values = k_all[j, :, at], v_all[j, :, at]
                terms = []
                for q_side, d_side, log_total, delta in sides:
                    weights = jnp.exp(against(q_side, keys) * scale - log_total)
                    d_scores = (weights * (against(d_side, values) - delta)).astype(low)
                    terms.append(jnp.dot(d_scores, keys, preferred_element_type=full))
                sum_q[:, at] += jnp.where(lane < HEAD_DIM, terms[0], terms[1])

        return carry

    for a, h in parts:
        src, here = own_block(a, h), block(a, h, s, x)
        near.append(start_copy(src, here, gsem.at[a, h, 0], grem.at[a, h, 0], (to_y, to_x)[h]))
    lax.fori_loop(0, width // 128, query_pair, 0)
    for a, h in parts:
        src, here = own_block(a, h), block(a, h, s, x)
        wide.append(start_copy(src, here, gsem.at[a, h, 1], grem.at[a, h, 1], (to_x, to_y)[h]))
    for copy in result_copies:
        copy.wait()
    far_sum[...] = (results[2].astype(full) + result_got[1].astype(full)).astype(low)
    result_copy = start_copy(far_sum, result_got.at[2], rsem.at[2], rrem.at[2], to_z[1])

    def key_side(j):
        @pl.when(j >= c)
        def _():
            def key_pair(g, carry):
                at = columns(g)
                keys, values = k_all[c, :, at], v_all[c, :, at]
                q, d_out = q_all[j, :, at], d_all[j, :, at]
                terms = []
                for h in range(2):
                    log_total = stats[j, 0, pl.ds(2 * g + h, 1), :]
                    delta = stats[j, 1, pl.ds(2 * g + h, 1), :]
                    weights = jnp.exp(against(inside(h, keys), q) * scale - log_total)
                    d_scores = (weights * (against(inside(h, values), d_out) - delta)).astype(low)
                    terms.append(
                        (
                            jnp.dot(d_scores, q, preferred_element_type=full),
                            jnp.dot(weights.astype(low), d_out, preferred_element_type=full),
                        )
                    )
                sum_k[:, at] += jnp.where(lane < HEAD_DIM, terms[0][0], terms[1][0])
                sum_v[:, at] += jnp.where(lane < HEAD_DIM, terms[0][1], terms[1][1])
                return carry

            lax.fori_loop(0, width // 128, key_pair, 0)

    def turned_back(total):
        parts = []
        for g in range(width // 128):
            part = total[:, g * 128 : (g + 1) * 128] * scale
            parts.append((part * cosine[c] - swapped(part) * sine[c]).astype(low))
        return jnp.concatenate(parts, axis=1)

    key_side(c)
    d_query = turned_back(sum_q)
    put(0, normed[...], d_query)
    d_normed = against(d_query, w_q[...])
    piece(3).finish(1)
    piece(3).start(2)
    for copy in core_copies:
        copy.wait()
    key_side(x * 2 + (1 - k))
    piece(0).finish(1)
    piece(0).start(2)
    for copy in x_copies:
        copy.wait()
    there = (1 - x) * 2 + k
    corner_copies = [
        start_copy(d_all.at[there], d_all.at[there], asem.at[2], arem.at[2], to_core),
        start_copy(stats.at[there], stats.at[there], tsem.at[2], trem.at[2], to_core),
    ]
    key_side(there)
    for i, (a, h) in enumerate(parts):
        near[i].wait()
        spot = block(a, h, (1 - s, s)[h], (x, 1 - x)[h])
        to_both_cores(a, h, 1, spot, spot)
    for copy in corner_copies:
        copy.wait()
    key_side((1 - x) * 2 + (1 - k))
    d_key = turned_back(sum_k)
    put(1, normed[...], d_key)
    d_value = sum_v[...].astype(low)
    put(2, normed[...], d_value)
    d_normed = d_normed + against(d_key, w_k[...]) + against(d_value, w_v[...])
    values = tokens[...].astype(full)
    inverse = lax.rsqrt(jnp.mean(values * values, axis=-1, keepdims=True) + 1e-06)
    unit = values * inverse
    misc_in[0:8, :] = small[0:8, :]
    misc_in[8:9, :] = jnp.sum(d_normed * unit, axis=0, keepdims=True)
    misc_in[9:10, :] = small[8:9, :]
    misc_in[10:16, :] = jnp.zeros((6, width), full)
    misc_copy = start_copy(misc_in, misc_got.at[0], msem.at[0], mrem.at[0], to_core)
    for a in (1, 2):
        piece(a).finish(1)
        piece(a).start(2)
    inner = d_normed * gain_one[...].reshape(1, width)
    mean = jnp.mean(inner * unit, axis=-1, keepdims=True)
    token_out[...] = d_mixed[...] + inverse * (inner - unit * mean)
    misc_copy.wait()
    misc_out[...] = misc_in[...] + misc_got[0]
    misc_copy = start_copy(misc_out, misc_got.at[1], msem.at[1], mrem.at[1], to_x)
    for a in (3, 0, 1, 2):
        piece(a).finish(2)
        piece(a).start(3)
    misc_copy.wait()
    misc_got[3] = misc_out[...] + misc_got[1]
    misc_copy = start_copy(misc_got.at[3], misc_got.at[2], msem.at[2], mrem.at[2], to_y)
    onward = []
    for a, h in parts:
        spot = block(a, h, (1 - s, s)[h], (x, 1 - x)[h])
        onward.append(start_copy(spot, spot, gsem.at[a, h, 2], grem.at[a, h, 2], (to_x, to_y)[h]))
    z_copies = []
    for number, pair in enumerate(((3, 0), (1, 2))):
        for i, a in enumerate(pair):
            piece(a).finish(3)
            spread(three.at[a], z_flat.at[number], i * (width // 4))
        z_copies.append(to_nearest(z_flat.at[number], got_flat.at[number], number))
    misc_copy.wait()
    misc_got[4] = misc_got[3] + misc_got[2]
    misc_copies = [
        start_copy(misc_got.at[4], misc_got.at[5 + i], msem.at[3 + i], mrem.at[3 + i], to_z[i]) for i in range(3)
    ]
    for i, (a, h) in enumerate(parts):
        wide[i].wait()
        spot = block(a, h, (s, 1 - s)[h], (1 - x, x)[h])
        to_both_cores(a, h, 2, spot, spot)
    for number in range(2):
        z_copies[number] = to_far(z_copies[number], z_flat.at[number], got_flat.at[number], number)

    result_copy.wait()
    total = mixed[...] + results[0].astype(full) + result_got[0].astype(full) + result_got[2].astype(full)
    output[...] = total.astype(low)
    for i, (a, h) in enumerate(parts):
        onward[i].wait()
        spot = block(a, h, 1 - s, 1 - x)
        to_both_cores(a, h, 3, spot, spot)
    for copy in misc_copies:
        copy.wait()
    sums = misc_got[4] + misc_got[5] + misc_got[6] + misc_got[7]
    one_out[...] = sums[8:9, :].reshape(width)
    two_out[...] = sums[9:10, :].reshape(width)
    mine = jnp.where(lax.broadcasted_iota(jnp.int32, (16, width), 0) == e, sums, 0.0)
    turned[...] = jnp.concatenate([mine, jnp.zeros((112, width), full)], axis=0).T
    high = router_out.shape[1]
    router_rows = turned[pl.ds(pl.multiple_of((s * 4 + c) * high, high), high), :]
    column = jnp.broadcast_to(jnp.sum(router_rows, axis=-1, keepdims=True), (high, 128))
    column = jnp.concatenate([column, jnp.zeros((128 - high, 128), full)], axis=0).T
    router_out[...] = column[0:1, 0:high]
    quarter = width // 4
    for number, targets in enumerate(((o_out, q_out), (k_out, v_out))):
        total = settled(z_copies[number], z_flat.at[number], got_flat.at[number])
        targets[0][...] = total[:, 0:quarter]
        targets[1][...] = total[:, quarter:]
    for copy in (*kept, *core_parts):
        copy.wait()


def back(expert_own, small, results, mixed, tokens, gain_one, d_mixed, kept, weights):
    low, full = jnp.bfloat16, jnp.float32
    dma = pltpu.SemaphoreType.DMA
    rows, width = mixed.shape
    ninth = width // 8
    hidden = expert_own[0].shape[2]
    tiles, unused, short, unused = expert_own[2].shape
    cosine, sine = (jnp.asarray(t).reshape(4, rows, 128) for t in place_tables(4 * rows))

    def vm(*shape, dtype=low):
        return pltpu.VMEM(shape, dtype)

    def out(*shape, dtype=low):
        return jax.ShapeDtypeStruct(shape, dtype)

    spec, anywhere = pl.BlockSpec(memory_space=pltpu.VMEM), pl.BlockSpec(memory_space=pl.ANY)
    out_shape = [
        out(2, 2, 2, ninth, hidden), out(2, 2, 2, ninth, hidden), out(tiles, 2, 2, 2, 2 * short, width),
        *[out(ninth, width // 4, dtype=full)] * 4, out(width, dtype=full), out(width, dtype=full),
        out(1, ninth, dtype=full), out(rows, width),
        out(rows, width, dtype=full),
    ]
    scratch = [
        vm(4, 2, 2, 2, ninth, width), vm(rows, width), vm(4, rows, width), vm(4, 2, 16, rows, dtype=full),
        vm(2, rows, 128, dtype=full), *[vm(rows, width, dtype=full)] * 3, vm(16, width, dtype=full),
        vm(16, width, dtype=full), vm(rows, width), vm(width, 128, dtype=full),
        dma((3,)), dma((3,)), dma((3,)), dma((3,)),
        vm(4, 2, 2, ninth, width), vm(4, 2, 2, ninth // 2, width), vm(4, 2, ninth // 2, width),
        vm(2, 4, ninth, width // 2),
        vm(2, 3, ninth, width // 2),
        vm(8, 16, width, dtype=full), vm(3, rows, width),
        vm(width, width), *[vm(4, rows, width)] * 3, *[vm(width, width)] * 3, dma((7,)),
        dma((3, 2)), *[dma((3, 2, 3))] * 2, *[dma((3, 2, 4))] * 2, *[dma((4, 5))] * 2, *[dma((2, 3))] * 2,
        dma((6,)), dma((6,)), dma((3,)), dma((3,)),
    ]
    attended, normed, q_all, k_all, v_all, log_sum = kept
    w_q, w_k, w_v, w_o = weights
    operands = (
        *expert_own, small, results, mixed, tokens, gain_one, d_mixed, attended, normed, log_sum, cosine, sine,
        w_o, q_all, k_all, v_all, w_q, w_k, w_v,
    )
    return pl.pallas_call(
        back_kernel,
        out_shape=out_shape,
        in_specs=[spec] * (len(operands) - 7) + [anywhere] * 7,
        out_specs=[anywhere] * 3 + [spec] * 9,
        scratch_shapes=scratch,
        compiler_params=pltpu.CompilerParams(
            collective_id=4, has_side_effects=True, vmem_limit_bytes=60 * 2**20
        ),
        name="back",
    )(*operands)


def finish_kernel(*refs):
    count = len(refs) // 2
    for i in range(3):
        refs[count + i][...] = refs[i][...].astype(jnp.float32)

    @pl.when(pl.program_id(0) == 0)
    def _():
        for i in range(3, count):
            refs[count + i][...] = refs[i][...]


def finish(expert_grads, others):
    steps = 4
    arrays = (*expert_grads, *others)

    def tile_of(a):
        return pl.BlockSpec((a.shape[0] // steps, a.shape[1]), lambda i: (i, 0))

    def all_of(a):
        return pl.BlockSpec(a.shape, lambda i: (0,) * a.ndim)

    specs = [tile_of(a) for a in expert_grads] + [all_of(a) for a in others]
    return pl.pallas_call(
        finish_kernel,
        out_shape=[jax.ShapeDtypeStruct(a.shape, jnp.float32) for a in expert_grads]
        + [jax.ShapeDtypeStruct(a.shape, a.dtype) for a in others],
        grid=(steps,),
        in_specs=specs,
        out_specs=specs,
        compiler_params=pltpu.CompilerParams(vmem_limit_bytes=60 * 2**20),
        name="finish",
    )(*arrays)


def per_device_dense(
    tokens,
    expert_ids,
    norm_one,
    w_query,
    w_key,
    w_value,
    w_out,
    norm_two,
    w_router,
    expert_gate,
    expert_up,
    expert_down,
    shared_gate,
    shared_up,
    shared_down,
    cotangent,
):
    upstream = cotangent[0]
    ids = expert_ids[0].T
    (
        q_all, k_all, v_all, upstream_all, named_all, normed, attended, mixed, second, log_sum,
    ) = front(
        tokens[0], upstream, ids, norm_one, norm_two, w_query, w_key, w_value, w_out
    )
    (
        results, d_mixed, small, eg_own, eu_own, ed_own, sg, su, sd,
    ) = ffn(
        second, mixed, upstream_all, named_all, w_router, norm_two,
        (expert_gate[0], expert_up[0], expert_down[0]), (shared_gate, shared_up, shared_down),
    )

    (
        eg, eu, ed, gq, gk, gv, go, grad_one, grad_two, router, output, grad_tokens,
    ) = back(
        (eg_own, eu_own, ed_own), small, results, mixed, tokens[0], norm_one, d_mixed,
        (attended, normed, q_all, k_all, v_all, log_sum), (w_query, w_key, w_value, w_out),
    )
    width = tokens.shape[2]
    (
        eg, eu, ed, output, grad_tokens, gq, gk, gv, go, grad_one, grad_two, router, sg, su, sd,
    ) = finish(
        (eg.reshape(width, -1), eu.reshape(width, -1), ed.reshape(-1, width)),
        (output, grad_tokens, gq, gk, gv, go, grad_one, grad_two, router, sg, su, sd),
    )
    return (
        output[None], grad_tokens[None], grad_one, gq, gk, gv, go, grad_two, router.T,
        eg[None], eu[None], ed[None], sg, su, sd.T,
    )


def fits(mesh):
    return dict(mesh.shape) == {"seq": 2, "ctx": 4, "exp": 4}


def solution(mesh):
    per_device = per_device_dense if fits(mesh) else per_device_slots
    in_specs = (
        P(("seq", "exp"), "ctx", None),
        P(("seq", "exp"), "ctx", None),
        P(),
        P(),
        P(),
        P(),
        P(),
        P(),
        P(),
        P("exp", None, None),
        P("exp", None, None),
        P("exp", None, None),
        P(),
        P(),
        P(),
        P(("seq", "exp"), "ctx", None),
    )
    out_specs = (
        P(("seq", "exp"), "ctx", None),
        P(("seq", "exp"), "ctx", None),
        P(),
        P(("seq", "ctx"), "exp"),
        P(("seq", "ctx"), "exp"),
        P(("seq", "ctx"), "exp"),
        P(("seq", "ctx"), "exp"),
        P(),
        P(("seq", "ctx"), "exp"),
        P("exp", None, None),
        P("exp", None, None),
        P("exp", None, None),
        P(("seq", "ctx"), "exp"),
        P(("seq", "ctx"), "exp"),
        P(("seq", "ctx"), "exp"),
    )
    return jax.shard_map(
        per_device, mesh=mesh, in_specs=in_specs, out_specs=out_specs, check_vma=False
    )
```
